32 devices in a mesh: grp: 8 (over y, x, core), fft: 4 (over z).
Axes of the slice: x: 2, y: 2, z: 4, core: 2. Of those that a mesh axis runs over, the one named last changes fastest.
Arguments:
- patches: bfloat16 [48, 16, 16, 2560], P('grp', 'fft'), may hold values from -6 to 6
- targets: bfloat16 [48, 16, 16, 256], P('grp', 'fft'), may hold values from -6 to 6
- grid_side: int32 [48], replicated, may hold values from 4 to 16, as said below
- dest_group: int32 [48], replicated, may hold values from 0 to 7, as said below
- embed_w: bfloat16 [2560, 1024], replicated, may hold values from -0.125 to 0.125
- embed_b: float32 [1024], replicated, may hold values from -3 to 3
- gain: float32 [1024], replicated, may hold values from 0.5 to 1.5
- spec_w: bfloat16 [2, 2, 8, 128, 128], replicated, may hold values from -0.375 to 0.375
- spec_b: float32 [2, 2, 8, 128], replicated, may hold values from -3 to 3
- head_w: bfloat16 [1024, 256], replicated, may hold values from -0.1875 to 0.1875
- head_b: float32 [256], replicated, may hold values from -3 to 3
Outputs:
- predictions: bfloat16 [48, 16, 16, 256], P('grp', 'fft')
- embed_grad: float32 [2560, 1024], P(('grp', 'fft'))
- embed_bias_grad: float32 [1024], replicated
- gain_grad: float32 [1024], replicated
- spec_w_grad: float32 [2, 2, 8, 128, 128], replicated
- spec_b_grad: float32 [2, 2, 8, 128], replicated
- head_grad: float32 [1024, 256], replicated
- head_bias_grad: float32 [256], replicated
The draws below stay inside these ranges and needn't reach their ends.
Inputs may be any that keep to these rules, and one draw needn't show every extreme that they name: `grid_side`: each entry is 16, 8 or 4, and 16 occurs in every draw. `dest_group`: every group index occurs exactly 6 times; the 6 samples held by one loader (indices q * 6 to q * 6 + 5) go to 6 different groups.
All inputs are finite; a program needn't handle non-finite values.
Results may differ from the reference program's by a relative error of at most 0.014.
The reference program's roundings to bfloat16 on the way count: a program that leaves them out, or rounds other values in their place, can miss the bound.
Values may be sent and summed in bfloat16 or wider, within the bound.
No kernel may reach another device: no remote copies, remote signals or barrier semaphores. Data moves between devices by JAX's collectives and lax.ppermute only.
A program may use at most 128 MiB of HBM per device.

```python
import jax
import jax.numpy as jnp
from jax import lax

D = 1024
NB = 8
BS = 128
PIN = 2560
POUT = 256
GM = 16
SLOTS = 6
SAMPLES = 48


def draw_grid_side(key, part):
    key = jax.random.fold_in(key, 11)
    level_key, forced_key = jax.random.split(key)
    levels = jax.random.randint(level_key, (SAMPLES,), 0, 3)
    forced = jax.random.randint(forced_key, (), 0, SAMPLES)
    levels = jnp.where(jnp.arange(SAMPLES) == forced, 0, levels).astype(jnp.int32)
    return jnp.right_shift(jnp.full((SAMPLES,), GM, jnp.int32), levels)


def draw_dest_group(key, part):
    key = jax.random.fold_in(key, 23)
    label_key, start_key, turn_key = jax.random.split(key, 3)
    groups = SAMPLES // SLOTS
    relabel = jax.random.permutation(label_key, groups)
    starts = jax.random.permutation(start_key, groups)
    turns = jax.random.randint(turn_key, (groups,), 0, SLOTS)
    loaders = jnp.arange(SAMPLES) // SLOTS
    places = (jnp.arange(SAMPLES) % SLOTS + turns[loaders]) % SLOTS
    return relabel[(starts[loaders] + places) % groups].astype(jnp.int32)


def raised(values, stream_key, source, target, shards_of, factor):
    def block_of(position):
        return (jnp.arange(values.shape[position]) // (values.shape[position] // shards_of)).reshape((-1,) + (1,) * (values.ndim - 1 - position))

    first = jax.random.permutation(stream_key, shards_of)[block_of(target)]
    other_side = (block_of(target) + shards_of // 2) % shards_of
    return jnp.where((block_of(source) == first) | (block_of(source) == other_side), factor * values, values)


def level_of(key, shape, pieces, smallest, largest):
    loudness = 1.0
    for position, parts in pieces:
        draws = jax.random.uniform(jax.random.fold_in(jax.random.fold_in(key, 6), position), (parts,), jnp.float32, smallest / len(pieces), largest / len(pieces))
        loudness = loudness * jnp.repeat(jnp.exp(draws), shape[position] // parts).reshape((-1,) + (1,) * (len(shape) - 1 - position))
    return loudness


def normal_values(stream_key, dims, width, limit, pieces=(), kind=jnp.bfloat16):
    entries = width * jax.random.normal(stream_key, dims, jnp.float32)
    if pieces:
        entries = entries * level_of(stream_key, dims, pieces, -0.22, 0.18)
    return jnp.clip(entries, -limit, limit).astype(kind)


def bell_draw_with(stream_key, extent, width, limit, shards, heavy, kind=jnp.bfloat16):
    entries = width * jax.random.normal(stream_key, extent, jnp.float32)
    if shards:
        entries = entries * level_of(stream_key, extent, shards, -0.22, 0.18)
    return jnp.clip(raised(entries, jax.random.fold_in(stream_key, 3), *heavy), -limit, limit).astype(kind)


def setup_inputs(seed: int = 0) -> dict:
    streams_of = jax.random.split(jax.random.key(seed), 12)
    return {
        "patches": bell_draw_with(streams_of[0], (SAMPLES, GM, GM, PIN), 1.0, 6.0, ((0, 8), (1, 4)), (0, 3, 8, 2.0)),
        "targets": normal_values(streams_of[1], (SAMPLES, GM, GM, POUT), 1.0, 6.0, ((0, 8), (1, 4))),
        "grid_side": draw_grid_side(jax.random.fold_in(streams_of[11], 71), 0),
        "dest_group": draw_dest_group(jax.random.fold_in(streams_of[11], 71), 0),
        "embed_w": normal_values(streams_of[4], (PIN, D), PIN ** -0.5, 0.125),
        "embed_b": normal_values(streams_of[5], (D,), 0.5, 3.0, (), jnp.float32),
        "gain": jnp.clip(1.0 + 0.1 * jax.random.normal(streams_of[6], (D,), jnp.float32), 0.5, 1.5),
        "spec_w": normal_values(streams_of[7], (2, 2, NB, BS, BS), (2 * BS) ** -0.5, 0.375),
        "spec_b": normal_values(streams_of[8], (2, 2, NB, BS), 0.5, 3.0, (), jnp.float32),
        "head_w": normal_values(streams_of[9], (D, POUT), D ** -0.5, 0.1875),
        "head_b": normal_values(streams_of[10], (POUT,), 0.5, 3.0, (), jnp.float32),
    }


EPSILON = 1e-05
SHRINK = 0.01
PRECISE = lax.Precision.HIGHEST

def to_half(values):
    return lax.optimization_barrier(values.astype(jnp.bfloat16))

def grid_valid(slot_edges, row_index, col_index):
    inside = (row_index[None, :, None] < slot_edges[:, None, None]) & (col_index[None, None, :] < slot_edges[:, None, None])
    return jnp.where(inside, 1.0, 0.0).astype(jnp.float32)

def slot_tables(slot_edges, grid_cells):
    positions = jnp.arange(grid_cells, dtype=jnp.int32)
    product = positions[None, :, None] * positions[None, None, :] % slot_edges[:, None, None]
    inside = (positions[None, :, None] < slot_edges[:, None, None]) & (positions[None, None, :] < slot_edges[:, None, None])
    edge_float = slot_edges.astype(jnp.float32)[:, None, None]
    angles = 2.0 * jnp.pi * product.astype(jnp.float32) / edge_float
    weights = jnp.where(inside, 1.0, 0.0).astype(jnp.float32) / jnp.sqrt(edge_float)
    return (jnp.cos(angles) * weights, jnp.sin(angles) * weights)

def embed_tokens(patch_grid, embed_w, embed_b, valid_mask):
    flat_rows = patch_grid.reshape(-1, patch_grid.shape[-1])
    mapped = jnp.dot(flat_rows, embed_w, preferred_element_type=jnp.float32) + embed_b
    mapped = mapped.reshape(valid_mask.shape + (embed_w.shape[1],)) * valid_mask[..., None]
    return to_half(mapped)

def normalize(embedded, gain):
    values = embedded.astype(jnp.float32)
    centered = values - lax.optimization_barrier(jnp.mean(values, axis=-1, keepdims=True))
    inv_std = lax.rsqrt(lax.optimization_barrier(jnp.mean(centered * centered, axis=-1, keepdims=True)) + EPSILON)
    unit_norm = centered * inv_std
    return (unit_norm, inv_std, to_half(unit_norm * gain))

def normalize_back(normed_grad, unit_norm, inv_std, gain):
    unit_grad = normed_grad * gain
    mean_grad = lax.optimization_barrier(jnp.mean(unit_grad, axis=-1, keepdims=True))
    mean_cross = lax.optimization_barrier(jnp.mean(unit_grad * unit_norm, axis=-1, keepdims=True))
    return inv_std * (unit_grad - mean_grad - unit_norm * mean_cross)

def column_transform(cosines, sines, normed):
    values = normed.astype(jnp.float32)
    real_part = jnp.einsum('skc,srcd->srkd', cosines, values, precision=PRECISE)
    imag_part = -jnp.einsum('skc,srcd->srkd', sines, values, precision=PRECISE)
    return to_half(jnp.stack([real_part, imag_part]))

def row_transform(cosines, sines, columns):
    values = columns.astype(jnp.float32)

    def contract(table, operand):
        return jnp.einsum('smr,srkd->smkd', table, operand, precision=PRECISE)
    real_part = contract(cosines, values[0]) + contract(sines, values[1])
    imag_part = contract(cosines, values[1]) - contract(sines, values[0])
    return to_half(jnp.stack([real_part, imag_part]))

def row_inverse(cosines, sines, filtered):

    def contract(table, operand):
        return jnp.einsum('srm,smkd->srkd', table, operand, precision=PRECISE)
    real_part = contract(cosines, filtered[0]) - contract(sines, filtered[1])
    imag_part = contract(cosines, filtered[1]) + contract(sines, filtered[0])
    return to_half(jnp.stack([real_part, imag_part]))

def column_inverse(cosines, sines, inverse):
    values = inverse.astype(jnp.float32)

    def contract(table, operand):
        return jnp.einsum('sck,srkd->srcd', table, operand, precision=PRECISE)
    return contract(cosines, values[0]) - contract(sines, values[1])

def column_inverse_back(cosines, sines, gradient):

    def contract(table, operand):
        return jnp.einsum('sck,srcd->srkd', table, operand, precision=PRECISE)
    return to_half(jnp.stack([contract(cosines, gradient), -contract(sines, gradient)]))

def row_inverse_back(cosines, sines, gradient):
    values = gradient.astype(jnp.float32)

    def contract(table, operand):
        return jnp.einsum('srm,srkd->smkd', table, operand, precision=PRECISE)
    real_part = contract(cosines, values[0]) + contract(sines, values[1])
    imag_part = contract(cosines, values[1]) - contract(sines, values[0])
    return jnp.stack([real_part, imag_part])

def row_transform_back(cosines, sines, gradient):

    def contract(table, operand):
        return jnp.einsum('smr,smkd->srkd', table, operand, precision=PRECISE)
    real_part = contract(cosines, gradient[0]) - contract(sines, gradient[1])
    imag_part = contract(sines, gradient[0]) + contract(cosines, gradient[1])
    return to_half(jnp.stack([real_part, imag_part]))

def column_transform_back(cosines, sines, gradient):
    values = gradient.astype(jnp.float32)

    def contract(table, operand):
        return jnp.einsum('skc,srkd->srcd', table, operand, precision=PRECISE)
    return contract(cosines, values[0]) - contract(sines, values[1])

def block_mult(left_side, weights):
    return jnp.einsum('pbc,bce->pbe', left_side.astype(jnp.float32), weights.astype(jnp.float32), precision=PRECISE)

def block_outer(left_side, gradient):
    return jnp.einsum('pbc,pbe->bce', left_side.astype(jnp.float32), gradient.astype(jnp.float32), precision=PRECISE)

def block_back(gradient, weights):
    return jnp.einsum('pbe,bce->pbc', gradient.astype(jnp.float32), weights.astype(jnp.float32), precision=PRECISE)

def complex_block(real_part, imag_part, weight_re, weight_im):
    return (block_mult(real_part, weight_re) - block_mult(imag_part, weight_im), block_mult(imag_part, weight_re) + block_mult(real_part, weight_im))

def spectral_mlp(spectrum, spec_w, spec_b):
    layer_one = complex_block(spectrum[0], spectrum[1], spec_w[0, 0], spec_w[0, 1])
    pre_one = jnp.stack([layer_one[0] + spec_b[0, 0], layer_one[1] + spec_b[0, 1]])
    hidden = to_half(jnp.maximum(pre_one, 0.0))
    layer_two = complex_block(hidden[0], hidden[1], spec_w[1, 0], spec_w[1, 1])
    pre_two = jnp.stack([layer_two[0] + spec_b[1, 0], layer_two[1] + spec_b[1, 1]])
    filtered = jnp.sign(pre_two) * jnp.maximum(jnp.abs(pre_two) - SHRINK, 0.0)
    return (pre_one, hidden, pre_two, filtered)

def layer_grads(inputs, gradient):
    weight_re = block_outer(inputs[0], gradient[0]) + block_outer(inputs[1], gradient[1])
    weight_im = block_outer(inputs[0], gradient[1]) - block_outer(inputs[1], gradient[0])
    return (jnp.stack([weight_re, weight_im]), lax.optimization_barrier(jnp.sum(gradient.astype(jnp.float32), axis=1)))

def input_grads(gradient, weight_re, weight_im):
    real_part = block_back(gradient[0], weight_re) + block_back(gradient[1], weight_im)
    imag_part = block_back(gradient[1], weight_re) - block_back(gradient[0], weight_im)
    return jnp.stack([real_part, imag_part])

def spectral_mlp_back(filtered_grad, spectrum, pre_one, hidden, pre_two, spec_w):
    two_grad = to_half(jnp.where(jnp.abs(pre_two) > SHRINK, filtered_grad, 0.0))
    weights_two, biases_two = layer_grads(hidden, two_grad)
    hidden_grad = input_grads(two_grad, spec_w[1, 0], spec_w[1, 1])
    one_grad = to_half(jnp.where(pre_one > 0.0, hidden_grad, 0.0))
    weights_one, biases_one = layer_grads(spectrum, one_grad)
    spectrum_grad = input_grads(one_grad, spec_w[0, 0], spec_w[0, 1])
    return (spectrum_grad, jnp.stack([weights_one, weights_two]), jnp.stack([biases_one, biases_two]))

def head_pass(embedded, normed, mixed, valid_mask, head_w, head_b, target_grid, loss_scale):
    updated = to_half(embedded.astype(jnp.float32) + normed.astype(jnp.float32) + mixed)
    flat_rows = updated.reshape(-1, updated.shape[-1])
    output = jnp.dot(flat_rows, head_w, preferred_element_type=jnp.float32) + head_b
    output = output.reshape(valid_mask.shape + (head_w.shape[1],)) * valid_mask[..., None]
    residual_grad = to_half(loss_scale[:, None, None, None] * valid_mask[..., None] * (output - target_grid.astype(jnp.float32)))
    return (updated, output.astype(jnp.bfloat16), residual_grad)

def head_back(updated, residual_grad, head_w):
    flat_up = updated.reshape(-1, updated.shape[-1])
    flat_res = residual_grad.reshape(-1, residual_grad.shape[-1])
    head_grad = jnp.dot(flat_up.T, flat_res, preferred_element_type=jnp.float32)
    bias_grad = lax.optimization_barrier(jnp.sum(flat_res.astype(jnp.float32), axis=0))
    updated_grad = jnp.dot(flat_res, head_w.T, preferred_element_type=jnp.float32)
    return (head_grad, bias_grad, to_half(updated_grad.reshape(updated.shape)))

def embedded_back(normed_spec_grad, updated_grad, unit_norm, inv_std, gain, valid_mask):
    direct = updated_grad.astype(jnp.float32)
    normed_grad = normed_spec_grad + direct
    gain_grad = lax.optimization_barrier(jnp.sum(normed_grad * unit_norm, axis=(0, 1, 2)))
    input_grad = normalize_back(normed_grad, unit_norm, inv_std, gain)
    return (gain_grad, to_half((input_grad + direct) * valid_mask[..., None]))

def sample_pass(patch_grid, target_grid, grid_edge, embed_w, embed_b, gain, spec_w, spec_b, head_w, head_b):
    slot_edges = grid_edge[None]
    positions = jnp.arange(GM, dtype=jnp.int32)
    valid_mask = grid_valid(slot_edges, positions, positions)
    cosines, sines = slot_tables(slot_edges, GM)
    embedded = embed_tokens(patch_grid[None], embed_w, embed_b, valid_mask)
    unit_norm, inv_std, normed = normalize(embedded, gain)
    columns = column_transform(cosines, sines, normed)
    spectrum = row_transform(cosines, sines, columns)
    grid_shape = spectrum.shape
    flat_spectrum = spectrum.reshape(2, -1, NB, BS)
    pre_one, hidden, pre_two, filtered = spectral_mlp(flat_spectrum, spec_w, spec_b)
    inverse = row_inverse(cosines, sines, filtered.reshape(grid_shape))
    mixed = column_inverse(cosines, sines, inverse)
    loss_scale = 2.0 / (slot_edges.astype(jnp.float32) * jnp.sqrt(jnp.float32(SAMPLES)))
    updated, predicted, residual_grad = head_pass(embedded, normed, mixed, valid_mask, head_w, head_b, target_grid[None], loss_scale)
    head_grad, head_bias_grad, updated_grad = head_back(updated, residual_grad, head_w)
    inverse_grad = column_inverse_back(cosines, sines, updated_grad.astype(jnp.float32))
    filtered_grad = row_inverse_back(cosines, sines, inverse_grad)
    spectrum_grad, spec_w_grad, spec_b_grad = spectral_mlp_back(filtered_grad.reshape(2, -1, NB, BS), flat_spectrum, pre_one, hidden, pre_two, spec_w)
    columns_grad = row_transform_back(cosines, sines, spectrum_grad.reshape(grid_shape))
    normed_spec_grad = column_transform_back(cosines, sines, columns_grad)
    gain_grad, embedded_grad = embedded_back(normed_spec_grad, updated_grad, unit_norm, inv_std, gain, valid_mask)
    flat_patches = patch_grid.reshape(-1, PIN)
    flat_grads = embedded_grad.reshape(-1, D)
    embed_grad = jnp.dot(flat_patches.T, flat_grads, preferred_element_type=jnp.float32)
    embed_bias_grad = lax.optimization_barrier(jnp.sum(flat_grads.astype(jnp.float32), axis=0))
    return (predicted[0], (embed_grad, embed_bias_grad, gain_grad, spec_w_grad, spec_b_grad, head_grad, head_bias_grad))

def reference(patches, targets, grid_side, dest_group, embed_w, embed_b, gain, spec_w, spec_b, head_w, head_b):

    def one_sample(totals, item):
        patch_grid, target_grid, grid_edge = item
        predicted, grads = sample_pass(patch_grid, target_grid, grid_edge, embed_w, embed_b, gain, spec_w, spec_b, head_w, head_b)
        return (jax.tree.map(jnp.add, totals, grads), predicted)
    zeros_start = (jnp.zeros((PIN, D), jnp.float32), jnp.zeros((D,), jnp.float32), jnp.zeros((D,), jnp.float32), jnp.zeros((2, 2, NB, BS, BS), jnp.float32), jnp.zeros((2, 2, NB, BS), jnp.float32), jnp.zeros((D, POUT), jnp.float32), jnp.zeros((POUT,), jnp.float32))
    totals, predicted = lax.scan(one_sample, zeros_start, (patches, targets, grid_side))
    slot_order = jnp.argsort(dest_group, stable=True).astype(jnp.int32)
    predictions = jnp.take(predicted, slot_order, axis=0)
    return (predictions, totals[0], totals[1], totals[2], totals[3], totals[4], totals[5], totals[6])
```

```python
import jax
import jax.numpy as jnp
import ml_dtypes
import numpy as np
from jax import lax
from jax.experimental import pallas as pl
from jax.experimental.pallas import tpu as pltpu
from jax.sharding import PartitionSpec as P

EPSILON = 1e-05
SHRINK = 0.01
CHUNKS = 2
VMEM_BYTES = 48 * 1024 * 1024
HALF = jnp.bfloat16
FULL = jnp.float32


def dft_tables(cells):
    levels = []
    for side in (cells, cells // 2, cells // 4):
        k = np.arange(cells)
        inside = (k < side).astype(np.float64)
        keep = inside[:, None] * inside[None, :]
        angle = 2.0 * np.pi * ((k[:, None] * k[None, :]) % side) / side
        one = np.exp(-1j * angle) * keep / np.sqrt(side)
        two = np.kron(one, one)
        levels.append(np.concatenate([two.real, two.imag], axis=0))
    table = np.stack(levels)
    table[np.abs(table) < 1e-12] = 0.0
    high = table.astype(np.float32).astype(ml_dtypes.bfloat16)
    low = (table - high.astype(np.float64)).astype(np.float32).astype(ml_dtypes.bfloat16)
    size = cells * cells

    def back(values):
        return np.concatenate([values[:, :size], values[:, size:]], axis=2)

    return high, low, back(high), back(low)


def dot(left, right):
    return jnp.dot(left, right, preferred_element_type=FULL)


def dot_tn(left, right):
    return lax.dot_general(left, right, (((0,), (0,)), ((), ())), preferred_element_type=FULL)


def dot_nt(left, right):
    return lax.dot_general(left, right, (((1,), (1,)), ((), ())), preferred_element_type=FULL)


def params():
    return pltpu.CompilerParams(vmem_limit_bytes=VMEM_BYTES)


def token_sides(scal_ref, first, count, per_sample, cells):
    token = lax.broadcasted_iota(jnp.int32, (count * per_sample, 1), 0)
    sample = token // per_sample
    side = jnp.zeros_like(token)
    for i in range(count):
        side = jnp.where(sample == i, scal_ref[1 + first + i], side)
    row = scal_ref[0] + (token % per_sample) // cells
    col = token % cells
    valid = jnp.where((row < side) & (col < side), 1.0, 0.0).astype(FULL)
    return side, valid


def layer_norm(values):
    centered = values - jnp.mean(values, axis=-1, keepdims=True)
    inv_std = lax.rsqrt(jnp.mean(centered * centered, axis=-1, keepdims=True) + EPSILON)
    return centered * inv_std, inv_std


def gather_features(ref, rows):
    parts = [ref[z].reshape(rows, ref.shape[-1]) for z in range(ref.shape[0])]
    return jnp.concatenate(parts, axis=1)


def embed_chunk(scal, patches, embed_w, embed_b, gain, first, count, per_sample, cells, shards):
    rows = count * per_sample
    depth, width = embed_w.shape
    share = width // shards
    steps = 4
    tile = depth // steps

    def body(scal_ref, x_ref, w_ref, b_ref, gain_ref, emb_ref, out_ref, acc):
        step = pl.program_id(0)
        part = dot(x_ref[...], w_ref[...])

        @pl.when(step == 0)
        def _():
            acc[...] = part

        @pl.when(step > 0)
        def _():
            acc[...] += part

        @pl.when(step == steps - 1)
        def _():
            _, valid = token_sides(scal_ref, first, count, per_sample, cells)
            embedded = ((acc[...] + b_ref[...]) * valid).astype(HALF)
            emb_ref[...] = embedded
            unit, _ = layer_norm(embedded.astype(FULL))
            normed = (unit * gain_ref[...]).astype(HALF)
            for z in range(shards):
                out_ref[z] = normed[:, z * share : (z + 1) * share].reshape(count, per_sample, share)

    at = first // count
    return pl.pallas_call(
        body,
        grid_spec=pltpu.PrefetchScalarGridSpec(
            num_scalar_prefetch=1,
            grid=(steps,),
            in_specs=[
                pl.BlockSpec((rows, tile), lambda k, s: (at, k)),
                pl.BlockSpec((tile, width), lambda k, s: (k, 0)),
                pl.BlockSpec((1, width), lambda k, s: (0, 0)),
                pl.BlockSpec((1, width), lambda k, s: (0, 0)),
            ],
            out_specs=[
                pl.BlockSpec((rows, width), lambda k, s: (0, 0)),
                pl.BlockSpec((shards, count, per_sample, share), lambda k, s: (0, 0, 0, 0)),
            ],
            scratch_shapes=[pltpu.VMEM((rows, width), FULL)],
        ),
        out_shape=[
            jax.ShapeDtypeStruct((rows, width), HALF),
            jax.ShapeDtypeStruct((shards, count, per_sample, share), HALF),
        ],
        compiler_params=params(),
        cost_estimate=pl.CostEstimate(
            flops=2 * rows * depth * width, bytes_accessed=2 * depth * (rows + width), transcendentals=0
        ),
        name="embed",
    )(scal, patches, embed_w, embed_b, gain)


def to_blocks(values, blocks, width):
    half = values.shape[0] // 2
    return [
        jnp.concatenate(
            [values[:half, b * width : (b + 1) * width], values[half:, b * width : (b + 1) * width]], axis=1
        )
        for b in range(blocks)
    ]


def from_blocks(parts, width):
    real = jnp.concatenate([p[:, :width] for p in parts], axis=1)
    imag = jnp.concatenate([p[:, width:] for p in parts], axis=1)
    return jnp.concatenate([real, imag], axis=0)


def inverse_table(high_ref, low_ref, values):
    top = values.astype(HALF)
    rest = (values - top.astype(FULL)).astype(HALF)
    return dot(high_ref[0], top) + (dot(low_ref[0], top) + dot(high_ref[0], rest))


def level_specs(first, size):
    forward = pl.BlockSpec((1, 2 * size, size), lambda i, s: (s[1 + first + i], 0, 0))
    backward = pl.BlockSpec((1, size, 2 * size), lambda i, s: (s[1 + first + i], 0, 0))
    return [forward, forward, backward, backward]


def spectral_chunk(scal, tables, moved, weights, biases, first):
    shards, count, per_sample, share = moved.shape
    size = shards * per_sample
    blocks, wide = weights.shape[1], weights.shape[2]
    width = wide // 2

    def body(s_ref, th, tl, bh, bl, x_ref, w_ref, b_ref, out_ref, spec_ref, hid_ref, fil_ref):
        grid = jnp.concatenate([x_ref[z, 0] for z in range(shards)], axis=0)
        spectrum = (dot(th[0], grid) + dot(tl[0], grid)).astype(HALF)
        kept = []
        for b, entry in enumerate(to_blocks(spectrum, blocks, width)):
            spec_ref[0, b] = entry
            pre_one = dot(entry, w_ref[0, b]) + b_ref[0, b : b + 1]
            hidden = jnp.maximum(pre_one, 0.0).astype(HALF)
            hid_ref[0, b] = hidden
            pre_two = dot(hidden, w_ref[1, b]) + b_ref[1, b : b + 1]
            filtered = jnp.where(
                pre_two > SHRINK, pre_two - SHRINK, jnp.where(pre_two < -SHRINK, pre_two + SHRINK, 0.0)
            )
            fil_ref[0, b] = filtered.astype(HALF)
            kept.append(filtered)
        mixed = inverse_table(bh, bl, from_blocks(kept, width)).astype(HALF)
        for z in range(shards):
            out_ref[z, 0] = mixed[z * per_sample : (z + 1) * per_sample]

    grid_block = pl.BlockSpec((shards, 1, per_sample, share), lambda i, s: (0, i, 0, 0))
    saved = pl.BlockSpec((1, blocks, size, wide), lambda i, s: (i, 0, 0, 0))
    saved_shape = jax.ShapeDtypeStruct((count, blocks, size, wide), HALF)
    return pl.pallas_call(
        body,
        grid_spec=pltpu.PrefetchScalarGridSpec(
            num_scalar_prefetch=1,
            grid=(count,),
            in_specs=level_specs(first, size)
            + [
                grid_block,
                pl.BlockSpec(weights.shape, lambda i, s: (0, 0, 0, 0)),
                pl.BlockSpec(biases.shape, lambda i, s: (0, 0, 0)),
            ],
            out_specs=[grid_block, saved, saved, saved],
        ),
        out_shape=[jax.ShapeDtypeStruct(moved.shape, HALF), saved_shape, saved_shape, saved_shape],
        compiler_params=params(),
        cost_estimate=pl.CostEstimate(
            flops=count * size * share * size * 20, bytes_accessed=count * size * share * 16, transcendentals=0
        ),
        name="spectral",
    )(scal[1], *tables, moved, weights, biases)


def head_chunk(scal, embedded, gain, mixed, targets, head_w, head_b, first, samples, cells):
    shards, count, per_sample, share = mixed.shape
    rows = count * per_sample
    width, outs = head_w.shape
    at = first // count
    scale_root = float(np.sqrt(np.float32(samples)))

    def body(scal_ref, emb_ref, gain_ref, mix_ref, tgt_ref, w_ref, b_ref, pred_ref, res_ref, grad_ref, bias_ref):
        side, valid = token_sides(scal_ref, first, count, per_sample, cells)
        embedded = emb_ref[...].astype(FULL)
        unit, _ = layer_norm(embedded)
        normed = (unit * gain_ref[...]).astype(HALF)
        mixed = gather_features(mix_ref, rows)
        updated = (embedded + normed.astype(FULL) + mixed.astype(FULL)).astype(HALF)
        output = (dot(updated, w_ref[...]) + b_ref[...]) * valid
        pred_ref[...] = output.astype(HALF)
        scale = 2.0 / (side.astype(FULL) * scale_root)
        residual = (scale * valid * (output - tgt_ref[...].astype(FULL))).astype(HALF)
        res_ref[...] = residual
        grad_ref[...] = dot_tn(updated, residual)
        total = jnp.sum(residual.astype(FULL), axis=0, keepdims=True)
        bias_ref[...] = jnp.broadcast_to(total, bias_ref.shape)

    def whole(shape):
        return pl.BlockSpec(shape, lambda i, s: (0,) * len(shape))

    return pl.pallas_call(
        body,
        grid_spec=pltpu.PrefetchScalarGridSpec(
            num_scalar_prefetch=1,
            grid=(1,),
            in_specs=[
                whole((rows, width)),
                whole((1, width)),
                whole(mixed.shape),
                pl.BlockSpec((rows, outs), lambda i, s: (at, 0)),
                whole((width, outs)),
                whole((1, outs)),
            ],
            out_specs=[whole((rows, outs)), whole((rows, outs)), whole((width, outs)), whole((8, outs))],
        ),
        out_shape=[
            jax.ShapeDtypeStruct((rows, outs), HALF),
            jax.ShapeDtypeStruct((rows, outs), HALF),
            jax.ShapeDtypeStruct((width, outs), FULL),
            jax.ShapeDtypeStruct((8, outs), FULL),
        ],
        compiler_params=params(),
        cost_estimate=pl.CostEstimate(
            flops=4 * rows * width * outs, bytes_accessed=rows * width * 4 + width * outs * 6, transcendentals=0
        ),
        name="head",
    )(scal, embedded, gain, mixed, targets, head_w, head_b)


def spectral_back_chunk(scal, tables, residual, head_w, weights_t, spectrum, hidden, filtered, first):
    shards, count, per_sample, outs = residual.shape
    size = shards * per_sample
    blocks, wide = weights_t.shape[1], weights_t.shape[2]
    width = wide // 2
    share = blocks * width

    def body(s_ref, th, tl, bh, bl, r_ref, h_ref, w_ref, spec_ref, hid_ref, fil_ref, out_ref, grad_ref, bias_ref):
        @pl.when(pl.program_id(0) == 0)
        def _():
            grad_ref[...] = jnp.zeros_like(grad_ref)
            bias_ref[...] = jnp.zeros_like(bias_ref)

        residual = jnp.concatenate([r_ref[z, 0] for z in range(shards)], axis=0)
        updated_grad = dot_nt(residual, h_ref[...]).astype(HALF)
        filtered_grad = dot(th[0], updated_grad) + dot(tl[0], updated_grad)
        kept = []
        for b, entry in enumerate(to_blocks(filtered_grad, blocks, width)):
            two_grad = jnp.where(fil_ref[0, b].astype(FULL) != 0.0, entry, 0.0).astype(HALF)
            hidden = hid_ref[0, b]
            grad_ref[1, b] += dot_tn(hidden, two_grad)
            bias_ref[1, b : b + 1] += jnp.sum(two_grad.astype(FULL), axis=0, keepdims=True)
            hidden_grad = dot(two_grad, w_ref[1, b])
            one_grad = jnp.where(hidden.astype(FULL) > 0.0, hidden_grad, 0.0).astype(HALF)
            grad_ref[0, b] += dot_tn(spec_ref[0, b], one_grad)
            bias_ref[0, b : b + 1] += jnp.sum(one_grad.astype(FULL), axis=0, keepdims=True)
            kept.append(dot(one_grad, w_ref[0, b]))
        grad = inverse_table(bh, bl, from_blocks(kept, width)).astype(HALF)
        for z in range(shards):
            out_ref[z, 0] = grad[z * per_sample : (z + 1) * per_sample]

    saved = pl.BlockSpec((1, blocks, size, wide), lambda i, s: (i, 0, 0, 0))
    return pl.pallas_call(
        body,
        grid_spec=pltpu.PrefetchScalarGridSpec(
            num_scalar_prefetch=1,
            grid=(count,),
            in_specs=level_specs(first, size)
            + [
                pl.BlockSpec((shards, 1, per_sample, outs), lambda i, s: (0, i, 0, 0)),
                pl.BlockSpec((share, outs), lambda i, s: (s[0], 0)),
                pl.BlockSpec(weights_t.shape, lambda i, s: (0, 0, 0, 0)),
                saved,
                saved,
                saved,
            ],
            out_specs=[
                pl.BlockSpec((shards, 1, per_sample, share), lambda i, s: (0, i, 0, 0)),
                pl.BlockSpec((2, blocks, wide, wide), lambda i, s: (0, 0, 0, 0)),
                pl.BlockSpec((2, blocks, wide), lambda i, s: (0, 0, 0)),
            ],
        ),
        out_shape=[
            jax.ShapeDtypeStruct((shards, count, per_sample, share), HALF),
            jax.ShapeDtypeStruct((2, blocks, wide, wide), FULL),
            jax.ShapeDtypeStruct((2, blocks, wide), FULL),
        ],
        compiler_params=params(),
        cost_estimate=pl.CostEstimate(
            flops=count * size * share * size * 24, bytes_accessed=count * size * share * 16, transcendentals=0
        ),
        name="spectral_back",
    )(scal[1], *tables, residual, head_w, weights_t, spectrum, hidden, filtered)


def embedded_back_chunk(scal, embedded, residual, head_w, gain, spec_grad, first, cells):
    shards, count, per_sample, share = spec_grad.shape
    rows = count * per_sample
    width, outs = head_w.shape

    def body(scal_ref, emb_ref, res_ref, w_ref, gain_ref, grad_ref, out_ref, sums_ref):
        _, valid = token_sides(scal_ref, first, count, per_sample, cells)
        unit, inv_std = layer_norm(emb_ref[...].astype(FULL))
        direct = dot_nt(res_ref[...], w_ref[...]).astype(HALF).astype(FULL)
        normed_grad = gather_features(grad_ref, rows).astype(FULL) + direct
        gain_grad = jnp.sum(normed_grad * unit, axis=0, keepdims=True)
        unit_grad = normed_grad * gain_ref[...]
        mean_grad = jnp.mean(unit_grad, axis=-1, keepdims=True)
        mean_cross = jnp.mean(unit_grad * unit, axis=-1, keepdims=True)
        input_grad = inv_std * (unit_grad - mean_grad - unit * mean_cross)
        result = ((input_grad + direct) * valid).astype(HALF)
        out_ref[...] = result
        bias_grad = jnp.sum(result.astype(FULL), axis=0, keepdims=True)
        sums_ref[0:4] = jnp.broadcast_to(gain_grad, (4, width))
        sums_ref[4:8] = jnp.broadcast_to(bias_grad, (4, width))

    def whole(shape):
        return pl.BlockSpec(shape, lambda i, s: (0,) * len(shape))

    return pl.pallas_call(
        body,
        grid_spec=pltpu.PrefetchScalarGridSpec(
            num_scalar_prefetch=1,
            grid=(1,),
            in_specs=[
                whole((rows, width)),
                whole((rows, outs)),
                whole((width, outs)),
                whole((1, width)),
                whole(spec_grad.shape),
            ],
            out_specs=[whole((rows, width)), whole((8, width))],
        ),
        out_shape=[jax.ShapeDtypeStruct((rows, width), HALF), jax.ShapeDtypeStruct((8, width), FULL)],
        compiler_params=params(),
        cost_estimate=pl.CostEstimate(
            flops=2 * rows * width * outs, bytes_accessed=rows * width * 6, transcendentals=0
        ),
        name="embedded_back",
    )(scal, embedded, residual, head_w, gain, spec_grad)


def embed_grad_parts(group_at, patches, grads, groups):
    tokens, depth = patches.shape
    width = grads[0].shape[1]
    block = depth // groups
    tile = 256
    piece = int(np.gcd(tile, block))
    per_block = block // piece
    count = len(grads)

    def body(at_ref, x_ref, *refs):
        grad_refs, (send_ref, keep_ref) = refs[:count], refs[count:]
        total, row = None, 0
        for ref in grad_refs:
            part = dot_tn(x_ref[row : row + ref.shape[0]], ref[...])
            total = part if total is None else total + part
            row += ref.shape[0]
        total = total.astype(HALF)
        for i in range(tile // piece):
            place = pl.program_id(0) * (tile // piece) + i
            relative = jnp.bitwise_xor(place // per_block, at_ref[0])
            at = relative // 2
            rows = pl.ds(pl.multiple_of((place % per_block) * piece, piece), piece)
            values = total[i * piece : (i + 1) * piece]

            @pl.when(relative % 2 == 1)
            def _(at=at, rows=rows, values=values):
                send_ref[at, rows] = values

            @pl.when(relative % 2 == 0)
            def _(at=at, rows=rows, values=values):
                keep_ref[at, rows] = values

    shape = (groups // 2, block, width)
    out = pl.BlockSpec(shape, lambda i, s: (0, 0, 0))
    return pl.pallas_call(
        body,
        grid_spec=pltpu.PrefetchScalarGridSpec(
            num_scalar_prefetch=1,
            grid=(depth // tile,),
            in_specs=[pl.BlockSpec((tokens, tile), lambda i, s: (0, i))]
            + [pl.BlockSpec(g.shape, lambda i, s: (0, 0)) for g in grads],
            out_specs=[out, out],
        ),
        out_shape=[jax.ShapeDtypeStruct(shape, HALF)] * 2,
        compiler_params=params(),
        cost_estimate=pl.CostEstimate(
            flops=2 * tokens * depth * width, bytes_accessed=depth * (tokens + width) * 2, transcendentals=0
        ),
        name="embed_grad",
    )(group_at, patches, *grads)


def swap_bit(values, bit, groups):
    return lax.ppermute(values, "grp", [(g, g ^ (1 << bit)) for g in range(groups)])


def add_half(left, right):
    return (left.astype(FULL) + right.astype(FULL)).astype(HALF)


def scatter_sum(send, keep, groups):
    bits = groups.bit_length() - 1
    shards = lax.axis_size("fft")
    total = add_half(keep, swap_bit(send, 0, groups))
    block, width = total.shape[1:]
    total = total.reshape((2,) * (bits - 1) + (block, width))
    done = []
    for turn in range(2):
        part = total[..., turn * (width // 2) : (turn + 1) * (width // 2)]
        left = list(range(1, bits))
        order = list(left) if turn == 0 else left[::-1]
        for bit in order:
            axis = len(left) - 1 - left.index(bit)
            left.remove(bit)
            moving = lax.index_in_dim(part, 1, axis, keepdims=False)
            staying = lax.index_in_dim(part, 0, axis, keepdims=False)
            part = add_half(staying, swap_bit(moving, bit, groups))
        done.append(part)
    part = jnp.concatenate(done, axis=-1).reshape(shards, block // shards, width)
    moved = lax.all_to_all(part, "fft", split_axis=0, concat_axis=0, tiled=True)
    return jnp.sum(moved.astype(FULL), axis=0)


def across(values):
    return lax.all_to_all(values, "fft", split_axis=0, concat_axis=0, tiled=True)


def route_predictions(predicted, dest_group, group_at, groups, slot_count):
    own_dest = lax.dynamic_slice_in_dim(dest_group, group_at * slot_count, slot_count)
    matches = own_dest[None, :] == jnp.arange(groups, dtype=jnp.int32)[:, None]
    chosen = jnp.sum(jnp.where(matches, jnp.arange(slot_count, dtype=jnp.int32)[None, :], 0), axis=1)
    outgoing = jnp.take(predicted, chosen, axis=0)
    moved = lax.all_to_all(outgoing, "grp", split_axis=0, concat_axis=0, tiled=True)
    slot_order = jnp.argsort(dest_group, stable=True)
    slot_samples = lax.dynamic_slice_in_dim(slot_order, group_at * slot_count, slot_count)
    return jnp.take(moved, slot_samples // slot_count, axis=0)


def on_device(
    patches, targets, grid_side, dest_group, embed_w, embed_b, gain, spec_w, spec_b, head_w, head_b
):
    slot_count, row_count, cells, depth = patches.shape
    samples = dest_group.shape[0]
    groups = lax.axis_size("grp")
    shards = lax.axis_size("fft")
    group_at = lax.axis_index("grp")
    shard_at = lax.axis_index("fft")
    outs = targets.shape[-1]
    width = embed_w.shape[1]
    blocks = spec_w.shape[2] // shards
    per_sample = row_count * cells
    count = slot_count // CHUNKS
    firsts = [c * count for c in range(CHUNKS)]

    sides = lax.dynamic_slice_in_dim(grid_side, group_at * slot_count, slot_count)
    level = jnp.where(sides == cells, 0, jnp.where(sides == cells // 2, 1, 2)).astype(jnp.int32)
    row_scal = jnp.concatenate([jnp.reshape(shard_at * row_count, (1,)).astype(jnp.int32), sides])
    level_scal = jnp.concatenate([jnp.reshape(shard_at, (1,)).astype(jnp.int32), level])
    tables = [jnp.asarray(t) for t in dft_tables(cells)]
    both = (row_scal, level_scal)
    flat_patches = patches.reshape(-1, depth)
    flat_targets = targets.reshape(-1, outs)
    gain_row, embed_b_row, head_b_row = gain[None], embed_b[None], head_b[None]

    own_w = lax.dynamic_slice_in_dim(spec_w, shard_at * blocks, blocks, axis=2)
    real, imag = own_w[:, 0], own_w[:, 1]
    weights = jnp.concatenate(
        [jnp.concatenate([real, imag], axis=-1), jnp.concatenate([-imag, real], axis=-1)], axis=-2
    )
    weights_t = jnp.swapaxes(weights, -1, -2)
    own_b = lax.dynamic_slice_in_dim(spec_b, shard_at * blocks, blocks, axis=2)
    biases = jnp.concatenate([own_b[:, 0], own_b[:, 1]], axis=-1)

    embedded, moved = [], []
    for first in firsts:
        emb, normed = embed_chunk(
            row_scal, flat_patches, embed_w, embed_b_row, gain_row, first, count, per_sample, cells, shards
        )
        embedded.append(emb)
        moved.append(across(normed))
    mixed, saved = [], []
    for first, values in zip(firsts, moved):
        out, *rest = spectral_chunk(both, tables, values, weights, biases, first)
        mixed.append(across(out))
        saved.append(rest)
    predicted, residual, head_grads, head_sums, gathered = [], [], [], [], []
    for first, emb, mix in zip(firsts, embedded, mixed):
        pred, res, grad, sums = head_chunk(
            row_scal, emb, gain_row, mix, flat_targets, head_w, head_b_row, first, samples, cells
        )
        predicted.append(pred)
        residual.append(res)
        head_grads.append(grad)
        head_sums.append(sums[0])
        gathered.append(lax.all_gather(res.reshape(count, per_sample, outs), "fft"))
    spec_back, weight_sums, bias_sums = [], [], []
    for first, res, rest in zip(firsts, gathered, saved):
        back, grad, sums = spectral_back_chunk(both, tables, res, head_w, weights_t, *rest, first)
        spec_back.append(across(back))
        weight_sums.append(grad)
        bias_sums.append(sums)
    embedded_grads, row_sums = [], []
    for first, emb, res, back in zip(firsts, embedded, residual, spec_back):
        grad, sums = embedded_back_chunk(row_scal, emb, res, head_w, gain_row, back, first, cells)
        embedded_grads.append(grad)
        row_sums.append(sums)
    send, keep = embed_grad_parts(
        jnp.reshape(group_at, (1,)).astype(jnp.int32), flat_patches, embedded_grads, groups
    )
    embed_grad = scatter_sum(send, keep, groups)

    predictions = route_predictions(
        jnp.concatenate(predicted, axis=0).reshape(slot_count, per_sample, outs),
        dest_group,
        group_at,
        groups,
        slot_count,
    ).reshape(targets.shape)

    head_grad, head_bias_grad = lax.psum((sum(head_grads), sum(head_sums)), ("grp", "fft"))
    raw = sum(weight_sums)
    half = raw.shape[-1] // 2
    spec_real = raw[:, :, :half, :half] + raw[:, :, half:, half:]
    spec_imag = raw[:, :, :half, half:] - raw[:, :, half:, :half]
    raw_b = sum(bias_sums)
    spec_part = jnp.stack([spec_real, spec_imag], axis=1)
    bias_part = jnp.stack([raw_b[..., :half], raw_b[..., half:]], axis=1)
    spec_part, bias_part = lax.psum((spec_part, bias_part), "grp")
    spec_w_grad = lax.all_gather(spec_part, "fft", axis=2, tiled=True)
    spec_b_grad = lax.all_gather(bias_part, "fft", axis=2, tiled=True)
    rows = sum(row_sums)
    gain_grad, embed_bias_grad = lax.psum((rows[0], rows[4]), ("grp", "fft"))
    return (
        predictions,
        embed_grad,
        embed_bias_grad,
        gain_grad,
        spec_w_grad,
        spec_b_grad,
        head_grad,
        head_bias_grad,
    )


def solution(mesh):
    return jax.shard_map(
        on_device,
        mesh=mesh,
        in_specs=(
            P("grp", "fft", None, None),
            P("grp", "fft", None, None),
            P(),
            P(),
            P(),
            P(),
            P(),
            P(),
            P(),
            P(),
            P(),
        ),
        out_specs=(
            P("grp", "fft", None, None),
            P(("grp", "fft"), None),
            P(),
            P(),
            P(),
            P(),
            P(),
            P(),
        ),
        check_vma=False,
    )
```

```python
import jax
import jax.numpy as jnp
import ml_dtypes
import numpy as np
from jax import lax
from jax.experimental import pallas as pl
from jax.experimental.pallas import tpu as pltpu
from jax.sharding import PartitionSpec as P

EPSILON = 1e-05
SHRINK = 0.01
CHUNKS = 2
VMEM_BYTES = 60 * 1024 * 1024
SLOTS = 6
SHARD, FIRST_ROW, GROUP, SIDES = 0, 1, 2, 3
HALF = jnp.bfloat16
FULL = jnp.float32


def dft_tables(cells):
    levels, factors = [], []
    for side, scale in ((cells, 1.1305), (cells // 2, 1.8633), (cells // 4, 1.0)):
        k = np.arange(cells)
        inside = (k < side).astype(np.float64)
        keep = inside[:, None] * inside[None, :]
        angle = 2.0 * np.pi * ((k[:, None] * k[None, :]) % side) / side
        one = np.exp(-1j * angle) * keep / np.sqrt(side)
        two = np.kron(one, one)
        table = np.concatenate([two.real, two.imag], axis=0)
        table[np.abs(table) < 1e-12] = 0.0
        rounded = (table * scale).astype(np.float32).astype(ml_dtypes.bfloat16)
        held = rounded.astype(np.float64)
        factors.append(float(np.sum(table * table) / np.sum(table * held)))
        levels.append(rounded)
    return np.stack(levels), factors


def dot(left, right):
    return jnp.dot(left, right, preferred_element_type=FULL)


def dot_tn(left, right):
    return lax.dot_general(left, right, (((0,), (0,)), ((), ())), preferred_element_type=FULL)


def dot_nt(left, right):
    return lax.dot_general(left, right, (((1,), (1,)), ((), ())), preferred_element_type=FULL)


def params():
    return pltpu.CompilerParams(vmem_limit_bytes=VMEM_BYTES)


def token_sides(scal_ref, first, count, per_sample, cells):
    token = lax.broadcasted_iota(jnp.int32, (count * per_sample, 1), 0)
    sample = token // per_sample
    side = jnp.zeros_like(token)
    for i in range(count):
        side = jnp.where(sample == i, scal_ref[SIDES + first + i], side)
    row = scal_ref[FIRST_ROW] + (token % per_sample) // cells
    col = token % cells
    valid = jnp.where((row < side) & (col < side), 1.0, 0.0).astype(FULL)
    return side, valid


def layer_norm(values):
    centered = values - jnp.mean(values, axis=-1, keepdims=True)
    inv_std = lax.rsqrt(jnp.mean(centered * centered, axis=-1, keepdims=True) + EPSILON)
    return centered * inv_std, inv_std


def whole(shape):
    return pl.BlockSpec(tuple(shape), lambda i, s: (0,) * len(shape))


def part_of(scal_ref, k, size):
    at = jnp.bitwise_xor(scal_ref[SHARD], k)
    return pl.ds(pl.multiple_of(at * size, size), size)


def fill_lanes(scal_ref, refs, held):
    share = refs[0].shape[-1]
    for k, ref in enumerate(refs):
        held[:, part_of(scal_ref, k, share)] = ref[...].reshape(held.shape[0], share)


def fill_rows(scal_ref, refs, held):
    rows = refs[0].shape[1]
    for k, ref in enumerate(refs):
        held[part_of(scal_ref, k, rows), :] = ref[0]


def split_lanes(scal_ref, held, refs):
    share = refs[0].shape[-1]
    for k, ref in enumerate(refs):
        ref[...] = held[:, part_of(scal_ref, k, share)].reshape(ref.shape)


def split_rows(scal_ref, held, refs):
    rows = refs[0].shape[1]
    for k, ref in enumerate(refs):
        ref[0] = held[part_of(scal_ref, k, rows), :]


def embed_chunk(scal, patches, embed_w, embed_b, gain, first, count, per_sample, cells, shards):
    rows = count * per_sample
    depth, width = embed_w.shape
    share = width // shards
    steps = 4
    tile = depth // steps

    def body(scal_ref, x_ref, w_ref, b_ref, gain_ref, emb_ref, *refs):
        outs, (acc, held) = refs[:shards], refs[shards:]
        step = pl.program_id(0)
        part = dot(x_ref[...], w_ref[...])

        @pl.when(step == 0)
        def _():
            acc[...] = part

        @pl.when(step > 0)
        def _():
            acc[...] += part

        @pl.when(step == steps - 1)
        def _():
            _, valid = token_sides(scal_ref, first, count, per_sample, cells)
            embedded = ((acc[...] + b_ref[...]) * valid).astype(HALF)
            emb_ref[...] = embedded
            unit, _ = layer_norm(embedded.astype(FULL))
            held[...] = (unit * gain_ref[...]).astype(HALF)
            split_lanes(scal_ref, held, outs)

    at = first // count
    piece = (count, per_sample, share)
    emb, *pieces = pl.pallas_call(
        body,
        grid_spec=pltpu.PrefetchScalarGridSpec(
            num_scalar_prefetch=1,
            grid=(steps,),
            in_specs=[
                pl.BlockSpec((rows, tile), lambda k, s: (at, k)),
                pl.BlockSpec((tile, width), lambda k, s: (k, 0)),
                whole((1, width)),
                whole((1, width)),
            ],
            out_specs=[whole((rows, width))] + [whole(piece)] * shards,
            scratch_shapes=[pltpu.VMEM((rows, width), FULL), pltpu.VMEM((rows, width), HALF)],
        ),
        out_shape=[jax.ShapeDtypeStruct((rows, width), HALF)] + [jax.ShapeDtypeStruct(piece, HALF)] * shards,
        compiler_params=params(),
        cost_estimate=pl.CostEstimate(
            flops=2 * rows * depth * width, bytes_accessed=2 * depth * (rows + width), transcendentals=0
        ),
        name="embed",
    )(scal, patches, embed_w, embed_b, gain)
    return emb, pieces


def to_blocks(values, blocks, width):
    half = values.shape[0] // 2
    return [
        jnp.concatenate(
            [values[:half, b * width : (b + 1) * width], values[half:, b * width : (b + 1) * width]], axis=1
        )
        for b in range(blocks)
    ]


def from_blocks(parts, width):
    real = jnp.concatenate([p[:, :width] for p in parts], axis=1)
    imag = jnp.concatenate([p[:, width:] for p in parts], axis=1)
    return real, imag


def table_factor(scal_ref, at, factors):
    level = scal_ref[at]
    return jnp.where(level == 0, factors[0], jnp.where(level == 1, factors[1], factors[2])).astype(FULL)


def table_back(table_ref, pair, factor):
    size = table_ref.shape[2]
    total = None
    for at, values in enumerate(pair):
        table = table_ref[0, at * size : (at + 1) * size]
        top = values.astype(HALF)
        rest = (values - top.astype(FULL)).astype(HALF)
        part = dot(table, top) + dot(table, rest)
        total = part if total is None else total + part
    return total * factor


def complex_weights(w_ref, held, blocks, width):
    for layer in range(2):
        for b in range(blocks):
            real, imag = w_ref[layer, 0, b], w_ref[layer, 1, b]
            held[layer, b, :width, :width] = real
            held[layer, b, :width, width:] = imag
            held[layer, b, width:, :width] = -imag
            held[layer, b, width:, width:] = real


def spectral_chunk(scal, table, factors, pieces, spec_w, spec_b, first):
    shards = len(pieces)
    count, per_sample, share = pieces[0].shape
    size = shards * per_sample
    width = spec_w.shape[-1]
    blocks = share // width
    wide = 2 * width

    def body(scal_ref, t_ref, w_ref, b_ref, *refs):
        ins, outs = refs[:shards], refs[shards : 2 * shards]
        spec_ref, hid_ref, fil_ref, weights, held = refs[2 * shards :]

        @pl.when(pl.program_id(0) == 0)
        def _():
            complex_weights(w_ref, weights, blocks, width)

        def bias(layer, b):
            row = pl.ds(scal_ref[SHARD] * blocks + b, 1)
            return jnp.concatenate([b_ref[layer, 0, row], b_ref[layer, 1, row]], axis=1)

        factor = table_factor(scal_ref, SIDES + SLOTS + first + pl.program_id(0), factors)
        fill_rows(scal_ref, ins, held)
        spectrum = (dot(t_ref[0], held[...]) * factor).astype(HALF)
        kept = []
        for b, entry in enumerate(to_blocks(spectrum, blocks, width)):
            spec_ref[0, b] = entry
            pre_one = dot(entry, weights[0, b]) + bias(0, b)
            hidden = jnp.maximum(pre_one, 0.0).astype(HALF)
            hid_ref[0, b] = hidden
            pre_two = dot(hidden, weights[1, b]) + bias(1, b)
            filtered = jnp.where(
                pre_two > SHRINK, pre_two - SHRINK, jnp.where(pre_two < -SHRINK, pre_two + SHRINK, 0.0)
            )
            fil_ref[0, b] = filtered.astype(HALF)
            kept.append(filtered)
        held[...] = table_back(t_ref, from_blocks(kept, width), factor).astype(HALF)
        split_rows(scal_ref, held, outs)

    piece = pl.BlockSpec((1, per_sample, share), lambda i, s: (i, 0, 0))
    saved = pl.BlockSpec((1, blocks, size, wide), lambda i, s: (i, 0, 0, 0))
    saved_shape = jax.ShapeDtypeStruct((count, blocks, size, wide), HALF)
    outs = pl.pallas_call(
        body,
        grid_spec=pltpu.PrefetchScalarGridSpec(
            num_scalar_prefetch=1,
            grid=(count,),
            in_specs=[
                pl.BlockSpec((1, 2 * size, size), lambda i, s: (s[SIDES + SLOTS + first + i], 0, 0)),
                pl.BlockSpec((2, 2, blocks, width, width), lambda i, s: (0, 0, s[SHARD], 0, 0)),
                whole(spec_b.shape),
            ]
            + [piece] * shards,
            out_specs=[piece] * shards + [saved] * 3,
            scratch_shapes=[pltpu.VMEM((2, blocks, wide, wide), HALF), pltpu.VMEM((size, share), HALF)],
        ),
        out_shape=[jax.ShapeDtypeStruct(pieces[0].shape, HALF)] * shards + [saved_shape] * 3,
        compiler_params=params(),
        cost_estimate=pl.CostEstimate(
            flops=count * size * share * size * 14, bytes_accessed=count * size * share * 16, transcendentals=0
        ),
        name="spectral",
    )(scal, table, spec_w, spec_b, *pieces)
    return outs[:shards], outs[shards:]


def head_chunk(scal, embedded, gain, mixed, targets, head_w, head_b, first, samples, cells):
    shards = len(mixed)
    count, per_sample, share = mixed[0].shape
    rows = count * per_sample
    width, outs = head_w.shape
    at = first // count
    scale_root = float(np.sqrt(np.float32(samples)))

    def body(scal_ref, emb_ref, gain_ref, tgt_ref, w_ref, b_ref, *refs):
        mix_refs, (pred_ref, res_ref, grad_ref, bias_ref, held) = refs[:shards], refs[shards:]
        fill_lanes(scal_ref, mix_refs, held)
        side, valid = token_sides(scal_ref, first, count, per_sample, cells)
        embedded = emb_ref[...].astype(FULL)
        unit, _ = layer_norm(embedded)
        normed = (unit * gain_ref[...]).astype(HALF)
        updated = (embedded + normed.astype(FULL) + held[...].astype(FULL)).astype(HALF)
        output = (dot(updated, w_ref[...]) + b_ref[...]) * valid
        pred_ref[...] = output.astype(HALF).reshape(pred_ref.shape)
        scale = 2.0 / (side.astype(FULL) * scale_root)
        residual = (scale * valid * (output - tgt_ref[...].astype(FULL))).astype(HALF)
        res_ref[...] = residual.reshape(res_ref.shape)
        grad_ref[...] = dot_tn(updated, residual)
        total = jnp.sum(residual.astype(FULL), axis=0, keepdims=True)
        bias_ref[...] = jnp.broadcast_to(total, bias_ref.shape)

    token_shape = (count, per_sample, outs)
    return pl.pallas_call(
        body,
        grid_spec=pltpu.PrefetchScalarGridSpec(
            num_scalar_prefetch=1,
            grid=(1,),
            in_specs=[
                whole((rows, width)),
                whole((1, width)),
                pl.BlockSpec((rows, outs), lambda i, s: (at, 0)),
                whole((width, outs)),
                whole((1, outs)),
            ]
            + [whole(mixed[0].shape)] * shards,
            out_specs=[whole(token_shape), whole(token_shape), whole((width, outs)), whole((8, outs))],
            scratch_shapes=[pltpu.VMEM((rows, width), HALF)],
        ),
        out_shape=[
            jax.ShapeDtypeStruct(token_shape, HALF),
            jax.ShapeDtypeStruct(token_shape, HALF),
            jax.ShapeDtypeStruct((width, outs), FULL),
            jax.ShapeDtypeStruct((8, outs), FULL),
        ],
        compiler_params=params(),
        cost_estimate=pl.CostEstimate(
            flops=4 * rows * width * outs, bytes_accessed=rows * width * 4 + width * outs * 6, transcendentals=0
        ),
        name="head",
    )(scal, embedded, gain, targets, head_w, head_b, *mixed)


def spectral_back_chunk(scal, table, factors, residual, head_w, spec_w, saved, first, before, last):
    shards = len(residual)
    count, per_sample, outs = residual[0].shape
    size = shards * per_sample
    width = spec_w.shape[-1]
    wide = 2 * width
    share = head_w.shape[0] // shards
    blocks = share // width
    raw_shape = (2, blocks, wide, wide)
    bias_shape = (2 * blocks, wide)
    has_before = before is not None

    def body(scal_ref, t_ref, h_ref, w_ref, spec_ref, hid_ref, fil_ref, *refs):
        ins, refs = refs[:shards], refs[shards:]
        if has_before:
            (old_ref, old_bias_ref), refs = refs[:2], refs[2:]
        pieces, (grad_ref, bias_ref, weights, held, gathered, total) = refs[:shards], refs[shards:]

        @pl.when(pl.program_id(0) == 0)
        def _():
            complex_weights(w_ref, weights, blocks, width)
            if has_before:
                total[...] = old_ref[...]
                bias_ref[...] = old_bias_ref[...]
            else:
                total[...] = jnp.zeros_like(total)
                bias_ref[...] = jnp.zeros_like(bias_ref)

        factor = table_factor(scal_ref, SIDES + SLOTS + first + pl.program_id(0), factors)
        fill_rows(scal_ref, ins, gathered)
        updated_grad = dot_nt(gathered[...], h_ref[...]).astype(HALF)
        filtered_grad = dot(t_ref[0], updated_grad) * factor
        kept = []
        for b, entry in enumerate(to_blocks(filtered_grad, blocks, width)):
            two_grad = jnp.where(fil_ref[0, b].astype(FULL) != 0.0, entry, 0.0).astype(HALF)
            hidden = hid_ref[0, b]
            total[1, b] += dot_tn(hidden, two_grad)
            bias_ref[blocks + b : blocks + b + 1] += jnp.sum(two_grad.astype(FULL), axis=0, keepdims=True)
            hidden_grad = dot_nt(two_grad, weights[1, b])
            one_grad = jnp.where(hidden.astype(FULL) > 0.0, hidden_grad, 0.0).astype(HALF)
            total[0, b] += dot_tn(spec_ref[0, b], one_grad)
            bias_ref[b : b + 1] += jnp.sum(one_grad.astype(FULL), axis=0, keepdims=True)
            kept.append(dot_nt(one_grad, weights[0, b]))
        held[...] = table_back(t_ref, from_blocks(kept, width), factor).astype(HALF)
        split_rows(scal_ref, held, pieces)

        @pl.when(pl.program_id(0) == count - 1)
        def _():
            if not last:
                grad_ref[...] = total[...]
                return
            for layer in range(2):
                for b in range(blocks):
                    raw = total[layer, b]
                    real = raw[:width, :width] + raw[width:, width:]
                    imag = raw[:width, width:] - raw[width:, :width]
                    row = (layer * blocks + b) * width
                    grad_ref[row : row + width] = jnp.concatenate([real, imag], axis=1).astype(HALF)

    saved_spec = pl.BlockSpec((1, blocks, size, wide), lambda i, s: (i, 0, 0, 0))
    piece = pl.BlockSpec((1, per_sample, share), lambda i, s: (i, 0, 0))
    if last:
        grad_out = jax.ShapeDtypeStruct((2 * blocks * width, wide), HALF)
    else:
        grad_out = jax.ShapeDtypeStruct(raw_shape, FULL)
    result = pl.pallas_call(
        body,
        grid_spec=pltpu.PrefetchScalarGridSpec(
            num_scalar_prefetch=1,
            grid=(count,),
            in_specs=[
                pl.BlockSpec((1, 2 * size, size), lambda i, s: (s[SIDES + SLOTS + first + i], 0, 0)),
                pl.BlockSpec((share, outs), lambda i, s: (s[SHARD], 0)),
                pl.BlockSpec((2, 2, blocks, width, width), lambda i, s: (0, 0, s[SHARD], 0, 0)),
                saved_spec,
                saved_spec,
                saved_spec,
            ]
            + [pl.BlockSpec((1, per_sample, outs), lambda i, s: (i, 0, 0))] * shards
            + ([whole(raw_shape), whole(bias_shape)] if has_before else []),
            out_specs=[piece] * shards + [whole(grad_out.shape), whole(bias_shape)],
            scratch_shapes=[
                pltpu.VMEM((2, blocks, wide, wide), HALF),
                pltpu.VMEM((size, share), HALF),
                pltpu.VMEM((size, outs), HALF),
                pltpu.VMEM(raw_shape, FULL),
            ],
        ),
        out_shape=[jax.ShapeDtypeStruct((count, per_sample, share), HALF)] * shards
        + [grad_out, jax.ShapeDtypeStruct(bias_shape, FULL)],
        compiler_params=params(),
        cost_estimate=pl.CostEstimate(
            flops=count * size * share * size * 20, bytes_accessed=count * size * share * 16, transcendentals=0
        ),
        name="spectral_back",
    )(scal, table, head_w, spec_w, *saved, *residual, *(before or ()))
    return result[:shards], result[shards:]


def embedded_back_chunk(scal, embedded, residual, head_w, gain, spec_grad, first, cells):
    shards = len(spec_grad)
    count, per_sample, share = spec_grad[0].shape
    rows = count * per_sample
    width, outs = head_w.shape

    def body(scal_ref, emb_ref, res_ref, w_ref, gain_ref, *refs):
        grad_refs, (out_ref, sums_ref, held) = refs[:shards], refs[shards:]
        fill_lanes(scal_ref, grad_refs, held)
        _, valid = token_sides(scal_ref, first, count, per_sample, cells)
        unit, inv_std = layer_norm(emb_ref[...].astype(FULL))
        direct = dot_nt(res_ref[...].reshape(rows, outs), w_ref[...]).astype(HALF).astype(FULL)
        normed_grad = held[...].astype(FULL) + direct
        gain_grad = jnp.sum(normed_grad * unit, axis=0, keepdims=True)
        unit_grad = normed_grad * gain_ref[...]
        mean_grad = jnp.mean(unit_grad, axis=-1, keepdims=True)
        mean_cross = jnp.mean(unit_grad * unit, axis=-1, keepdims=True)
        input_grad = inv_std * (unit_grad - mean_grad - unit * mean_cross)
        result = ((input_grad + direct) * valid).astype(HALF)
        out_ref[...] = result
        bias_grad = jnp.sum(result.astype(FULL), axis=0, keepdims=True)
        sums_ref[0:4] = jnp.broadcast_to(gain_grad, (4, width))
        sums_ref[4:8] = jnp.broadcast_to(bias_grad, (4, width))

    return pl.pallas_call(
        body,
        grid_spec=pltpu.PrefetchScalarGridSpec(
            num_scalar_prefetch=1,
            grid=(1,),
            in_specs=[
                whole((rows, width)),
                whole((count, per_sample, outs)),
                whole((width, outs)),
                whole((1, width)),
            ]
            + [whole(spec_grad[0].shape)] * shards,
            out_specs=[whole((rows, width)), whole((8, width))],
            scratch_shapes=[pltpu.VMEM((rows, width), HALF)],
        ),
        out_shape=[jax.ShapeDtypeStruct((rows, width), HALF), jax.ShapeDtypeStruct((8, width), FULL)],
        compiler_params=params(),
        cost_estimate=pl.CostEstimate(
            flops=2 * rows * width * outs, bytes_accessed=rows * width * 6, transcendentals=0
        ),
        name="embedded_back",
    )(scal, embedded, residual, head_w, gain, *spec_grad)


def turned_patches(scal, patches, groups):
    tokens, depth = patches.shape
    block = depth // groups
    tile = 256
    piece = int(np.gcd(tile, block))
    per_block = block // piece

    def body(scal_ref, x_ref, send_ref, keep_ref):
        turned = x_ref[...].T
        for i in range(tile // piece):
            place = pl.program_id(0) * (tile // piece) + i
            group = place // per_block
            rows = pl.ds(pl.multiple_of((place % per_block) * piece, piece), piece)
            values = turned[i * piece : (i + 1) * piece]
            away = jnp.bitwise_xor(group, scal_ref[GROUP]) % 2

            @pl.when(away == 1)
            def _(group=group, rows=rows, values=values):
                send_ref[group // 2, rows] = values

            @pl.when(away == 0)
            def _(group=group, rows=rows, values=values):
                keep_ref[group // 2, rows] = values

    shape = (groups // 2, block, tokens)
    return pl.pallas_call(
        body,
        grid_spec=pltpu.PrefetchScalarGridSpec(
            num_scalar_prefetch=1,
            grid=(depth // tile,),
            in_specs=[pl.BlockSpec((tokens, tile), lambda i, s: (0, i))],
            out_specs=[whole(shape)] * 2,
        ),
        out_shape=[jax.ShapeDtypeStruct(shape, HALF)] * 2,
        compiler_params=params(),
        cost_estimate=pl.CostEstimate(flops=0, bytes_accessed=4 * tokens * depth, transcendentals=0),
        name="turned_patches",
    )(scal, patches)


def embed_grad_parts(scal, turned, grads, groups):
    pairs, block, tokens = turned[0].shape
    width = grads[0].shape[1]
    half = width // 2
    top = pairs // 2
    count = len(turned)
    depth = tokens * count

    def body(scal_ref, *refs):
        turned_refs, grad_refs = refs[:count], refs[count : count + len(grads)]
        left_send, left_keep, right_send, right_keep, held = refs[count + len(grads) :]
        step = pl.program_id(0)

        @pl.when(step == 0)
        def _():
            row = 0
            for ref in grad_refs:
                held[row : row + ref.shape[0]] = ref[...]
                row += ref.shape[0]

        rows = jnp.concatenate([ref[0] for ref in turned_refs], axis=1)
        total = dot(rows, held[...]).astype(HALF)

        @pl.when(step % 2 == 1)
        def _():
            left_send[step // 2] = total[:, :half]

        @pl.when(step % 2 == 0)
        def _():
            left_keep[step // 2] = total[:, :half]

        @pl.when(step >= top)
        def _():
            right_send[step - top] = total[:, half:]

        @pl.when(step < top)
        def _():
            right_keep[step] = total[:, half:]

    shape = (top, block, half)
    return pl.pallas_call(
        body,
        grid_spec=pltpu.PrefetchScalarGridSpec(
            num_scalar_prefetch=1,
            grid=(pairs,),
            in_specs=[
                pl.BlockSpec((1, block, tokens), lambda i, s: (jnp.bitwise_xor(s[GROUP] // 2, i), 0, 0))
                for _ in turned
            ]
            + [whole(g.shape) for g in grads],
            out_specs=[whole(shape)] * 4,
            scratch_shapes=[pltpu.VMEM((depth, width), HALF)],
        ),
        out_shape=[jax.ShapeDtypeStruct(shape, HALF)] * 4,
        compiler_params=params(),
        cost_estimate=pl.CostEstimate(
            flops=2 * depth * pairs * block * width,
            bytes_accessed=2 * (pairs * block * (depth + width) + depth * width),
            transcendentals=0,
        ),
        name="embed_grad",
    )(scal, *turned, *grads)


def swap_bit(values, bit, groups):
    return lax.ppermute(values, "grp", [(g, g ^ (1 << bit)) for g in range(groups)])


def across(pieces):
    shards = len(pieces)
    return [pieces[0]] + [
        lax.ppermute(pieces[k], "fft", [(z, z ^ k) for z in range(shards)]) for k in range(1, shards)
    ]


def add_half(left, right):
    return (left.astype(FULL) + right.astype(FULL)).astype(HALF)


def scatter_sum(parts, groups, shard_at):
    bits = groups.bit_length() - 1
    shards = lax.axis_size("fft")
    ends = []
    for send, keep, order, low in (
        (parts[0], parts[1], list(range(1, bits)), True),
        (parts[2], parts[3], list(range(bits - 1, 0, -1)), False),
    ):
        total = add_half(keep, swap_bit(send, order[0], groups))
        for bit in order[1:]:
            count, block, width = total.shape
            if low:
                split = total.reshape(count // 2, 2, block, width)
                keep, send = split[:, 0], split[:, 1]
            else:
                split = total.reshape(2, count // 2, block, width)
                keep, send = split[0], split[1]
            total = add_half(keep, swap_bit(send, bit, groups))
        ends.append(total[0])
    block = ends[0].shape[0]
    share = block // shards
    part = jnp.concatenate(ends, axis=-1).reshape(shards, share, -1)
    moved = lax.all_to_all(part, "fft", split_axis=0, concat_axis=0, tiled=True)
    return jnp.sum(moved.astype(FULL), axis=0)


def to_all(values, axes, count):
    return lax.all_to_all(
        jnp.broadcast_to(values[None], (count,) + values.shape), axes, split_axis=0, concat_axis=0, tiled=True
    )


def small_grads(head_grad, head_bias, spec_grad, spec_bias, groups, shards, shard_at):
    outs = head_grad.shape[1]
    head_rows = head_grad.shape[0] // groups
    spec_rows = spec_grad.shape[0] // groups
    small = jnp.concatenate([spec_bias, head_bias[None], jnp.zeros((7 - spec_bias.shape[0], outs), FULL)], axis=0)
    high = lax.optimization_barrier(small.astype(HALF))
    small = jnp.concatenate([high, (small - high.astype(FULL)).astype(HALF)], axis=0)
    packed = jnp.concatenate(
        [
            head_grad.astype(HALF).reshape(groups, head_rows, outs),
            spec_grad.reshape(groups, spec_rows, outs),
            jnp.broadcast_to(small[None], (groups,) + small.shape),
        ],
        axis=1,
    )
    moved = lax.all_to_all(packed, "grp", split_axis=0, concat_axis=0, tiled=True)
    summed = jnp.sum(moved.astype(FULL), axis=0)
    small = summed[head_rows + spec_rows :]
    small = small[:8] + small[8:]
    high = lax.optimization_barrier(small.astype(HALF))
    small = jnp.concatenate([high, (small - high.astype(FULL)).astype(HALF)], axis=0)
    summed = jnp.concatenate([summed[: head_rows + spec_rows].astype(HALF), small], axis=0)
    rows = across([summed] * shards)
    head_part = sum(r[:head_rows].astype(FULL) for r in rows).astype(HALF)
    order = jnp.bitwise_xor(jnp.arange(shards, dtype=jnp.int32), shard_at)
    rest = jnp.take(jnp.stack([r[head_rows:] for r in rows]), order, axis=0)
    small = rest[:, spec_rows:].astype(FULL)
    small = small[:, :8] + small[:, 8:]
    spec_bias_all = small[:, : spec_bias.shape[0]]
    head_bias_all = jnp.sum(small[:, spec_bias.shape[0]], axis=0)
    spec_part = rest[:, :spec_rows].reshape(shards * spec_rows, outs)
    gathered = to_all(jnp.concatenate([head_part, spec_part], axis=0), "grp", groups)
    head_all = gathered[:, :head_rows].reshape(groups * head_rows, outs).astype(FULL)
    spec_all = gathered[:, head_rows:].reshape(groups, shards, spec_rows, outs)
    return head_all, head_bias_all, jnp.swapaxes(spec_all, 0, 1), spec_bias_all


def route_predictions(predicted, dest_group, group_at, groups, slot_count):
    own_dest = lax.dynamic_slice_in_dim(dest_group, group_at * slot_count, slot_count)
    matches = own_dest[None, :] == jnp.arange(groups, dtype=jnp.int32)[:, None]
    chosen = jnp.sum(jnp.where(matches, jnp.arange(slot_count, dtype=jnp.int32)[None, :], 0), axis=1)
    outgoing = jnp.take(predicted, chosen, axis=0)
    moved = lax.all_to_all(outgoing, "grp", split_axis=0, concat_axis=0, tiled=True)
    loaders = jnp.arange(groups, dtype=jnp.int32)
    holds = jnp.any(dest_group.reshape(groups, slot_count) == group_at, axis=1)
    rank = jnp.sum(jnp.where(holds[None, :] & (loaders[None, :] < loaders[:, None]), 1, 0), axis=1)
    slots = jnp.arange(slot_count, dtype=jnp.int32)
    sources = jnp.sum(jnp.where(holds[None, :] & (rank[None, :] == slots[:, None]), loaders[None, :], 0), axis=1)
    return jnp.take(moved, sources, axis=0)


def on_device(
    patches, targets, grid_side, dest_group, embed_w, embed_b, gain, spec_w, spec_b, head_w, head_b
):
    slot_count, row_count, cells, depth = patches.shape
    samples = dest_group.shape[0]
    groups = lax.axis_size("grp")
    shards = lax.axis_size("fft")
    group_at = lax.axis_index("grp").astype(jnp.int32)
    shard_at = lax.axis_index("fft").astype(jnp.int32)
    outs = targets.shape[-1]
    per_sample = row_count * cells
    count = slot_count // CHUNKS
    firsts = [c * count for c in range(CHUNKS)]
    assert slot_count == SLOTS

    sides = lax.dynamic_slice_in_dim(grid_side, group_at * slot_count, slot_count)
    level = jnp.where(sides == cells, 0, jnp.where(sides == cells // 2, 1, 2)).astype(jnp.int32)
    scal = jnp.concatenate([jnp.stack([shard_at, shard_at * row_count, group_at]), sides, level])
    table_values, factors = dft_tables(cells)
    table = jnp.asarray(table_values)
    flat_patches = patches.reshape(-1, depth)
    flat_targets = targets.reshape(-1, outs)
    gain_row, embed_b_row, head_b_row = gain[None], embed_b[None], head_b[None]

    embedded, moved = [], []
    for first in firsts:
        emb, pieces = embed_chunk(
            scal, flat_patches, embed_w, embed_b_row, gain_row, first, count, per_sample, cells, shards
        )
        embedded.append(emb)
        moved.append(across(pieces))
    turned_send, turned_keep = turned_patches(scal, flat_patches, groups)
    turned = [turned_keep, swap_bit(turned_send, 0, groups)]
    mixed, saved = [], []
    for first, pieces in zip(firsts, moved):
        out, rest = spectral_chunk(scal, table, factors, pieces, spec_w, spec_b, first)
        mixed.append(across(out))
        saved.append(rest)
    predicted, residual, head_grads, head_sums, gathered = [], [], [], [], []
    for first, emb, mix in zip(firsts, embedded, mixed):
        pred, res, grad, sums = head_chunk(
            scal, emb, gain_row, mix, flat_targets, head_w, head_b_row, first, samples, cells
        )
        predicted.append(pred)
        residual.append(res)
        head_grads.append(grad)
        head_sums.append(sums[0])
        gathered.append(across([res] * shards))
    spec_back, sums = [], None
    for first, res, rest in zip(firsts, gathered, saved):
        pieces, sums = spectral_back_chunk(
            scal, table, factors, res, head_w, spec_w, rest, first, sums, first == firsts[-1]
        )
        spec_back.append(across(pieces))
    own_grads, other_grads, row_sums = [], [], []
    for first, emb, res, back in zip(firsts, embedded, residual, spec_back):
        grad, row_sum = embedded_back_chunk(scal, emb, res, head_w, gain_row, back, first, cells)
        own_grads.append(grad)
        other_grads.append(swap_bit(grad, 0, groups))
        row_sums.append(row_sum)
    parts = embed_grad_parts(scal, turned, own_grads + other_grads, groups)
    embed_grad = scatter_sum(parts, groups, shard_at)

    predictions = route_predictions(
        jnp.concatenate(predicted, axis=0), dest_group, group_at, groups, slot_count
    ).reshape(targets.shape)
    spec_grad, spec_bias = sums
    head_grad, head_bias_grad, spec_all, spec_bias_all = small_grads(
        sum(head_grads), sum(head_sums), spec_grad, spec_bias, groups, shards, shard_at
    )
    width = spec_w.shape[-1]
    blocks = spec_w.shape[2] // shards
    spec_all = spec_all.reshape(shards, 2, blocks, width, 2, width)
    spec_w_grad = jnp.transpose(spec_all, (1, 4, 0, 2, 3, 5)).reshape(spec_w.shape).astype(FULL)
    spec_bias_all = spec_bias_all.reshape(shards, 2, blocks, 2, width)
    spec_b_grad = jnp.transpose(spec_bias_all, (1, 3, 0, 2, 4)).reshape(spec_b.shape)
    rows = sum(row_sums)
    rows = jnp.sum(to_all(rows.reshape(2, 4, -1)[:, 0], ("grp", "fft"), groups * shards), axis=0)
    gain_grad, embed_bias_grad = rows[0], rows[1]
    return (
        predictions,
        embed_grad,
        embed_bias_grad,
        gain_grad,
        spec_w_grad,
        spec_b_grad,
        head_grad,
        head_bias_grad,
    )


def solution(mesh):
    return jax.shard_map(
        on_device,
        mesh=mesh,
        in_specs=(
            P("grp", "fft", None, None),
            P("grp", "fft", None, None),
            P(),
            P(),
            P(),
            P(),
            P(),
            P(),
            P(),
            P(),
            P(),
        ),
        out_specs=(
            P("grp", "fft", None, None),
            P(("grp", "fft"), None),
            P(),
            P(),
            P(),
            P(),
            P(),
            P(),
        ),
        check_vma=False,
    )
```

```python
import jax
import jax.numpy as jnp
import ml_dtypes
import numpy as np
from jax import lax
from jax.experimental import pallas as pl
from jax.experimental.pallas import tpu as pltpu
from jax.sharding import PartitionSpec as P

EPSILON = 1e-05
SHRINK = 0.01
CHUNKS = 2
VMEM_BYTES = 60 * 1024 * 1024
SLOTS = 6
SHARD, FIRST_ROW, GROUP, SIDES = 0, 1, 2, 3
HALF = jnp.bfloat16
FULL = jnp.float32


def dft_tables(cells):
    levels, factors = [], []
    for side, scale in ((cells, 1.1305), (cells // 2, 1.8633), (cells // 4, 1.0)):
        k = np.arange(cells)
        inside = (k < side).astype(np.float64)
        keep = inside[:, None] * inside[None, :]
        angle = 2.0 * np.pi * ((k[:, None] * k[None, :]) % side) / side
        one = np.exp(-1j * angle) * keep / np.sqrt(side)
        two = np.kron(one, one)
        table = np.concatenate([two.real, two.imag], axis=0)
        table[np.abs(table) < 1e-12] = 0.0
        rounded = (table * scale).astype(np.float32).astype(ml_dtypes.bfloat16)
        held = rounded.astype(np.float64)
        factors.append(float(np.sum(table * table) / np.sum(table * held)))
        levels.append(rounded)
    return np.stack(levels), factors


def dot(left, right):
    return jnp.dot(left, right, preferred_element_type=FULL)


def dot_tn(left, right):
    return lax.dot_general(left, right, (((0,), (0,)), ((), ())), preferred_element_type=FULL)


def dot_nt(left, right):
    return lax.dot_general(left, right, (((1,), (1,)), ((), ())), preferred_element_type=FULL)


def params():
    return pltpu.CompilerParams(vmem_limit_bytes=VMEM_BYTES)


def token_sides(scal_ref, first, count, per_sample, cells):
    token = lax.broadcasted_iota(jnp.int32, (count * per_sample, 1), 0)
    sample = token // per_sample
    side = jnp.zeros_like(token)
    for i in range(count):
        side = jnp.where(sample == i, scal_ref[SIDES + first + i], side)
    row = scal_ref[FIRST_ROW] + (token % per_sample) // cells
    col = token % cells
    valid = jnp.where((row < side) & (col < side), 1.0, 0.0).astype(FULL)
    return side, valid


def whole(shape):
    return pl.BlockSpec(tuple(shape), lambda i, s: (0,) * len(shape))


def part_of(scal_ref, k, size):
    at = jnp.bitwise_xor(scal_ref[SHARD], k)
    return pl.ds(pl.multiple_of(at * size, size), size)


def fill_lanes(scal_ref, refs, held):
    share = refs[0].shape[-1]
    for k, ref in enumerate(refs):
        held[:, part_of(scal_ref, k, share)] = ref[...].reshape(held.shape[0], share)


def fill_rows(scal_ref, refs, held):
    rows = refs[0].shape[1]
    for k, ref in enumerate(refs):
        held[:, part_of(scal_ref, k, rows), :] = ref[...]


def split_lanes(scal_ref, held, refs):
    share = refs[0].shape[-1]
    for k, ref in enumerate(refs):
        ref[...] = held[:, part_of(scal_ref, k, share)].reshape(ref.shape)


def split_rows(scal_ref, held, refs):
    rows = refs[0].shape[1]
    for k, ref in enumerate(refs):
        ref[...] = held[:, part_of(scal_ref, k, rows), :]


def embed(scal, patches, embed_w, embed_b, gain, firsts, count, per_sample, cells, shards):
    rows, depth = patches.shape
    width = embed_w.shape[1]
    share = width // shards
    chunk_rows = count * per_sample
    chunks = len(firsts)
    steps = 4
    tile = depth // steps

    def body(scal_ref, x_ref, w_ref, b_ref, gain_ref, emb_ref, norm_ref, stat_ref, *refs):
        outs, acc = refs[:-1], refs[-1]
        step = pl.program_id(0)
        part = dot(x_ref[...], w_ref[...])

        @pl.when(step == 0)
        def _():
            acc[...] = part

        @pl.when(step > 0)
        def _():
            acc[...] += part

        @pl.when(step == steps - 1)
        def _():
            for c, first in enumerate(firsts):
                at = slice(c * chunk_rows, (c + 1) * chunk_rows)
                _, valid = token_sides(scal_ref, first, count, per_sample, cells)
                embedded = ((acc[at] + b_ref[...]) * valid).astype(HALF)
                emb_ref[at] = embedded
                values = embedded.astype(FULL)
                mean = jnp.mean(values, axis=-1, keepdims=True)
                centered = values - mean
                inv_std = lax.rsqrt(jnp.mean(centered * centered, axis=-1, keepdims=True) + EPSILON)
                norm_ref[at] = (centered * inv_std * gain_ref[...]).astype(HALF)
                stat_ref[at, :128] = jnp.broadcast_to(mean, (chunk_rows, 128))
                stat_ref[at, 128:] = jnp.broadcast_to(inv_std, (chunk_rows, 128))
                for k in range(shards):
                    piece = norm_ref[at, part_of(scal_ref, k, share)]
                    outs[c * shards + k][...] = piece.reshape(count, per_sample, share)

    piece = (count, per_sample, share)
    emb, normed, stats, *pieces = pl.pallas_call(
        body,
        grid_spec=pltpu.PrefetchScalarGridSpec(
            num_scalar_prefetch=1,
            grid=(steps,),
            in_specs=[
                pl.BlockSpec((rows, tile), lambda k, s: (0, k)),
                pl.BlockSpec((tile, width), lambda k, s: (k, 0)),
                whole((1, width)),
                whole((1, width)),
            ],
            out_specs=[whole((rows, width)), whole((rows, width)), whole((rows, 256))]
            + [whole(piece)] * (shards * chunks),
            scratch_shapes=[pltpu.VMEM((rows, width), FULL)],
        ),
        out_shape=[
            jax.ShapeDtypeStruct((rows, width), HALF),
            jax.ShapeDtypeStruct((rows, width), HALF),
            jax.ShapeDtypeStruct((rows, 256), FULL),
        ]
        + [jax.ShapeDtypeStruct(piece, HALF)] * (shards * chunks),
        compiler_params=params(),
        cost_estimate=pl.CostEstimate(
            flops=2 * rows * depth * width, bytes_accessed=2 * depth * (rows + width), transcendentals=0
        ),
        name="embed",
    )(scal, patches, embed_w, embed_b, gain)
    return emb, normed, stats, [pieces[c * shards : (c + 1) * shards] for c in range(chunks)]


def to_blocks(values, blocks, width):
    half = values.shape[0] // 2
    return [
        jnp.concatenate(
            [values[:half, b * width : (b + 1) * width], values[half:, b * width : (b + 1) * width]], axis=1
        )
        for b in range(blocks)
    ]


def from_blocks(parts, width):
    real = jnp.concatenate([p[:, :width] for p in parts], axis=1)
    imag = jnp.concatenate([p[:, width:] for p in parts], axis=1)
    return real, imag


def table_factor(level, factors):
    return jnp.where(level == 0, factors[0], jnp.where(level == 1, factors[1], factors[2])).astype(FULL)


def table_back(table_ref, level, tops, rests, factor):
    size = table_ref.shape[2]
    total = None
    for at, (top, rest) in enumerate(zip(tops, rests)):
        table = table_ref[level, at * size : (at + 1) * size]
        part = dot(table, top) + dot(table, rest)
        total = part if total is None else total + part
    return total * factor


def two_terms(values):
    top = values.astype(HALF)
    return top, (values - top.astype(FULL)).astype(HALF)


def complex_weights(w_ref, held, blocks, width):
    for layer in range(2):
        for b in range(blocks):
            real, imag = w_ref[layer, 0, b], w_ref[layer, 1, b]
            held[layer, b, :width, :width] = real
            held[layer, b, :width, width:] = imag
            held[layer, b, width:, :width] = -imag
            held[layer, b, width:, width:] = real


def spectral_chunk(scal, table, factors, pieces, spec_w, spec_b, first):
    shards = len(pieces)
    count, per_sample, share = pieces[0].shape
    size = shards * per_sample
    width = spec_w.shape[-1]
    blocks = share // width
    wide = 2 * width

    def body(scal_ref, t_ref, w_ref, b_ref, *refs):
        ins, outs = refs[:shards], refs[shards : 2 * shards]
        spec_ref, hid_ref, fil_ref, weights, held = refs[2 * shards :]

        def bias(layer, b):
            row = pl.ds(scal_ref[SHARD] * blocks + b, 1)
            return jnp.concatenate([b_ref[layer, 0, row], b_ref[layer, 1, row]], axis=1)

        complex_weights(w_ref, weights, blocks, width)
        fill_rows(scal_ref, ins, held)
        levels = [scal_ref[SIDES + SLOTS + first + i] for i in range(count)]
        for i, level in enumerate(levels):
            spectrum = (dot(t_ref[level], held[i]) * table_factor(level, factors)).astype(HALF)
            for b, entry in enumerate(to_blocks(spectrum, blocks, width)):
                spec_ref[b, i * size : (i + 1) * size] = entry
        kept = []
        for b in range(blocks):
            pre_one = dot(spec_ref[b], weights[0, b]) + bias(0, b)
            hidden = jnp.maximum(pre_one, 0.0).astype(HALF)
            hid_ref[b] = hidden
            pre_two = dot(hidden, weights[1, b]) + bias(1, b)
            filtered = jnp.where(
                pre_two > SHRINK, pre_two - SHRINK, jnp.where(pre_two < -SHRINK, pre_two + SHRINK, 0.0)
            )
            top, rest = two_terms(filtered)
            fil_ref[b] = top
            kept.append((top, rest))
        for i, level in enumerate(levels):
            at = slice(i * size, (i + 1) * size)
            tops = from_blocks([top[at] for top, _ in kept], width)
            rests = from_blocks([rest[at] for _, rest in kept], width)
            held[i] = table_back(t_ref, level, tops, rests, table_factor(level, factors)).astype(HALF)
        split_rows(scal_ref, held, outs)

    saved = (blocks, count * size, wide)
    outs = pl.pallas_call(
        body,
        grid_spec=pltpu.PrefetchScalarGridSpec(
            num_scalar_prefetch=1,
            grid=(1,),
            in_specs=[
                whole(table.shape),
                pl.BlockSpec((2, 2, blocks, width, width), lambda i, s: (0, 0, s[SHARD], 0, 0)),
                whole(spec_b.shape),
            ]
            + [whole(pieces[0].shape)] * shards,
            out_specs=[whole(pieces[0].shape)] * shards + [whole(saved)] * 3,
            scratch_shapes=[pltpu.VMEM((2, blocks, wide, wide), HALF), pltpu.VMEM((count, size, share), HALF)],
        ),
        out_shape=[jax.ShapeDtypeStruct(pieces[0].shape, HALF)] * shards + [jax.ShapeDtypeStruct(saved, HALF)] * 3,
        compiler_params=params(),
        cost_estimate=pl.CostEstimate(
            flops=count * size * share * size * 14, bytes_accessed=count * size * share * 16, transcendentals=0
        ),
        name="spectral",
    )(scal, table, spec_w, spec_b, *pieces)
    return outs[:shards], outs[shards:]


def head_chunk(scal, embedded, normed, mixed, targets, head_w, head_b, first, samples, cells):
    shards = len(mixed)
    count, per_sample, share = mixed[0].shape
    rows = count * per_sample
    width, outs = head_w.shape
    at = first // count
    scale_root = float(np.sqrt(np.float32(samples)))

    def body(scal_ref, emb_ref, norm_ref, tgt_ref, w_ref, b_ref, *refs):
        mix_refs, (pred_ref, res_ref, grad_ref, bias_ref, held) = refs[:shards], refs[shards:]
        fill_lanes(scal_ref, mix_refs, held)
        side, valid = token_sides(scal_ref, first, count, per_sample, cells)
        updated = (emb_ref[...].astype(FULL) + norm_ref[...].astype(FULL) + held[...].astype(FULL)).astype(HALF)
        output = (dot(updated, w_ref[...]) + b_ref[...]) * valid
        pred_ref[...] = output.astype(HALF).reshape(pred_ref.shape)
        scale = 2.0 / (side.astype(FULL) * scale_root)
        residual = (scale * valid * (output - tgt_ref[...].astype(FULL))).astype(HALF)
        res_ref[...] = residual.reshape(res_ref.shape)
        grad_ref[...] = dot_tn(updated, residual)
        total = jnp.sum(residual.astype(FULL), axis=0, keepdims=True)
        bias_ref[...] = jnp.broadcast_to(total, bias_ref.shape)

    token_shape = (count, per_sample, outs)
    return pl.pallas_call(
        body,
        grid_spec=pltpu.PrefetchScalarGridSpec(
            num_scalar_prefetch=1,
            grid=(1,),
            in_specs=[
                pl.BlockSpec((rows, width), lambda i, s: (at, 0)),
                pl.BlockSpec((rows, width), lambda i, s: (at, 0)),
                pl.BlockSpec((rows, outs), lambda i, s: (at, 0)),
                whole((width, outs)),
                whole((1, outs)),
            ]
            + [whole(mixed[0].shape)] * shards,
            out_specs=[whole(token_shape), whole(token_shape), whole((width, outs)), whole((8, outs))],
            scratch_shapes=[pltpu.VMEM((rows, width), HALF)],
        ),
        out_shape=[
            jax.ShapeDtypeStruct(token_shape, HALF),
            jax.ShapeDtypeStruct(token_shape, HALF),
            jax.ShapeDtypeStruct((width, outs), FULL),
            jax.ShapeDtypeStruct((8, outs), FULL),
        ],
        compiler_params=params(),
        cost_estimate=pl.CostEstimate(
            flops=4 * rows * width * outs, bytes_accessed=rows * width * 4 + width * outs * 6, transcendentals=0
        ),
        name="head",
    )(scal, embedded, normed, targets, head_w, head_b, *mixed)


def spectral_back_chunk(scal, table, factors, residual, head_w, spec_w, saved, first, before, last):
    shards = len(residual)
    count, per_sample, outs = residual[0].shape
    size = shards * per_sample
    width = spec_w.shape[-1]
    wide = 2 * width
    share = head_w.shape[0] // shards
    blocks = share // width
    raw_shape = (2, blocks, wide, wide)
    bias_shape = (2 * blocks, wide)
    has_before = before is not None

    def body(scal_ref, t_ref, h_ref, w_ref, spec_ref, hid_ref, fil_ref, *refs):
        ins, refs = refs[:shards], refs[shards:]
        if has_before:
            (old_ref, old_bias_ref), refs = refs[:2], refs[2:]
        pieces, (grad_ref, bias_ref, weights, held, gathered) = refs[:shards], refs[shards:]

        def weight_sums(layer, b, inputs, grads):
            raw = dot_tn(inputs, grads)
            sums = jnp.sum(grads.astype(FULL), axis=0, keepdims=True)
            at = layer * blocks + b
            if has_before:
                raw = raw + old_ref[layer, b]
                sums = sums + old_bias_ref[at : at + 1]
            bias_ref[at : at + 1] = sums
            if not last:
                grad_ref[layer, b] = raw
                return
            real = raw[:width, :width] + raw[width:, width:]
            imag = raw[:width, width:] - raw[width:, :width]
            grad_ref[at * width : (at + 1) * width] = jnp.concatenate([real, imag], axis=1).astype(HALF)

        complex_weights(w_ref, weights, blocks, width)
        fill_rows(scal_ref, ins, gathered)
        levels = [scal_ref[SIDES + SLOTS + first + i] for i in range(count)]
        updated_grad = dot_nt(gathered[...].reshape(count * size, outs), h_ref[...]).astype(HALF)
        entries = []
        for i, level in enumerate(levels):
            filtered_grad = dot(t_ref[level], updated_grad[i * size : (i + 1) * size]) * table_factor(level, factors)
            entries.append(to_blocks(filtered_grad, blocks, width))
        kept = []
        for b in range(blocks):
            entry = jnp.concatenate([e[b] for e in entries], axis=0)
            two_grad = jnp.where(fil_ref[b].astype(FULL) != 0.0, entry, 0.0).astype(HALF)
            hidden = hid_ref[b]
            hidden_grad = dot_nt(two_grad, weights[1, b])
            one_grad = jnp.where(hidden.astype(FULL) > 0.0, hidden_grad, 0.0).astype(HALF)
            kept.append(two_terms(dot_nt(one_grad, weights[0, b])))
            weight_sums(1, b, hidden, two_grad)
            weight_sums(0, b, spec_ref[b], one_grad)
        for i, level in enumerate(levels):
            at = slice(i * size, (i + 1) * size)
            tops = from_blocks([top[at] for top, _ in kept], width)
            rests = from_blocks([rest[at] for _, rest in kept], width)
            held[i] = table_back(t_ref, level, tops, rests, table_factor(level, factors)).astype(HALF)
        split_rows(scal_ref, held, pieces)

    piece = (count, per_sample, share)
    if last:
        grad_out = jax.ShapeDtypeStruct((2 * blocks * width, wide), HALF)
    else:
        grad_out = jax.ShapeDtypeStruct(raw_shape, FULL)
    result = pl.pallas_call(
        body,
        grid_spec=pltpu.PrefetchScalarGridSpec(
            num_scalar_prefetch=1,
            grid=(1,),
            in_specs=[
                whole(table.shape),
                pl.BlockSpec((share, outs), lambda i, s: (s[SHARD], 0)),
                pl.BlockSpec((2, 2, blocks, width, width), lambda i, s: (0, 0, s[SHARD], 0, 0)),
            ]
            + [whole(saved[0].shape)] * 3
            + [whole(residual[0].shape)] * shards
            + ([whole(raw_shape), whole(bias_shape)] if has_before else []),
            out_specs=[whole(piece)] * shards + [whole(grad_out.shape), whole(bias_shape)],
            scratch_shapes=[
                pltpu.VMEM((2, blocks, wide, wide), HALF),
                pltpu.VMEM((count, size, share), HALF),
                pltpu.VMEM((count, size, outs), HALF),
            ],
        ),
        out_shape=[jax.ShapeDtypeStruct(piece, HALF)] * shards
        + [grad_out, jax.ShapeDtypeStruct(bias_shape, FULL)],
        compiler_params=params(),
        cost_estimate=pl.CostEstimate(
            flops=count * size * share * size * 20, bytes_accessed=count * size * share * 16, transcendentals=0
        ),
        name="spectral_back",
    )(scal, table, head_w, spec_w, *saved, *residual, *(before or ()))
    return result[:shards], result[shards:]


def embedded_back_chunk(scal, embedded, stats, residual, head_w, gain, spec_grad, first, cells):
    shards = len(spec_grad)
    count, per_sample, share = spec_grad[0].shape
    rows = count * per_sample
    width, outs = head_w.shape
    at = first // count

    def body(scal_ref, emb_ref, stat_ref, res_ref, w_ref, gain_ref, *refs):
        grad_refs, (out_ref, sums_ref, held) = refs[:shards], refs[shards:]
        fill_lanes(scal_ref, grad_refs, held)
        _, valid = token_sides(scal_ref, first, count, per_sample, cells)
        inv_std = stat_ref[:, 128:129]
        unit = (emb_ref[...].astype(FULL) - stat_ref[:, 0:1]) * inv_std
        direct = dot_nt(res_ref[...].reshape(rows, outs), w_ref[...]).astype(HALF).astype(FULL)
        normed_grad = held[...].astype(FULL) + direct
        gain_grad = jnp.sum(normed_grad * unit, axis=0, keepdims=True)
        unit_grad = normed_grad * gain_ref[...]
        mean_grad = jnp.mean(unit_grad, axis=-1, keepdims=True)
        mean_cross = jnp.mean(unit_grad * unit, axis=-1, keepdims=True)
        input_grad = inv_std * (unit_grad - mean_grad - unit * mean_cross)
        result = ((input_grad + direct) * valid).astype(HALF)
        out_ref[...] = result
        bias_grad = jnp.sum(result.astype(FULL), axis=0, keepdims=True)
        sums_ref[0:4] = jnp.broadcast_to(gain_grad, (4, width))
        sums_ref[4:8] = jnp.broadcast_to(bias_grad, (4, width))

    return pl.pallas_call(
        body,
        grid_spec=pltpu.PrefetchScalarGridSpec(
            num_scalar_prefetch=1,
            grid=(1,),
            in_specs=[
                pl.BlockSpec((rows, width), lambda i, s: (at, 0)),
                pl.BlockSpec((rows, 256), lambda i, s: (at, 0)),
                whole((count, per_sample, outs)),
                whole((width, outs)),
                whole((1, width)),
            ]
            + [whole(spec_grad[0].shape)] * shards,
            out_specs=[whole((rows, width)), whole((8, width))],
            scratch_shapes=[pltpu.VMEM((rows, width), HALF)],
        ),
        out_shape=[jax.ShapeDtypeStruct((rows, width), HALF), jax.ShapeDtypeStruct((8, width), FULL)],
        compiler_params=params(),
        cost_estimate=pl.CostEstimate(
            flops=2 * rows * width * outs, bytes_accessed=rows * width * 6, transcendentals=0
        ),
        name="embedded_back",
    )(scal, embedded, stats, residual, head_w, gain, *spec_grad)


def turned_patches(scal, patches, groups):
    tokens, depth = patches.shape
    block = depth // groups
    tile = 256
    piece = int(np.gcd(tile, block))
    per_block = block // piece

    def body(scal_ref, x_ref, send_ref, keep_ref):
        turned = x_ref[...].T
        for i in range(tile // piece):
            place = pl.program_id(0) * (tile // piece) + i
            group = place // per_block
            rows = pl.ds(pl.multiple_of((place % per_block) * piece, piece), piece)
            values = turned[i * piece : (i + 1) * piece]
            away = jnp.bitwise_xor(group, scal_ref[GROUP]) % 2

            @pl.when(away == 1)
            def _(group=group, rows=rows, values=values):
                send_ref[group // 2, rows] = values

            @pl.when(away == 0)
            def _(group=group, rows=rows, values=values):
                keep_ref[group // 2, rows] = values

    shape = (groups // 2, block, tokens)
    return pl.pallas_call(
        body,
        grid_spec=pltpu.PrefetchScalarGridSpec(
            num_scalar_prefetch=1,
            grid=(depth // tile,),
            in_specs=[pl.BlockSpec((tokens, tile), lambda i, s: (0, i))],
            out_specs=[whole(shape)] * 2,
        ),
        out_shape=[jax.ShapeDtypeStruct(shape, HALF)] * 2,
        compiler_params=params(),
        cost_estimate=pl.CostEstimate(flops=0, bytes_accessed=4 * tokens * depth, transcendentals=0),
        name="turned_patches",
    )(scal, patches)


def embed_grad_parts(scal, turned, grads, groups):
    pairs, block, tokens = turned[0].shape
    width = grads[0].shape[1]
    half = width // 2
    top = pairs // 2
    count = len(turned)
    depth = tokens * count

    def body(scal_ref, *refs):
        turned_refs, grad_refs = refs[:count], refs[count : count + len(grads)]
        left_send, left_keep, right_send, right_keep, held = refs[count + len(grads) :]
        step = pl.program_id(0)

        @pl.when(step == 0)
        def _():
            row = 0
            for ref in grad_refs:
                held[row : row + ref.shape[0]] = ref[...]
                row += ref.shape[0]

        rows = jnp.concatenate([ref[0] for ref in turned_refs], axis=1)
        total = dot(rows, held[...]).astype(HALF)

        @pl.when(step % 2 == 1)
        def _():
            left_send[step // 2] = total[:, :half]

        @pl.when(step % 2 == 0)
        def _():
            left_keep[step // 2] = total[:, :half]

        @pl.when(step >= top)
        def _():
            right_send[step - top] = total[:, half:]

        @pl.when(step < top)
        def _():
            right_keep[step] = total[:, half:]

    shape = (top, block, half)
    return pl.pallas_call(
        body,
        grid_spec=pltpu.PrefetchScalarGridSpec(
            num_scalar_prefetch=1,
            grid=(pairs,),
            in_specs=[
                pl.BlockSpec((1, block, tokens), lambda i, s: (jnp.bitwise_xor(s[GROUP] // 2, i), 0, 0))
                for _ in turned
            ]
            + [whole(g.shape) for g in grads],
            out_specs=[whole(shape)] * 4,
            scratch_shapes=[pltpu.VMEM((depth, width), HALF)],
        ),
        out_shape=[jax.ShapeDtypeStruct(shape, HALF)] * 4,
        compiler_params=params(),
        cost_estimate=pl.CostEstimate(
            flops=2 * depth * pairs * block * width,
            bytes_accessed=2 * (pairs * block * (depth + width) + depth * width),
            transcendentals=0,
        ),
        name="embed_grad",
    )(scal, *turned, *grads)


def swap_bit(values, bit, groups):
    return lax.ppermute(values, "grp", [(g, g ^ (1 << bit)) for g in range(groups)])


def across(pieces):
    shards = len(pieces)
    return [pieces[0]] + [
        lax.ppermute(pieces[k], "fft", [(z, z ^ k) for z in range(shards)]) for k in range(1, shards)
    ]


def add_half(left, right):
    return (left.astype(FULL) + right.astype(FULL)).astype(HALF)


def scatter_start(parts, groups):
    bits = groups.bit_length() - 1
    ends = []
    for send, keep, order, low in (
        (parts[0], parts[1], list(range(1, bits)), True),
        (parts[2], parts[3], list(range(bits - 1, 0, -1)), False),
    ):
        total = add_half(keep, swap_bit(send, order[0], groups))
        for bit in order[1:]:
            count, block, width = total.shape
            if low:
                split = total.reshape(count // 2, 2, block, width)
                keep, send = split[:, 0], split[:, 1]
            else:
                split = total.reshape(2, count // 2, block, width)
                keep, send = split[0], split[1]
            total = add_half(keep, swap_bit(send, bit, groups))
        ends.append(total[0])
    return jnp.concatenate(ends, axis=-1)


def scatter_end(part, shards):
    part = part.reshape(shards, part.shape[0] // shards, -1)
    moved = lax.all_to_all(part, "fft", split_axis=0, concat_axis=0, tiled=True)
    return jnp.sum(moved.astype(FULL), axis=0)


def to_all(values, axes, count):
    return lax.all_to_all(
        jnp.broadcast_to(values[None], (count,) + values.shape), axes, split_axis=0, concat_axis=0, tiled=True
    )


def hi_lo(values):
    high = lax.optimization_barrier(values.astype(HALF))
    return jnp.concatenate([high, (values - high.astype(FULL)).astype(HALF)], axis=-2)


def from_hi_lo(values):
    half = values.shape[-2] // 2
    values = values.astype(FULL)
    return values[..., :half, :] + values[..., half:, :]


def sum_over_groups(head_grad, spec_grad, groups):
    outs = head_grad.shape[1]
    packed = jnp.concatenate(
        [head_grad.astype(HALF).reshape(groups, -1, outs), spec_grad.reshape(groups, -1, outs)], axis=1
    )
    return lax.all_to_all(packed, "grp", split_axis=0, concat_axis=0, tiled=True)


def over_shards(moved, small, head_rows, shards, shard_at):
    summed = jnp.sum(moved.astype(FULL), axis=0).astype(HALF)
    rows = across([jnp.concatenate([summed, hi_lo(small)], axis=0)] * shards)
    head_part = sum(r[:head_rows].astype(FULL) for r in rows).astype(HALF)
    order = jnp.bitwise_xor(jnp.arange(shards, dtype=jnp.int32), shard_at)
    rest = jnp.take(jnp.stack([r[head_rows:] for r in rows]), order, axis=0)
    spec_rows = summed.shape[0] - head_rows
    return head_part, rest[:, :spec_rows], from_hi_lo(rest[:, spec_rows:])


def assembled(gathered, head_rows, shards, blocks, width):
    groups = gathered.shape[0]
    total_blocks = shards * blocks
    spec_rows = 2 * blocks * width // groups

    def body(x_ref, head_ref, spec_ref):
        for g in range(groups):
            head_ref[g * head_rows : (g + 1) * head_rows] = x_ref[g, :head_rows].astype(FULL)
            start = g * spec_rows
            layer, b = start // (blocks * width), (start // width) % blocks
            rows = slice(start % width, start % width + spec_rows)
            for z in range(shards):
                values = x_ref[g, head_rows + z * spec_rows : head_rows + (z + 1) * spec_rows].astype(FULL)
                spec_ref[layer, 0, z * blocks + b, rows] = values[:, :width]
                spec_ref[layer, 1, z * blocks + b, rows] = values[:, width:]

    return pl.pallas_call(
        body,
        out_shape=[
            jax.ShapeDtypeStruct((groups * head_rows, 2 * width), FULL),
            jax.ShapeDtypeStruct((2, 2, total_blocks, width, width), FULL),
        ],
        compiler_params=params(),
        name="assembled",
    )(gathered)


def route_predictions(predicted, dest_group, group_at, groups, slot_count):
    own_dest = lax.dynamic_slice_in_dim(dest_group, group_at * slot_count, slot_count)
    matches = own_dest[None, :] == jnp.arange(groups, dtype=jnp.int32)[:, None]
    chosen = jnp.sum(jnp.where(matches, jnp.arange(slot_count, dtype=jnp.int32)[None, :], 0), axis=1)
    outgoing = jnp.take(predicted, chosen, axis=0)
    moved = lax.all_to_all(outgoing, "grp", split_axis=0, concat_axis=0, tiled=True)
    loaders = jnp.arange(groups, dtype=jnp.int32)
    holds = jnp.any(dest_group.reshape(groups, slot_count) == group_at, axis=1)
    rank = jnp.sum(jnp.where(holds[None, :] & (loaders[None, :] < loaders[:, None]), 1, 0), axis=1)
    slots = jnp.arange(slot_count, dtype=jnp.int32)
    sources = jnp.sum(jnp.where(holds[None, :] & (rank[None, :] == slots[:, None]), loaders[None, :], 0), axis=1)
    return jnp.take(moved, sources, axis=0)


def on_device(
    patches, targets, grid_side, dest_group, embed_w, embed_b, gain, spec_w, spec_b, head_w, head_b
):
    slot_count, row_count, cells, depth = patches.shape
    samples = dest_group.shape[0]
    groups = lax.axis_size("grp")
    shards = lax.axis_size("fft")
    group_at = lax.axis_index("grp").astype(jnp.int32)
    shard_at = lax.axis_index("fft").astype(jnp.int32)
    outs = targets.shape[-1]
    per_sample = row_count * cells
    count = slot_count // CHUNKS
    firsts = [c * count for c in range(CHUNKS)]
    assert slot_count == SLOTS

    sides = lax.dynamic_slice_in_dim(grid_side, group_at * slot_count, slot_count)
    level = jnp.where(sides == cells, 0, jnp.where(sides == cells // 2, 1, 2)).astype(jnp.int32)
    scal = jnp.concatenate([jnp.stack([shard_at, shard_at * row_count, group_at]), sides, level])
    table_values, factors = dft_tables(cells)
    table = jnp.asarray(table_values)
    flat_patches = patches.reshape(-1, depth)
    flat_targets = targets.reshape(-1, outs)
    gain_row, embed_b_row, head_b_row = gain[None], embed_b[None], head_b[None]

    embedded, normed, stats, pieces = embed(
        scal, flat_patches, embed_w, embed_b_row, gain_row, firsts, count, per_sample, cells, shards
    )
    moved = [across(p) for p in pieces]
    turned_send, turned_keep = turned_patches(scal, flat_patches, groups)
    turned = [turned_keep, swap_bit(turned_send, 0, groups)]
    mixed, saved = [], []
    for first, values in zip(firsts, moved):
        out, rest = spectral_chunk(scal, table, factors, values, spec_w, spec_b, first)
        mixed.append(across(out))
        saved.append(rest)
    predicted, residual, head_grads, head_sums, gathered = [], [], [], [], []
    for first, mix in zip(firsts, mixed):
        pred, res, grad, sums = head_chunk(
            scal, embedded, normed, mix, flat_targets, head_w, head_b_row, first, samples, cells
        )
        predicted.append(pred)
        residual.append(res)
        head_grads.append(grad)
        head_sums.append(sums[0])
        gathered.append(across([res] * shards))
    spec_back, sums = [], None
    for first, res, rest in zip(firsts, gathered, saved):
        values, sums = spectral_back_chunk(
            scal, table, factors, res, head_w, spec_w, rest, first, sums, first == firsts[-1]
        )
        spec_back.append(across(values))
    spec_grad, spec_bias = sums
    width = spec_w.shape[-1]
    blocks = spec_w.shape[2] // shards
    head_rows = head_w.shape[0] // groups
    weight_sums = sum_over_groups(sum(head_grads), spec_grad, groups)
    own_grads, other_grads, row_sums = [], [], []
    for first, res, back in zip(firsts, residual, spec_back):
        grad, row_sum = embedded_back_chunk(scal, embedded, stats, res, head_w, gain_row, back, first, cells)
        own_grads.append(grad)
        other_grads.append(swap_bit(grad, 0, groups))
        row_sums.append(row_sum)
    parts = embed_grad_parts(scal, turned, own_grads + other_grads, groups)
    parts, weight_sums, predicted, row_sums = lax.optimization_barrier((parts, weight_sums, predicted, row_sums))
    part = scatter_start(parts, groups)
    predictions = route_predictions(
        jnp.concatenate(predicted, axis=0), dest_group, group_at, groups, slot_count
    ).reshape(targets.shape)
    rows = sum(row_sums)
    vectors = jnp.concatenate([rows[0].reshape(-1, outs), rows[4].reshape(-1, outs), sum(head_sums)[None]], axis=0)
    own_rows, all_rows = spec_bias.shape[0], vectors.shape[0]
    small = jnp.concatenate([spec_bias, vectors, jnp.zeros((16 - own_rows - all_rows, outs), FULL)], axis=0)
    head_part, spec_part, small = over_shards(weight_sums, small, head_rows, shards, shard_at)
    small = jnp.concatenate([small[:, :own_rows].reshape(-1, outs), jnp.sum(small[:, own_rows:], axis=0)], axis=0)
    small = jnp.concatenate([small, jnp.zeros((-small.shape[0] % 16, outs), FULL)], axis=0)
    outgoing = jnp.concatenate([head_part, spec_part.reshape(-1, outs), hi_lo(small)], axis=0)
    part, outgoing = lax.optimization_barrier((part, outgoing))
    embed_grad = scatter_end(part, shards)
    gathered = to_all(outgoing, "grp", groups)
    head_grad, spec_w_grad = assembled(gathered, head_rows, shards, blocks, width)
    small = jnp.sum(from_hi_lo(gathered[:, head_rows + shards * (2 * blocks * width // groups) :]), axis=0)
    spec_bias_all = small[: shards * own_rows].reshape(shards, 2, blocks, 2, width)
    spec_b_grad = jnp.transpose(spec_bias_all, (1, 3, 0, 2, 4)).reshape(spec_b.shape)
    vectors = small[shards * own_rows : shards * own_rows + all_rows]
    quarter = (all_rows - 1) // 2
    gain_grad, embed_bias_grad = vectors[:quarter].reshape(-1), vectors[quarter : 2 * quarter].reshape(-1)
    head_bias_grad = vectors[2 * quarter]
    return (
        predictions,
        embed_grad,
        embed_bias_grad,
        gain_grad,
        spec_w_grad,
        spec_b_grad,
        head_grad,
        head_bias_grad,
    )


def solution(mesh):
    return jax.shard_map(
        on_device,
        mesh=mesh,
        in_specs=(
            P("grp", "fft", None, None),
            P("grp", "fft", None, None),
            P(),
            P(),
            P(),
            P(),
            P(),
            P(),
            P(),
            P(),
            P(),
        ),
        out_specs=(
            P("grp", "fft", None, None),
            P(("grp", "fft"), None),
            P(),
            P(),
            P(),
            P(),
            P(),
            P(),
        ),
        check_vma=False,
    )
```

```python
import jax
import jax.numpy as jnp
import ml_dtypes
import numpy as np
from jax import lax
from jax.experimental import pallas as pl
from jax.experimental.pallas import tpu as pltpu
from jax.sharding import PartitionSpec as P

EPSILON = 1e-05
SHRINK = 0.01
CHUNKS = 2
VMEM_BYTES = 24 * 1024 * 1024
SLOTS = 6
SHARD, FIRST_ROW, GROUP, SIDES = 0, 1, 2, 3
HALF = jnp.bfloat16
FULL = jnp.float32


def dft_tables(cells):
    levels, factors = [], []
    for side, scale in ((cells, 1.1305), (cells // 2, 1.8633), (cells // 4, 1.0)):
        k = np.arange(cells)
        inside = (k < side).astype(np.float64)
        keep = inside[:, None] * inside[None, :]
        angle = 2.0 * np.pi * ((k[:, None] * k[None, :]) % side) / side
        one = np.exp(-1j * angle) * keep / np.sqrt(side)
        two = np.kron(one, one)
        table = np.concatenate([two.real, two.imag], axis=0)
        table[np.abs(table) < 1e-12] = 0.0
        rounded = (table * scale).astype(np.float32).astype(ml_dtypes.bfloat16)
        held = rounded.astype(np.float64)
        factors.append(float(np.sum(table * table) / np.sum(table * held)))
        levels.append(rounded)
    return np.stack(levels), factors


def dot(left, right):
    return jnp.dot(left, right, preferred_element_type=FULL)


def dot_tn(left, right):
    return lax.dot_general(left, right, (((0,), (0,)), ((), ())), preferred_element_type=FULL)


def dot_nt(left, right):
    return lax.dot_general(left, right, (((1,), (1,)), ((), ())), preferred_element_type=FULL)


def params():
    return pltpu.CompilerParams(vmem_limit_bytes=VMEM_BYTES)


def token_sides(scal_ref, first, count, per_sample, cells):
    token = lax.broadcasted_iota(jnp.int32, (count * per_sample, 1), 0)
    sample = token // per_sample
    side = jnp.zeros_like(token)
    for i in range(count):
        side = jnp.where(sample == i, scal_ref[SIDES + first + i], side)
    row = scal_ref[FIRST_ROW] + (token % per_sample) // cells
    col = token % cells
    valid = jnp.where((row < side) & (col < side), 1.0, 0.0).astype(FULL)
    return side, valid


def whole(shape):
    return pl.BlockSpec(tuple(shape), lambda i, s: (0,) * len(shape))


def part_of(scal_ref, k, size):
    at = jnp.bitwise_xor(scal_ref[SHARD], k)
    return pl.ds(pl.multiple_of(at * size, size), size)


def fill_lanes(scal_ref, refs, held):
    share = refs[0].shape[-1]
    for k, ref in enumerate(refs):
        held[:, part_of(scal_ref, k, share)] = ref[...].reshape(held.shape[0], share)


def fill_rows(scal_ref, refs, held):
    rows = refs[0].shape[1]
    for k, ref in enumerate(refs):
        held[:, part_of(scal_ref, k, rows), :] = ref[...]


def split_lanes(scal_ref, held, refs):
    share = refs[0].shape[-1]
    for k, ref in enumerate(refs):
        ref[...] = held[:, part_of(scal_ref, k, share)].reshape(ref.shape)


def split_rows(scal_ref, held, refs):
    rows = refs[0].shape[1]
    for k, ref in enumerate(refs):
        ref[...] = held[:, part_of(scal_ref, k, rows), :]


def embed(scal, patches, embed_w, embed_b, gain, firsts, count, per_sample, cells, shards):
    rows, depth = patches.shape
    width = embed_w.shape[1]
    share = width // shards
    chunk_rows = count * per_sample
    chunks = len(firsts)
    steps = 4
    tile = depth // steps

    def body(scal_ref, x_ref, w_ref, b_ref, gain_ref, emb_ref, norm_ref, stat_ref, *refs):
        outs, acc = refs[:-1], refs[-1]
        step = pl.program_id(0)
        part = dot(x_ref[...], w_ref[...])

        @pl.when(step == 0)
        def _():
            acc[...] = part

        @pl.when(step > 0)
        def _():
            acc[...] += part

        @pl.when(step == steps - 1)
        def _():
            for c, first in enumerate(firsts):
                at = slice(c * chunk_rows, (c + 1) * chunk_rows)
                _, valid = token_sides(scal_ref, first, count, per_sample, cells)
                embedded = ((acc[at] + b_ref[...]) * valid).astype(HALF)
                emb_ref[at] = embedded
                values = embedded.astype(FULL)
                mean = jnp.mean(values, axis=-1, keepdims=True)
                centered = values - mean
                inv_std = lax.rsqrt(jnp.mean(centered * centered, axis=-1, keepdims=True) + EPSILON)
                norm_ref[at] = (centered * inv_std * gain_ref[...]).astype(HALF)
                stat_ref[at, :128] = jnp.broadcast_to(mean, (chunk_rows, 128))
                stat_ref[at, 128:] = jnp.broadcast_to(inv_std, (chunk_rows, 128))
                for k in range(shards):
                    piece = norm_ref[at, part_of(scal_ref, k, share)]
                    outs[c * shards + k][...] = piece.reshape(count, per_sample, share)

    piece = (count, per_sample, share)
    emb, normed, stats, *pieces = pl.pallas_call(
        body,
        grid_spec=pltpu.PrefetchScalarGridSpec(
            num_scalar_prefetch=1,
            grid=(steps,),
            in_specs=[
                pl.BlockSpec((rows, tile), lambda k, s: (0, k)),
                pl.BlockSpec((tile, width), lambda k, s: (k, 0)),
                whole((1, width)),
                whole((1, width)),
            ],
            out_specs=[whole((rows, width)), whole((rows, width)), whole((rows, 256))]
            + [whole(piece)] * (shards * chunks),
            scratch_shapes=[pltpu.VMEM((rows, width), FULL)],
        ),
        out_shape=[
            jax.ShapeDtypeStruct((rows, width), HALF),
            jax.ShapeDtypeStruct((rows, width), HALF),
            jax.ShapeDtypeStruct((rows, 256), FULL),
        ]
        + [jax.ShapeDtypeStruct(piece, HALF)] * (shards * chunks),
        compiler_params=params(),
        cost_estimate=pl.CostEstimate(
            flops=2 * rows * depth * width, bytes_accessed=2 * depth * (rows + width), transcendentals=0
        ),
        name="embed",
    )(scal, patches, embed_w, embed_b, gain)
    return emb, normed, stats, [pieces[c * shards : (c + 1) * shards] for c in range(chunks)]


def to_blocks(values, blocks, width):
    half = values.shape[0] // 2
    return [
        jnp.concatenate(
            [values[:half, b * width : (b + 1) * width], values[half:, b * width : (b + 1) * width]], axis=1
        )
        for b in range(blocks)
    ]


def from_blocks(parts, width):
    real = jnp.concatenate([p[:, :width] for p in parts], axis=1)
    imag = jnp.concatenate([p[:, width:] for p in parts], axis=1)
    return real, imag


def table_factor(level, factors):
    return jnp.where(level == 0, factors[0], jnp.where(level == 1, factors[1], factors[2])).astype(FULL)


def table_back(table_ref, level, tops, rests, factor):
    size = table_ref.shape[2]
    total = None
    for at, (top, rest) in enumerate(zip(tops, rests)):
        table = table_ref[level, at * size : (at + 1) * size]
        part = dot(table, top) + dot(table, rest)
        total = part if total is None else total + part
    return total * factor


def two_terms(values):
    top = values.astype(HALF)
    return top, (values - top.astype(FULL)).astype(HALF)


def complex_weights(w_ref, held, blocks, width):
    for layer in range(2):
        for b in range(blocks):
            real, imag = w_ref[layer, 0, b], w_ref[layer, 1, b]
            held[layer, b, :width, :width] = real
            held[layer, b, :width, width:] = imag
            held[layer, b, width:, :width] = -imag
            held[layer, b, width:, width:] = real


def spectral_chunk(scal, table, factors, pieces, spec_w, spec_b, first):
    shards = len(pieces)
    count, per_sample, share = pieces[0].shape
    size = shards * per_sample
    width = spec_w.shape[-1]
    blocks = share // width
    wide = 2 * width

    def body(scal_ref, t_ref, w_ref, b_ref, *refs):
        ins, outs = refs[:shards], refs[shards : 2 * shards]
        spec_ref, hid_ref, fil_ref, weights, held = refs[2 * shards :]

        def bias(layer, b):
            row = pl.ds(scal_ref[SHARD] * blocks + b, 1)
            return jnp.concatenate([b_ref[layer, 0, row], b_ref[layer, 1, row]], axis=1)

        complex_weights(w_ref, weights, blocks, width)
        fill_rows(scal_ref, ins, held)
        levels = [scal_ref[SIDES + SLOTS + first + i] for i in range(count)]
        for i, level in enumerate(levels):
            spectrum = (dot(t_ref[level], held[i]) * table_factor(level, factors)).astype(HALF)
            for b, entry in enumerate(to_blocks(spectrum, blocks, width)):
                spec_ref[b, i * size : (i + 1) * size] = entry
        kept = []
        for b in range(blocks):
            pre_one = dot(spec_ref[b], weights[0, b]) + bias(0, b)
            hidden = jnp.maximum(pre_one, 0.0).astype(HALF)
            hid_ref[b] = hidden
            pre_two = dot(hidden, weights[1, b]) + bias(1, b)
            filtered = jnp.where(
                pre_two > SHRINK, pre_two - SHRINK, jnp.where(pre_two < -SHRINK, pre_two + SHRINK, 0.0)
            )
            top, rest = two_terms(filtered)
            fil_ref[b] = top
            kept.append((top, rest))
        for i, level in enumerate(levels):
            at = slice(i * size, (i + 1) * size)
            tops = from_blocks([top[at] for top, _ in kept], width)
            rests = from_blocks([rest[at] for _, rest in kept], width)
            held[i] = table_back(t_ref, level, tops, rests, table_factor(level, factors)).astype(HALF)
        split_rows(scal_ref, held, outs)

    saved = (blocks, count * size, wide)
    outs = pl.pallas_call(
        body,
        grid_spec=pltpu.PrefetchScalarGridSpec(
            num_scalar_prefetch=1,
            grid=(1,),
            in_specs=[
                whole(table.shape),
                pl.BlockSpec((2, 2, blocks, width, width), lambda i, s: (0, 0, s[SHARD], 0, 0)),
                whole(spec_b.shape),
            ]
            + [whole(pieces[0].shape)] * shards,
            out_specs=[whole(pieces[0].shape)] * shards + [whole(saved)] * 3,
            scratch_shapes=[pltpu.VMEM((2, blocks, wide, wide), HALF), pltpu.VMEM((count, size, share), HALF)],
        ),
        out_shape=[jax.ShapeDtypeStruct(pieces[0].shape, HALF)] * shards + [jax.ShapeDtypeStruct(saved, HALF)] * 3,
        compiler_params=params(),
        cost_estimate=pl.CostEstimate(
            flops=count * size * share * size * 14, bytes_accessed=count * size * share * 16, transcendentals=0
        ),
        name="spectral",
    )(scal, table, spec_w, spec_b, *pieces)
    return outs[:shards], outs[shards:]


def head_chunk(scal, embedded, normed, mixed, targets, head_w, head_b, first, samples, cells):
    shards = len(mixed)
    count, per_sample, share = mixed[0].shape
    rows = count * per_sample
    width, outs = head_w.shape
    at = first // count
    scale_root = float(np.sqrt(np.float32(samples)))

    def body(scal_ref, emb_ref, norm_ref, tgt_ref, w_ref, b_ref, *refs):
        mix_refs, (pred_ref, res_ref, up_ref, bias_ref, held) = refs[:shards], refs[shards:]
        fill_lanes(scal_ref, mix_refs, held)
        side, valid = token_sides(scal_ref, first, count, per_sample, cells)
        updated = (emb_ref[...].astype(FULL) + norm_ref[...].astype(FULL) + held[...].astype(FULL)).astype(HALF)
        output = (dot(updated, w_ref[...]) + b_ref[...]) * valid
        pred_ref[...] = output.astype(HALF).reshape(pred_ref.shape)
        scale = 2.0 / (side.astype(FULL) * scale_root)
        residual = (scale * valid * (output - tgt_ref[...].astype(FULL))).astype(HALF)
        res_ref[...] = residual.reshape(res_ref.shape)
        up_ref[...] = updated
        total = jnp.sum(residual.astype(FULL), axis=0, keepdims=True)
        bias_ref[...] = jnp.broadcast_to(total, bias_ref.shape)

    token_shape = (count, per_sample, outs)
    return pl.pallas_call(
        body,
        grid_spec=pltpu.PrefetchScalarGridSpec(
            num_scalar_prefetch=1,
            grid=(1,),
            in_specs=[
                pl.BlockSpec((rows, width), lambda i, s: (at, 0)),
                pl.BlockSpec((rows, width), lambda i, s: (at, 0)),
                pl.BlockSpec((rows, outs), lambda i, s: (at, 0)),
                whole((width, outs)),
                whole((1, outs)),
            ]
            + [whole(mixed[0].shape)] * shards,
            out_specs=[whole(token_shape), whole(token_shape), whole((rows, width)), whole((8, outs))],
            scratch_shapes=[pltpu.VMEM((rows, width), HALF)],
        ),
        out_shape=[
            jax.ShapeDtypeStruct(token_shape, HALF),
            jax.ShapeDtypeStruct(token_shape, HALF),
            jax.ShapeDtypeStruct((rows, width), HALF),
            jax.ShapeDtypeStruct((8, outs), FULL),
        ],
        compiler_params=params(),
        cost_estimate=pl.CostEstimate(
            flops=2 * rows * width * outs, bytes_accessed=rows * width * 4 + width * outs * 6, transcendentals=0
        ),
        name="head",
    )(scal, embedded, normed, targets, head_w, head_b, *mixed)


def head_gradient(updated, residual):
    width = updated[0].shape[1]
    outs = residual[0].shape[-1]
    count = len(updated)

    def body(*refs):
        total = None
        for up_ref, res_ref in zip(refs[:count], refs[count : 2 * count]):
            part = dot_tn(up_ref[...], res_ref[...].reshape(up_ref.shape[0], outs))
            total = part if total is None else total + part
        refs[-1][...] = total.astype(HALF)

    return pl.pallas_call(
        body,
        out_shape=jax.ShapeDtypeStruct((width, outs), HALF),
        compiler_params=params(),
        cost_estimate=pl.CostEstimate(
            flops=2 * count * updated[0].size * outs, bytes_accessed=2 * count * updated[0].size, transcendentals=0
        ),
        name="head_gradient",
    )(*updated, *residual)


def spectral_back_chunk(scal, table, factors, residual, head_w, spec_w, saved, first, before, last):
    shards = len(residual)
    count, per_sample, outs = residual[0].shape
    size = shards * per_sample
    width = spec_w.shape[-1]
    wide = 2 * width
    share = head_w.shape[0] // shards
    blocks = share // width
    raw_shape = (2, blocks, wide, wide)
    bias_shape = (2 * blocks, wide)
    has_before = before is not None

    def body(scal_ref, t_ref, h_ref, w_ref, spec_ref, hid_ref, fil_ref, *refs):
        ins, refs = refs[:shards], refs[shards:]
        if has_before:
            (old_ref, old_bias_ref), refs = refs[:2], refs[2:]
        pieces, (grad_ref, bias_ref, weights, held, gathered) = refs[:shards], refs[shards:]

        def weight_sums(layer, b, inputs, grads):
            raw = dot_tn(inputs, grads)
            sums = jnp.sum(grads.astype(FULL), axis=0, keepdims=True)
            at = layer * blocks + b
            if has_before:
                raw = raw + old_ref[layer, b]
                sums = sums + old_bias_ref[at : at + 1]
            bias_ref[at : at + 1] = sums
            if not last:
                grad_ref[layer, b] = raw
                return
            real = raw[:width, :width] + raw[width:, width:]
            imag = raw[:width, width:] - raw[width:, :width]
            grad_ref[at * width : (at + 1) * width] = jnp.concatenate([real, imag], axis=1).astype(HALF)

        complex_weights(w_ref, weights, blocks, width)
        fill_rows(scal_ref, ins, gathered)
        levels = [scal_ref[SIDES + SLOTS + first + i] for i in range(count)]
        updated_grad = dot_nt(gathered[...].reshape(count * size, outs), h_ref[...]).astype(HALF)
        entries = []
        for i, level in enumerate(levels):
            filtered_grad = dot(t_ref[level], updated_grad[i * size : (i + 1) * size]) * table_factor(level, factors)
            entries.append(to_blocks(filtered_grad, blocks, width))
        kept = []
        for b in range(blocks):
            entry = jnp.concatenate([e[b] for e in entries], axis=0)
            two_grad = jnp.where(fil_ref[b].astype(FULL) != 0.0, entry, 0.0).astype(HALF)
            hidden = hid_ref[b]
            hidden_grad = dot_nt(two_grad, weights[1, b])
            one_grad = jnp.where(hidden.astype(FULL) > 0.0, hidden_grad, 0.0).astype(HALF)
            kept.append(two_terms(dot_nt(one_grad, weights[0, b])))
            weight_sums(1, b, hidden, two_grad)
            weight_sums(0, b, spec_ref[b], one_grad)
        for i, level in enumerate(levels):
            at = slice(i * size, (i + 1) * size)
            tops = from_blocks([top[at] for top, _ in kept], width)
            rests = from_blocks([rest[at] for _, rest in kept], width)
            held[i] = table_back(t_ref, level, tops, rests, table_factor(level, factors)).astype(HALF)
        split_rows(scal_ref, held, pieces)

    piece = (count, per_sample, share)
    if last:
        grad_out = jax.ShapeDtypeStruct((2 * blocks * width, wide), HALF)
    else:
        grad_out = jax.ShapeDtypeStruct(raw_shape, FULL)
    result = pl.pallas_call(
        body,
        grid_spec=pltpu.PrefetchScalarGridSpec(
            num_scalar_prefetch=1,
            grid=(1,),
            in_specs=[
                whole(table.shape),
                pl.BlockSpec((share, outs), lambda i, s: (s[SHARD], 0)),
                pl.BlockSpec((2, 2, blocks, width, width), lambda i, s: (0, 0, s[SHARD], 0, 0)),
            ]
            + [whole(saved[0].shape)] * 3
            + [whole(residual[0].shape)] * shards
            + ([whole(raw_shape), whole(bias_shape)] if has_before else []),
            out_specs=[whole(piece)] * shards + [whole(grad_out.shape), whole(bias_shape)],
            scratch_shapes=[
                pltpu.VMEM((2, blocks, wide, wide), HALF),
                pltpu.VMEM((count, size, share), HALF),
                pltpu.VMEM((count, size, outs), HALF),
            ],
        ),
        out_shape=[jax.ShapeDtypeStruct(piece, HALF)] * shards
        + [grad_out, jax.ShapeDtypeStruct(bias_shape, FULL)],
        compiler_params=params(),
        cost_estimate=pl.CostEstimate(
            flops=count * size * share * size * 20, bytes_accessed=count * size * share * 16, transcendentals=0
        ),
        name="spectral_back",
    )(scal, table, head_w, spec_w, *saved, *residual, *(before or ()))
    return result[:shards], result[shards:]


def embedded_back_chunk(scal, embedded, stats, residual, head_w, gain, spec_grad, first, cells):
    shards = len(spec_grad)
    count, per_sample, share = spec_grad[0].shape
    rows = count * per_sample
    width, outs = head_w.shape
    at = first // count

    def body(scal_ref, emb_ref, stat_ref, res_ref, w_ref, gain_ref, *refs):
        grad_refs, (out_ref, sums_ref, held) = refs[:shards], refs[shards:]
        fill_lanes(scal_ref, grad_refs, held)
        _, valid = token_sides(scal_ref, first, count, per_sample, cells)
        inv_std = stat_ref[:, 128:129]
        unit = (emb_ref[...].astype(FULL) - stat_ref[:, 0:1]) * inv_std
        direct = dot_nt(res_ref[...].reshape(rows, outs), w_ref[...]).astype(HALF).astype(FULL)
        normed_grad = held[...].astype(FULL) + direct
        gain_grad = jnp.sum(normed_grad * unit, axis=0, keepdims=True)
        unit_grad = normed_grad * gain_ref[...]
        mean_grad = jnp.mean(unit_grad, axis=-1, keepdims=True)
        mean_cross = jnp.mean(unit_grad * unit, axis=-1, keepdims=True)
        input_grad = inv_std * (unit_grad - mean_grad - unit * mean_cross)
        result = ((input_grad + direct) * valid).astype(HALF)
        out_ref[...] = result
        bias_grad = jnp.sum(result.astype(FULL), axis=0, keepdims=True)
        sums_ref[0:4] = jnp.broadcast_to(gain_grad, (4, width))
        sums_ref[4:8] = jnp.broadcast_to(bias_grad, (4, width))

    return pl.pallas_call(
        body,
        grid_spec=pltpu.PrefetchScalarGridSpec(
            num_scalar_prefetch=1,
            grid=(1,),
            in_specs=[
                pl.BlockSpec((rows, width), lambda i, s: (at, 0)),
                pl.BlockSpec((rows, 256), lambda i, s: (at, 0)),
                whole((count, per_sample, outs)),
                whole((width, outs)),
                whole((1, width)),
            ]
            + [whole(spec_grad[0].shape)] * shards,
            out_specs=[whole((rows, width)), whole((8, width))],
            scratch_shapes=[pltpu.VMEM((rows, width), HALF)],
        ),
        out_shape=[jax.ShapeDtypeStruct((rows, width), HALF), jax.ShapeDtypeStruct((8, width), FULL)],
        compiler_params=params(),
        cost_estimate=pl.CostEstimate(
            flops=2 * rows * width * outs, bytes_accessed=rows * width * 6, transcendentals=0
        ),
        name="embedded_back",
    )(scal, embedded, stats, residual, head_w, gain, *spec_grad)


def turned_patches(scal, patches, groups):
    tokens, depth = patches.shape
    block = depth // groups
    tile = 256
    piece = int(np.gcd(tile, block))
    per_block = block // piece

    def body(scal_ref, x_ref, send_ref, keep_ref):
        turned = x_ref[...].T
        for i in range(tile // piece):
            place = pl.program_id(0) * (tile // piece) + i
            group = place // per_block
            rows = pl.ds(pl.multiple_of((place % per_block) * piece, piece), piece)
            values = turned[i * piece : (i + 1) * piece]
            away = jnp.bitwise_xor(group, scal_ref[GROUP]) % 2

            @pl.when(away == 1)
            def _(group=group, rows=rows, values=values):
                send_ref[group // 2, rows] = values

            @pl.when(away == 0)
            def _(group=group, rows=rows, values=values):
                keep_ref[group // 2, rows] = values

    shape = (groups // 2, block, tokens)
    return pl.pallas_call(
        body,
        grid_spec=pltpu.PrefetchScalarGridSpec(
            num_scalar_prefetch=1,
            grid=(depth // tile,),
            in_specs=[pl.BlockSpec((tokens, tile), lambda i, s: (0, i))],
            out_specs=[whole(shape)] * 2,
        ),
        out_shape=[jax.ShapeDtypeStruct(shape, HALF)] * 2,
        compiler_params=params(),
        cost_estimate=pl.CostEstimate(flops=0, bytes_accessed=4 * tokens * depth, transcendentals=0),
        name="turned_patches",
    )(scal, patches)


def embed_grad_parts(scal, turned, grads, groups, away):
    pairs, block, tokens = turned[0].shape
    chunk_rows, width = grads[0].shape
    half = width // 2
    top = pairs // 2
    count = len(turned)
    depth = tokens * count

    def relative(unit):
        return jnp.where(unit < top, 2 * unit + away, unit - top + away * top)

    def body(scal_ref, *refs):
        turned_refs, grad_refs = refs[:count], refs[count : count + len(grads)]
        left_ref, right_ref, held = refs[count + len(grads) :]
        unit = pl.program_id(0)

        @pl.when(unit % top == 0)
        def _():
            for i, ref in enumerate(grad_refs):
                held[i * chunk_rows : (i + 1) * chunk_rows] = ref[...]

        rows = jnp.concatenate([ref[0] for ref in turned_refs], axis=1)
        total = dot(rows, held[...]).astype(HALF)

        @pl.when(unit < top)
        def _():
            left_ref[0] = total

        @pl.when(unit >= top)
        def _():
            right_ref[0] = total

    shape = (top, block, half)
    return pl.pallas_call(
        body,
        grid_spec=pltpu.PrefetchScalarGridSpec(
            num_scalar_prefetch=1,
            grid=(pairs,),
            in_specs=[
                pl.BlockSpec((1, block, tokens), lambda i, s: (jnp.bitwise_xor(s[GROUP] // 2, relative(i)), 0, 0))
                for _ in turned
            ]
            + [pl.BlockSpec((chunk_rows, half), lambda i, s: (0, i // top)) for _ in grads],
            out_specs=[
                pl.BlockSpec((1, block, half), lambda i, s: (jnp.minimum(i, top - 1), 0, 0)),
                pl.BlockSpec((1, block, half), lambda i, s: (jnp.maximum(i - top, 0), 0, 0)),
            ],
            scratch_shapes=[pltpu.VMEM((depth, half), HALF)],
        ),
        out_shape=[jax.ShapeDtypeStruct(shape, HALF)] * 2,
        compiler_params=params(),
        cost_estimate=pl.CostEstimate(
            flops=depth * pairs * block * width,
            bytes_accessed=pairs * block * (2 * depth + width) + depth * width,
            transcendentals=0,
        ),
        name="embed_grad",
    )(scal, *turned, *grads)


def swap_bit(values, bit, groups):
    return lax.ppermute(values, "grp", [(g, g ^ (1 << bit)) for g in range(groups)])


def across(pieces):
    shards = len(pieces)
    return [pieces[0]] + [
        lax.ppermute(pieces[k], "fft", [(z, z ^ k) for z in range(shards)]) for k in range(1, shards)
    ]


def add_half(left, right):
    return (left.astype(FULL) + right.astype(FULL)).astype(HALF)


def scatter_start(received, kept, groups):
    bits = groups.bit_length() - 1
    ends = []
    for first, keep, order, low in (
        (received[0], kept[0], list(range(2, bits)), True),
        (received[1], kept[1], list(range(bits - 2, 0, -1)), False),
    ):
        total = add_half(keep, first)
        for bit in order:
            count, block, width = total.shape
            if low:
                split = total.reshape(count // 2, 2, block, width)
                keep, send = split[:, 0], split[:, 1]
            else:
                split = total.reshape(2, count // 2, block, width)
                keep, send = split[0], split[1]
            total = add_half(keep, swap_bit(send, bit, groups))
        ends.append(total[0])
    return ends


def scatter_end(ends, shards, shard_at):
    share = ends[0].shape[0] // shards

    def piece(k):
        at = jnp.bitwise_xor(shard_at, k) * share
        return jnp.concatenate([lax.dynamic_slice_in_dim(e, at, share) for e in ends], axis=-1)

    return sum(p.astype(FULL) for p in across([piece(k) for k in range(shards)]))


def from_all_groups(values, groups):
    even = [values] + [
        lax.ppermute(values, "grp", [(g, g ^ k) for g in range(groups)]) for k in range(2, groups, 2)
    ]
    odd = [swap_bit(v, 0, groups) for v in even]
    return [v for pair in zip(even, odd) for v in pair]


def hi_lo(values):
    high = lax.optimization_barrier(values.astype(HALF))
    return jnp.concatenate([high, (values - high.astype(FULL)).astype(HALF)], axis=-2)


def from_hi_lo(values):
    half = values.shape[-2] // 2
    values = values.astype(FULL)
    return values[..., :half, :] + values[..., half:, :]


def sum_over_groups(head_grad, spec_grad, groups):
    outs = head_grad.shape[1]
    packed = jnp.concatenate(
        [head_grad.reshape(groups, -1, outs), spec_grad.reshape(groups, -1, outs)], axis=1
    )
    return lax.all_to_all(packed, "grp", split_axis=0, concat_axis=0, tiled=True)


def over_shards(moved, small, head_rows, shards, shard_at):
    summed = jnp.sum(moved.astype(FULL), axis=0).astype(HALF)
    rows = across([jnp.concatenate([summed, hi_lo(small)], axis=0)] * shards)
    head_part = sum(r[:head_rows].astype(FULL) for r in rows).astype(HALF)
    order = jnp.bitwise_xor(jnp.arange(shards, dtype=jnp.int32), shard_at)
    rest = jnp.take(jnp.stack([r[head_rows:] for r in rows]), order, axis=0)
    spec_rows = summed.shape[0] - head_rows
    return head_part, rest[:, :spec_rows], from_hi_lo(rest[:, spec_rows:])


def assembled(scal, gathered, head_rows, shards, blocks, width):
    groups = len(gathered)
    total_blocks = shards * blocks
    spec_rows = 2 * blocks * width // groups
    small_at = head_rows + shards * spec_rows
    small_rows = (gathered[0].shape[0] - small_at) // 2

    def body(scal_ref, *refs):
        ins, (head_ref, spec_ref, small_ref) = refs[:groups], refs[groups:]
        small = None
        for k, ref in enumerate(ins):
            group = jnp.bitwise_xor(scal_ref[GROUP], k)
            at = pl.ds(pl.multiple_of(group * head_rows, head_rows), head_rows)
            head_ref[at, :] = ref[:head_rows].astype(FULL)
            start = group * spec_rows
            layer, b = start // (blocks * width), (start // width) % blocks
            rows = pl.ds(pl.multiple_of(start % width, spec_rows), spec_rows)
            for z in range(shards):
                values = ref[head_rows + z * spec_rows : head_rows + (z + 1) * spec_rows].astype(FULL)
                spec_ref[layer, 0, z * blocks + b, rows] = values[:, :width]
                spec_ref[layer, 1, z * blocks + b, rows] = values[:, width:]
            part = ref[small_at : small_at + small_rows].astype(FULL) + ref[small_at + small_rows :].astype(FULL)
            small = part if small is None else small + part
        small_ref[...] = small

    out_shape = [
        jax.ShapeDtypeStruct((groups * head_rows, 2 * width), FULL),
        jax.ShapeDtypeStruct((2, 2, total_blocks, width, width), FULL),
        jax.ShapeDtypeStruct((small_rows, 2 * width), FULL),
    ]
    return pl.pallas_call(
        body,
        grid_spec=pltpu.PrefetchScalarGridSpec(
            num_scalar_prefetch=1,
            grid=(1,),
            in_specs=[whole(gathered[0].shape)] * groups,
            out_specs=[whole(o.shape) for o in out_shape],
        ),
        out_shape=out_shape,
        compiler_params=params(),
        name="assembled",
    )(scal, *gathered)


def route_predictions(predicted, dest_group, group_at, groups, slot_count):
    own_dest = lax.dynamic_slice_in_dim(dest_group, group_at * slot_count, slot_count)
    matches = own_dest[None, :] == jnp.arange(groups, dtype=jnp.int32)[:, None]
    chosen = jnp.sum(jnp.where(matches, jnp.arange(slot_count, dtype=jnp.int32)[None, :], 0), axis=1)
    outgoing = jnp.take(predicted, chosen, axis=0)
    moved = lax.all_to_all(outgoing, "grp", split_axis=0, concat_axis=0, tiled=True)
    loaders = jnp.arange(groups, dtype=jnp.int32)
    holds = jnp.any(dest_group.reshape(groups, slot_count) == group_at, axis=1)
    rank = jnp.sum(jnp.where(holds[None, :] & (loaders[None, :] < loaders[:, None]), 1, 0), axis=1)
    slots = jnp.arange(slot_count, dtype=jnp.int32)
    sources = jnp.sum(jnp.where(holds[None, :] & (rank[None, :] == slots[:, None]), loaders[None, :], 0), axis=1)
    return jnp.take(moved, sources, axis=0)


def on_device(
    patches, targets, grid_side, dest_group, embed_w, embed_b, gain, spec_w, spec_b, head_w, head_b
):
    slot_count, row_count, cells, depth = patches.shape
    samples = dest_group.shape[0]
    groups = lax.axis_size("grp")
    shards = lax.axis_size("fft")
    group_at = lax.axis_index("grp").astype(jnp.int32)
    shard_at = lax.axis_index("fft").astype(jnp.int32)
    outs = targets.shape[-1]
    per_sample = row_count * cells
    count = slot_count // CHUNKS
    firsts = [c * count for c in range(CHUNKS)]
    assert slot_count == SLOTS

    sides = lax.dynamic_slice_in_dim(grid_side, group_at * slot_count, slot_count)
    level = jnp.where(sides == cells, 0, jnp.where(sides == cells // 2, 1, 2)).astype(jnp.int32)
    scal = jnp.concatenate([jnp.stack([shard_at, shard_at * row_count, group_at]), sides, level])
    table_values, factors = dft_tables(cells)
    table = jnp.asarray(table_values)
    flat_patches = patches.reshape(-1, depth)
    flat_targets = targets.reshape(-1, outs)
    gain_row, embed_b_row, head_b_row = gain[None], embed_b[None], head_b[None]

    embedded, normed, stats, pieces = embed(
        scal, flat_patches, embed_w, embed_b_row, gain_row, firsts, count, per_sample, cells, shards
    )
    moved = [across(p) for p in pieces]
    turned_send, turned_keep = turned_patches(scal, flat_patches, groups)
    turned = [turned_keep, swap_bit(turned_send, 0, groups)]
    moved[0], turned_keep = lax.optimization_barrier((moved[0], turned_keep))
    turned[0] = turned_keep
    mixed, saved = [], []
    for first, values in zip(firsts, moved):
        out, rest = spectral_chunk(scal, table, factors, values, spec_w, spec_b, first)
        mixed.append(across(out))
        saved.append(rest)
    predicted, residual, updated, head_sums, gathered = [], [], [], [], []
    for first, mix in zip(firsts, mixed):
        pred, res, up, sums = head_chunk(
            scal, embedded, normed, mix, flat_targets, head_w, head_b_row, first, samples, cells
        )
        predicted.append(pred)
        residual.append(res)
        updated.append(up)
        head_sums.append(sums[0])
        gathered.append(across([res] * shards))
    head_grad, gathered[0] = lax.optimization_barrier((head_gradient(updated, residual), gathered[0]))
    spec_back, sums = [], None
    for first, res, rest in zip(firsts, gathered, saved):
        values, sums = spectral_back_chunk(
            scal, table, factors, res, head_w, spec_w, rest, first, sums, first == firsts[-1]
        )
        spec_back.append(across(values))
    spec_grad, spec_bias = sums
    width = spec_w.shape[-1]
    blocks = spec_w.shape[2] // shards
    head_rows = head_w.shape[0] // groups
    weight_sums = sum_over_groups(head_grad, spec_grad, groups)
    own_grads, other_grads, row_sums = [], [], []
    for first, res, back in zip(firsts, residual, spec_back):
        grad, row_sum = embedded_back_chunk(scal, embedded, stats, res, head_w, gain_row, back, first, cells)
        own_grads.append(grad)
        other_grads.append(swap_bit(grad, 0, groups))
        row_sums.append(row_sum)
    grads = own_grads + other_grads
    sent = embed_grad_parts(scal, turned, grads, groups, 1)
    top_bit = groups.bit_length() - 2
    received = [swap_bit(sent[0], 1, groups), swap_bit(sent[1], top_bit, groups)]
    kept = embed_grad_parts(scal, turned, grads, groups, 0)
    kept, weight_sums, predicted, row_sums = lax.optimization_barrier((kept, weight_sums, predicted, row_sums))
    ends = scatter_start(received, kept, groups)
    predictions = route_predictions(
        jnp.concatenate(predicted, axis=0), dest_group, group_at, groups, slot_count
    ).reshape(targets.shape)
    rows = sum(row_sums)
    vectors = jnp.concatenate([rows[0].reshape(-1, outs), rows[4].reshape(-1, outs), sum(head_sums)[None]], axis=0)
    own_rows, all_rows = spec_bias.shape[0], vectors.shape[0]
    small = jnp.concatenate([spec_bias, vectors, jnp.zeros((16 - own_rows - all_rows, outs), FULL)], axis=0)
    head_part, spec_part, small = over_shards(weight_sums, small, head_rows, shards, shard_at)
    small = jnp.concatenate([small[:, :own_rows].reshape(-1, outs), jnp.sum(small[:, own_rows:], axis=0)], axis=0)
    small = jnp.concatenate([small, jnp.zeros((-small.shape[0] % 16, outs), FULL)], axis=0)
    outgoing = jnp.concatenate([head_part, spec_part.reshape(-1, outs), hi_lo(small)], axis=0)
    ends, outgoing = lax.optimization_barrier((ends, outgoing))
    gathered = from_all_groups(outgoing, groups)
    embed_grad = scatter_end(ends, shards, shard_at)
    head_grad, spec_w_grad, small = assembled(scal, gathered, head_rows, shards, blocks, width)
    spec_bias_all = small[: shards * own_rows].reshape(shards, 2, blocks, 2, width)
    spec_b_grad = jnp.transpose(spec_bias_all, (1, 3, 0, 2, 4)).reshape(spec_b.shape)
    vectors = small[shards * own_rows : shards * own_rows + all_rows]
    quarter = (all_rows - 1) // 2
    gain_grad, embed_bias_grad = vectors[:quarter].reshape(-1), vectors[quarter : 2 * quarter].reshape(-1)
    head_bias_grad = vectors[2 * quarter]
    return (
        predictions,
        embed_grad,
        embed_bias_grad,
        gain_grad,
        spec_w_grad,
        spec_b_grad,
        head_grad,
        head_bias_grad,
    )


def solution(mesh):
    return jax.shard_map(
        on_device,
        mesh=mesh,
        in_specs=(
            P("grp", "fft", None, None),
            P("grp", "fft", None, None),
            P(),
            P(),
            P(),
            P(),
            P(),
            P(),
            P(),
            P(),
            P(),
        ),
        out_specs=(
            P("grp", "fft", None, None),
            P(("grp", "fft"), None),
            P(),
            P(),
            P(),
            P(),
            P(),
            P(),
        ),
        check_vma=False,
    )
```

```python
import jax
import jax.numpy as jnp
import ml_dtypes
import numpy as np
from jax import lax
from jax.experimental import pallas as pl
from jax.experimental.pallas import tpu as pltpu
from jax.sharding import PartitionSpec as P

EPSILON = 1e-05
SHRINK = 0.01
CHUNKS = 2
VMEM_BYTES = 24 * 1024 * 1024
SLOTS = 6
SHARD, FIRST_ROW, GROUP, SIDES = 0, 1, 2, 3
HALF = jnp.bfloat16
FULL = jnp.float32


def dft_tables(cells):
    levels, factors = [], []
    for side, scale in ((cells, 1.1305), (cells // 2, 1.8633), (cells // 4, 1.0)):
        k = np.arange(cells)
        inside = (k < side).astype(np.float64)
        keep = inside[:, None] * inside[None, :]
        angle = 2.0 * np.pi * ((k[:, None] * k[None, :]) % side) / side
        one = np.exp(-1j * angle) * keep / np.sqrt(side)
        two = np.kron(one, one)
        table = np.concatenate([two.real, two.imag], axis=0)
        table[np.abs(table) < 1e-12] = 0.0
        rounded = (table * scale).astype(np.float32).astype(ml_dtypes.bfloat16)
        held = rounded.astype(np.float64)
        factors.append(float(np.sum(table * table) / np.sum(table * held)))
        levels.append(rounded)
    return np.stack(levels), factors


def dot(left, right):
    return jnp.dot(left, right, preferred_element_type=FULL)


def dot_tn(left, right):
    return lax.dot_general(left, right, (((0,), (0,)), ((), ())), preferred_element_type=FULL)


def dot_nt(left, right):
    return lax.dot_general(left, right, (((1,), (1,)), ((), ())), preferred_element_type=FULL)


def params(limit=VMEM_BYTES):
    return pltpu.CompilerParams(vmem_limit_bytes=limit)


def token_sides(scal_ref, first, count, per_sample, cells):
    token = lax.broadcasted_iota(jnp.int32, (count * per_sample, 1), 0)
    sample = token // per_sample
    side = jnp.zeros_like(token)
    for i in range(count):
        side = jnp.where(sample == i, scal_ref[SIDES + first + i], side)
    row = scal_ref[FIRST_ROW] + (token % per_sample) // cells
    col = token % cells
    valid = jnp.where((row < side) & (col < side), 1.0, 0.0).astype(FULL)
    return side, valid


def whole(shape):
    return pl.BlockSpec(tuple(shape), lambda i, s: (0,) * len(shape))


def part_of(scal_ref, k, size):
    at = jnp.bitwise_xor(scal_ref[SHARD], k)
    return pl.ds(pl.multiple_of(at * size, size), size)


def fill_lanes(scal_ref, refs, held):
    share = refs[0].shape[-1]
    for k, ref in enumerate(refs):
        held[:, part_of(scal_ref, k, share)] = ref[...].reshape(held.shape[0], share)


def fill_rows(scal_ref, refs, held):
    rows = refs[0].shape[1]
    for k, ref in enumerate(refs):
        held[:, part_of(scal_ref, k, rows), :] = ref[...]


def split_lanes(scal_ref, held, refs):
    share = refs[0].shape[-1]
    for k, ref in enumerate(refs):
        ref[...] = held[:, part_of(scal_ref, k, share)].reshape(ref.shape)


def split_rows(scal_ref, held, refs):
    rows = refs[0].shape[1]
    for k, ref in enumerate(refs):
        ref[...] = held[:, part_of(scal_ref, k, rows), :]


def embed(scal, patches, embed_w, embed_b, gain, firsts, count, per_sample, cells, shards, groups):
    rows, depth = patches.shape
    block = depth // groups
    width = embed_w.shape[1]
    share = width // shards
    chunk_rows = count * per_sample
    chunks = len(firsts)
    steps = 4
    tile = depth // steps

    def body(scal_ref, x_ref, w_ref, b_ref, gain_ref, emb_ref, norm_ref, stat_ref, *refs):
        (send_ref, keep_ref), outs, acc = refs[:2], refs[2:-1], refs[-1]
        step = pl.program_id(0)
        turned = x_ref[...].T
        for i in range(tile // block):
            values = turned[i * block : (i + 1) * block]
            away = (scal_ref[GROUP] + i) % 2

            @pl.when(away == 1)
            def _(i=i, values=values):
                send_ref[i // 2] = values

            @pl.when(away == 0)
            def _(i=i, values=values):
                keep_ref[i // 2] = values

        part = dot(x_ref[...], w_ref[...])

        @pl.when(step == 0)
        def _():
            acc[...] = part

        @pl.when(step > 0)
        def _():
            acc[...] += part

        @pl.when(step == steps - 1)
        def _():
            for c, first in enumerate(firsts):
                at = slice(c * chunk_rows, (c + 1) * chunk_rows)
                _, valid = token_sides(scal_ref, first, count, per_sample, cells)
                embedded = ((acc[at] + b_ref[...]) * valid).astype(HALF)
                emb_ref[at] = embedded
                values = embedded.astype(FULL)
                mean = jnp.mean(values, axis=-1, keepdims=True)
                centered = values - mean
                inv_std = lax.rsqrt(jnp.mean(centered * centered, axis=-1, keepdims=True) + EPSILON)
                norm_ref[at] = (centered * inv_std * gain_ref[...]).astype(HALF)
                stat_ref[at, :128] = jnp.broadcast_to(mean, (chunk_rows, 128))
                stat_ref[at, 128:] = jnp.broadcast_to(inv_std, (chunk_rows, 128))
                for k in range(shards):
                    piece = norm_ref[at, part_of(scal_ref, k, share)]
                    outs[c * shards + k][...] = piece.reshape(count, per_sample, share)

    piece = (count, per_sample, share)
    turned_spec = pl.BlockSpec((tile // (2 * block), block, rows), lambda k, s: (k, 0, 0))
    turned_shape = jax.ShapeDtypeStruct((groups // 2, block, rows), HALF)
    emb, normed, stats, send, keep, *pieces = pl.pallas_call(
        body,
        grid_spec=pltpu.PrefetchScalarGridSpec(
            num_scalar_prefetch=1,
            grid=(steps,),
            in_specs=[
                pl.BlockSpec((rows, tile), lambda k, s: (0, k)),
                pl.BlockSpec((tile, width), lambda k, s: (k, 0)),
                whole((1, width)),
                whole((1, width)),
            ],
            out_specs=[whole((rows, width)), whole((rows, width)), whole((rows, 256)), turned_spec, turned_spec]
            + [whole(piece)] * (shards * chunks),
            scratch_shapes=[pltpu.VMEM((rows, width), FULL)],
        ),
        out_shape=[
            jax.ShapeDtypeStruct((rows, width), HALF),
            jax.ShapeDtypeStruct((rows, width), HALF),
            jax.ShapeDtypeStruct((rows, 256), FULL),
            turned_shape,
            turned_shape,
        ]
        + [jax.ShapeDtypeStruct(piece, HALF)] * (shards * chunks),
        compiler_params=params(60 * 1024 * 1024),
        cost_estimate=pl.CostEstimate(
            flops=2 * rows * depth * width, bytes_accessed=2 * depth * (rows + width), transcendentals=0
        ),
        name="embed",
    )(scal, patches, embed_w, embed_b, gain)
    return emb, normed, stats, send, keep, [pieces[c * shards : (c + 1) * shards] for c in range(chunks)]


def to_blocks(values, blocks, width):
    half = values.shape[0] // 2
    return [
        jnp.concatenate(
            [values[:half, b * width : (b + 1) * width], values[half:, b * width : (b + 1) * width]], axis=1
        )
        for b in range(blocks)
    ]


def from_blocks(parts, width):
    real = jnp.concatenate([p[:, :width] for p in parts], axis=1)
    imag = jnp.concatenate([p[:, width:] for p in parts], axis=1)
    return real, imag


def table_factor(level, factors):
    return jnp.where(level == 0, factors[0], jnp.where(level == 1, factors[1], factors[2])).astype(FULL)


def table_back(table_ref, level, tops, rests, factor):
    size = table_ref.shape[2]
    total = None
    for at, (top, rest) in enumerate(zip(tops, rests)):
        table = table_ref[level, at * size : (at + 1) * size]
        part = dot(table, top) + dot(table, rest)
        total = part if total is None else total + part
    return total * factor


def two_terms(values):
    top = values.astype(HALF)
    return top, (values - top.astype(FULL)).astype(HALF)


def complex_weights(w_ref, held, blocks, width):
    for layer in range(2):
        for b in range(blocks):
            real, imag = w_ref[layer, 0, b], w_ref[layer, 1, b]
            held[layer, b, :width, :width] = real
            held[layer, b, :width, width:] = imag
            held[layer, b, width:, :width] = -imag
            held[layer, b, width:, width:] = real


def spectral_chunk(scal, table, factors, pieces, spec_w, spec_b, first):
    shards = len(pieces)
    count, per_sample, share = pieces[0].shape
    size = shards * per_sample
    width = spec_w.shape[-1]
    blocks = share // width
    wide = 2 * width

    def body(scal_ref, t_ref, w_ref, b_ref, *refs):
        ins, outs = refs[:shards], refs[shards : 2 * shards]
        spec_ref, hid_ref, fil_ref, weights, held = refs[2 * shards :]

        def bias(layer, b):
            row = pl.ds(scal_ref[SHARD] * blocks + b, 1)
            return jnp.concatenate([b_ref[layer, 0, row], b_ref[layer, 1, row]], axis=1)

        complex_weights(w_ref, weights, blocks, width)
        fill_rows(scal_ref, ins, held)
        levels = [scal_ref[SIDES + SLOTS + first + i] for i in range(count)]
        for i, level in enumerate(levels):
            spectrum = (dot(t_ref[level], held[i]) * table_factor(level, factors)).astype(HALF)
            for b, entry in enumerate(to_blocks(spectrum, blocks, width)):
                spec_ref[b, i * size : (i + 1) * size] = entry
        kept = []
        for b in range(blocks):
            pre_one = dot(spec_ref[b], weights[0, b]) + bias(0, b)
            hidden = jnp.maximum(pre_one, 0.0).astype(HALF)
            hid_ref[b] = hidden
            pre_two = dot(hidden, weights[1, b]) + bias(1, b)
            filtered = jnp.where(
                pre_two > SHRINK, pre_two - SHRINK, jnp.where(pre_two < -SHRINK, pre_two + SHRINK, 0.0)
            )
            top, rest = two_terms(filtered)
            fil_ref[b] = top
            kept.append((top, rest))
        for i, level in enumerate(levels):
            at = slice(i * size, (i + 1) * size)
            tops = from_blocks([top[at] for top, _ in kept], width)
            rests = from_blocks([rest[at] for _, rest in kept], width)
            held[i] = table_back(t_ref, level, tops, rests, table_factor(level, factors)).astype(HALF)
        split_rows(scal_ref, held, outs)

    saved = (blocks, count * size, wide)
    outs = pl.pallas_call(
        body,
        grid_spec=pltpu.PrefetchScalarGridSpec(
            num_scalar_prefetch=1,
            grid=(1,),
            in_specs=[
                whole(table.shape),
                pl.BlockSpec((2, 2, blocks, width, width), lambda i, s: (0, 0, s[SHARD], 0, 0)),
                whole(spec_b.shape),
            ]
            + [whole(pieces[0].shape)] * shards,
            out_specs=[whole(pieces[0].shape)] * shards + [whole(saved)] * 3,
            scratch_shapes=[pltpu.VMEM((2, blocks, wide, wide), HALF), pltpu.VMEM((count, size, share), HALF)],
        ),
        out_shape=[jax.ShapeDtypeStruct(pieces[0].shape, HALF)] * shards + [jax.ShapeDtypeStruct(saved, HALF)] * 3,
        compiler_params=params(),
        cost_estimate=pl.CostEstimate(
            flops=count * size * share * size * 14, bytes_accessed=count * size * share * 16, transcendentals=0
        ),
        name="spectral",
    )(scal, table, spec_w, spec_b, *pieces)
    return outs[:shards], outs[shards:]


def head_chunk(scal, embedded, normed, mixed, targets, head_w, head_b, first, samples, cells):
    shards = len(mixed)
    count, per_sample, share = mixed[0].shape
    rows = count * per_sample
    width, outs = head_w.shape
    at = first // count
    scale_root = float(np.sqrt(np.float32(samples)))

    def body(scal_ref, emb_ref, norm_ref, tgt_ref, w_ref, b_ref, *refs):
        mix_refs, (pred_ref, res_ref, all_ref, up_ref, bias_ref, held) = refs[:shards], refs[shards:]
        fill_lanes(scal_ref, mix_refs, held)
        side, valid = token_sides(scal_ref, first, count, per_sample, cells)
        updated = (emb_ref[...].astype(FULL) + norm_ref[...].astype(FULL) + held[...].astype(FULL)).astype(HALF)
        output = (dot(updated, w_ref[...]) + b_ref[...]) * valid
        pred_ref[...] = output.astype(HALF).reshape(pred_ref.shape)
        scale = 2.0 / (side.astype(FULL) * scale_root)
        residual = (scale * valid * (output - tgt_ref[...].astype(FULL))).astype(HALF)
        res_ref[...] = residual.reshape(res_ref.shape)
        for z in range(shards):
            all_ref[z] = residual.reshape(res_ref.shape)
        up_ref[...] = updated
        total = jnp.sum(residual.astype(FULL), axis=0, keepdims=True)
        bias_ref[...] = jnp.broadcast_to(total, bias_ref.shape)

    token_shape = (count, per_sample, outs)
    return pl.pallas_call(
        body,
        grid_spec=pltpu.PrefetchScalarGridSpec(
            num_scalar_prefetch=1,
            grid=(1,),
            in_specs=[
                pl.BlockSpec((rows, width), lambda i, s: (at, 0)),
                pl.BlockSpec((rows, width), lambda i, s: (at, 0)),
                pl.BlockSpec((rows, outs), lambda i, s: (at, 0)),
                whole((width, outs)),
                whole((1, outs)),
            ]
            + [whole(mixed[0].shape)] * shards,
            out_specs=[
                whole(token_shape),
                whole(token_shape),
                whole((shards,) + token_shape),
                whole((rows, width)),
                whole((8, outs)),
            ],
            scratch_shapes=[pltpu.VMEM((rows, width), HALF)],
        ),
        out_shape=[
            jax.ShapeDtypeStruct(token_shape, HALF),
            jax.ShapeDtypeStruct(token_shape, HALF),
            jax.ShapeDtypeStruct((shards,) + token_shape, HALF),
            jax.ShapeDtypeStruct((rows, width), HALF),
            jax.ShapeDtypeStruct((8, outs), FULL),
        ],
        compiler_params=params(),
        cost_estimate=pl.CostEstimate(
            flops=2 * rows * width * outs, bytes_accessed=rows * width * 4 + width * outs * 6, transcendentals=0
        ),
        name="head",
    )(scal, embedded, normed, targets, head_w, head_b, *mixed)


def head_gradient(updated, residual):
    width = updated[0].shape[1]
    outs = residual[0].shape[-1]
    count = len(updated)

    def body(*refs):
        total = None
        for up_ref, res_ref in zip(refs[:count], refs[count : 2 * count]):
            part = dot_tn(up_ref[...], res_ref[...].reshape(up_ref.shape[0], outs))
            total = part if total is None else total + part
        refs[-1][...] = total.astype(HALF)

    return pl.pallas_call(
        body,
        out_shape=jax.ShapeDtypeStruct((width, outs), HALF),
        compiler_params=params(),
        cost_estimate=pl.CostEstimate(
            flops=2 * count * updated[0].size * outs, bytes_accessed=2 * count * updated[0].size, transcendentals=0
        ),
        name="head_gradient",
    )(*updated, *residual)


def spectral_back_chunk(scal, table, factors, residual, head_w, spec_w, saved, first, before, last):
    shards, count, per_sample, outs = residual.shape
    size = shards * per_sample
    width = spec_w.shape[-1]
    wide = 2 * width
    share = head_w.shape[0] // shards
    blocks = share // width
    raw_shape = (2, blocks, wide, wide)
    bias_shape = (2 * blocks, wide)
    has_before = before is not None

    def body(scal_ref, t_ref, h_ref, w_ref, spec_ref, hid_ref, fil_ref, *refs):
        in_ref, refs = refs[0], refs[1:]
        if has_before:
            (old_ref, old_bias_ref), refs = refs[:2], refs[2:]
        pieces, (grad_ref, bias_ref, weights, held, gathered) = refs[:shards], refs[shards:]

        def weight_sums(layer, b, inputs, grads):
            raw = dot_tn(inputs, grads)
            sums = jnp.sum(grads.astype(FULL), axis=0, keepdims=True)
            at = layer * blocks + b
            if has_before:
                raw = raw + old_ref[layer, b]
                sums = sums + old_bias_ref[at : at + 1]
            bias_ref[at : at + 1] = sums
            if not last:
                grad_ref[layer, b] = raw
                return
            real = raw[:width, :width] + raw[width:, width:]
            imag = raw[:width, width:] - raw[width:, :width]
            grad_ref[at * width : (at + 1) * width] = jnp.concatenate([real, imag], axis=1).astype(HALF)

        complex_weights(w_ref, weights, blocks, width)
        for z in range(shards):
            gathered[:, z * per_sample : (z + 1) * per_sample, :] = in_ref[z]
        levels = [scal_ref[SIDES + SLOTS + first + i] for i in range(count)]
        updated_grad = dot_nt(gathered[...].reshape(count * size, outs), h_ref[...]).astype(HALF)
        entries = []
        for i, level in enumerate(levels):
            filtered_grad = dot(t_ref[level], updated_grad[i * size : (i + 1) * size]) * table_factor(level, factors)
            entries.append(to_blocks(filtered_grad, blocks, width))
        kept = []
        for b in range(blocks):
            entry = jnp.concatenate([e[b] for e in entries], axis=0)
            two_grad = jnp.where(fil_ref[b].astype(FULL) != 0.0, entry, 0.0).astype(HALF)
            hidden = hid_ref[b]
            hidden_grad = dot_nt(two_grad, weights[1, b])
            one_grad = jnp.where(hidden.astype(FULL) > 0.0, hidden_grad, 0.0).astype(HALF)
            kept.append(two_terms(dot_nt(one_grad, weights[0, b])))
            weight_sums(1, b, hidden, two_grad)
            weight_sums(0, b, spec_ref[b], one_grad)
        for i, level in enumerate(levels):
            at = slice(i * size, (i + 1) * size)
            tops = from_blocks([top[at] for top, _ in kept], width)
            rests = from_blocks([rest[at] for _, rest in kept], width)
            held[i] = table_back(t_ref, level, tops, rests, table_factor(level, factors)).astype(HALF)
        split_rows(scal_ref, held, pieces)

    piece = (count, per_sample, share)
    if last:
        grad_out = jax.ShapeDtypeStruct((2 * blocks * width, wide), HALF)
    else:
        grad_out = jax.ShapeDtypeStruct(raw_shape, FULL)
    result = pl.pallas_call(
        body,
        grid_spec=pltpu.PrefetchScalarGridSpec(
            num_scalar_prefetch=1,
            grid=(1,),
            in_specs=[
                whole(table.shape),
                pl.BlockSpec((share, outs), lambda i, s: (s[SHARD], 0)),
                pl.BlockSpec((2, 2, blocks, width, width), lambda i, s: (0, 0, s[SHARD], 0, 0)),
            ]
            + [whole(saved[0].shape)] * 3
            + [whole(residual.shape)]
            + ([whole(raw_shape), whole(bias_shape)] if has_before else []),
            out_specs=[whole(piece)] * shards + [whole(grad_out.shape), whole(bias_shape)],
            scratch_shapes=[
                pltpu.VMEM((2, blocks, wide, wide), HALF),
                pltpu.VMEM((count, size, share), HALF),
                pltpu.VMEM((count, size, outs), HALF),
            ],
        ),
        out_shape=[jax.ShapeDtypeStruct(piece, HALF)] * shards
        + [grad_out, jax.ShapeDtypeStruct(bias_shape, FULL)],
        compiler_params=params(),
        cost_estimate=pl.CostEstimate(
            flops=count * size * share * size * 20, bytes_accessed=count * size * share * 16, transcendentals=0
        ),
        name="spectral_back",
    )(scal, table, head_w, spec_w, *saved, residual, *(before or ()))
    return result[:shards], result[shards:]


def embedded_back_chunk(scal, embedded, stats, residual, head_w, gain, spec_grad, first, cells):
    shards = len(spec_grad)
    count, per_sample, share = spec_grad[0].shape
    rows = count * per_sample
    width, outs = head_w.shape
    at = first // count

    def body(scal_ref, emb_ref, stat_ref, res_ref, w_ref, gain_ref, *refs):
        grad_refs, (out_ref, sums_ref, held) = refs[:shards], refs[shards:]
        fill_lanes(scal_ref, grad_refs, held)
        _, valid = token_sides(scal_ref, first, count, per_sample, cells)
        inv_std = stat_ref[:, 128:129]
        unit = (emb_ref[...].astype(FULL) - stat_ref[:, 0:1]) * inv_std
        direct = dot_nt(res_ref[...].reshape(rows, outs), w_ref[...]).astype(HALF).astype(FULL)
        normed_grad = held[...].astype(FULL) + direct
        gain_grad = jnp.sum(normed_grad * unit, axis=0, keepdims=True)
        unit_grad = normed_grad * gain_ref[...]
        mean_grad = jnp.mean(unit_grad, axis=-1, keepdims=True)
        mean_cross = jnp.mean(unit_grad * unit, axis=-1, keepdims=True)
        input_grad = inv_std * (unit_grad - mean_grad - unit * mean_cross)
        result = ((input_grad + direct) * valid).astype(HALF)
        out_ref[...] = result
        bias_grad = jnp.sum(result.astype(FULL), axis=0, keepdims=True)
        sums_ref[0:4] = jnp.broadcast_to(gain_grad, (4, width))
        sums_ref[4:8] = jnp.broadcast_to(bias_grad, (4, width))

    return pl.pallas_call(
        body,
        grid_spec=pltpu.PrefetchScalarGridSpec(
            num_scalar_prefetch=1,
            grid=(1,),
            in_specs=[
                pl.BlockSpec((rows, width), lambda i, s: (at, 0)),
                pl.BlockSpec((rows, 256), lambda i, s: (at, 0)),
                whole((count, per_sample, outs)),
                whole((width, outs)),
                whole((1, width)),
            ]
            + [whole(spec_grad[0].shape)] * shards,
            out_specs=[whole((rows, width)), whole((8, width))],
            scratch_shapes=[pltpu.VMEM((rows, width), HALF)],
        ),
        out_shape=[jax.ShapeDtypeStruct((rows, width), HALF), jax.ShapeDtypeStruct((8, width), FULL)],
        compiler_params=params(),
        cost_estimate=pl.CostEstimate(
            flops=2 * rows * width * outs, bytes_accessed=rows * width * 6, transcendentals=0
        ),
        name="embedded_back",
    )(scal, embedded, stats, residual, head_w, gain, *spec_grad)


def embed_grad_parts(scal, turned, grads, groups, away):
    pairs, block, tokens = turned[0].shape
    chunk_rows, width = grads[0].shape
    half = width // 2
    top = pairs // 2
    count = len(turned)
    depth = tokens * count

    def relative(unit):
        return jnp.where(unit < top, 2 * unit + away, unit - top + away * top)

    def body(scal_ref, *refs):
        turned_refs, grad_refs = refs[:count], refs[count : count + len(grads)]
        left_ref, right_ref, held = refs[count + len(grads) :]
        unit = pl.program_id(0)

        @pl.when(unit % top == 0)
        def _():
            for i, ref in enumerate(grad_refs):
                held[i * chunk_rows : (i + 1) * chunk_rows] = ref[...]

        rows = jnp.concatenate([ref[0] for ref in turned_refs], axis=1)
        total = dot(rows, held[...]).astype(HALF)

        @pl.when(unit < top)
        def _():
            left_ref[0] = total

        @pl.when(unit >= top)
        def _():
            right_ref[0] = total

    shape = (top, block, half)
    return pl.pallas_call(
        body,
        grid_spec=pltpu.PrefetchScalarGridSpec(
            num_scalar_prefetch=1,
            grid=(pairs,),
            in_specs=[
                pl.BlockSpec((1, block, tokens), lambda i, s: (jnp.bitwise_xor(s[GROUP] // 2, relative(i)), 0, 0))
                for _ in turned
            ]
            + [pl.BlockSpec((chunk_rows, half), lambda i, s: (0, i // top)) for _ in grads],
            out_specs=[
                pl.BlockSpec((1, block, half), lambda i, s: (jnp.minimum(i, top - 1), 0, 0)),
                pl.BlockSpec((1, block, half), lambda i, s: (jnp.maximum(i - top, 0), 0, 0)),
            ],
            scratch_shapes=[pltpu.VMEM((depth, half), HALF)],
        ),
        out_shape=[jax.ShapeDtypeStruct(shape, HALF)] * 2,
        compiler_params=params(),
        cost_estimate=pl.CostEstimate(
            flops=depth * pairs * block * width,
            bytes_accessed=pairs * block * (2 * depth + width) + depth * width,
            transcendentals=0,
        ),
        name="embed_grad",
    )(scal, *turned, *grads)


def swap_bit(values, bit, groups):
    return lax.ppermute(values, "grp", [(g, g ^ (1 << bit)) for g in range(groups)])


def across(pieces):
    shards = len(pieces)
    return [pieces[0]] + [
        lax.ppermute(pieces[k], "fft", [(z, z ^ k) for z in range(shards)]) for k in range(1, shards)
    ]


def add_half(left, right):
    return (left.astype(FULL) + right.astype(FULL)).astype(HALF)


def scatter_start(received, kept, groups):
    bits = groups.bit_length() - 1
    ends = []
    for first, keep, order, low in (
        (received[0], kept[0], list(range(2, bits)), True),
        (received[1], kept[1], list(range(bits - 2, 0, -1)), False),
    ):
        total = add_half(keep, first)
        for bit in order:
            count, block, width = total.shape
            if low:
                split = total.reshape(count // 2, 2, block, width)
                keep, send = split[:, 0], split[:, 1]
            else:
                split = total.reshape(2, count // 2, block, width)
                keep, send = split[0], split[1]
            total = add_half(keep, swap_bit(send, bit, groups))
        ends.append(total[0])
    return ends


def scatter_end(ends, shards, shard_at):
    part = jnp.concatenate(ends, axis=-1)
    part = part.reshape(shards, part.shape[0] // shards, -1)
    bit = 1
    while bit < shards:
        split = part.reshape(part.shape[0] // 2, 2, *part.shape[1:])
        mine = (shard_at // bit) % 2
        keep = lax.dynamic_index_in_dim(split, mine, 1, keepdims=False)
        send = lax.dynamic_index_in_dim(split, 1 - mine, 1, keepdims=False)
        received = lax.ppermute(send, "fft", [(z, z ^ bit) for z in range(shards)])
        part = keep.astype(FULL) + received.astype(FULL)
        bit *= 2
        if bit < shards:
            part = part.astype(HALF)
    return part[0]


def from_all_groups(values, groups):
    even = [values] + [
        lax.ppermute(values, "grp", [(g, g ^ k) for g in range(groups)]) for k in range(2, groups, 2)
    ]
    odd = [swap_bit(v, 0, groups) for v in even]
    return [v for pair in zip(even, odd) for v in pair]


def hi_lo(values):
    high = lax.optimization_barrier(values.astype(HALF))
    return jnp.concatenate([high, (values - high.astype(FULL)).astype(HALF)], axis=-2)


def from_hi_lo(values):
    half = values.shape[-2] // 2
    values = values.astype(FULL)
    return values[..., :half, :] + values[..., half:, :]


def sum_over_groups(head_grad, spec_grad, groups):
    outs = head_grad.shape[1]
    packed = jnp.concatenate(
        [head_grad.reshape(groups, -1, outs), spec_grad.reshape(groups, -1, outs)], axis=1
    )
    return lax.all_to_all(packed, "grp", split_axis=0, concat_axis=0, tiled=True)


def over_shards(moved, small, head_rows, shards, shard_at):
    summed = jnp.sum(moved.astype(FULL), axis=0).astype(HALF)
    rows = across([jnp.concatenate([summed, hi_lo(small)], axis=0)] * shards)
    head_part = sum(r[:head_rows].astype(FULL) for r in rows).astype(HALF)
    order = jnp.bitwise_xor(jnp.arange(shards, dtype=jnp.int32), shard_at)
    small = jnp.take(jnp.stack([from_hi_lo(r[summed.shape[0] :]) for r in rows]), order, axis=0)
    return head_part, [r[head_rows : summed.shape[0]] for r in rows], small


def assembled(scal, gathered, head_rows, shards, blocks, width):
    groups = len(gathered)
    total_blocks = shards * blocks
    spec_rows = 2 * blocks * width // groups
    small_at = head_rows + shards * spec_rows
    small_rows = (gathered[0].shape[0] - small_at) // 2

    def body(scal_ref, *refs):
        ins, (head_ref, spec_ref, bias_ref, gain_ref, embed_ref, out_ref) = refs[:groups], refs[groups:]
        small = None
        for k, ref in enumerate(ins):
            group = jnp.bitwise_xor(scal_ref[GROUP], k)
            at = pl.ds(pl.multiple_of(group * head_rows, head_rows), head_rows)
            head_ref[at, :] = ref[:head_rows].astype(FULL)
            start = group * spec_rows
            layer, b = start // (blocks * width), (start // width) % blocks
            rows = pl.ds(pl.multiple_of(start % width, spec_rows), spec_rows)
            for j in range(shards):
                values = ref[head_rows + j * spec_rows : head_rows + (j + 1) * spec_rows].astype(FULL)
                z = jnp.bitwise_xor(scal_ref[SHARD], j)
                spec_ref[layer, 0, z * blocks + b, rows] = values[:, :width]
                spec_ref[layer, 1, z * blocks + b, rows] = values[:, width:]
            part = ref[small_at : small_at + small_rows].astype(FULL) + ref[small_at + small_rows :].astype(FULL)
            small = part if small is None else small + part
        for z in range(shards):
            for layer in range(2):
                for b in range(blocks):
                    row = (z * 2 + layer) * blocks + b
                    for p in range(2):
                        bias_ref[layer, p, z * blocks + b : z * blocks + b + 1] = small[
                            row : row + 1, p * width : (p + 1) * width
                        ]
        row = shards * 2 * blocks
        quarter = gain_ref.shape[1] // (2 * width)
        for ref in (gain_ref, embed_ref):
            for i in range(quarter):
                ref[:, i * 2 * width : (i + 1) * 2 * width] = small[row + i : row + i + 1]
            row += quarter
        out_ref[...] = small[row : row + 1]

    out_shape = [
        jax.ShapeDtypeStruct((groups * head_rows, 2 * width), FULL),
        jax.ShapeDtypeStruct((2, 2, total_blocks, width, width), FULL),
        jax.ShapeDtypeStruct((2, 2, total_blocks, width), FULL),
        jax.ShapeDtypeStruct((1, groups * head_rows), FULL),
        jax.ShapeDtypeStruct((1, groups * head_rows), FULL),
        jax.ShapeDtypeStruct((1, 2 * width), FULL),
    ]
    return pl.pallas_call(
        body,
        grid_spec=pltpu.PrefetchScalarGridSpec(
            num_scalar_prefetch=1,
            grid=(1,),
            in_specs=[whole(gathered[0].shape)] * groups,
            out_specs=[whole(o.shape) for o in out_shape],
        ),
        out_shape=out_shape,
        compiler_params=params(),
        name="assembled",
    )(scal, *gathered)


def route_predictions(predicted, dest_group, group_at, groups, slot_count):
    own_dest = lax.dynamic_slice_in_dim(dest_group, group_at * slot_count, slot_count)
    matches = own_dest[None, :] == jnp.arange(groups, dtype=jnp.int32)[:, None]
    chosen = jnp.sum(jnp.where(matches, jnp.arange(slot_count, dtype=jnp.int32)[None, :], 0), axis=1)
    outgoing = jnp.take(predicted, chosen, axis=0)
    moved = lax.all_to_all(outgoing, "grp", split_axis=0, concat_axis=0, tiled=True)
    loaders = jnp.arange(groups, dtype=jnp.int32)
    holds = jnp.any(dest_group.reshape(groups, slot_count) == group_at, axis=1)
    rank = jnp.sum(jnp.where(holds[None, :] & (loaders[None, :] < loaders[:, None]), 1, 0), axis=1)
    slots = jnp.arange(slot_count, dtype=jnp.int32)
    sources = jnp.sum(jnp.where(holds[None, :] & (rank[None, :] == slots[:, None]), loaders[None, :], 0), axis=1)
    return jnp.take(moved, sources, axis=0)


def on_device(
    patches, targets, grid_side, dest_group, embed_w, embed_b, gain, spec_w, spec_b, head_w, head_b
):
    slot_count, row_count, cells, depth = patches.shape
    samples = dest_group.shape[0]
    groups = lax.axis_size("grp")
    shards = lax.axis_size("fft")
    group_at = lax.axis_index("grp").astype(jnp.int32)
    shard_at = lax.axis_index("fft").astype(jnp.int32)
    outs = targets.shape[-1]
    per_sample = row_count * cells
    count = slot_count // CHUNKS
    firsts = [c * count for c in range(CHUNKS)]
    assert slot_count == SLOTS

    sides = lax.dynamic_slice_in_dim(grid_side, group_at * slot_count, slot_count)
    level = jnp.where(sides == cells, 0, jnp.where(sides == cells // 2, 1, 2)).astype(jnp.int32)
    scal = jnp.concatenate([jnp.stack([shard_at, shard_at * row_count, group_at]), sides, level])
    table_values, factors = dft_tables(cells)
    table = jnp.asarray(table_values)
    flat_patches = patches.reshape(-1, depth)
    flat_targets = targets.reshape(-1, outs)
    gain_row, embed_b_row, head_b_row = gain[None], embed_b[None], head_b[None]

    embedded, normed, stats, turned_send, turned_keep, pieces = embed(
        scal, flat_patches, embed_w, embed_b_row, gain_row, firsts, count, per_sample, cells, shards, groups
    )
    moved = [across(p) for p in pieces]
    turned = [turned_keep, swap_bit(turned_send, 0, groups)]
    mixed, saved = [], []
    for first, values in zip(firsts, moved):
        out, rest = spectral_chunk(scal, table, factors, values, spec_w, spec_b, first)
        mixed.append(across(out))
        saved.append(rest)
    predicted, residual, updated, head_sums, gathered = [], [], [], [], []
    for first, mix in zip(firsts, mixed):
        pred, res, copies, up, sums = head_chunk(
            scal, embedded, normed, mix, flat_targets, head_w, head_b_row, first, samples, cells
        )
        predicted.append(pred)
        residual.append(res)
        updated.append(up)
        head_sums.append(sums[0])
        gathered.append(lax.all_to_all(copies, "fft", split_axis=0, concat_axis=0, tiled=True))
    head_grad, gathered[0] = lax.optimization_barrier((head_gradient(updated, residual), gathered[0]))
    spec_back, sums = [], None
    for first, res, rest in zip(firsts, gathered, saved):
        values, sums = spectral_back_chunk(
            scal, table, factors, res, head_w, spec_w, rest, first, sums, first == firsts[-1]
        )
        spec_back.append(across(values))
    spec_grad, spec_bias = sums
    width = spec_w.shape[-1]
    blocks = spec_w.shape[2] // shards
    head_rows = head_w.shape[0] // groups
    own_grads, other_grads, row_sums = [], [], []
    for first, res, back in zip(firsts, residual, spec_back):
        grad, row_sum = embedded_back_chunk(scal, embedded, stats, res, head_w, gain_row, back, first, cells)
        if first == firsts[0]:
            grad, head_grad, spec_grad = lax.optimization_barrier((grad, head_grad, spec_grad))
            weight_sums = sum_over_groups(head_grad, spec_grad, groups)
        own_grads.append(grad)
        other_grads.append(swap_bit(grad, 0, groups))
        row_sums.append(row_sum)
    grads = own_grads + other_grads
    sent = embed_grad_parts(scal, turned, grads, groups, 1)
    sent, kept_turned = lax.optimization_barrier((sent, turned))
    top_bit = groups.bit_length() - 2
    received = [swap_bit(sent[0], 1, groups), swap_bit(sent[1], top_bit, groups)]
    kept = embed_grad_parts(scal, kept_turned, grads, groups, 0)
    kept, weight_sums, predicted, row_sums = lax.optimization_barrier((kept, weight_sums, predicted, row_sums))
    ends = scatter_start(received, kept, groups)
    predictions = route_predictions(
        jnp.concatenate(predicted, axis=0), dest_group, group_at, groups, slot_count
    ).reshape(targets.shape)
    rows = sum(row_sums)
    vectors = jnp.concatenate([rows[0].reshape(-1, outs), rows[4].reshape(-1, outs), sum(head_sums)[None]], axis=0)
    own_rows, all_rows = spec_bias.shape[0], vectors.shape[0]
    small = jnp.concatenate([spec_bias, vectors, jnp.zeros((16 - own_rows - all_rows, outs), FULL)], axis=0)
    head_part, spec_parts, small = over_shards(weight_sums, small, head_rows, shards, shard_at)
    small = jnp.concatenate([small[:, :own_rows].reshape(-1, outs), jnp.sum(small[:, own_rows:], axis=0)], axis=0)
    small = jnp.concatenate([small, jnp.zeros((-small.shape[0] % 16, outs), FULL)], axis=0)
    outgoing = jnp.concatenate([head_part, *spec_parts, hi_lo(small)], axis=0)
    ends, outgoing = lax.optimization_barrier((ends, outgoing))
    gathered = from_all_groups(outgoing, groups)
    embed_grad = scatter_end(ends, shards, shard_at)
    head_grad, spec_w_grad, spec_b_grad, gain_grad, embed_bias_grad, head_bias_grad = assembled(
        scal, gathered, head_rows, shards, blocks, width
    )
    gain_grad, embed_bias_grad, head_bias_grad = gain_grad[0], embed_bias_grad[0], head_bias_grad[0]
    return (
        predictions,
        embed_grad,
        embed_bias_grad,
        gain_grad,
        spec_w_grad,
        spec_b_grad,
        head_grad,
        head_bias_grad,
    )


def solution(mesh):
    return jax.shard_map(
        on_device,
        mesh=mesh,
        in_specs=(
            P("grp", "fft", None, None),
            P("grp", "fft", None, None),
            P(),
            P(),
            P(),
            P(),
            P(),
            P(),
            P(),
            P(),
            P(),
        ),
        out_specs=(
            P("grp", "fft", None, None),
            P(("grp", "fft"), None),
            P(),
            P(),
            P(),
            P(),
            P(),
            P(),
        ),
        check_vma=False,
    )
```

```python
import jax
import jax.numpy as jnp
import ml_dtypes
import numpy as np
from jax import lax
from jax.experimental import pallas as pl
from jax.experimental.pallas import tpu as pltpu
from jax.sharding import PartitionSpec as P

EPSILON = 1e-05
SHRINK = 0.01
CHUNKS = 2
VMEM_BYTES = 24 * 1024 * 1024
SLOTS = 6
SHARD, FIRST_ROW, GROUP, SIDES = 0, 1, 2, 3
ROUTES = 3
HALF = jnp.bfloat16
FULL = jnp.float32


def dft_tables(cells):
    levels, factors = [], []
    for side, scale in ((cells, 1.1305), (cells // 2, 1.8633), (cells // 4, 1.0)):
        k = np.arange(cells)
        inside = (k < side).astype(np.float64)
        keep = inside[:, None] * inside[None, :]
        angle = 2.0 * np.pi * ((k[:, None] * k[None, :]) % side) / side
        one = np.exp(-1j * angle) * keep / np.sqrt(side)
        two = np.kron(one, one)
        table = np.concatenate([two.real, two.imag], axis=0)
        table[np.abs(table) < 1e-12] = 0.0
        rounded = (table * scale).astype(np.float32).astype(ml_dtypes.bfloat16)
        held = rounded.astype(np.float64)
        factors.append(float(np.sum(table * table) / np.sum(table * held)))
        levels.append(rounded)
    return np.stack(levels), factors


def dot(left, right):
    return jnp.dot(left, right, preferred_element_type=FULL)


def dot_tn(left, right):
    return lax.dot_general(left, right, (((0,), (0,)), ((), ())), preferred_element_type=FULL)


def dot_nt(left, right):
    return lax.dot_general(left, right, (((1,), (1,)), ((), ())), preferred_element_type=FULL)


def params(limit=VMEM_BYTES):
    return pltpu.CompilerParams(vmem_limit_bytes=limit)


def token_sides(scal_ref, first, count, per_sample, cells):
    token = lax.broadcasted_iota(jnp.int32, (count * per_sample, 1), 0)
    sample = token // per_sample
    side = jnp.zeros_like(token)
    for i in range(count):
        side = jnp.where(sample == i, scal_ref[SIDES + first + i], side)
    row = scal_ref[FIRST_ROW] + (token % per_sample) // cells
    col = token % cells
    valid = jnp.where((row < side) & (col < side), 1.0, 0.0).astype(FULL)
    return side, valid


def whole(shape):
    return pl.BlockSpec(tuple(shape), lambda i, s: (0,) * len(shape))


def part_of(scal_ref, k, size):
    at = jnp.bitwise_xor(scal_ref[SHARD], k)
    return pl.ds(pl.multiple_of(at * size, size), size)


def fill_lanes(scal_ref, refs, held):
    share = refs[0].shape[-1]
    for k, ref in enumerate(refs):
        held[:, part_of(scal_ref, k, share)] = ref[...].reshape(held.shape[0], share)


def fill_rows(scal_ref, refs, held):
    rows = refs[0].shape[1]
    for k, ref in enumerate(refs):
        held[:, part_of(scal_ref, k, rows), :] = ref[...]


def split_lanes(scal_ref, held, refs):
    share = refs[0].shape[-1]
    for k, ref in enumerate(refs):
        ref[...] = held[:, part_of(scal_ref, k, share)].reshape(ref.shape)


def split_rows(scal_ref, held, refs):
    rows = refs[0].shape[1]
    for k, ref in enumerate(refs):
        ref[...] = held[:, part_of(scal_ref, k, rows), :]


def embed(scal, patches, embed_w, embed_b, gain, firsts, count, per_sample, cells, shards, groups):
    rows, depth = patches.shape
    block = depth // groups
    width = embed_w.shape[1]
    share = width // shards
    chunk_rows = count * per_sample
    chunks = len(firsts)
    steps = 4
    tile = depth // steps

    def body(scal_ref, x_ref, w_ref, b_ref, gain_ref, emb_ref, norm_ref, stat_ref, *refs):
        (send_ref, keep_ref), outs, acc = refs[:2], refs[2:-1], refs[-1]
        step = pl.program_id(0)
        turned = x_ref[...].T
        for i in range(tile // block):
            values = turned[i * block : (i + 1) * block]
            away = (scal_ref[GROUP] + i) % 2

            @pl.when(away == 1)
            def _(i=i, values=values):
                send_ref[i // 2] = values

            @pl.when(away == 0)
            def _(i=i, values=values):
                keep_ref[i // 2] = values

        part = dot(x_ref[...], w_ref[...])

        @pl.when(step == 0)
        def _():
            acc[...] = part

        @pl.when(step > 0)
        def _():
            acc[...] += part

        @pl.when(step == steps - 1)
        def _():
            for c, first in enumerate(firsts):
                at = slice(c * chunk_rows, (c + 1) * chunk_rows)
                _, valid = token_sides(scal_ref, first, count, per_sample, cells)
                embedded = ((acc[at] + b_ref[...]) * valid).astype(HALF)
                emb_ref[at] = embedded
                values = embedded.astype(FULL)
                mean = jnp.mean(values, axis=-1, keepdims=True)
                centered = values - mean
                inv_std = lax.rsqrt(jnp.mean(centered * centered, axis=-1, keepdims=True) + EPSILON)
                norm_ref[at] = (centered * inv_std * gain_ref[...]).astype(HALF)
                stat_ref[at, :128] = jnp.broadcast_to(mean, (chunk_rows, 128))
                stat_ref[at, 128:] = jnp.broadcast_to(inv_std, (chunk_rows, 128))
                for k in range(shards):
                    piece = norm_ref[at, part_of(scal_ref, k, share)]
                    outs[c * shards + k][...] = piece.reshape(count, per_sample, share)

    piece = (count, per_sample, share)
    turned_spec = pl.BlockSpec((tile // (2 * block), block, rows), lambda k, s: (k, 0, 0))
    turned_shape = jax.ShapeDtypeStruct((groups // 2, block, rows), HALF)
    emb, normed, stats, send, keep, *pieces = pl.pallas_call(
        body,
        grid_spec=pltpu.PrefetchScalarGridSpec(
            num_scalar_prefetch=1,
            grid=(steps,),
            in_specs=[
                pl.BlockSpec((rows, tile), lambda k, s: (0, k)),
                pl.BlockSpec((tile, width), lambda k, s: (k, 0)),
                whole((1, width)),
                whole((1, width)),
            ],
            out_specs=[whole((rows, width)), whole((rows, width)), whole((rows, 256)), turned_spec, turned_spec]
            + [whole(piece)] * (shards * chunks),
            scratch_shapes=[pltpu.VMEM((rows, width), FULL)],
        ),
        out_shape=[
            jax.ShapeDtypeStruct((rows, width), HALF),
            jax.ShapeDtypeStruct((rows, width), HALF),
            jax.ShapeDtypeStruct((rows, 256), FULL),
            turned_shape,
            turned_shape,
        ]
        + [jax.ShapeDtypeStruct(piece, HALF)] * (shards * chunks),
        compiler_params=params(60 * 1024 * 1024),
        cost_estimate=pl.CostEstimate(
            flops=2 * rows * depth * width, bytes_accessed=2 * depth * (rows + width), transcendentals=0
        ),
        name="embed",
    )(scal, patches, embed_w, embed_b, gain)
    return emb, normed, stats, send, keep, [pieces[c * shards : (c + 1) * shards] for c in range(chunks)]


def to_blocks(values, blocks, width):
    half = values.shape[0] // 2
    return [
        jnp.concatenate(
            [values[:half, b * width : (b + 1) * width], values[half:, b * width : (b + 1) * width]], axis=1
        )
        for b in range(blocks)
    ]


def from_blocks(parts, width):
    real = jnp.concatenate([p[:, :width] for p in parts], axis=1)
    imag = jnp.concatenate([p[:, width:] for p in parts], axis=1)
    return real, imag


def table_factor(level, factors):
    return jnp.where(level == 0, factors[0], jnp.where(level == 1, factors[1], factors[2])).astype(FULL)


def table_back(table_ref, level, tops, rests, factor):
    size = table_ref.shape[2]
    total = None
    for at, (top, rest) in enumerate(zip(tops, rests)):
        table = table_ref[level, at * size : (at + 1) * size]
        part = dot(table, top) + dot(table, rest)
        total = part if total is None else total + part
    return total * factor


def two_terms(values):
    top = values.astype(HALF)
    return top, (values - top.astype(FULL)).astype(HALF)


def complex_weights(w_ref, held, blocks, width):
    for layer in range(2):
        for b in range(blocks):
            real, imag = w_ref[layer, 0, b], w_ref[layer, 1, b]
            held[layer, b, :width, :width] = real
            held[layer, b, :width, width:] = imag
            held[layer, b, width:, :width] = -imag
            held[layer, b, width:, width:] = real


def spectral_chunk(scal, table, factors, pieces, spec_w, spec_b, first):
    shards = len(pieces)
    count, per_sample, share = pieces[0].shape
    size = shards * per_sample
    width = spec_w.shape[-1]
    blocks = share // width
    wide = 2 * width

    def body(scal_ref, t_ref, w_ref, b_ref, *refs):
        ins, outs = refs[:shards], refs[shards : 2 * shards]
        spec_ref, hid_ref, fil_ref, weights, held = refs[2 * shards :]

        def bias(layer, b):
            row = pl.ds(scal_ref[SHARD] * blocks + b, 1)
            return jnp.concatenate([b_ref[layer, 0, row], b_ref[layer, 1, row]], axis=1)

        complex_weights(w_ref, weights, blocks, width)
        fill_rows(scal_ref, ins, held)
        levels = [scal_ref[SIDES + SLOTS + first + i] for i in range(count)]
        for i, level in enumerate(levels):
            spectrum = (dot(t_ref[level], held[i]) * table_factor(level, factors)).astype(HALF)
            for b, entry in enumerate(to_blocks(spectrum, blocks, width)):
                spec_ref[b, i * size : (i + 1) * size] = entry
        kept = []
        for b in range(blocks):
            pre_one = dot(spec_ref[b], weights[0, b]) + bias(0, b)
            hidden = jnp.maximum(pre_one, 0.0).astype(HALF)
            hid_ref[b] = hidden
            pre_two = dot(hidden, weights[1, b]) + bias(1, b)
            filtered = jnp.where(
                pre_two > SHRINK, pre_two - SHRINK, jnp.where(pre_two < -SHRINK, pre_two + SHRINK, 0.0)
            )
            top, rest = two_terms(filtered)
            fil_ref[b] = top
            kept.append((top, rest))
        for i, level in enumerate(levels):
            at = slice(i * size, (i + 1) * size)
            tops = from_blocks([top[at] for top, _ in kept], width)
            rests = from_blocks([rest[at] for _, rest in kept], width)
            held[i] = table_back(t_ref, level, tops, rests, table_factor(level, factors)).astype(HALF)
        split_rows(scal_ref, held, outs)

    saved = (blocks, count * size, wide)
    outs = pl.pallas_call(
        body,
        grid_spec=pltpu.PrefetchScalarGridSpec(
            num_scalar_prefetch=1,
            grid=(1,),
            in_specs=[
                whole(table.shape),
                pl.BlockSpec((2, 2, blocks, width, width), lambda i, s: (0, 0, s[SHARD], 0, 0)),
                whole(spec_b.shape),
            ]
            + [whole(pieces[0].shape)] * shards,
            out_specs=[whole(pieces[0].shape)] * shards + [whole(saved)] * 3,
            scratch_shapes=[pltpu.VMEM((2, blocks, wide, wide), HALF), pltpu.VMEM((count, size, share), HALF)],
        ),
        out_shape=[jax.ShapeDtypeStruct(pieces[0].shape, HALF)] * shards + [jax.ShapeDtypeStruct(saved, HALF)] * 3,
        compiler_params=params(),
        cost_estimate=pl.CostEstimate(
            flops=count * size * share * size * 14, bytes_accessed=count * size * share * 16, transcendentals=0
        ),
        name="spectral",
    )(scal, table, spec_w, spec_b, *pieces)
    return outs[:shards], outs[shards:]


def head_chunk(scal, embedded, normed, mixed, targets, head_w, head_b, first, samples, cells):
    shards = len(mixed)
    count, per_sample, share = mixed[0].shape
    rows = count * per_sample
    width, outs = head_w.shape
    at = first // count
    scale_root = float(np.sqrt(np.float32(samples)))

    def body(scal_ref, emb_ref, norm_ref, tgt_ref, w_ref, b_ref, *refs):
        mix_refs, (pred_ref, res_ref, up_ref, bias_ref, held) = refs[:shards], refs[shards:]
        fill_lanes(scal_ref, mix_refs, held)
        side, valid = token_sides(scal_ref, first, count, per_sample, cells)
        updated = (emb_ref[...].astype(FULL) + norm_ref[...].astype(FULL) + held[...].astype(FULL)).astype(HALF)
        output = (dot(updated, w_ref[...]) + b_ref[...]) * valid
        pred_ref[...] = output.astype(HALF).reshape(pred_ref.shape)
        scale = 2.0 / (side.astype(FULL) * scale_root)
        residual = (scale * valid * (output - tgt_ref[...].astype(FULL))).astype(HALF)
        res_ref[...] = residual.reshape(res_ref.shape)
        up_ref[...] = updated
        total = jnp.sum(residual.astype(FULL), axis=0, keepdims=True)
        bias_ref[...] = jnp.broadcast_to(total, bias_ref.shape)

    token_shape = (count, per_sample, outs)
    return pl.pallas_call(
        body,
        grid_spec=pltpu.PrefetchScalarGridSpec(
            num_scalar_prefetch=1,
            grid=(1,),
            in_specs=[
                pl.BlockSpec((rows, width), lambda i, s: (at, 0)),
                pl.BlockSpec((rows, width), lambda i, s: (at, 0)),
                pl.BlockSpec((rows, outs), lambda i, s: (at, 0)),
                whole((width, outs)),
                whole((1, outs)),
            ]
            + [whole(mixed[0].shape)] * shards,
            out_specs=[whole(token_shape), whole(token_shape), whole((rows, width)), whole((8, outs))],
            scratch_shapes=[pltpu.VMEM((rows, width), HALF)],
        ),
        out_shape=[
            jax.ShapeDtypeStruct(token_shape, HALF),
            jax.ShapeDtypeStruct(token_shape, HALF),
            jax.ShapeDtypeStruct((rows, width), HALF),
            jax.ShapeDtypeStruct((8, outs), FULL),
        ],
        compiler_params=params(),
        cost_estimate=pl.CostEstimate(
            flops=2 * rows * width * outs, bytes_accessed=rows * width * 4 + width * outs * 6, transcendentals=0
        ),
        name="head",
    )(scal, embedded, normed, targets, head_w, head_b, *mixed)


def head_gradient(updated, residual):
    width = updated[0].shape[1]
    outs = residual[0].shape[-1]
    count = len(updated)

    def body(*refs):
        total = None
        for up_ref, res_ref in zip(refs[:count], refs[count : 2 * count]):
            part = dot_tn(up_ref[...], res_ref[...].reshape(up_ref.shape[0], outs))
            total = part if total is None else total + part
        refs[-1][...] = total.astype(HALF)

    return pl.pallas_call(
        body,
        out_shape=jax.ShapeDtypeStruct((width, outs), HALF),
        compiler_params=params(),
        cost_estimate=pl.CostEstimate(
            flops=2 * count * updated[0].size * outs, bytes_accessed=2 * count * updated[0].size, transcendentals=0
        ),
        name="head_gradient",
    )(*updated, *residual)


def spectral_back_chunk(scal, table, factors, residual, head_w, spec_w, saved, first, before, last):
    shards = len(residual)
    count, per_sample, outs = residual[0].shape
    size = shards * per_sample
    width = spec_w.shape[-1]
    wide = 2 * width
    share = head_w.shape[0] // shards
    blocks = share // width
    raw_shape = (2, blocks, wide, wide)
    bias_shape = (2 * blocks, wide)
    has_before = before is not None

    def body(scal_ref, t_ref, h_ref, w_ref, spec_ref, hid_ref, fil_ref, *refs):
        ins, refs = refs[:shards], refs[shards:]
        if has_before:
            (old_ref, old_bias_ref), refs = refs[:2], refs[2:]
        pieces, (grad_ref, bias_ref, weights, held, gathered) = refs[:shards], refs[shards:]

        def weight_sums(layer, b, inputs, grads):
            raw = dot_tn(inputs, grads)
            sums = jnp.sum(grads.astype(FULL), axis=0, keepdims=True)
            at = layer * blocks + b
            if has_before:
                raw = raw + old_ref[layer, b]
                sums = sums + old_bias_ref[at : at + 1]
            bias_ref[at : at + 1] = sums
            if not last:
                grad_ref[layer, b] = raw
                return
            real = raw[:width, :width] + raw[width:, width:]
            imag = raw[:width, width:] - raw[width:, :width]
            grad_ref[at * width : (at + 1) * width] = jnp.concatenate([real, imag], axis=1).astype(HALF)

        complex_weights(w_ref, weights, blocks, width)
        fill_rows(scal_ref, ins, gathered)
        levels = [scal_ref[SIDES + SLOTS + first + i] for i in range(count)]
        updated_grad = dot_nt(gathered[...].reshape(count * size, outs), h_ref[...]).astype(HALF)
        entries = []
        for i, level in enumerate(levels):
            filtered_grad = dot(t_ref[level], updated_grad[i * size : (i + 1) * size]) * table_factor(level, factors)
            entries.append(to_blocks(filtered_grad, blocks, width))
        kept = []
        for b in range(blocks):
            entry = jnp.concatenate([e[b] for e in entries], axis=0)
            two_grad = jnp.where(fil_ref[b].astype(FULL) != 0.0, entry, 0.0).astype(HALF)
            hidden = hid_ref[b]
            hidden_grad = dot_nt(two_grad, weights[1, b])
            one_grad = jnp.where(hidden.astype(FULL) > 0.0, hidden_grad, 0.0).astype(HALF)
            kept.append(two_terms(dot_nt(one_grad, weights[0, b])))
            weight_sums(1, b, hidden, two_grad)
            weight_sums(0, b, spec_ref[b], one_grad)
        for i, level in enumerate(levels):
            at = slice(i * size, (i + 1) * size)
            tops = from_blocks([top[at] for top, _ in kept], width)
            rests = from_blocks([rest[at] for _, rest in kept], width)
            held[i] = table_back(t_ref, level, tops, rests, table_factor(level, factors)).astype(HALF)
        split_rows(scal_ref, held, pieces)

    piece = (count, per_sample, share)
    if last:
        grad_out = jax.ShapeDtypeStruct((2 * blocks * width, wide), HALF)
    else:
        grad_out = jax.ShapeDtypeStruct(raw_shape, FULL)
    result = pl.pallas_call(
        body,
        grid_spec=pltpu.PrefetchScalarGridSpec(
            num_scalar_prefetch=1,
            grid=(1,),
            in_specs=[
                whole(table.shape),
                pl.BlockSpec((share, outs), lambda i, s: (s[SHARD], 0)),
                pl.BlockSpec((2, 2, blocks, width, width), lambda i, s: (0, 0, s[SHARD], 0, 0)),
            ]
            + [whole(saved[0].shape)] * 3
            + [whole(residual[0].shape)] * shards
            + ([whole(raw_shape), whole(bias_shape)] if has_before else []),
            out_specs=[whole(piece)] * shards + [whole(grad_out.shape), whole(bias_shape)],
            scratch_shapes=[
                pltpu.VMEM((2, blocks, wide, wide), HALF),
                pltpu.VMEM((count, size, share), HALF),
                pltpu.VMEM((count, size, outs), HALF),
            ],
        ),
        out_shape=[jax.ShapeDtypeStruct(piece, HALF)] * shards
        + [grad_out, jax.ShapeDtypeStruct(bias_shape, FULL)],
        compiler_params=params(),
        cost_estimate=pl.CostEstimate(
            flops=count * size * share * size * 20, bytes_accessed=count * size * share * 16, transcendentals=0
        ),
        name="spectral_back",
    )(scal, table, head_w, spec_w, *saved, *residual, *(before or ()))
    return result[:shards], result[shards:]


def embedded_back_chunk(scal, embedded, stats, residual, head_w, gain, spec_grad, first, cells):
    shards = len(spec_grad)
    count, per_sample, share = spec_grad[0].shape
    rows = count * per_sample
    width, outs = head_w.shape
    at = first // count

    def body(scal_ref, emb_ref, stat_ref, res_ref, w_ref, gain_ref, *refs):
        grad_refs, (out_ref, sums_ref, held) = refs[:shards], refs[shards:]
        fill_lanes(scal_ref, grad_refs, held)
        _, valid = token_sides(scal_ref, first, count, per_sample, cells)
        inv_std = stat_ref[:, 128:129]
        unit = (emb_ref[...].astype(FULL) - stat_ref[:, 0:1]) * inv_std
        direct = dot_nt(res_ref[...].reshape(rows, outs), w_ref[...]).astype(HALF).astype(FULL)
        normed_grad = held[...].astype(FULL) + direct
        gain_grad = jnp.sum(normed_grad * unit, axis=0, keepdims=True)
        unit_grad = normed_grad * gain_ref[...]
        mean_grad = jnp.mean(unit_grad, axis=-1, keepdims=True)
        mean_cross = jnp.mean(unit_grad * unit, axis=-1, keepdims=True)
        input_grad = inv_std * (unit_grad - mean_grad - unit * mean_cross)
        result = ((input_grad + direct) * valid).astype(HALF)
        out_ref[...] = result
        bias_grad = jnp.sum(result.astype(FULL), axis=0, keepdims=True)
        sums_ref[0:4] = jnp.broadcast_to(gain_grad, (4, width))
        sums_ref[4:8] = jnp.broadcast_to(bias_grad, (4, width))

    return pl.pallas_call(
        body,
        grid_spec=pltpu.PrefetchScalarGridSpec(
            num_scalar_prefetch=1,
            grid=(1,),
            in_specs=[
                pl.BlockSpec((rows, width), lambda i, s: (at, 0)),
                pl.BlockSpec((rows, 256), lambda i, s: (at, 0)),
                whole((count, per_sample, outs)),
                whole((width, outs)),
                whole((1, width)),
            ]
            + [whole(spec_grad[0].shape)] * shards,
            out_specs=[whole((rows, width)), whole((8, width))],
            scratch_shapes=[pltpu.VMEM((rows, width), HALF)],
        ),
        out_shape=[jax.ShapeDtypeStruct((rows, width), HALF), jax.ShapeDtypeStruct((8, width), FULL)],
        compiler_params=params(),
        cost_estimate=pl.CostEstimate(
            flops=2 * rows * width * outs, bytes_accessed=rows * width * 6, transcendentals=0
        ),
        name="embedded_back",
    )(scal, embedded, stats, residual, head_w, gain, *spec_grad)


def embed_grad_parts(scal, turned, grads, groups, away):
    pairs, block, tokens = turned[0].shape
    chunk_rows, width = grads[0].shape
    half = width // 2
    top = pairs // 2
    count = len(turned)
    depth = tokens * count

    def relative(unit):
        return jnp.where(unit < top, 2 * unit + away, unit - top + away * top)

    def body(scal_ref, *refs):
        turned_refs, grad_refs = refs[:count], refs[count : count + len(grads)]
        left_ref, right_ref, held = refs[count + len(grads) :]
        unit = pl.program_id(0)

        @pl.when(unit % top == 0)
        def _():
            for i, ref in enumerate(grad_refs):
                held[i * chunk_rows : (i + 1) * chunk_rows] = ref[...]

        rows = jnp.concatenate([ref[0] for ref in turned_refs], axis=1)
        total = dot(rows, held[...]).astype(HALF)

        @pl.when(unit < top)
        def _():
            left_ref[0] = total

        @pl.when(unit >= top)
        def _():
            right_ref[0] = total

    shape = (top, block, half)
    return pl.pallas_call(
        body,
        grid_spec=pltpu.PrefetchScalarGridSpec(
            num_scalar_prefetch=1,
            grid=(pairs,),
            in_specs=[
                pl.BlockSpec((1, block, tokens), lambda i, s: (jnp.bitwise_xor(s[GROUP] // 2, relative(i)), 0, 0))
                for _ in turned
            ]
            + [pl.BlockSpec((chunk_rows, half), lambda i, s: (0, i // top)) for _ in grads],
            out_specs=[
                pl.BlockSpec((1, block, half), lambda i, s: (jnp.minimum(i, top - 1), 0, 0)),
                pl.BlockSpec((1, block, half), lambda i, s: (jnp.maximum(i - top, 0), 0, 0)),
            ],
            scratch_shapes=[pltpu.VMEM((depth, half), HALF)],
        ),
        out_shape=[jax.ShapeDtypeStruct(shape, HALF)] * 2,
        compiler_params=params(),
        cost_estimate=pl.CostEstimate(
            flops=depth * pairs * block * width,
            bytes_accessed=pairs * block * (2 * depth + width) + depth * width,
            transcendentals=0,
        ),
        name="embed_grad",
    )(scal, *turned, *grads)


def swap_bit(values, bit, groups):
    return lax.ppermute(values, "grp", [(g, g ^ (1 << bit)) for g in range(groups)])


def across(pieces):
    shards = len(pieces)
    return [pieces[0]] + [
        lax.ppermute(pieces[k], "fft", [(z, z ^ k) for z in range(shards)]) for k in range(1, shards)
    ]


def add_half(left, right):
    return (left.astype(FULL) + right.astype(FULL)).astype(HALF)


def scatter_start(received, kept, groups):
    bits = groups.bit_length() - 1
    ends = []
    for first, keep, order, low in (
        (received[0], kept[0], list(range(2, bits)), True),
        (received[1], kept[1], list(range(bits - 2, 0, -1)), False),
    ):
        total = add_half(keep, first)
        for bit in order:
            count, block, width = total.shape
            if low:
                split = total.reshape(count // 2, 2, block, width)
                keep, send = split[:, 0], split[:, 1]
            else:
                split = total.reshape(2, count // 2, block, width)
                keep, send = split[0], split[1]
            total = add_half(keep, swap_bit(send, bit, groups))
        ends.append(total[0])
    return ends


def scatter_end(ends, shards, shard_at):
    part = jnp.concatenate(ends, axis=-1)
    part = part.reshape(shards, part.shape[0] // shards, -1)
    bit = 1
    while bit < shards:
        split = part.reshape(part.shape[0] // 2, 2, *part.shape[1:])
        mine = (shard_at // bit) % 2
        keep = lax.dynamic_index_in_dim(split, mine, 1, keepdims=False)
        send = lax.dynamic_index_in_dim(split, 1 - mine, 1, keepdims=False)
        received = lax.ppermute(send, "fft", [(z, z ^ bit) for z in range(shards)])
        part = keep.astype(FULL) + received.astype(FULL)
        bit *= 2
        if bit < shards:
            part = part.astype(HALF)
    return part[0]


def from_all_groups(values, groups):
    even = [values] + [
        lax.ppermute(values, "grp", [(g, g ^ k) for g in range(groups)]) for k in range(2, groups, 2)
    ]
    odd = [swap_bit(v, 0, groups) for v in even]
    return [v for pair in zip(even, odd) for v in pair]


def hi_lo(values):
    high = values.astype(HALF)
    return jnp.concatenate([high, (values - high.astype(FULL)).astype(HALF)], axis=0)


def from_hi_lo(values):
    half = values.shape[0] // 2
    values = values.astype(FULL)
    return values[:half] + values[half:]


def one_step(body, name, operands, out_shape):
    return pl.pallas_call(
        body,
        grid_spec=pltpu.PrefetchScalarGridSpec(
            num_scalar_prefetch=1,
            grid=(1,),
            in_specs=[whole(o.shape) for o in operands[1:]],
            out_specs=[whole(o.shape) for o in out_shape],
        ),
        out_shape=out_shape,
        compiler_params=params(),
        name=name,
    )(*operands)


def packed(routes, head_grad, spec_grad, predicted, groups):
    outs = head_grad.shape[1]
    head_rows, spec_rows = head_grad.shape[0] // groups, spec_grad.shape[0] // groups
    count, per_sample, _ = predicted[0].shape

    def body(routes_ref, head_ref, spec_ref, *refs):
        pred_refs, out_ref = refs[:-1], refs[-1]
        for g in range(groups):
            out_ref[g, :head_rows] = head_ref[g * head_rows : (g + 1) * head_rows]
            out_ref[g, head_rows : head_rows + spec_rows] = spec_ref[g * spec_rows : (g + 1) * spec_rows]
            chosen = routes_ref[ROUTES + g]
            for c, ref in enumerate(pred_refs):

                @pl.when(chosen // count == c)
                def _(g=g, c=c, ref=ref, chosen=chosen):
                    out_ref[g, head_rows + spec_rows :] = ref[chosen - c * count]

    shape = (groups, head_rows + spec_rows + per_sample, outs)
    return one_step(
        body, "packed", (routes, head_grad, spec_grad, *predicted), [jax.ShapeDtypeStruct(shape, HALF)]
    )[0]


def group_sums(routes, moved, spec_bias, head_sums, row_sums, slot_count, per_sample):
    groups, rows, outs = moved.shape
    weight_rows = rows - per_sample
    own_rows = spec_bias.shape[0]
    chunks = len(head_sums)
    parts = row_sums[0].shape[1] // outs
    spare = 16 - own_rows - 2 * parts - 1

    def body(routes_ref, moved_ref, bias_ref, *refs):
        head_refs, row_refs, (out_ref, pred_ref) = refs[:chunks], refs[chunks : 2 * chunks], refs[2 * chunks :]
        total = moved_ref[0, :weight_rows].astype(FULL)
        for g in range(1, groups):
            total = total + moved_ref[g, :weight_rows].astype(FULL)
        out_ref[:weight_rows] = total.astype(HALF)
        lines = [bias_ref[...]]
        for row in (0, 4):
            line = sum(ref[row : row + 1] for ref in row_refs)
            lines += [line[:, i * outs : (i + 1) * outs] for i in range(parts)]
        lines += [sum(ref[0:1] for ref in head_refs), jnp.zeros((spare, outs), FULL)]
        out_ref[weight_rows:] = hi_lo(jnp.concatenate(lines, axis=0))
        for i in range(slot_count):
            pred_ref[i] = moved_ref[routes_ref[ROUTES + groups + i], weight_rows:]

    return one_step(
        body,
        "group_sums",
        (routes, moved, spec_bias, *head_sums, *row_sums),
        [
            jax.ShapeDtypeStruct((weight_rows + 32, outs), HALF),
            jax.ShapeDtypeStruct((slot_count, per_sample, outs), HALF),
        ],
    )


def shard_sums(routes, rows, head_rows, spec_rows, own_rows):
    shards = len(rows)
    outs = rows[0].shape[1]
    small_rows = 32

    def body(routes_ref, *refs):
        ins, out_ref = refs[:-1], refs[-1]
        total = sum(ref[:head_rows].astype(FULL) for ref in ins)
        out_ref[:head_rows] = total.astype(HALF)
        for k, ref in enumerate(ins):
            at = head_rows + k * spec_rows
            out_ref[at : at + spec_rows] = ref[head_rows : head_rows + spec_rows]
        smalls = [from_hi_lo(ref[head_rows + spec_rows :]) for ref in ins]
        lines = []
        for z in range(shards):
            here = [jnp.bitwise_xor(routes_ref[SHARD], k) == z for k in range(shards)]
            lines.append(sum(jnp.where(h, v[:own_rows], 0.0) for h, v in zip(here, smalls)))
        lines.append(sum(v[own_rows:] for v in smalls))
        have = shards * own_rows + 16 - own_rows
        lines.append(jnp.zeros((small_rows - have, outs), FULL))
        out_ref[head_rows + shards * spec_rows :] = hi_lo(jnp.concatenate(lines, axis=0))

    shape = (head_rows + shards * spec_rows + 2 * small_rows, outs)
    return one_step(body, "shard_sums", (routes, *rows), [jax.ShapeDtypeStruct(shape, HALF)])[0]


def assembled(scal, gathered, head_rows, shards, blocks, width):
    groups = len(gathered)
    total_blocks = shards * blocks
    spec_rows = 2 * blocks * width // groups
    small_at = head_rows + shards * spec_rows
    small_rows = (gathered[0].shape[0] - small_at) // 2

    def body(scal_ref, *refs):
        ins, (head_ref, spec_ref, bias_ref, gain_ref, embed_ref, out_ref) = refs[:groups], refs[groups:]
        small = None
        for k, ref in enumerate(ins):
            group = jnp.bitwise_xor(scal_ref[GROUP], k)
            at = pl.ds(pl.multiple_of(group * head_rows, head_rows), head_rows)
            head_ref[at, :] = ref[:head_rows].astype(FULL)
            start = group * spec_rows
            layer, b = start // (blocks * width), (start // width) % blocks
            rows = pl.ds(pl.multiple_of(start % width, spec_rows), spec_rows)
            for j in range(shards):
                values = ref[head_rows + j * spec_rows : head_rows + (j + 1) * spec_rows].astype(FULL)
                z = jnp.bitwise_xor(scal_ref[SHARD], j)
                spec_ref[layer, 0, z * blocks + b, rows] = values[:, :width]
                spec_ref[layer, 1, z * blocks + b, rows] = values[:, width:]
            part = ref[small_at : small_at + small_rows].astype(FULL) + ref[small_at + small_rows :].astype(FULL)
            small = part if small is None else small + part
        for z in range(shards):
            for layer in range(2):
                for b in range(blocks):
                    row = (z * 2 + layer) * blocks + b
                    for p in range(2):
                        bias_ref[layer, p, z * blocks + b : z * blocks + b + 1] = small[
                            row : row + 1, p * width : (p + 1) * width
                        ]
        row = shards * 2 * blocks
        quarter = gain_ref.shape[1] // (2 * width)
        for ref in (gain_ref, embed_ref):
            for i in range(quarter):
                ref[:, i * 2 * width : (i + 1) * 2 * width] = small[row + i : row + i + 1]
            row += quarter
        out_ref[...] = small[row : row + 1]

    out_shape = [
        jax.ShapeDtypeStruct((groups * head_rows, 2 * width), FULL),
        jax.ShapeDtypeStruct((2, 2, total_blocks, width, width), FULL),
        jax.ShapeDtypeStruct((2, 2, total_blocks, width), FULL),
        jax.ShapeDtypeStruct((1, groups * head_rows), FULL),
        jax.ShapeDtypeStruct((1, groups * head_rows), FULL),
        jax.ShapeDtypeStruct((1, 2 * width), FULL),
    ]
    return pl.pallas_call(
        body,
        grid_spec=pltpu.PrefetchScalarGridSpec(
            num_scalar_prefetch=1,
            grid=(1,),
            in_specs=[whole(gathered[0].shape)] * groups,
            out_specs=[whole(o.shape) for o in out_shape],
        ),
        out_shape=out_shape,
        compiler_params=params(),
        name="assembled",
    )(scal, *gathered)


def prediction_routes(dest_group, group_at, groups, slot_count):
    own_dest = lax.dynamic_slice_in_dim(dest_group, group_at * slot_count, slot_count)
    loaders = jnp.arange(groups, dtype=jnp.int32)
    slots = jnp.arange(slot_count, dtype=jnp.int32)
    chosen = jnp.sum(jnp.where(own_dest[None, :] == loaders[:, None], slots[None, :], 0), axis=1)
    holds = jnp.any(dest_group.reshape(groups, slot_count) == group_at, axis=1)
    rank = jnp.sum(jnp.where(holds[None, :] & (loaders[None, :] < loaders[:, None]), 1, 0), axis=1)
    sources = jnp.sum(jnp.where(holds[None, :] & (rank[None, :] == slots[:, None]), loaders[None, :], 0), axis=1)
    return jnp.concatenate([chosen, sources]).astype(jnp.int32)


def on_device(
    patches, targets, grid_side, dest_group, embed_w, embed_b, gain, spec_w, spec_b, head_w, head_b
):
    slot_count, row_count, cells, depth = patches.shape
    samples = dest_group.shape[0]
    groups = lax.axis_size("grp")
    shards = lax.axis_size("fft")
    group_at = lax.axis_index("grp").astype(jnp.int32)
    shard_at = lax.axis_index("fft").astype(jnp.int32)
    outs = targets.shape[-1]
    per_sample = row_count * cells
    count = slot_count // CHUNKS
    firsts = [c * count for c in range(CHUNKS)]
    assert slot_count == SLOTS

    sides = lax.dynamic_slice_in_dim(grid_side, group_at * slot_count, slot_count)
    level = jnp.where(sides == cells, 0, jnp.where(sides == cells // 2, 1, 2)).astype(jnp.int32)
    place = jnp.stack([shard_at, shard_at * row_count, group_at])
    scal = jnp.concatenate([place, sides, level])
    routes = jnp.concatenate([place, prediction_routes(dest_group, group_at, groups, slot_count)])
    table_values, factors = dft_tables(cells)
    table = jnp.asarray(table_values)
    flat_patches = patches.reshape(-1, depth)
    flat_targets = targets.reshape(-1, outs)
    gain_row, embed_b_row, head_b_row = gain[None], embed_b[None], head_b[None]

    embedded, normed, stats, turned_send, turned_keep, pieces = embed(
        scal, flat_patches, embed_w, embed_b_row, gain_row, firsts, count, per_sample, cells, shards, groups
    )
    moved = [across(p) for p in pieces]
    mixed, saved = [], []
    for first, values in zip(firsts, moved):
        out, rest = spectral_chunk(scal, table, factors, values, spec_w, spec_b, first)
        mixed.append(across(out))
        saved.append(rest)
    predicted, residual, updated, head_sums, gathered = [], [], [], [], []
    for first, mix in zip(firsts, mixed):
        pred, res, up, sums = head_chunk(
            scal, embedded, normed, mix, flat_targets, head_w, head_b_row, first, samples, cells
        )
        predicted.append(pred)
        residual.append(res)
        updated.append(up)
        head_sums.append(sums)
        gathered.append(across([res] * shards))
    head_grad, gathered[0] = lax.optimization_barrier((head_gradient(updated, residual), gathered[0]))
    spec_back, sums = [], None
    for first, res, rest in zip(firsts, gathered, saved):
        values, sums = spectral_back_chunk(
            scal, table, factors, res, head_w, spec_w, rest, first, sums, first == firsts[-1]
        )
        if first == firsts[-1]:
            values, turned_send = lax.optimization_barrier((values, turned_send))
        spec_back.append(across(values))
    turned = [turned_keep, swap_bit(turned_send, 0, groups)]
    spec_grad, spec_bias = sums
    width = spec_w.shape[-1]
    blocks = spec_w.shape[2] // shards
    head_rows = head_w.shape[0] // groups
    own_grads, other_grads, row_sums = [], [], []
    for first, res, back in zip(firsts, residual, spec_back):
        grad, row_sum = embedded_back_chunk(scal, embedded, stats, res, head_w, gain_row, back, first, cells)
        if first == firsts[0]:
            grad, head_grad, spec_grad = lax.optimization_barrier((grad, head_grad, spec_grad))
            weight_sums = lax.all_to_all(
                packed(routes, head_grad, spec_grad, predicted, groups), "grp", split_axis=0, concat_axis=0, tiled=True
            )
        own_grads.append(grad)
        other_grads.append(swap_bit(grad, 0, groups))
        row_sums.append(row_sum)
    grads = own_grads + other_grads
    sent = embed_grad_parts(scal, turned, grads, groups, 1)
    sent, kept_turned = lax.optimization_barrier((sent, turned))
    top_bit = groups.bit_length() - 2
    received = [swap_bit(sent[0], 1, groups), swap_bit(sent[1], top_bit, groups)]
    kept = embed_grad_parts(scal, kept_turned, grads, groups, 0)
    kept, weight_sums = lax.optimization_barrier((kept, weight_sums))
    ends = scatter_start(received, kept, groups)
    small, predictions = group_sums(routes, weight_sums, spec_bias, head_sums, row_sums, slot_count, per_sample)
    predictions = predictions.reshape(targets.shape)
    spec_rows = spec_grad.shape[0] // groups
    outgoing = shard_sums(routes, across([small] * shards), head_rows, spec_rows, spec_bias.shape[0])
    ends, outgoing = lax.optimization_barrier((ends, outgoing))
    gathered = from_all_groups(outgoing, groups)
    embed_grad = scatter_end(ends, shards, shard_at)
    head_grad, spec_w_grad, spec_b_grad, gain_grad, embed_bias_grad, head_bias_grad = assembled(
        scal, gathered, head_rows, shards, blocks, width
    )
    gain_grad, embed_bias_grad, head_bias_grad = gain_grad[0], embed_bias_grad[0], head_bias_grad[0]
    return (
        predictions,
        embed_grad,
        embed_bias_grad,
        gain_grad,
        spec_w_grad,
        spec_b_grad,
        head_grad,
        head_bias_grad,
    )


def solution(mesh):
    return jax.shard_map(
        on_device,
        mesh=mesh,
        in_specs=(
            P("grp", "fft", None, None),
            P("grp", "fft", None, None),
            P(),
            P(),
            P(),
            P(),
            P(),
            P(),
            P(),
            P(),
            P(),
        ),
        out_specs=(
            P("grp", "fft", None, None),
            P(("grp", "fft"), None),
            P(),
            P(),
            P(),
            P(),
            P(),
            P(),
        ),
        check_vma=False,
    )
```

```python
import jax
import jax.numpy as jnp
import ml_dtypes
import numpy as np
from jax import lax
from jax.experimental import pallas as pl
from jax.experimental.pallas import tpu as pltpu
from jax.sharding import PartitionSpec as P

EPSILON = 1e-05
SHRINK = 0.01
CHUNKS = 2
VMEM_BYTES = 24 * 1024 * 1024
SLOTS = 6
SHARD, FIRST_ROW, GROUP, SIDES = 0, 1, 2, 3
ROUTES = 3
HALF = jnp.bfloat16
FULL = jnp.float32


def dft_tables(cells):
    levels, factors = [], []
    for side, scale in ((cells, 1.1305), (cells // 2, 1.8633), (cells // 4, 1.0)):
        k = np.arange(cells)
        inside = (k < side).astype(np.float64)
        keep = inside[:, None] * inside[None, :]
        angle = 2.0 * np.pi * ((k[:, None] * k[None, :]) % side) / side
        one = np.exp(-1j * angle) * keep / np.sqrt(side)
        two = np.kron(one, one)
        table = np.concatenate([two.real, two.imag], axis=0)
        table[np.abs(table) < 1e-12] = 0.0
        rounded = (table * scale).astype(np.float32).astype(ml_dtypes.bfloat16)
        held = rounded.astype(np.float64)
        factors.append(float(np.sum(table * table) / np.sum(table * held)))
        levels.append(rounded)
    return np.stack(levels), factors


def dot(left, right):
    return jnp.dot(left, right, preferred_element_type=FULL)


def dot_tn(left, right):
    return lax.dot_general(left, right, (((0,), (0,)), ((), ())), preferred_element_type=FULL)


def dot_nt(left, right):
    return lax.dot_general(left, right, (((1,), (1,)), ((), ())), preferred_element_type=FULL)


def params(limit=VMEM_BYTES):
    return pltpu.CompilerParams(vmem_limit_bytes=limit)


def token_sides(scal_ref, first, count, per_sample, cells):
    token = lax.broadcasted_iota(jnp.int32, (count * per_sample, 1), 0)
    sample = token // per_sample
    side = jnp.zeros_like(token)
    for i in range(count):
        side = jnp.where(sample == i, scal_ref[SIDES + first + i], side)
    row = scal_ref[FIRST_ROW] + (token % per_sample) // cells
    col = token % cells
    valid = jnp.where((row < side) & (col < side), 1.0, 0.0).astype(FULL)
    return side, valid


def whole(shape):
    return pl.BlockSpec(tuple(shape), lambda i, s: (0,) * len(shape))


def part_of(scal_ref, k, size):
    at = jnp.bitwise_xor(scal_ref[SHARD], k)
    return pl.ds(pl.multiple_of(at * size, size), size)


def fill_lanes(scal_ref, refs, held):
    share = refs[0].shape[-1]
    for k, ref in enumerate(refs):
        held[:, part_of(scal_ref, k, share)] = ref[...].reshape(held.shape[0], share)


def fill_rows(scal_ref, refs, held):
    rows = refs[0].shape[1]
    for k, ref in enumerate(refs):
        held[:, part_of(scal_ref, k, rows), :] = ref[...]


def split_lanes(scal_ref, held, refs):
    share = refs[0].shape[-1]
    for k, ref in enumerate(refs):
        ref[...] = held[:, part_of(scal_ref, k, share)].reshape(ref.shape)


def split_rows(scal_ref, held, refs):
    rows = refs[0].shape[1]
    for k, ref in enumerate(refs):
        ref[...] = held[:, part_of(scal_ref, k, rows), :]


def embed(scal, patches, embed_w, embed_b, gain, firsts, count, per_sample, cells, shards, groups):
    rows, depth = patches.shape
    block = depth // groups
    width = embed_w.shape[1]
    share = width // shards
    chunk_rows = count * per_sample
    chunks = len(firsts)
    steps = 4
    tile = depth // steps

    def body(scal_ref, x_ref, w_ref, b_ref, gain_ref, emb_ref, norm_ref, stat_ref, *refs):
        (send_ref, keep_ref), outs, acc = refs[:2], refs[2:-1], refs[-1]
        step = pl.program_id(0)
        turned = x_ref[...].T
        for i in range(tile // block):
            values = turned[i * block : (i + 1) * block]
            away = (scal_ref[GROUP] + i) % 2

            @pl.when(away == 1)
            def _(i=i, values=values):
                send_ref[i // 2] = values

            @pl.when(away == 0)
            def _(i=i, values=values):
                keep_ref[i // 2] = values

        part = dot(x_ref[...], w_ref[...])

        @pl.when(step == 0)
        def _():
            acc[...] = part

        @pl.when(step > 0)
        def _():
            acc[...] += part

        @pl.when(step == steps - 1)
        def _():
            for c, first in enumerate(firsts):
                at = slice(c * chunk_rows, (c + 1) * chunk_rows)
                _, valid = token_sides(scal_ref, first, count, per_sample, cells)
                embedded = ((acc[at] + b_ref[...]) * valid).astype(HALF)
                emb_ref[at] = embedded
                values = embedded.astype(FULL)
                mean = jnp.mean(values, axis=-1, keepdims=True)
                centered = values - mean
                inv_std = lax.rsqrt(jnp.mean(centered * centered, axis=-1, keepdims=True) + EPSILON)
                norm_ref[at] = (centered * inv_std * gain_ref[...]).astype(HALF)
                stat_ref[at, :128] = jnp.broadcast_to(mean, (chunk_rows, 128))
                stat_ref[at, 128:] = jnp.broadcast_to(inv_std, (chunk_rows, 128))
                for k in range(shards):
                    piece = norm_ref[at, part_of(scal_ref, k, share)]
                    outs[c * shards + k][...] = piece.reshape(count, per_sample, share)

    piece = (count, per_sample, share)
    turned_spec = pl.BlockSpec((tile // (2 * block), block, rows), lambda k, s: (k, 0, 0))
    turned_shape = jax.ShapeDtypeStruct((groups // 2, block, rows), HALF)
    emb, normed, stats, send, keep, *pieces = pl.pallas_call(
        body,
        grid_spec=pltpu.PrefetchScalarGridSpec(
            num_scalar_prefetch=1,
            grid=(steps,),
            in_specs=[
                pl.BlockSpec((rows, tile), lambda k, s: (0, k)),
                pl.BlockSpec((tile, width), lambda k, s: (k, 0)),
                whole((1, width)),
                whole((1, width)),
            ],
            out_specs=[whole((rows, width)), whole((rows, width)), whole((rows, 256)), turned_spec, turned_spec]
            + [whole(piece)] * (shards * chunks),
            scratch_shapes=[pltpu.VMEM((rows, width), FULL)],
        ),
        out_shape=[
            jax.ShapeDtypeStruct((rows, width), HALF),
            jax.ShapeDtypeStruct((rows, width), HALF),
            jax.ShapeDtypeStruct((rows, 256), FULL),
            turned_shape,
            turned_shape,
        ]
        + [jax.ShapeDtypeStruct(piece, HALF)] * (shards * chunks),
        compiler_params=params(60 * 1024 * 1024),
        cost_estimate=pl.CostEstimate(
            flops=2 * rows * depth * width, bytes_accessed=2 * depth * (rows + width), transcendentals=0
        ),
        name="embed",
    )(scal, patches, embed_w, embed_b, gain)
    return emb, normed, stats, send, keep, [pieces[c * shards : (c + 1) * shards] for c in range(chunks)]


def to_blocks(values, blocks, width):
    half = values.shape[0] // 2
    return [
        jnp.concatenate(
            [values[:half, b * width : (b + 1) * width], values[half:, b * width : (b + 1) * width]], axis=1
        )
        for b in range(blocks)
    ]


def from_blocks(parts, width):
    real = jnp.concatenate([p[:, :width] for p in parts], axis=1)
    imag = jnp.concatenate([p[:, width:] for p in parts], axis=1)
    return real, imag


def table_factor(level, factors):
    return jnp.where(level == 0, factors[0], jnp.where(level == 1, factors[1], factors[2])).astype(FULL)


def table_back(table_ref, level, tops, rests, factor):
    size = table_ref.shape[2]
    total = None
    for at, (top, rest) in enumerate(zip(tops, rests)):
        table = table_ref[level, at * size : (at + 1) * size]
        part = dot(table, top) + dot(table, rest)
        total = part if total is None else total + part
    return total * factor


def two_terms(values):
    top = values.astype(HALF)
    return top, (values - top.astype(FULL)).astype(HALF)


def complex_weights(w_ref, held, blocks, width):
    for layer in range(2):
        for b in range(blocks):
            real, imag = w_ref[layer, 0, b], w_ref[layer, 1, b]
            held[layer, b, :width, :width] = real
            held[layer, b, :width, width:] = imag
            held[layer, b, width:, :width] = -imag
            held[layer, b, width:, width:] = real


def spectral_chunk(scal, table, factors, pieces, spec_w, spec_b, first):
    shards = len(pieces)
    count, per_sample, share = pieces[0].shape
    size = shards * per_sample
    width = spec_w.shape[-1]
    blocks = share // width
    wide = 2 * width

    def body(scal_ref, t_ref, w_ref, b_ref, *refs):
        ins, outs = refs[:shards], refs[shards : 2 * shards]
        spec_ref, hid_ref, fil_ref, weights, held = refs[2 * shards :]

        def bias(layer, b):
            row = pl.ds(scal_ref[SHARD] * blocks + b, 1)
            return jnp.concatenate([b_ref[layer, 0, row], b_ref[layer, 1, row]], axis=1)

        complex_weights(w_ref, weights, blocks, width)
        fill_rows(scal_ref, ins, held)
        levels = [scal_ref[SIDES + SLOTS + first + i] for i in range(count)]
        for i, level in enumerate(levels):
            spectrum = (dot(t_ref[level], held[i]) * table_factor(level, factors)).astype(HALF)
            for b, entry in enumerate(to_blocks(spectrum, blocks, width)):
                spec_ref[b, i * size : (i + 1) * size] = entry
        kept = []
        for b in range(blocks):
            pre_one = dot(spec_ref[b], weights[0, b]) + bias(0, b)
            hidden = jnp.maximum(pre_one, 0.0).astype(HALF)
            hid_ref[b] = hidden
            pre_two = dot(hidden, weights[1, b]) + bias(1, b)
            filtered = jnp.where(
                pre_two > SHRINK, pre_two - SHRINK, jnp.where(pre_two < -SHRINK, pre_two + SHRINK, 0.0)
            )
            top, rest = two_terms(filtered)
            fil_ref[b] = top
            kept.append((top, rest))
        for i, level in enumerate(levels):
            at = slice(i * size, (i + 1) * size)
            tops = from_blocks([top[at] for top, _ in kept], width)
            rests = from_blocks([rest[at] for _, rest in kept], width)
            held[i] = table_back(t_ref, level, tops, rests, table_factor(level, factors)).astype(HALF)
        split_rows(scal_ref, held, outs)

    saved = (blocks, count * size, wide)
    outs = pl.pallas_call(
        body,
        grid_spec=pltpu.PrefetchScalarGridSpec(
            num_scalar_prefetch=1,
            grid=(1,),
            in_specs=[
                whole(table.shape),
                pl.BlockSpec((2, 2, blocks, width, width), lambda i, s: (0, 0, s[SHARD], 0, 0)),
                whole(spec_b.shape),
            ]
            + [whole(pieces[0].shape)] * shards,
            out_specs=[whole(pieces[0].shape)] * shards + [whole(saved)] * 3,
            scratch_shapes=[pltpu.VMEM((2, blocks, wide, wide), HALF), pltpu.VMEM((count, size, share), HALF)],
        ),
        out_shape=[jax.ShapeDtypeStruct(pieces[0].shape, HALF)] * shards + [jax.ShapeDtypeStruct(saved, HALF)] * 3,
        compiler_params=params(),
        cost_estimate=pl.CostEstimate(
            flops=count * size * share * size * 14, bytes_accessed=count * size * share * 16, transcendentals=0
        ),
        name="spectral",
    )(scal, table, spec_w, spec_b, *pieces)
    return outs[:shards], outs[shards:]


def head_chunk(scal, embedded, normed, mixed, targets, head_w, head_b, first, samples, cells):
    shards = len(mixed)
    count, per_sample, share = mixed[0].shape
    rows = count * per_sample
    width, outs = head_w.shape
    at = first // count
    scale_root = float(np.sqrt(np.float32(samples)))

    def body(scal_ref, emb_ref, norm_ref, tgt_ref, w_ref, b_ref, *refs):
        mix_refs, (pred_ref, res_ref, up_ref, bias_ref, held) = refs[:shards], refs[shards:]
        fill_lanes(scal_ref, mix_refs, held)
        side, valid = token_sides(scal_ref, first, count, per_sample, cells)
        updated = (emb_ref[...].astype(FULL) + norm_ref[...].astype(FULL) + held[...].astype(FULL)).astype(HALF)
        output = (dot(updated, w_ref[...]) + b_ref[...]) * valid
        pred_ref[...] = output.astype(HALF).reshape(pred_ref.shape)
        scale = 2.0 / (side.astype(FULL) * scale_root)
        residual = (scale * valid * (output - tgt_ref[...].astype(FULL))).astype(HALF)
        res_ref[...] = residual.reshape(res_ref.shape)
        up_ref[...] = updated
        total = jnp.sum(residual.astype(FULL), axis=0, keepdims=True)
        bias_ref[...] = jnp.broadcast_to(total, bias_ref.shape)

    token_shape = (count, per_sample, outs)
    return pl.pallas_call(
        body,
        grid_spec=pltpu.PrefetchScalarGridSpec(
            num_scalar_prefetch=1,
            grid=(1,),
            in_specs=[
                pl.BlockSpec((rows, width), lambda i, s: (at, 0)),
                pl.BlockSpec((rows, width), lambda i, s: (at, 0)),
                pl.BlockSpec((rows, outs), lambda i, s: (at, 0)),
                whole((width, outs)),
                whole((1, outs)),
            ]
            + [whole(mixed[0].shape)] * shards,
            out_specs=[whole(token_shape), whole(token_shape), whole((rows, width)), whole((8, outs))],
            scratch_shapes=[pltpu.VMEM((rows, width), HALF)],
        ),
        out_shape=[
            jax.ShapeDtypeStruct(token_shape, HALF),
            jax.ShapeDtypeStruct(token_shape, HALF),
            jax.ShapeDtypeStruct((rows, width), HALF),
            jax.ShapeDtypeStruct((8, outs), FULL),
        ],
        compiler_params=params(),
        cost_estimate=pl.CostEstimate(
            flops=2 * rows * width * outs, bytes_accessed=rows * width * 4 + width * outs * 6, transcendentals=0
        ),
        name="head",
    )(scal, embedded, normed, targets, head_w, head_b, *mixed)


def head_gradient(updated, residual):
    width = updated[0].shape[1]
    outs = residual[0].shape[-1]
    count = len(updated)

    def body(*refs):
        total = None
        for up_ref, res_ref in zip(refs[:count], refs[count : 2 * count]):
            part = dot_tn(up_ref[...], res_ref[...].reshape(up_ref.shape[0], outs))
            total = part if total is None else total + part
        refs[-1][...] = total.astype(HALF)

    return pl.pallas_call(
        body,
        out_shape=jax.ShapeDtypeStruct((width, outs), HALF),
        compiler_params=params(),
        cost_estimate=pl.CostEstimate(
            flops=2 * count * updated[0].size * outs, bytes_accessed=2 * count * updated[0].size, transcendentals=0
        ),
        name="head_gradient",
    )(*updated, *residual)


def spectral_back_chunk(scal, table, factors, residual, head_w, spec_w, saved, first, before, last):
    shards = len(residual)
    count, per_sample, outs = residual[0].shape
    size = shards * per_sample
    width = spec_w.shape[-1]
    wide = 2 * width
    share = head_w.shape[0] // shards
    blocks = share // width
    raw_shape = (2, blocks, wide, wide)
    bias_shape = (2 * blocks, wide)
    has_before = before is not None

    def body(scal_ref, t_ref, h_ref, w_ref, spec_ref, hid_ref, fil_ref, *refs):
        ins, refs = refs[:shards], refs[shards:]
        if has_before:
            (old_ref, old_bias_ref), refs = refs[:2], refs[2:]
        pieces, (grad_ref, bias_ref, weights, held, gathered) = refs[:shards], refs[shards:]

        def weight_sums(layer, b, inputs, grads):
            raw = dot_tn(inputs, grads)
            sums = jnp.sum(grads.astype(FULL), axis=0, keepdims=True)
            at = layer * blocks + b
            if has_before:
                raw = raw + old_ref[layer, b]
                sums = sums + old_bias_ref[at : at + 1]
            bias_ref[at : at + 1] = sums
            if not last:
                grad_ref[layer, b] = raw
                return
            real = raw[:width, :width] + raw[width:, width:]
            imag = raw[:width, width:] - raw[width:, :width]
            grad_ref[at * width : (at + 1) * width] = jnp.concatenate([real, imag], axis=1).astype(HALF)

        complex_weights(w_ref, weights, blocks, width)
        fill_rows(scal_ref, ins, gathered)
        levels = [scal_ref[SIDES + SLOTS + first + i] for i in range(count)]
        updated_grad = dot_nt(gathered[...].reshape(count * size, outs), h_ref[...]).astype(HALF)
        entries = []
        for i, level in enumerate(levels):
            filtered_grad = dot(t_ref[level], updated_grad[i * size : (i + 1) * size]) * table_factor(level, factors)
            entries.append(to_blocks(filtered_grad, blocks, width))
        kept = []
        for b in range(blocks):
            entry = jnp.concatenate([e[b] for e in entries], axis=0)
            two_grad = jnp.where(fil_ref[b].astype(FULL) != 0.0, entry, 0.0).astype(HALF)
            hidden = hid_ref[b]
            hidden_grad = dot_nt(two_grad, weights[1, b])
            one_grad = jnp.where(hidden.astype(FULL) > 0.0, hidden_grad, 0.0).astype(HALF)
            kept.append(two_terms(dot_nt(one_grad, weights[0, b])))
            weight_sums(1, b, hidden, two_grad)
            weight_sums(0, b, spec_ref[b], one_grad)
        for i, level in enumerate(levels):
            at = slice(i * size, (i + 1) * size)
            tops = from_blocks([top[at] for top, _ in kept], width)
            rests = from_blocks([rest[at] for _, rest in kept], width)
            held[i] = table_back(t_ref, level, tops, rests, table_factor(level, factors)).astype(HALF)
        split_rows(scal_ref, held, pieces)

    piece = (count, per_sample, share)
    if last:
        grad_out = jax.ShapeDtypeStruct((2 * blocks * width, wide), HALF)
    else:
        grad_out = jax.ShapeDtypeStruct(raw_shape, FULL)
    result = pl.pallas_call(
        body,
        grid_spec=pltpu.PrefetchScalarGridSpec(
            num_scalar_prefetch=1,
            grid=(1,),
            in_specs=[
                whole(table.shape),
                pl.BlockSpec((share, outs), lambda i, s: (s[SHARD], 0)),
                pl.BlockSpec((2, 2, blocks, width, width), lambda i, s: (0, 0, s[SHARD], 0, 0)),
            ]
            + [whole(saved[0].shape)] * 3
            + [whole(residual[0].shape)] * shards
            + ([whole(raw_shape), whole(bias_shape)] if has_before else []),
            out_specs=[whole(piece)] * shards + [whole(grad_out.shape), whole(bias_shape)],
            scratch_shapes=[
                pltpu.VMEM((2, blocks, wide, wide), HALF),
                pltpu.VMEM((count, size, share), HALF),
                pltpu.VMEM((count, size, outs), HALF),
            ],
        ),
        out_shape=[jax.ShapeDtypeStruct(piece, HALF)] * shards
        + [grad_out, jax.ShapeDtypeStruct(bias_shape, FULL)],
        compiler_params=params(),
        cost_estimate=pl.CostEstimate(
            flops=count * size * share * size * 20, bytes_accessed=count * size * share * 16, transcendentals=0
        ),
        name="spectral_back",
    )(scal, table, head_w, spec_w, *saved, *residual, *(before or ()))
    return result[:shards], result[shards:]


def embedded_back_chunk(scal, embedded, stats, residual, head_w, gain, spec_grad, first, cells):
    shards = len(spec_grad)
    count, per_sample, share = spec_grad[0].shape
    rows = count * per_sample
    width, outs = head_w.shape
    at = first // count

    def body(scal_ref, emb_ref, stat_ref, res_ref, w_ref, gain_ref, *refs):
        grad_refs, (out_ref, sums_ref, held) = refs[:shards], refs[shards:]
        fill_lanes(scal_ref, grad_refs, held)
        _, valid = token_sides(scal_ref, first, count, per_sample, cells)
        inv_std = stat_ref[:, 128:129]
        unit = (emb_ref[...].astype(FULL) - stat_ref[:, 0:1]) * inv_std
        direct = dot_nt(res_ref[...].reshape(rows, outs), w_ref[...]).astype(HALF).astype(FULL)
        normed_grad = held[...].astype(FULL) + direct
        gain_grad = jnp.sum(normed_grad * unit, axis=0, keepdims=True)
        unit_grad = normed_grad * gain_ref[...]
        mean_grad = jnp.mean(unit_grad, axis=-1, keepdims=True)
        mean_cross = jnp.mean(unit_grad * unit, axis=-1, keepdims=True)
        input_grad = inv_std * (unit_grad - mean_grad - unit * mean_cross)
        result = ((input_grad + direct) * valid).astype(HALF)
        out_ref[...] = result
        bias_grad = jnp.sum(result.astype(FULL), axis=0, keepdims=True)
        sums_ref[0:4] = jnp.broadcast_to(gain_grad, (4, width))
        sums_ref[4:8] = jnp.broadcast_to(bias_grad, (4, width))

    return pl.pallas_call(
        body,
        grid_spec=pltpu.PrefetchScalarGridSpec(
            num_scalar_prefetch=1,
            grid=(1,),
            in_specs=[
                pl.BlockSpec((rows, width), lambda i, s: (at, 0)),
                pl.BlockSpec((rows, 256), lambda i, s: (at, 0)),
                whole((count, per_sample, outs)),
                whole((width, outs)),
                whole((1, width)),
            ]
            + [whole(spec_grad[0].shape)] * shards,
            out_specs=[whole((rows, width)), whole((8, width))],
            scratch_shapes=[pltpu.VMEM((rows, width), HALF)],
        ),
        out_shape=[jax.ShapeDtypeStruct((rows, width), HALF), jax.ShapeDtypeStruct((8, width), FULL)],
        compiler_params=params(),
        cost_estimate=pl.CostEstimate(
            flops=2 * rows * width * outs, bytes_accessed=rows * width * 6, transcendentals=0
        ),
        name="embedded_back",
    )(scal, embedded, stats, residual, head_w, gain, *spec_grad)


def embed_grad_parts(scal, turned, grads, groups, away):
    pairs, block, tokens = turned[0].shape
    chunk_rows, width = grads[0].shape
    half = width // 2
    top = pairs // 2
    count = len(turned)
    depth = tokens * count

    def relative(unit):
        return jnp.where(unit < top, 2 * unit + away, unit - top + away * top)

    def body(scal_ref, *refs):
        turned_refs, grad_refs = refs[:count], refs[count : count + len(grads)]
        left_ref, right_ref, held = refs[count + len(grads) :]
        unit = pl.program_id(0)

        @pl.when(unit % top == 0)
        def _():
            for i, ref in enumerate(grad_refs):
                held[i * chunk_rows : (i + 1) * chunk_rows] = ref[...]

        rows = jnp.concatenate([ref[0] for ref in turned_refs], axis=1)
        total = dot(rows, held[...]).astype(HALF)

        @pl.when(unit < top)
        def _():
            left_ref[0] = total

        @pl.when(unit >= top)
        def _():
            right_ref[0] = total

    shape = (top, block, half)
    return pl.pallas_call(
        body,
        grid_spec=pltpu.PrefetchScalarGridSpec(
            num_scalar_prefetch=1,
            grid=(pairs,),
            in_specs=[
                pl.BlockSpec((1, block, tokens), lambda i, s: (jnp.bitwise_xor(s[GROUP] // 2, relative(i)), 0, 0))
                for _ in turned
            ]
            + [pl.BlockSpec((chunk_rows, half), lambda i, s: (0, i // top)) for _ in grads],
            out_specs=[
                pl.BlockSpec((1, block, half), lambda i, s: (jnp.minimum(i, top - 1), 0, 0)),
                pl.BlockSpec((1, block, half), lambda i, s: (jnp.maximum(i - top, 0), 0, 0)),
            ],
            scratch_shapes=[pltpu.VMEM((depth, half), HALF)],
        ),
        out_shape=[jax.ShapeDtypeStruct(shape, HALF)] * 2,
        compiler_params=params(),
        cost_estimate=pl.CostEstimate(
            flops=depth * pairs * block * width,
            bytes_accessed=pairs * block * (2 * depth + width) + depth * width,
            transcendentals=0,
        ),
        name="embed_grad",
    )(scal, *turned, *grads)


def swap_bit(values, bit, groups):
    return lax.ppermute(values, "grp", [(g, g ^ (1 << bit)) for g in range(groups)])


def across(pieces):
    shards = len(pieces)
    return [pieces[0]] + [
        lax.ppermute(pieces[k], "fft", [(z, z ^ k) for z in range(shards)]) for k in range(1, shards)
    ]


def add_half(left, right):
    return (left.astype(FULL) + right.astype(FULL)).astype(HALF)


def scatter_start(received, kept, groups):
    bits = groups.bit_length() - 1
    ends = []
    for first, keep, order, low in (
        (received[0], kept[0], list(range(2, bits)), True),
        (received[1], kept[1], list(range(bits - 2, 0, -1)), False),
    ):
        total = add_half(keep, first)
        for bit in order:
            count, block, width = total.shape
            if low:
                split = total.reshape(count // 2, 2, block, width)
                keep, send = split[:, 0], split[:, 1]
            else:
                split = total.reshape(2, count // 2, block, width)
                keep, send = split[0], split[1]
            total = add_half(keep, swap_bit(send, bit, groups))
        ends.append(total[0])
    return ends


def scatter_step(part, bit, shards, shard_at):
    split = part.reshape(part.shape[0] // 2, 2, *part.shape[1:])
    mine = (shard_at // bit) % 2
    keep = lax.dynamic_index_in_dim(split, mine, 1, keepdims=False)
    send = lax.dynamic_index_in_dim(split, 1 - mine, 1, keepdims=False)
    received = lax.ppermute(send, "fft", [(z, z ^ bit) for z in range(shards)])
    return keep.astype(FULL) + received.astype(FULL)


def from_same_core(values, groups):
    return [values] + [
        lax.ppermute(values, "grp", [(g, g ^ k) for g in range(groups)]) for k in range(2, groups, 2)
    ]


def hi_lo(values):
    high = values.astype(HALF)
    return jnp.concatenate([high, (values - high.astype(FULL)).astype(HALF)], axis=0)


def from_hi_lo(values):
    half = values.shape[0] // 2
    values = values.astype(FULL)
    return values[:half] + values[half:]


def one_step(body, name, operands, out_shape):
    return pl.pallas_call(
        body,
        grid_spec=pltpu.PrefetchScalarGridSpec(
            num_scalar_prefetch=1,
            grid=(1,),
            in_specs=[whole(o.shape) for o in operands[1:]],
            out_specs=[whole(o.shape) for o in out_shape],
        ),
        out_shape=out_shape,
        compiler_params=params(),
        name=name,
    )(*operands)


def packed(routes, head_grad, spec_grad, predicted, groups):
    outs = head_grad.shape[1]
    head_rows, spec_rows = head_grad.shape[0] // groups, spec_grad.shape[0] // groups
    count, per_sample, _ = predicted[0].shape

    def body(routes_ref, head_ref, spec_ref, *refs):
        pred_refs, out_ref = refs[:-1], refs[-1]
        for g in range(groups):
            out_ref[g, :head_rows] = head_ref[g * head_rows : (g + 1) * head_rows]
            out_ref[g, head_rows : head_rows + spec_rows] = spec_ref[g * spec_rows : (g + 1) * spec_rows]
            chosen = routes_ref[ROUTES + g]
            for c, ref in enumerate(pred_refs):

                @pl.when(chosen // count == c)
                def _(g=g, c=c, ref=ref, chosen=chosen):
                    out_ref[g, head_rows + spec_rows :] = ref[chosen - c * count]

    shape = (groups, head_rows + spec_rows + per_sample, outs)
    return one_step(
        body, "packed", (routes, head_grad, spec_grad, *predicted), [jax.ShapeDtypeStruct(shape, HALF)]
    )[0]


def group_sums(routes, moved, spec_bias, head_sums, row_sums, slot_count, per_sample):
    groups, rows, outs = moved.shape
    weight_rows = rows - per_sample
    own_rows = spec_bias.shape[0]
    chunks = len(head_sums)
    parts = row_sums[0].shape[1] // outs
    spare = 16 - own_rows - 2 * parts - 1

    def body(routes_ref, moved_ref, bias_ref, *refs):
        head_refs, row_refs, (out_ref, pred_ref) = refs[:chunks], refs[chunks : 2 * chunks], refs[2 * chunks :]
        total = moved_ref[0, :weight_rows].astype(FULL)
        for g in range(1, groups):
            total = total + moved_ref[g, :weight_rows].astype(FULL)
        out_ref[:weight_rows] = total.astype(HALF)
        lines = [bias_ref[...]]
        for row in (0, 4):
            line = sum(ref[row : row + 1] for ref in row_refs)
            lines += [line[:, i * outs : (i + 1) * outs] for i in range(parts)]
        lines += [sum(ref[0:1] for ref in head_refs), jnp.zeros((spare, outs), FULL)]
        out_ref[weight_rows:] = hi_lo(jnp.concatenate(lines, axis=0))
        for i in range(slot_count):
            pred_ref[i] = moved_ref[routes_ref[ROUTES + groups + i], weight_rows:]

    return one_step(
        body,
        "group_sums",
        (routes, moved, spec_bias, *head_sums, *row_sums),
        [
            jax.ShapeDtypeStruct((weight_rows + 32, outs), HALF),
            jax.ShapeDtypeStruct((slot_count, per_sample, outs), HALF),
        ],
    )


def shard_sums(routes, rows, head_rows, spec_rows, own_rows):
    shards = len(rows)
    outs = rows[0].shape[1]
    small_rows = 32

    def body(routes_ref, *refs):
        ins, out_ref = refs[:-1], refs[-1]
        total = sum(ref[:head_rows].astype(FULL) for ref in ins)
        out_ref[:head_rows] = total.astype(HALF)
        for k, ref in enumerate(ins):
            at = head_rows + k * spec_rows
            out_ref[at : at + spec_rows] = ref[head_rows : head_rows + spec_rows]
        smalls = [from_hi_lo(ref[head_rows + spec_rows :]) for ref in ins]
        lines = []
        for z in range(shards):
            here = [jnp.bitwise_xor(routes_ref[SHARD], k) == z for k in range(shards)]
            lines.append(sum(jnp.where(h, v[:own_rows], 0.0) for h, v in zip(here, smalls)))
        lines.append(sum(v[own_rows:] for v in smalls))
        have = shards * own_rows + 16 - own_rows
        lines.append(jnp.zeros((small_rows - have, outs), FULL))
        out_ref[head_rows + shards * spec_rows :] = hi_lo(jnp.concatenate(lines, axis=0))

    shape = (head_rows + shards * spec_rows + 2 * small_rows, outs)
    return one_step(body, "shard_sums", (routes, *rows), [jax.ShapeDtypeStruct(shape, HALF)])[0]


def assembled(scal, gathered, head_rows, shards, blocks, width):
    groups = len(gathered)
    total_blocks = shards * blocks
    spec_rows = 2 * blocks * width // groups
    small_at = head_rows + shards * spec_rows
    small_rows = (gathered[0].shape[0] - small_at) // 2

    def body(scal_ref, *refs):
        ins, (head_ref, spec_ref, bias_ref, gain_ref, embed_ref, out_ref) = refs[:groups], refs[groups:]
        small = None
        for k, ref in enumerate(ins):
            group = jnp.bitwise_xor(scal_ref[GROUP], k)
            at = pl.ds(pl.multiple_of(group * head_rows, head_rows), head_rows)
            head_ref[at, :] = ref[:head_rows].astype(FULL)
            start = group * spec_rows
            layer, b = start // (blocks * width), (start // width) % blocks
            rows = pl.ds(pl.multiple_of(start % width, spec_rows), spec_rows)
            for j in range(shards):
                values = ref[head_rows + j * spec_rows : head_rows + (j + 1) * spec_rows].astype(FULL)
                z = jnp.bitwise_xor(scal_ref[SHARD], j)
                spec_ref[layer, 0, z * blocks + b, rows] = values[:, :width]
                spec_ref[layer, 1, z * blocks + b, rows] = values[:, width:]
            part = ref[small_at : small_at + small_rows].astype(FULL) + ref[small_at + small_rows :].astype(FULL)
            small = part if small is None else small + part
        for z in range(shards):
            for layer in range(2):
                for b in range(blocks):
                    row = (z * 2 + layer) * blocks + b
                    for p in range(2):
                        bias_ref[layer, p, z * blocks + b : z * blocks + b + 1] = small[
                            row : row + 1, p * width : (p + 1) * width
                        ]
        row = shards * 2 * blocks
        quarter = gain_ref.shape[1] // (2 * width)
        for ref in (gain_ref, embed_ref):
            for i in range(quarter):
                ref[:, i * 2 * width : (i + 1) * 2 * width] = small[row + i : row + i + 1]
            row += quarter
        out_ref[...] = small[row : row + 1]

    out_shape = [
        jax.ShapeDtypeStruct((groups * head_rows, 2 * width), FULL),
        jax.ShapeDtypeStruct((2, 2, total_blocks, width, width), FULL),
        jax.ShapeDtypeStruct((2, 2, total_blocks, width), FULL),
        jax.ShapeDtypeStruct((1, groups * head_rows), FULL),
        jax.ShapeDtypeStruct((1, groups * head_rows), FULL),
        jax.ShapeDtypeStruct((1, 2 * width), FULL),
    ]
    return pl.pallas_call(
        body,
        grid_spec=pltpu.PrefetchScalarGridSpec(
            num_scalar_prefetch=1,
            grid=(1,),
            in_specs=[whole(gathered[0].shape)] * groups,
            out_specs=[whole(o.shape) for o in out_shape],
        ),
        out_shape=out_shape,
        compiler_params=params(),
        name="assembled",
    )(scal, *gathered)


def prediction_routes(dest_group, group_at, groups, slot_count):
    own_dest = lax.dynamic_slice_in_dim(dest_group, group_at * slot_count, slot_count)
    loaders = jnp.arange(groups, dtype=jnp.int32)
    slots = jnp.arange(slot_count, dtype=jnp.int32)
    chosen = jnp.sum(jnp.where(own_dest[None, :] == loaders[:, None], slots[None, :], 0), axis=1)
    holds = jnp.any(dest_group.reshape(groups, slot_count) == group_at, axis=1)
    rank = jnp.sum(jnp.where(holds[None, :] & (loaders[None, :] < loaders[:, None]), 1, 0), axis=1)
    sources = jnp.sum(jnp.where(holds[None, :] & (rank[None, :] == slots[:, None]), loaders[None, :], 0), axis=1)
    return jnp.concatenate([chosen, sources]).astype(jnp.int32)


def on_device(
    patches, targets, grid_side, dest_group, embed_w, embed_b, gain, spec_w, spec_b, head_w, head_b
):
    slot_count, row_count, cells, depth = patches.shape
    samples = dest_group.shape[0]
    groups = lax.axis_size("grp")
    shards = lax.axis_size("fft")
    group_at = lax.axis_index("grp").astype(jnp.int32)
    shard_at = lax.axis_index("fft").astype(jnp.int32)
    outs = targets.shape[-1]
    per_sample = row_count * cells
    count = slot_count // CHUNKS
    firsts = [c * count for c in range(CHUNKS)]
    assert slot_count == SLOTS

    sides = lax.dynamic_slice_in_dim(grid_side, group_at * slot_count, slot_count)
    level = jnp.where(sides == cells, 0, jnp.where(sides == cells // 2, 1, 2)).astype(jnp.int32)
    place = jnp.stack([shard_at, shard_at * row_count, group_at])
    scal = jnp.concatenate([place, sides, level])
    routes = jnp.concatenate([place, prediction_routes(dest_group, group_at, groups, slot_count)])
    table_values, factors = dft_tables(cells)
    table = jnp.asarray(table_values)
    flat_patches = patches.reshape(-1, depth)
    flat_targets = targets.reshape(-1, outs)
    gain_row, embed_b_row, head_b_row = gain[None], embed_b[None], head_b[None]

    embedded, normed, stats, turned_send, turned_keep, pieces = embed(
        scal, flat_patches, embed_w, embed_b_row, gain_row, firsts, count, per_sample, cells, shards, groups
    )
    moved = [across(p) for p in pieces]
    mixed, saved = [], []
    for first, values in zip(firsts, moved):
        out, rest = spectral_chunk(scal, table, factors, values, spec_w, spec_b, first)
        mixed.append(across(out))
        saved.append(rest)
    predicted, residual, updated, head_sums, gathered = [], [], [], [], []
    for first, mix in zip(firsts, mixed):
        pred, res, up, sums = head_chunk(
            scal, embedded, normed, mix, flat_targets, head_w, head_b_row, first, samples, cells
        )
        predicted.append(pred)
        residual.append(res)
        updated.append(up)
        head_sums.append(sums)
        gathered.append(across([res] * shards))
    head_grad, gathered[0] = lax.optimization_barrier((head_gradient(updated, residual), gathered[0]))
    spec_back, sums = [], None
    for first, res, rest in zip(firsts, gathered, saved):
        values, sums = spectral_back_chunk(
            scal, table, factors, res, head_w, spec_w, rest, first, sums, first == firsts[-1]
        )
        if first == firsts[-1]:
            values, turned_send = lax.optimization_barrier((values, turned_send))
        spec_back.append(across(values))
    turned = [turned_keep, swap_bit(turned_send, 0, groups)]
    spec_grad, spec_bias = sums
    width = spec_w.shape[-1]
    blocks = spec_w.shape[2] // shards
    head_rows = head_w.shape[0] // groups
    weight_sums = lax.all_to_all(
        packed(routes, head_grad, spec_grad, predicted, groups), "grp", split_axis=0, concat_axis=0, tiled=True
    )
    own_grads, other_grads, row_sums = [], [], []
    for first, res, back in zip(firsts, residual, spec_back):
        grad, row_sum = embedded_back_chunk(scal, embedded, stats, res, head_w, gain_row, back, first, cells)
        own_grads.append(grad)
        other_grads.append(swap_bit(grad, 0, groups))
        row_sums.append(row_sum)
    grads = own_grads + other_grads
    grads, weight_sums = lax.optimization_barrier((grads, weight_sums))
    sent = embed_grad_parts(scal, turned, grads, groups, 1)
    sent, kept_turned = lax.optimization_barrier((sent, turned))
    top_bit = groups.bit_length() - 2
    received = [swap_bit(sent[0], 1, groups), swap_bit(sent[1], top_bit, groups)]
    kept = embed_grad_parts(scal, kept_turned, grads, groups, 0)
    kept, weight_sums = lax.optimization_barrier((kept, weight_sums))
    ends = scatter_start(received, kept, groups)
    small, predictions = group_sums(routes, weight_sums, spec_bias, head_sums, row_sums, slot_count, per_sample)
    predictions = predictions.reshape(targets.shape)
    spec_rows = spec_grad.shape[0] // groups
    outgoing = shard_sums(routes, across([small] * shards), head_rows, spec_rows, spec_bias.shape[0])
    _, outgoing = lax.optimization_barrier((ends, outgoing))
    part = jnp.concatenate(ends, axis=-1)
    part = part.reshape(shards, part.shape[0] // shards, -1)
    part = scatter_step(part, 1, shards, shard_at)
    even = from_same_core(outgoing, groups)
    bit = 2
    while bit < shards:
        part = part.astype(HALF)
        if bit == 2:
            _, even = lax.optimization_barrier((part, even))
        part = scatter_step(part, bit, shards, shard_at)
        bit *= 2
    embed_grad = part[0]
    gathered = [v for pair in zip(even, [swap_bit(v, 0, groups) for v in even]) for v in pair]
    head_grad, spec_w_grad, spec_b_grad, gain_grad, embed_bias_grad, head_bias_grad = assembled(
        scal, gathered, head_rows, shards, blocks, width
    )
    gain_grad, embed_bias_grad, head_bias_grad = gain_grad[0], embed_bias_grad[0], head_bias_grad[0]
    return (
        predictions,
        embed_grad,
        embed_bias_grad,
        gain_grad,
        spec_w_grad,
        spec_b_grad,
        head_grad,
        head_bias_grad,
    )


def solution(mesh):
    return jax.shard_map(
        on_device,
        mesh=mesh,
        in_specs=(
            P("grp", "fft", None, None),
            P("grp", "fft", None, None),
            P(),
            P(),
            P(),
            P(),
            P(),
            P(),
            P(),
            P(),
            P(),
        ),
        out_specs=(
            P("grp", "fft", None, None),
            P(("grp", "fft"), None),
            P(),
            P(),
            P(),
            P(),
            P(),
            P(),
        ),
        check_vma=False,
    )
```

```python
import jax
import jax.numpy as jnp
import ml_dtypes
import numpy as np
from jax import lax
from jax.experimental import pallas as pl
from jax.experimental.pallas import tpu as pltpu
from jax.sharding import PartitionSpec as P

EPSILON = 1e-05
SHRINK = 0.01
CHUNKS = 2
VMEM_BYTES = 24 * 1024 * 1024
SLOTS = 6
SHARD, FIRST_ROW, GROUP, SIDES = 0, 1, 2, 3
ROUTES = 3
HALF = jnp.bfloat16
FULL = jnp.float32


def dft_tables(cells):
    levels, factors = [], []
    for side, scale in ((cells, 1.1305), (cells // 2, 1.8633), (cells // 4, 1.0)):
        k = np.arange(cells)
        inside = (k < side).astype(np.float64)
        keep = inside[:, None] * inside[None, :]
        angle = 2.0 * np.pi * ((k[:, None] * k[None, :]) % side) / side
        one = np.exp(-1j * angle) * keep / np.sqrt(side)
        two = np.kron(one, one)
        table = np.concatenate([two.real, two.imag], axis=0)
        table[np.abs(table) < 1e-12] = 0.0
        rounded = (table * scale).astype(np.float32).astype(ml_dtypes.bfloat16)
        held = rounded.astype(np.float64)
        factors.append(float(np.sum(table * table) / np.sum(table * held)))
        levels.append(rounded)
    return np.stack(levels), factors


def dot(left, right):
    return jnp.dot(left, right, preferred_element_type=FULL)


def dot_tn(left, right):
    return lax.dot_general(left, right, (((0,), (0,)), ((), ())), preferred_element_type=FULL)


def dot_nt(left, right):
    return lax.dot_general(left, right, (((1,), (1,)), ((), ())), preferred_element_type=FULL)


def params(limit=VMEM_BYTES):
    return pltpu.CompilerParams(vmem_limit_bytes=limit)


def token_sides(scal_ref, first, count, per_sample, cells):
    token = lax.broadcasted_iota(jnp.int32, (count * per_sample, 1), 0)
    sample = token // per_sample
    side = jnp.zeros_like(token)
    for i in range(count):
        side = jnp.where(sample == i, scal_ref[SIDES + first + i], side)
    row = scal_ref[FIRST_ROW] + (token % per_sample) // cells
    col = token % cells
    valid = jnp.where((row < side) & (col < side), 1.0, 0.0).astype(FULL)
    return side, valid


def whole(shape):
    return pl.BlockSpec(tuple(shape), lambda i, s: (0,) * len(shape))


def part_of(scal_ref, k, size):
    at = jnp.bitwise_xor(scal_ref[SHARD], k)
    return pl.ds(pl.multiple_of(at * size, size), size)


def fill_lanes(scal_ref, refs, held):
    share = refs[0].shape[-1]
    for k, ref in enumerate(refs):
        held[:, part_of(scal_ref, k, share)] = ref[...].reshape(held.shape[0], share)


def fill_rows(scal_ref, refs, held):
    rows = refs[0].shape[1]
    for k, ref in enumerate(refs):
        held[:, part_of(scal_ref, k, rows), :] = ref[...]


def split_lanes(scal_ref, held, refs):
    share = refs[0].shape[-1]
    for k, ref in enumerate(refs):
        ref[...] = held[:, part_of(scal_ref, k, share)].reshape(ref.shape)


def split_rows(scal_ref, held, refs):
    rows = refs[0].shape[1]
    for k, ref in enumerate(refs):
        ref[...] = held[:, part_of(scal_ref, k, rows), :]


def embed(scal, patches, embed_w, embed_b, gain, firsts, count, per_sample, cells, shards, groups):
    rows, depth = patches.shape
    block = depth // groups
    width = embed_w.shape[1]
    share = width // shards
    chunk_rows = count * per_sample
    chunks = len(firsts)
    steps = 4
    tile = depth // steps

    def body(scal_ref, x_ref, w_ref, b_ref, gain_ref, emb_ref, norm_ref, stat_ref, *refs):
        (send_ref, keep_ref), outs, acc = refs[:2], refs[2:-1], refs[-1]
        step = pl.program_id(0)
        turned = x_ref[...].T
        for i in range(tile // block):
            values = turned[i * block : (i + 1) * block]
            away = (scal_ref[GROUP] + i) % 2

            @pl.when(away == 1)
            def _(i=i, values=values):
                send_ref[i // 2] = values

            @pl.when(away == 0)
            def _(i=i, values=values):
                keep_ref[i // 2] = values

        part = dot(x_ref[...], w_ref[...])

        @pl.when(step == 0)
        def _():
            acc[...] = part

        @pl.when(step > 0)
        def _():
            acc[...] += part

        @pl.when(step == steps - 1)
        def _():
            for c, first in enumerate(firsts):
                at = slice(c * chunk_rows, (c + 1) * chunk_rows)
                _, valid = token_sides(scal_ref, first, count, per_sample, cells)
                embedded = ((acc[at] + b_ref[...]) * valid).astype(HALF)
                emb_ref[at] = embedded
                values = embedded.astype(FULL)
                mean = jnp.mean(values, axis=-1, keepdims=True)
                centered = values - mean
                inv_std = lax.rsqrt(jnp.mean(centered * centered, axis=-1, keepdims=True) + EPSILON)
                norm_ref[at] = (centered * inv_std * gain_ref[...]).astype(HALF)
                stat_ref[at, :128] = jnp.broadcast_to(mean, (chunk_rows, 128))
                stat_ref[at, 128:] = jnp.broadcast_to(inv_std, (chunk_rows, 128))
                for k in range(shards):
                    piece = norm_ref[at, part_of(scal_ref, k, share)]
                    outs[c * shards + k][...] = piece.reshape(count, per_sample, share)

    piece = (count, per_sample, share)
    turned_spec = pl.BlockSpec((tile // (2 * block), block, rows), lambda k, s: (k, 0, 0))
    turned_shape = jax.ShapeDtypeStruct((groups // 2, block, rows), HALF)
    emb, normed, stats, send, keep, *pieces = pl.pallas_call(
        body,
        grid_spec=pltpu.PrefetchScalarGridSpec(
            num_scalar_prefetch=1,
            grid=(steps,),
            in_specs=[
                pl.BlockSpec((rows, tile), lambda k, s: (0, k)),
                pl.BlockSpec((tile, width), lambda k, s: (k, 0)),
                whole((1, width)),
                whole((1, width)),
            ],
            out_specs=[whole((rows, width)), whole((rows, width)), whole((rows, 256)), turned_spec, turned_spec]
            + [whole(piece)] * (shards * chunks),
            scratch_shapes=[pltpu.VMEM((rows, width), FULL)],
        ),
        out_shape=[
            jax.ShapeDtypeStruct((rows, width), HALF),
            jax.ShapeDtypeStruct((rows, width), HALF),
            jax.ShapeDtypeStruct((rows, 256), FULL),
            turned_shape,
            turned_shape,
        ]
        + [jax.ShapeDtypeStruct(piece, HALF)] * (shards * chunks),
        compiler_params=params(60 * 1024 * 1024),
        cost_estimate=pl.CostEstimate(
            flops=2 * rows * depth * width, bytes_accessed=2 * depth * (rows + width), transcendentals=0
        ),
        name="embed",
    )(scal, patches, embed_w, embed_b, gain)
    return emb, normed, stats, send, keep, [pieces[c * shards : (c + 1) * shards] for c in range(chunks)]


def to_blocks(values, blocks, width):
    half = values.shape[0] // 2
    return [
        jnp.concatenate(
            [values[:half, b * width : (b + 1) * width], values[half:, b * width : (b + 1) * width]], axis=1
        )
        for b in range(blocks)
    ]


def from_blocks(parts, width):
    real = jnp.concatenate([p[:, :width] for p in parts], axis=1)
    imag = jnp.concatenate([p[:, width:] for p in parts], axis=1)
    return real, imag


def table_factor(level, factors):
    return jnp.where(level == 0, factors[0], jnp.where(level == 1, factors[1], factors[2])).astype(FULL)


def table_back(table_ref, level, tops, rests, factor):
    size = table_ref.shape[2]
    total = None
    for at, (top, rest) in enumerate(zip(tops, rests)):
        table = table_ref[level, at * size : (at + 1) * size]
        part = dot(table, top) + dot(table, rest)
        total = part if total is None else total + part
    return total * factor


def two_terms(values):
    top = values.astype(HALF)
    return top, (values - top.astype(FULL)).astype(HALF)


def complex_weights(w_ref, held, blocks, width):
    for layer in range(2):
        for b in range(blocks):
            real, imag = w_ref[layer, 0, b], w_ref[layer, 1, b]
            held[layer, b, :width, :width] = real
            held[layer, b, :width, width:] = imag
            held[layer, b, width:, :width] = -imag
            held[layer, b, width:, width:] = real


def spectral_chunk(scal, table, factors, pieces, spec_w, spec_b, first):
    shards = len(pieces)
    count, per_sample, share = pieces[0].shape
    size = shards * per_sample
    width = spec_w.shape[-1]
    blocks = share // width
    wide = 2 * width

    def body(scal_ref, t_ref, w_ref, b_ref, *refs):
        ins, outs = refs[:shards], refs[shards : 2 * shards]
        spec_ref, hid_ref, fil_ref, weights, held = refs[2 * shards :]

        def bias(layer, b):
            row = pl.ds(scal_ref[SHARD] * blocks + b, 1)
            return jnp.concatenate([b_ref[layer, 0, row], b_ref[layer, 1, row]], axis=1)

        complex_weights(w_ref, weights, blocks, width)
        fill_rows(scal_ref, ins, held)
        levels = [scal_ref[SIDES + SLOTS + first + i] for i in range(count)]
        for i, level in enumerate(levels):
            spectrum = (dot(t_ref[level], held[i]) * table_factor(level, factors)).astype(HALF)
            for b, entry in enumerate(to_blocks(spectrum, blocks, width)):
                spec_ref[b, i * size : (i + 1) * size] = entry
        kept = []
        for b in range(blocks):
            pre_one = dot(spec_ref[b], weights[0, b]) + bias(0, b)
            hidden = jnp.maximum(pre_one, 0.0).astype(HALF)
            hid_ref[b] = hidden
            pre_two = dot(hidden, weights[1, b]) + bias(1, b)
            filtered = jnp.where(
                pre_two > SHRINK, pre_two - SHRINK, jnp.where(pre_two < -SHRINK, pre_two + SHRINK, 0.0)
            )
            top, rest = two_terms(filtered)
            fil_ref[b] = top
            kept.append((top, rest))
        for i, level in enumerate(levels):
            at = slice(i * size, (i + 1) * size)
            tops = from_blocks([top[at] for top, _ in kept], width)
            rests = from_blocks([rest[at] for _, rest in kept], width)
            held[i] = table_back(t_ref, level, tops, rests, table_factor(level, factors)).astype(HALF)
        split_rows(scal_ref, held, outs)

    saved = (blocks, count * size, wide)
    outs = pl.pallas_call(
        body,
        grid_spec=pltpu.PrefetchScalarGridSpec(
            num_scalar_prefetch=1,
            grid=(1,),
            in_specs=[
                whole(table.shape),
                pl.BlockSpec((2, 2, blocks, width, width), lambda i, s: (0, 0, s[SHARD], 0, 0)),
                whole(spec_b.shape),
            ]
            + [whole(pieces[0].shape)] * shards,
            out_specs=[whole(pieces[0].shape)] * shards + [whole(saved)] * 3,
            scratch_shapes=[pltpu.VMEM((2, blocks, wide, wide), HALF), pltpu.VMEM((count, size, share), HALF)],
        ),
        out_shape=[jax.ShapeDtypeStruct(pieces[0].shape, HALF)] * shards + [jax.ShapeDtypeStruct(saved, HALF)] * 3,
        compiler_params=params(),
        cost_estimate=pl.CostEstimate(
            flops=count * size * share * size * 14, bytes_accessed=count * size * share * 16, transcendentals=0
        ),
        name="spectral",
    )(scal, table, spec_w, spec_b, *pieces)
    return outs[:shards], outs[shards:]


def head_chunk(scal, embedded, normed, mixed, targets, head_w, head_b, first, samples, cells):
    shards = len(mixed)
    count, per_sample, share = mixed[0].shape
    rows = count * per_sample
    width, outs = head_w.shape
    at = first // count
    scale_root = float(np.sqrt(np.float32(samples)))

    def body(scal_ref, emb_ref, norm_ref, tgt_ref, w_ref, b_ref, *refs):
        mix_refs, (pred_ref, res_ref, up_ref, bias_ref, held) = refs[:shards], refs[shards:]
        fill_lanes(scal_ref, mix_refs, held)
        side, valid = token_sides(scal_ref, first, count, per_sample, cells)
        updated = (emb_ref[...].astype(FULL) + norm_ref[...].astype(FULL) + held[...].astype(FULL)).astype(HALF)
        output = (dot(updated, w_ref[...]) + b_ref[...]) * valid
        pred_ref[...] = output.astype(HALF).reshape(pred_ref.shape)
        scale = 2.0 / (side.astype(FULL) * scale_root)
        residual = (scale * valid * (output - tgt_ref[...].astype(FULL))).astype(HALF)
        res_ref[...] = residual.reshape(res_ref.shape)
        up_ref[...] = updated
        total = jnp.sum(residual.astype(FULL), axis=0, keepdims=True)
        bias_ref[...] = jnp.broadcast_to(total, bias_ref.shape)

    token_shape = (count, per_sample, outs)
    return pl.pallas_call(
        body,
        grid_spec=pltpu.PrefetchScalarGridSpec(
            num_scalar_prefetch=1,
            grid=(1,),
            in_specs=[
                pl.BlockSpec((rows, width), lambda i, s: (at, 0)),
                pl.BlockSpec((rows, width), lambda i, s: (at, 0)),
                pl.BlockSpec((rows, outs), lambda i, s: (at, 0)),
                whole((width, outs)),
                whole((1, outs)),
            ]
            + [whole(mixed[0].shape)] * shards,
            out_specs=[whole(token_shape), whole(token_shape), whole((rows, width)), whole((8, outs))],
            scratch_shapes=[pltpu.VMEM((rows, width), HALF)],
        ),
        out_shape=[
            jax.ShapeDtypeStruct(token_shape, HALF),
            jax.ShapeDtypeStruct(token_shape, HALF),
            jax.ShapeDtypeStruct((rows, width), HALF),
            jax.ShapeDtypeStruct((8, outs), FULL),
        ],
        compiler_params=params(),
        cost_estimate=pl.CostEstimate(
            flops=2 * rows * width * outs, bytes_accessed=rows * width * 4 + width * outs * 6, transcendentals=0
        ),
        name="head",
    )(scal, embedded, normed, targets, head_w, head_b, *mixed)


def head_gradient(updated, residual):
    width = updated[0].shape[1]
    outs = residual[0].shape[-1]
    count = len(updated)

    def body(*refs):
        total = None
        for up_ref, res_ref in zip(refs[:count], refs[count : 2 * count]):
            part = dot_tn(up_ref[...], res_ref[...].reshape(up_ref.shape[0], outs))
            total = part if total is None else total + part
        refs[-1][...] = total.astype(HALF)

    return pl.pallas_call(
        body,
        out_shape=jax.ShapeDtypeStruct((width, outs), HALF),
        compiler_params=params(),
        cost_estimate=pl.CostEstimate(
            flops=2 * count * updated[0].size * outs, bytes_accessed=2 * count * updated[0].size, transcendentals=0
        ),
        name="head_gradient",
    )(*updated, *residual)


def spectral_back_chunk(scal, table, factors, residual, head_w, spec_w, saved, first, before, last):
    shards = len(residual)
    count, per_sample, outs = residual[0].shape
    size = shards * per_sample
    width = spec_w.shape[-1]
    wide = 2 * width
    share = head_w.shape[0] // shards
    blocks = share // width
    raw_shape = (2, blocks, wide, wide)
    bias_shape = (2 * blocks, wide)
    has_before = before is not None

    def body(scal_ref, t_ref, h_ref, w_ref, spec_ref, hid_ref, fil_ref, *refs):
        ins, refs = refs[:shards], refs[shards:]
        if has_before:
            (old_ref, old_bias_ref), refs = refs[:2], refs[2:]
        pieces, (grad_ref, bias_ref, weights, held, gathered) = refs[:shards], refs[shards:]

        def weight_sums(layer, b, inputs, grads):
            raw = dot_tn(inputs, grads)
            sums = jnp.sum(grads.astype(FULL), axis=0, keepdims=True)
            at = layer * blocks + b
            if has_before:
                raw = raw + old_ref[layer, b]
                sums = sums + old_bias_ref[at : at + 1]
            bias_ref[at : at + 1] = sums
            if not last:
                grad_ref[layer, b] = raw
                return
            real = raw[:width, :width] + raw[width:, width:]
            imag = raw[:width, width:] - raw[width:, :width]
            grad_ref[at * width : (at + 1) * width] = jnp.concatenate([real, imag], axis=1).astype(HALF)

        complex_weights(w_ref, weights, blocks, width)
        fill_rows(scal_ref, ins, gathered)
        levels = [scal_ref[SIDES + SLOTS + first + i] for i in range(count)]
        updated_grad = dot_nt(gathered[...].reshape(count * size, outs), h_ref[...]).astype(HALF)
        entries = []
        for i, level in enumerate(levels):
            filtered_grad = dot(t_ref[level], updated_grad[i * size : (i + 1) * size]) * table_factor(level, factors)
            entries.append(to_blocks(filtered_grad, blocks, width))
        kept = []
        for b in range(blocks):
            entry = jnp.concatenate([e[b] for e in entries], axis=0)
            two_grad = jnp.where(fil_ref[b].astype(FULL) != 0.0, entry, 0.0).astype(HALF)
            hidden = hid_ref[b]
            hidden_grad = dot_nt(two_grad, weights[1, b])
            one_grad = jnp.where(hidden.astype(FULL) > 0.0, hidden_grad, 0.0).astype(HALF)
            kept.append(two_terms(dot_nt(one_grad, weights[0, b])))
            weight_sums(1, b, hidden, two_grad)
            weight_sums(0, b, spec_ref[b], one_grad)
        for i, level in enumerate(levels):
            at = slice(i * size, (i + 1) * size)
            tops = from_blocks([top[at] for top, _ in kept], width)
            rests = from_blocks([rest[at] for _, rest in kept], width)
            held[i] = table_back(t_ref, level, tops, rests, table_factor(level, factors)).astype(HALF)
        split_rows(scal_ref, held, pieces)

    piece = (count, per_sample, share)
    if last:
        grad_out = jax.ShapeDtypeStruct((2 * blocks * width, wide), HALF)
    else:
        grad_out = jax.ShapeDtypeStruct(raw_shape, FULL)
    result = pl.pallas_call(
        body,
        grid_spec=pltpu.PrefetchScalarGridSpec(
            num_scalar_prefetch=1,
            grid=(1,),
            in_specs=[
                whole(table.shape),
                pl.BlockSpec((share, outs), lambda i, s: (s[SHARD], 0)),
                pl.BlockSpec((2, 2, blocks, width, width), lambda i, s: (0, 0, s[SHARD], 0, 0)),
            ]
            + [whole(saved[0].shape)] * 3
            + [whole(residual[0].shape)] * shards
            + ([whole(raw_shape), whole(bias_shape)] if has_before else []),
            out_specs=[whole(piece)] * shards + [whole(grad_out.shape), whole(bias_shape)],
            scratch_shapes=[
                pltpu.VMEM((2, blocks, wide, wide), HALF),
                pltpu.VMEM((count, size, share), HALF),
                pltpu.VMEM((count, size, outs), HALF),
            ],
        ),
        out_shape=[jax.ShapeDtypeStruct(piece, HALF)] * shards
        + [grad_out, jax.ShapeDtypeStruct(bias_shape, FULL)],
        compiler_params=params(),
        cost_estimate=pl.CostEstimate(
            flops=count * size * share * size * 20, bytes_accessed=count * size * share * 16, transcendentals=0
        ),
        name="spectral_back",
    )(scal, table, head_w, spec_w, *saved, *residual, *(before or ()))
    return result[:shards], result[shards:]


def embedded_back_chunk(scal, embedded, stats, residual, head_w, gain, spec_grad, first, cells):
    shards = len(spec_grad)
    count, per_sample, share = spec_grad[0].shape
    rows = count * per_sample
    width, outs = head_w.shape
    at = first // count

    def body(scal_ref, emb_ref, stat_ref, res_ref, w_ref, gain_ref, *refs):
        grad_refs, (out_ref, sums_ref, held) = refs[:shards], refs[shards:]
        fill_lanes(scal_ref, grad_refs, held)
        _, valid = token_sides(scal_ref, first, count, per_sample, cells)
        inv_std = stat_ref[:, 128:129]
        unit = (emb_ref[...].astype(FULL) - stat_ref[:, 0:1]) * inv_std
        direct = dot_nt(res_ref[...].reshape(rows, outs), w_ref[...]).astype(HALF).astype(FULL)
        normed_grad = held[...].astype(FULL) + direct
        gain_grad = jnp.sum(normed_grad * unit, axis=0, keepdims=True)
        unit_grad = normed_grad * gain_ref[...]
        mean_grad = jnp.mean(unit_grad, axis=-1, keepdims=True)
        mean_cross = jnp.mean(unit_grad * unit, axis=-1, keepdims=True)
        input_grad = inv_std * (unit_grad - mean_grad - unit * mean_cross)
        result = ((input_grad + direct) * valid).astype(HALF)
        out_ref[...] = result
        bias_grad = jnp.sum(result.astype(FULL), axis=0, keepdims=True)
        sums_ref[0:4] = jnp.broadcast_to(gain_grad, (4, width))
        sums_ref[4:8] = jnp.broadcast_to(bias_grad, (4, width))

    return pl.pallas_call(
        body,
        grid_spec=pltpu.PrefetchScalarGridSpec(
            num_scalar_prefetch=1,
            grid=(1,),
            in_specs=[
                pl.BlockSpec((rows, width), lambda i, s: (at, 0)),
                pl.BlockSpec((rows, 256), lambda i, s: (at, 0)),
                whole((count, per_sample, outs)),
                whole((width, outs)),
                whole((1, width)),
            ]
            + [whole(spec_grad[0].shape)] * shards,
            out_specs=[whole((rows, width)), whole((8, width))],
            scratch_shapes=[pltpu.VMEM((rows, width), HALF)],
        ),
        out_shape=[jax.ShapeDtypeStruct((rows, width), HALF), jax.ShapeDtypeStruct((8, width), FULL)],
        compiler_params=params(),
        cost_estimate=pl.CostEstimate(
            flops=2 * rows * width * outs, bytes_accessed=rows * width * 6, transcendentals=0
        ),
        name="embedded_back",
    )(scal, embedded, stats, residual, head_w, gain, *spec_grad)


def embed_grad_parts(scal, turned, grads, groups, away):
    pairs, block, tokens = turned[0].shape
    chunk_rows, width = grads[0].shape
    half = width // 2
    top = pairs // 2
    count = len(turned)
    depth = tokens * count

    def relative(unit):
        return jnp.where(unit < top, 2 * unit + away, unit - top + away * top)

    def body(scal_ref, *refs):
        turned_refs, grad_refs = refs[:count], refs[count : count + len(grads)]
        left_ref, right_ref, held = refs[count + len(grads) :]
        unit = pl.program_id(0)

        @pl.when(unit % top == 0)
        def _():
            for i, ref in enumerate(grad_refs):
                held[i * chunk_rows : (i + 1) * chunk_rows] = ref[...]

        rows = jnp.concatenate([ref[0] for ref in turned_refs], axis=1)
        total = dot(rows, held[...]).astype(HALF)

        @pl.when(unit < top)
        def _():
            left_ref[0] = total

        @pl.when(unit >= top)
        def _():
            right_ref[0] = total

    shape = (top, block, half)
    return pl.pallas_call(
        body,
        grid_spec=pltpu.PrefetchScalarGridSpec(
            num_scalar_prefetch=1,
            grid=(pairs,),
            in_specs=[
                pl.BlockSpec((1, block, tokens), lambda i, s: (jnp.bitwise_xor(s[GROUP] // 2, relative(i)), 0, 0))
                for _ in turned
            ]
            + [pl.BlockSpec((chunk_rows, half), lambda i, s: (0, i // top)) for _ in grads],
            out_specs=[
                pl.BlockSpec((1, block, half), lambda i, s: (jnp.minimum(i, top - 1), 0, 0)),
                pl.BlockSpec((1, block, half), lambda i, s: (jnp.maximum(i - top, 0), 0, 0)),
            ],
            scratch_shapes=[pltpu.VMEM((depth, half), HALF)],
        ),
        out_shape=[jax.ShapeDtypeStruct(shape, HALF)] * 2,
        compiler_params=params(),
        cost_estimate=pl.CostEstimate(
            flops=depth * pairs * block * width,
            bytes_accessed=pairs * block * (2 * depth + width) + depth * width,
            transcendentals=0,
        ),
        name="embed_grad",
    )(scal, *turned, *grads)


def swap_bit(values, bit, groups):
    return lax.ppermute(values, "grp", [(g, g ^ (1 << bit)) for g in range(groups)])


def across(pieces):
    shards = len(pieces)
    return [pieces[0]] + [
        lax.ppermute(pieces[k], "fft", [(z, z ^ k) for z in range(shards)]) for k in range(1, shards)
    ]


def add_half(left, right):
    return (left.astype(FULL) + right.astype(FULL)).astype(HALF)


def scatter_start(received, kept, groups):
    bits = groups.bit_length() - 1
    ends = []
    for first, keep, order, low in (
        (received[0], kept[0], list(range(2, bits)), True),
        (received[1], kept[1], list(range(bits - 2, 0, -1)), False),
    ):
        total = add_half(keep, first)
        for bit in order:
            count, block, width = total.shape
            if low:
                split = total.reshape(count // 2, 2, block, width)
                keep, send = split[:, 0], split[:, 1]
            else:
                split = total.reshape(2, count // 2, block, width)
                keep, send = split[0], split[1]
            total = add_half(keep, swap_bit(send, bit, groups))
        ends.append(total[0])
    return ends


def scatter_step(part, bit, shards, shard_at):
    split = part.reshape(part.shape[0] // 2, 2, *part.shape[1:])
    mine = (shard_at // bit) % 2
    keep = lax.dynamic_index_in_dim(split, mine, 1, keepdims=False)
    send = lax.dynamic_index_in_dim(split, 1 - mine, 1, keepdims=False)
    received = lax.ppermute(send, "fft", [(z, z ^ bit) for z in range(shards)])
    return keep.astype(FULL) + received.astype(FULL)


def from_same_core(values, groups):
    return [values] + [
        lax.ppermute(values, "grp", [(g, g ^ k) for g in range(groups)]) for k in range(2, groups, 2)
    ]


def hi_lo(values):
    high = values.astype(HALF)
    return jnp.concatenate([high, (values - high.astype(FULL)).astype(HALF)], axis=0)


def from_hi_lo(values):
    half = values.shape[0] // 2
    values = values.astype(FULL)
    return values[:half] + values[half:]


def one_step(body, name, operands, out_shape):
    return pl.pallas_call(
        body,
        grid_spec=pltpu.PrefetchScalarGridSpec(
            num_scalar_prefetch=1,
            grid=(1,),
            in_specs=[whole(o.shape) for o in operands[1:]],
            out_specs=[whole(o.shape) for o in out_shape],
        ),
        out_shape=out_shape,
        compiler_params=params(),
        name=name,
    )(*operands)


def packed(routes, head_grad, spec_grad, predicted, groups):
    outs = head_grad.shape[1]
    head_rows, spec_rows = head_grad.shape[0] // groups, spec_grad.shape[0] // groups
    count, per_sample, _ = predicted[0].shape

    def body(routes_ref, head_ref, spec_ref, *refs):
        pred_refs, out_ref = refs[:-1], refs[-1]
        for g in range(groups):
            out_ref[g, :head_rows] = head_ref[g * head_rows : (g + 1) * head_rows]
            out_ref[g, head_rows : head_rows + spec_rows] = spec_ref[g * spec_rows : (g + 1) * spec_rows]
            chosen = routes_ref[ROUTES + g]
            for c, ref in enumerate(pred_refs):

                @pl.when(chosen // count == c)
                def _(g=g, c=c, ref=ref, chosen=chosen):
                    out_ref[g, head_rows + spec_rows :] = ref[chosen - c * count]

    shape = (groups, head_rows + spec_rows + per_sample, outs)
    return one_step(
        body, "packed", (routes, head_grad, spec_grad, *predicted), [jax.ShapeDtypeStruct(shape, HALF)]
    )[0]


def group_sums(routes, moved, spec_bias, head_sums, row_sums, slot_count, per_sample):
    groups, rows, outs = moved.shape
    weight_rows = rows - per_sample
    own_rows = spec_bias.shape[0]
    chunks = len(head_sums)
    parts = row_sums[0].shape[1] // outs
    spare = 16 - own_rows - 2 * parts - 1

    def body(routes_ref, moved_ref, bias_ref, *refs):
        head_refs, row_refs, (out_ref, pred_ref) = refs[:chunks], refs[chunks : 2 * chunks], refs[2 * chunks :]
        total = moved_ref[0, :weight_rows].astype(FULL)
        for g in range(1, groups):
            total = total + moved_ref[g, :weight_rows].astype(FULL)
        out_ref[:weight_rows] = total.astype(HALF)
        lines = [bias_ref[...]]
        for row in (0, 4):
            line = sum(ref[row : row + 1] for ref in row_refs)
            lines += [line[:, i * outs : (i + 1) * outs] for i in range(parts)]
        lines += [sum(ref[0:1] for ref in head_refs), jnp.zeros((spare, outs), FULL)]
        out_ref[weight_rows:] = hi_lo(jnp.concatenate(lines, axis=0))
        for i in range(slot_count):
            pred_ref[i] = moved_ref[routes_ref[ROUTES + groups + i], weight_rows:]

    return one_step(
        body,
        "group_sums",
        (routes, moved, spec_bias, *head_sums, *row_sums),
        [
            jax.ShapeDtypeStruct((weight_rows + 32, outs), HALF),
            jax.ShapeDtypeStruct((slot_count, per_sample, outs), HALF),
        ],
    )


def shard_sums(routes, rows, head_rows, spec_rows, own_rows):
    shards = len(rows)
    outs = rows[0].shape[1]
    small_rows = 32

    def body(routes_ref, *refs):
        ins, out_ref = refs[:-1], refs[-1]
        total = sum(ref[:head_rows].astype(FULL) for ref in ins)
        out_ref[:head_rows] = total.astype(HALF)
        for k, ref in enumerate(ins):
            at = head_rows + k * spec_rows
            out_ref[at : at + spec_rows] = ref[head_rows : head_rows + spec_rows]
        smalls = [from_hi_lo(ref[head_rows + spec_rows :]) for ref in ins]
        lines = []
        for z in range(shards):
            here = [jnp.bitwise_xor(routes_ref[SHARD], k) == z for k in range(shards)]
            lines.append(sum(jnp.where(h, v[:own_rows], 0.0) for h, v in zip(here, smalls)))
        lines.append(sum(v[own_rows:] for v in smalls))
        have = shards * own_rows + 16 - own_rows
        lines.append(jnp.zeros((small_rows - have, outs), FULL))
        out_ref[head_rows + shards * spec_rows :] = hi_lo(jnp.concatenate(lines, axis=0))

    shape = (head_rows + shards * spec_rows + 2 * small_rows, outs)
    return one_step(body, "shard_sums", (routes, *rows), [jax.ShapeDtypeStruct(shape, HALF)])[0]


def assembled(scal, gathered, head_rows, shards, blocks, width):
    groups = len(gathered)
    total_blocks = shards * blocks
    spec_rows = 2 * blocks * width // groups
    small_at = head_rows + shards * spec_rows
    small_rows = (gathered[0].shape[0] - small_at) // 2

    def body(scal_ref, *refs):
        ins, (head_ref, spec_ref, bias_ref, gain_ref, embed_ref, out_ref) = refs[:groups], refs[groups:]
        small = None
        for k, ref in enumerate(ins):
            group = jnp.bitwise_xor(scal_ref[GROUP], k)
            at = pl.ds(pl.multiple_of(group * head_rows, head_rows), head_rows)
            head_ref[at, :] = ref[:head_rows].astype(FULL)
            start = group * spec_rows
            layer, b = start // (blocks * width), (start // width) % blocks
            rows = pl.ds(pl.multiple_of(start % width, spec_rows), spec_rows)
            for j in range(shards):
                values = ref[head_rows + j * spec_rows : head_rows + (j + 1) * spec_rows].astype(FULL)
                z = jnp.bitwise_xor(scal_ref[SHARD], j)
                spec_ref[layer, 0, z * blocks + b, rows] = values[:, :width]
                spec_ref[layer, 1, z * blocks + b, rows] = values[:, width:]
            part = ref[small_at : small_at + small_rows].astype(FULL) + ref[small_at + small_rows :].astype(FULL)
            small = part if small is None else small + part
        for z in range(shards):
            for layer in range(2):
                for b in range(blocks):
                    row = (z * 2 + layer) * blocks + b
                    for p in range(2):
                        bias_ref[layer, p, z * blocks + b : z * blocks + b + 1] = small[
                            row : row + 1, p * width : (p + 1) * width
                        ]
        row = shards * 2 * blocks
        quarter = gain_ref.shape[1] // (2 * width)
        for ref in (gain_ref, embed_ref):
            for i in range(quarter):
                ref[:, i * 2 * width : (i + 1) * 2 * width] = small[row + i : row + i + 1]
            row += quarter
        out_ref[...] = small[row : row + 1]

    out_shape = [
        jax.ShapeDtypeStruct((groups * head_rows, 2 * width), FULL),
        jax.ShapeDtypeStruct((2, 2, total_blocks, width, width), FULL),
        jax.ShapeDtypeStruct((2, 2, total_blocks, width), FULL),
        jax.ShapeDtypeStruct((1, groups * head_rows), FULL),
        jax.ShapeDtypeStruct((1, groups * head_rows), FULL),
        jax.ShapeDtypeStruct((1, 2 * width), FULL),
    ]
    return pl.pallas_call(
        body,
        grid_spec=pltpu.PrefetchScalarGridSpec(
            num_scalar_prefetch=1,
            grid=(1,),
            in_specs=[whole(gathered[0].shape)] * groups,
            out_specs=[whole(o.shape) for o in out_shape],
        ),
        out_shape=out_shape,
        compiler_params=params(),
        name="assembled",
    )(scal, *gathered)


def prediction_routes(dest_group, group_at, groups, slot_count):
    own_dest = lax.dynamic_slice_in_dim(dest_group, group_at * slot_count, slot_count)
    loaders = jnp.arange(groups, dtype=jnp.int32)
    slots = jnp.arange(slot_count, dtype=jnp.int32)
    chosen = jnp.sum(jnp.where(own_dest[None, :] == loaders[:, None], slots[None, :], 0), axis=1)
    holds = jnp.any(dest_group.reshape(groups, slot_count) == group_at, axis=1)
    rank = jnp.sum(jnp.where(holds[None, :] & (loaders[None, :] < loaders[:, None]), 1, 0), axis=1)
    sources = jnp.sum(jnp.where(holds[None, :] & (rank[None, :] == slots[:, None]), loaders[None, :], 0), axis=1)
    return jnp.concatenate([chosen, sources]).astype(jnp.int32)


def on_device(
    patches, targets, grid_side, dest_group, embed_w, embed_b, gain, spec_w, spec_b, head_w, head_b
):
    slot_count, row_count, cells, depth = patches.shape
    samples = dest_group.shape[0]
    groups = lax.axis_size("grp")
    shards = lax.axis_size("fft")
    group_at = lax.axis_index("grp").astype(jnp.int32)
    shard_at = lax.axis_index("fft").astype(jnp.int32)
    outs = targets.shape[-1]
    per_sample = row_count * cells
    count = slot_count // CHUNKS
    firsts = [c * count for c in range(CHUNKS)]
    assert slot_count == SLOTS

    sides = lax.dynamic_slice_in_dim(grid_side, group_at * slot_count, slot_count)
    level = jnp.where(sides == cells, 0, jnp.where(sides == cells // 2, 1, 2)).astype(jnp.int32)
    place = jnp.stack([shard_at, shard_at * row_count, group_at])
    scal = jnp.concatenate([place, sides, level])
    routes = jnp.concatenate([place, prediction_routes(dest_group, group_at, groups, slot_count)])
    table_values, factors = dft_tables(cells)
    table = jnp.asarray(table_values)
    flat_patches = patches.reshape(-1, depth)
    flat_targets = targets.reshape(-1, outs)
    gain_row, embed_b_row, head_b_row = gain[None], embed_b[None], head_b[None]

    embedded, normed, stats, turned_send, turned_keep, pieces = embed(
        scal, flat_patches, embed_w, embed_b_row, gain_row, firsts, count, per_sample, cells, shards, groups
    )
    moved = [across(p) for p in pieces]
    mixed, saved = [], []
    for first, values in zip(firsts, moved):
        out, rest = spectral_chunk(scal, table, factors, values, spec_w, spec_b, first)
        mixed.append(across(out))
        saved.append(rest)
    predicted, residual, updated, head_sums, gathered = [], [], [], [], []
    for first, mix in zip(firsts, mixed):
        pred, res, up, sums = head_chunk(
            scal, embedded, normed, mix, flat_targets, head_w, head_b_row, first, samples, cells
        )
        predicted.append(pred)
        residual.append(res)
        updated.append(up)
        head_sums.append(sums)
        gathered.append(across([res] * shards))
    head_grad, gathered[0] = lax.optimization_barrier((head_gradient(updated, residual), gathered[0]))
    spec_back, sums = [], None
    for first, res, rest in zip(firsts, gathered, saved):
        values, sums = spectral_back_chunk(
            scal, table, factors, res, head_w, spec_w, rest, first, sums, first == firsts[-1]
        )
        if first == firsts[-1]:
            values, turned_send = lax.optimization_barrier((values, turned_send))
        spec_back.append(across(values))
    turned = [turned_keep, swap_bit(turned_send, 0, groups)]
    spec_grad, spec_bias = sums
    width = spec_w.shape[-1]
    blocks = spec_w.shape[2] // shards
    head_rows = head_w.shape[0] // groups
    own_grads, other_grads, row_sums = [], [], []
    for first, res, back in zip(firsts, residual, spec_back):
        grad, row_sum = embedded_back_chunk(scal, embedded, stats, res, head_w, gain_row, back, first, cells)
        if first == firsts[0]:
            grad, head_grad, spec_grad = lax.optimization_barrier((grad, head_grad, spec_grad))
            weight_sums = lax.all_to_all(
                packed(routes, head_grad, spec_grad, predicted, groups), "grp", split_axis=0, concat_axis=0, tiled=True
            )
        own_grads.append(grad)
        other_grads.append(swap_bit(grad, 0, groups))
        row_sums.append(row_sum)
    grads = own_grads + other_grads
    grads, weight_sums = lax.optimization_barrier((grads, weight_sums))
    sent = embed_grad_parts(scal, turned, grads, groups, 1)
    sent, kept_turned = lax.optimization_barrier((sent, turned))
    top_bit = groups.bit_length() - 2
    received = [swap_bit(sent[0], 1, groups), swap_bit(sent[1], top_bit, groups)]
    kept = embed_grad_parts(scal, kept_turned, grads, groups, 0)
    kept, weight_sums = lax.optimization_barrier((kept, weight_sums))
    ends = scatter_start(received, kept, groups)
    small, predictions = group_sums(routes, weight_sums, spec_bias, head_sums, row_sums, slot_count, per_sample)
    predictions = predictions.reshape(targets.shape)
    spec_rows = spec_grad.shape[0] // groups
    outgoing = shard_sums(routes, across([small] * shards), head_rows, spec_rows, spec_bias.shape[0])
    ends, outgoing = lax.optimization_barrier((ends, outgoing))
    part = jnp.concatenate(ends, axis=-1)
    part = part.reshape(shards, part.shape[0] // shards, -1)
    part = scatter_step(part, 1, shards, shard_at)
    even = from_same_core(outgoing, groups)
    bit = 2
    while bit < shards:
        part = part.astype(HALF)
        if bit == 2:
            _, even = lax.optimization_barrier((part, even))
        part = scatter_step(part, bit, shards, shard_at)
        bit *= 2
    embed_grad = part[0]
    gathered = [v for pair in zip(even, [swap_bit(v, 0, groups) for v in even]) for v in pair]
    head_grad, spec_w_grad, spec_b_grad, gain_grad, embed_bias_grad, head_bias_grad = assembled(
        scal, gathered, head_rows, shards, blocks, width
    )
    gain_grad, embed_bias_grad, head_bias_grad = gain_grad[0], embed_bias_grad[0], head_bias_grad[0]
    return (
        predictions,
        embed_grad,
        embed_bias_grad,
        gain_grad,
        spec_w_grad,
        spec_b_grad,
        head_grad,
        head_bias_grad,
    )


def solution(mesh):
    return jax.shard_map(
        on_device,
        mesh=mesh,
        in_specs=(
            P("grp", "fft", None, None),
            P("grp", "fft", None, None),
            P(),
            P(),
            P(),
            P(),
            P(),
            P(),
            P(),
            P(),
            P(),
        ),
        out_specs=(
            P("grp", "fft", None, None),
            P(("grp", "fft"), None),
            P(),
            P(),
            P(),
            P(),
            P(),
            P(),
        ),
        check_vma=False,
    )
```

```python
import jax
import jax.numpy as jnp
import ml_dtypes
import numpy as np
from jax import lax
from jax.experimental import pallas as pl
from jax.experimental.pallas import tpu as pltpu
from jax.sharding import PartitionSpec as P

EPSILON = 1e-05
SHRINK = 0.01
CHUNKS = 2
VMEM_BYTES = 24 * 1024 * 1024
SLOTS = 6
SHARD, FIRST_ROW, GROUP, SIDES = 0, 1, 2, 3
ROUTES = 3
HALF = jnp.bfloat16
FULL = jnp.float32


def dft_tables(cells):
    levels, factors = [], []
    for side, scale in ((cells, 1.1305), (cells // 2, 1.8633), (cells // 4, 1.0)):
        k = np.arange(cells)
        inside = (k < side).astype(np.float64)
        keep = inside[:, None] * inside[None, :]
        angle = 2.0 * np.pi * ((k[:, None] * k[None, :]) % side) / side
        one = np.exp(-1j * angle) * keep / np.sqrt(side)
        two = np.kron(one, one)
        table = np.concatenate([two.real, two.imag], axis=0)
        table[np.abs(table) < 1e-12] = 0.0
        rounded = (table * scale).astype(np.float32).astype(ml_dtypes.bfloat16)
        held = rounded.astype(np.float64)
        factors.append(float(np.sum(table * table) / np.sum(table * held)))
        levels.append(rounded)
    return np.stack(levels), factors


def dot(left, right):
    return jnp.dot(left, right, preferred_element_type=FULL)


def dot_tn(left, right):
    return lax.dot_general(left, right, (((0,), (0,)), ((), ())), preferred_element_type=FULL)


def dot_nt(left, right):
    return lax.dot_general(left, right, (((1,), (1,)), ((), ())), preferred_element_type=FULL)


def params(limit=VMEM_BYTES):
    return pltpu.CompilerParams(vmem_limit_bytes=limit)


def token_sides(scal_ref, first, count, per_sample, cells):
    token = lax.broadcasted_iota(jnp.int32, (count * per_sample, 1), 0)
    sample = token // per_sample
    side = jnp.zeros_like(token)
    for i in range(count):
        side = jnp.where(sample == i, scal_ref[SIDES + first + i], side)
    row = scal_ref[FIRST_ROW] + (token % per_sample) // cells
    col = token % cells
    valid = jnp.where((row < side) & (col < side), 1.0, 0.0).astype(FULL)
    return side, valid


def whole(shape):
    return pl.BlockSpec(tuple(shape), lambda i, s: (0,) * len(shape))


def part_of(scal_ref, k, size):
    at = jnp.bitwise_xor(scal_ref[SHARD], k)
    return pl.ds(pl.multiple_of(at * size, size), size)


def fill_lanes(scal_ref, refs, held):
    share = refs[0].shape[-1]
    for k, ref in enumerate(refs):
        held[:, part_of(scal_ref, k, share)] = ref[...].reshape(held.shape[0], share)


def fill_rows(scal_ref, refs, held):
    rows = refs[0].shape[1]
    for k, ref in enumerate(refs):
        held[:, part_of(scal_ref, k, rows), :] = ref[...]


def split_lanes(scal_ref, held, refs):
    share = refs[0].shape[-1]
    for k, ref in enumerate(refs):
        ref[...] = held[:, part_of(scal_ref, k, share)].reshape(ref.shape)


def split_rows(scal_ref, held, refs):
    rows = refs[0].shape[1]
    for k, ref in enumerate(refs):
        ref[...] = held[:, part_of(scal_ref, k, rows), :]


def embed(scal, patches, embed_w, embed_b, gain, firsts, count, per_sample, cells, shards, groups):
    rows, depth = patches.shape
    block = depth // groups
    width = embed_w.shape[1]
    share = width // shards
    chunk_rows = count * per_sample
    chunks = len(firsts)
    steps = 4
    tile = depth // steps

    def body(scal_ref, x_ref, w_ref, b_ref, gain_ref, emb_ref, norm_ref, stat_ref, *refs):
        (send_ref, keep_ref), outs, acc = refs[:2], refs[2:-1], refs[-1]
        step = pl.program_id(0)
        turned = x_ref[...].T
        for i in range(tile // block):
            values = turned[i * block : (i + 1) * block]
            away = (scal_ref[GROUP] + i) % 2

            @pl.when(away == 1)
            def _(i=i, values=values):
                send_ref[i // 2] = values

            @pl.when(away == 0)
            def _(i=i, values=values):
                keep_ref[i // 2] = values

        part = dot(x_ref[...], w_ref[...])

        @pl.when(step == 0)
        def _():
            acc[...] = part

        @pl.when(step > 0)
        def _():
            acc[...] += part

        @pl.when(step == steps - 1)
        def _():
            for c, first in enumerate(firsts):
                at = slice(c * chunk_rows, (c + 1) * chunk_rows)
                _, valid = token_sides(scal_ref, first, count, per_sample, cells)
                embedded = ((acc[at] + b_ref[...]) * valid).astype(HALF)
                emb_ref[at] = embedded
                values = embedded.astype(FULL)
                mean = jnp.mean(values, axis=-1, keepdims=True)
                centered = values - mean
                inv_std = lax.rsqrt(jnp.mean(centered * centered, axis=-1, keepdims=True) + EPSILON)
                norm_ref[at] = (centered * inv_std * gain_ref[...]).astype(HALF)
                stat_ref[at, :128] = jnp.broadcast_to(mean, (chunk_rows, 128))
                stat_ref[at, 128:] = jnp.broadcast_to(inv_std, (chunk_rows, 128))
                for k in range(shards):
                    piece = norm_ref[at, part_of(scal_ref, k, share)]
                    outs[c * shards + k][...] = piece.reshape(count, per_sample, share)

    piece = (count, per_sample, share)
    turned_spec = pl.BlockSpec((tile // (2 * block), block, rows), lambda k, s: (k, 0, 0))
    turned_shape = jax.ShapeDtypeStruct((groups // 2, block, rows), HALF)
    emb, normed, stats, send, keep, *pieces = pl.pallas_call(
        body,
        grid_spec=pltpu.PrefetchScalarGridSpec(
            num_scalar_prefetch=1,
            grid=(steps,),
            in_specs=[
                pl.BlockSpec((rows, tile), lambda k, s: (0, k)),
                pl.BlockSpec((tile, width), lambda k, s: (k, 0)),
                whole((1, width)),
                whole((1, width)),
            ],
            out_specs=[whole((rows, width)), whole((rows, width)), whole((rows, 256)), turned_spec, turned_spec]
            + [whole(piece)] * (shards * chunks),
            scratch_shapes=[pltpu.VMEM((rows, width), FULL)],
        ),
        out_shape=[
            jax.ShapeDtypeStruct((rows, width), HALF),
            jax.ShapeDtypeStruct((rows, width), HALF),
            jax.ShapeDtypeStruct((rows, 256), FULL),
            turned_shape,
            turned_shape,
        ]
        + [jax.ShapeDtypeStruct(piece, HALF)] * (shards * chunks),
        compiler_params=params(60 * 1024 * 1024),
        cost_estimate=pl.CostEstimate(
            flops=2 * rows * depth * width, bytes_accessed=2 * depth * (rows + width), transcendentals=0
        ),
        name="embed",
    )(scal, patches, embed_w, embed_b, gain)
    return emb, normed, stats, send, keep, [pieces[c * shards : (c + 1) * shards] for c in range(chunks)]


def to_blocks(values, blocks, width):
    half = values.shape[0] // 2
    return [
        jnp.concatenate(
            [values[:half, b * width : (b + 1) * width], values[half:, b * width : (b + 1) * width]], axis=1
        )
        for b in range(blocks)
    ]


def from_blocks(parts, width):
    real = jnp.concatenate([p[:, :width] for p in parts], axis=1)
    imag = jnp.concatenate([p[:, width:] for p in parts], axis=1)
    return real, imag


def table_factor(level, factors):
    return jnp.where(level == 0, factors[0], jnp.where(level == 1, factors[1], factors[2])).astype(FULL)


def table_back(table_ref, level, tops, rests, factor):
    size = table_ref.shape[2]
    total = None
    for at, (top, rest) in enumerate(zip(tops, rests)):
        table = table_ref[level, at * size : (at + 1) * size]
        part = dot(table, top) + dot(table, rest)
        total = part if total is None else total + part
    return total * factor


def two_terms(values):
    top = values.astype(HALF)
    return top, (values - top.astype(FULL)).astype(HALF)


def complex_weights(w_ref, held, blocks, width):
    for layer in range(2):
        for b in range(blocks):
            real, imag = w_ref[layer, 0, b], w_ref[layer, 1, b]
            held[layer, b, :width, :width] = real
            held[layer, b, :width, width:] = imag
            held[layer, b, width:, :width] = -imag
            held[layer, b, width:, width:] = real


def spectral_chunk(scal, table, factors, pieces, spec_w, spec_b, first):
    shards = len(pieces)
    count, per_sample, share = pieces[0].shape
    size = shards * per_sample
    width = spec_w.shape[-1]
    blocks = share // width
    wide = 2 * width

    def body(scal_ref, t_ref, w_ref, b_ref, *refs):
        ins, outs = refs[:shards], refs[shards : 2 * shards]
        spec_ref, hid_ref, fil_ref, weights, held = refs[2 * shards :]

        def bias(layer, b):
            row = pl.ds(scal_ref[SHARD] * blocks + b, 1)
            return jnp.concatenate([b_ref[layer, 0, row], b_ref[layer, 1, row]], axis=1)

        complex_weights(w_ref, weights, blocks, width)
        fill_rows(scal_ref, ins, held)
        levels = [scal_ref[SIDES + SLOTS + first + i] for i in range(count)]
        for i, level in enumerate(levels):
            spectrum = (dot(t_ref[level], held[i]) * table_factor(level, factors)).astype(HALF)
            for b, entry in enumerate(to_blocks(spectrum, blocks, width)):
                spec_ref[b, i * size : (i + 1) * size] = entry
        kept = []
        for b in range(blocks):
            pre_one = dot(spec_ref[b], weights[0, b]) + bias(0, b)
            hidden = jnp.maximum(pre_one, 0.0).astype(HALF)
            hid_ref[b] = hidden
            pre_two = dot(hidden, weights[1, b]) + bias(1, b)
            filtered = jnp.where(
                pre_two > SHRINK, pre_two - SHRINK, jnp.where(pre_two < -SHRINK, pre_two + SHRINK, 0.0)
            )
            top, rest = two_terms(filtered)
            fil_ref[b] = top
            kept.append((top, rest))
        for i, level in enumerate(levels):
            at = slice(i * size, (i + 1) * size)
            tops = from_blocks([top[at] for top, _ in kept], width)
            rests = from_blocks([rest[at] for _, rest in kept], width)
            held[i] = table_back(t_ref, level, tops, rests, table_factor(level, factors)).astype(HALF)
        split_rows(scal_ref, held, outs)

    saved = (blocks, count * size, wide)
    outs = pl.pallas_call(
        body,
        grid_spec=pltpu.PrefetchScalarGridSpec(
            num_scalar_prefetch=1,
            grid=(1,),
            in_specs=[
                whole(table.shape),
                pl.BlockSpec((2, 2, blocks, width, width), lambda i, s: (0, 0, s[SHARD], 0, 0)),
                whole(spec_b.shape),
            ]
            + [whole(pieces[0].shape)] * shards,
            out_specs=[whole(pieces[0].shape)] * shards + [whole(saved)] * 3,
            scratch_shapes=[pltpu.VMEM((2, blocks, wide, wide), HALF), pltpu.VMEM((count, size, share), HALF)],
        ),
        out_shape=[jax.ShapeDtypeStruct(pieces[0].shape, HALF)] * shards + [jax.ShapeDtypeStruct(saved, HALF)] * 3,
        compiler_params=params(),
        cost_estimate=pl.CostEstimate(
            flops=count * size * share * size * 14, bytes_accessed=count * size * share * 16, transcendentals=0
        ),
        name="spectral",
    )(scal, table, spec_w, spec_b, *pieces)
    return outs[:shards], outs[shards:]


def head_chunk(scal, embedded, normed, mixed, targets, head_w, head_b, first, samples, cells):
    shards = len(mixed)
    count, per_sample, share = mixed[0].shape
    rows = count * per_sample
    width, outs = head_w.shape
    at = first // count
    scale_root = float(np.sqrt(np.float32(samples)))

    def body(scal_ref, emb_ref, norm_ref, tgt_ref, w_ref, b_ref, *refs):
        mix_refs, (pred_ref, res_ref, up_ref, bias_ref, held) = refs[:shards], refs[shards:]
        fill_lanes(scal_ref, mix_refs, held)
        side, valid = token_sides(scal_ref, first, count, per_sample, cells)
        updated = (emb_ref[...].astype(FULL) + norm_ref[...].astype(FULL) + held[...].astype(FULL)).astype(HALF)
        output = (dot(updated, w_ref[...]) + b_ref[...]) * valid
        pred_ref[...] = output.astype(HALF).reshape(pred_ref.shape)
        scale = 2.0 / (side.astype(FULL) * scale_root)
        residual = (scale * valid * (output - tgt_ref[...].astype(FULL))).astype(HALF)
        res_ref[...] = residual.reshape(res_ref.shape)
        up_ref[...] = updated
        total = jnp.sum(residual.astype(FULL), axis=0, keepdims=True)
        bias_ref[...] = jnp.broadcast_to(total, bias_ref.shape)

    token_shape = (count, per_sample, outs)
    return pl.pallas_call(
        body,
        grid_spec=pltpu.PrefetchScalarGridSpec(
            num_scalar_prefetch=1,
            grid=(1,),
            in_specs=[
                pl.BlockSpec((rows, width), lambda i, s: (at, 0)),
                pl.BlockSpec((rows, width), lambda i, s: (at, 0)),
                pl.BlockSpec((rows, outs), lambda i, s: (at, 0)),
                whole((width, outs)),
                whole((1, outs)),
            ]
            + [whole(mixed[0].shape)] * shards,
            out_specs=[whole(token_shape), whole(token_shape), whole((rows, width)), whole((8, outs))],
            scratch_shapes=[pltpu.VMEM((rows, width), HALF)],
        ),
        out_shape=[
            jax.ShapeDtypeStruct(token_shape, HALF),
            jax.ShapeDtypeStruct(token_shape, HALF),
            jax.ShapeDtypeStruct((rows, width), HALF),
            jax.ShapeDtypeStruct((8, outs), FULL),
        ],
        compiler_params=params(),
        cost_estimate=pl.CostEstimate(
            flops=2 * rows * width * outs, bytes_accessed=rows * width * 4 + width * outs * 6, transcendentals=0
        ),
        name="head",
    )(scal, embedded, normed, targets, head_w, head_b, *mixed)


def head_gradient(updated, residual):
    width = updated[0].shape[1]
    outs = residual[0].shape[-1]
    count = len(updated)

    def body(*refs):
        total = None
        for up_ref, res_ref in zip(refs[:count], refs[count : 2 * count]):
            part = dot_tn(up_ref[...], res_ref[...].reshape(up_ref.shape[0], outs))
            total = part if total is None else total + part
        refs[-1][...] = total.astype(HALF)

    return pl.pallas_call(
        body,
        out_shape=jax.ShapeDtypeStruct((width, outs), HALF),
        compiler_params=params(),
        cost_estimate=pl.CostEstimate(
            flops=2 * count * updated[0].size * outs, bytes_accessed=2 * count * updated[0].size, transcendentals=0
        ),
        name="head_gradient",
    )(*updated, *residual)


def spectral_back_chunk(scal, table, factors, residual, head_w, spec_w, saved, first, before, last):
    shards = len(residual)
    count, per_sample, outs = residual[0].shape
    size = shards * per_sample
    width = spec_w.shape[-1]
    wide = 2 * width
    share = head_w.shape[0] // shards
    blocks = share // width
    raw_shape = (2, blocks, wide, wide)
    bias_shape = (2 * blocks, wide)
    has_before = before is not None

    def body(scal_ref, t_ref, h_ref, w_ref, spec_ref, hid_ref, fil_ref, *refs):
        ins, refs = refs[:shards], refs[shards:]
        if has_before:
            (old_ref, old_bias_ref), refs = refs[:2], refs[2:]
        pieces, (grad_ref, bias_ref, weights, held, gathered) = refs[:shards], refs[shards:]

        def weight_sums(layer, b, inputs, grads):
            raw = dot_tn(inputs, grads)
            sums = jnp.sum(grads.astype(FULL), axis=0, keepdims=True)
            at = layer * blocks + b
            if has_before:
                raw = raw + old_ref[layer, b]
                sums = sums + old_bias_ref[at : at + 1]
            bias_ref[at : at + 1] = sums
            if not last:
                grad_ref[layer, b] = raw
                return
            real = raw[:width, :width] + raw[width:, width:]
            imag = raw[:width, width:] - raw[width:, :width]
            grad_ref[at * width : (at + 1) * width] = jnp.concatenate([real, imag], axis=1).astype(HALF)

        complex_weights(w_ref, weights, blocks, width)
        fill_rows(scal_ref, ins, gathered)
        levels = [scal_ref[SIDES + SLOTS + first + i] for i in range(count)]
        updated_grad = dot_nt(gathered[...].reshape(count * size, outs), h_ref[...]).astype(HALF)
        entries = []
        for i, level in enumerate(levels):
            filtered_grad = dot(t_ref[level], updated_grad[i * size : (i + 1) * size]) * table_factor(level, factors)
            entries.append(to_blocks(filtered_grad, blocks, width))
        kept = []
        for b in range(blocks):
            entry = jnp.concatenate([e[b] for e in entries], axis=0)
            two_grad = jnp.where(fil_ref[b].astype(FULL) != 0.0, entry, 0.0).astype(HALF)
            hidden = hid_ref[b]
            hidden_grad = dot_nt(two_grad, weights[1, b])
            one_grad = jnp.where(hidden.astype(FULL) > 0.0, hidden_grad, 0.0).astype(HALF)
            kept.append(two_terms(dot_nt(one_grad, weights[0, b])))
            weight_sums(1, b, hidden, two_grad)
            weight_sums(0, b, spec_ref[b], one_grad)
        for i, level in enumerate(levels):
            at = slice(i * size, (i + 1) * size)
            tops = from_blocks([top[at] for top, _ in kept], width)
            rests = from_blocks([rest[at] for _, rest in kept], width)
            held[i] = table_back(t_ref, level, tops, rests, table_factor(level, factors)).astype(HALF)
        split_rows(scal_ref, held, pieces)

    piece = (count, per_sample, share)
    if last:
        grad_out = jax.ShapeDtypeStruct((2 * blocks * width, wide), HALF)
    else:
        grad_out = jax.ShapeDtypeStruct(raw_shape, FULL)
    result = pl.pallas_call(
        body,
        grid_spec=pltpu.PrefetchScalarGridSpec(
            num_scalar_prefetch=1,
            grid=(1,),
            in_specs=[
                whole(table.shape),
                pl.BlockSpec((share, outs), lambda i, s: (s[SHARD], 0)),
                pl.BlockSpec((2, 2, blocks, width, width), lambda i, s: (0, 0, s[SHARD], 0, 0)),
            ]
            + [whole(saved[0].shape)] * 3
            + [whole(residual[0].shape)] * shards
            + ([whole(raw_shape), whole(bias_shape)] if has_before else []),
            out_specs=[whole(piece)] * shards + [whole(grad_out.shape), whole(bias_shape)],
            scratch_shapes=[
                pltpu.VMEM((2, blocks, wide, wide), HALF),
                pltpu.VMEM((count, size, share), HALF),
                pltpu.VMEM((count, size, outs), HALF),
            ],
        ),
        out_shape=[jax.ShapeDtypeStruct(piece, HALF)] * shards
        + [grad_out, jax.ShapeDtypeStruct(bias_shape, FULL)],
        compiler_params=params(),
        cost_estimate=pl.CostEstimate(
            flops=count * size * share * size * 20, bytes_accessed=count * size * share * 16, transcendentals=0
        ),
        name="spectral_back",
    )(scal, table, head_w, spec_w, *saved, *residual, *(before or ()))
    return result[:shards], result[shards:]


def embedded_back_chunk(scal, embedded, stats, residual, head_w, gain, spec_grad, first, cells):
    shards = len(spec_grad)
    count, per_sample, share = spec_grad[0].shape
    rows = count * per_sample
    width, outs = head_w.shape
    at = first // count

    def body(scal_ref, emb_ref, stat_ref, res_ref, w_ref, gain_ref, *refs):
        grad_refs, (out_ref, sums_ref, held) = refs[:shards], refs[shards:]
        fill_lanes(scal_ref, grad_refs, held)
        _, valid = token_sides(scal_ref, first, count, per_sample, cells)
        inv_std = stat_ref[:, 128:129]
        unit = (emb_ref[...].astype(FULL) - stat_ref[:, 0:1]) * inv_std
        direct = dot_nt(res_ref[...].reshape(rows, outs), w_ref[...]).astype(HALF).astype(FULL)
        normed_grad = held[...].astype(FULL) + direct
        gain_grad = jnp.sum(normed_grad * unit, axis=0, keepdims=True)
        unit_grad = normed_grad * gain_ref[...]
        mean_grad = jnp.mean(unit_grad, axis=-1, keepdims=True)
        mean_cross = jnp.mean(unit_grad * unit, axis=-1, keepdims=True)
        input_grad = inv_std * (unit_grad - mean_grad - unit * mean_cross)
        result = ((input_grad + direct) * valid).astype(HALF)
        out_ref[...] = result
        bias_grad = jnp.sum(result.astype(FULL), axis=0, keepdims=True)
        sums_ref[0:4] = jnp.broadcast_to(gain_grad, (4, width))
        sums_ref[4:8] = jnp.broadcast_to(bias_grad, (4, width))

    return pl.pallas_call(
        body,
        grid_spec=pltpu.PrefetchScalarGridSpec(
            num_scalar_prefetch=1,
            grid=(1,),
            in_specs=[
                pl.BlockSpec((rows, width), lambda i, s: (at, 0)),
                pl.BlockSpec((rows, 256), lambda i, s: (at, 0)),
                whole((count, per_sample, outs)),
                whole((width, outs)),
                whole((1, width)),
            ]
            + [whole(spec_grad[0].shape)] * shards,
            out_specs=[whole((rows, width)), whole((8, width))],
            scratch_shapes=[pltpu.VMEM((rows, width), HALF)],
        ),
        out_shape=[jax.ShapeDtypeStruct((rows, width), HALF), jax.ShapeDtypeStruct((8, width), FULL)],
        compiler_params=params(),
        cost_estimate=pl.CostEstimate(
            flops=2 * rows * width * outs, bytes_accessed=rows * width * 6, transcendentals=0
        ),
        name="embedded_back",
    )(scal, embedded, stats, residual, head_w, gain, *spec_grad)


def embed_grad_parts(scal, turned, grads, groups, away):
    pairs, block, tokens = turned[0].shape
    chunk_rows, width = grads[0].shape
    half = width // 2
    top = pairs // 2
    count = len(turned)
    depth = tokens * count

    def relative(unit):
        return jnp.where(unit < top, 2 * unit + away, unit - top + away * top)

    def body(scal_ref, *refs):
        turned_refs, grad_refs = refs[:count], refs[count : count + len(grads)]
        left_ref, right_ref, held = refs[count + len(grads) :]
        unit = pl.program_id(0)

        @pl.when(unit % top == 0)
        def _():
            for i, ref in enumerate(grad_refs):
                held[i * chunk_rows : (i + 1) * chunk_rows] = ref[...]

        rows = jnp.concatenate([ref[0] for ref in turned_refs], axis=1)
        total = dot(rows, held[...]).astype(HALF)

        @pl.when(unit < top)
        def _():
            left_ref[0] = total

        @pl.when(unit >= top)
        def _():
            right_ref[0] = total

    shape = (top, block, half)
    return pl.pallas_call(
        body,
        grid_spec=pltpu.PrefetchScalarGridSpec(
            num_scalar_prefetch=1,
            grid=(pairs,),
            in_specs=[
                pl.BlockSpec((1, block, tokens), lambda i, s: (jnp.bitwise_xor(s[GROUP] // 2, relative(i)), 0, 0))
                for _ in turned
            ]
            + [pl.BlockSpec((chunk_rows, half), lambda i, s: (0, i // top)) for _ in grads],
            out_specs=[
                pl.BlockSpec((1, block, half), lambda i, s: (jnp.minimum(i, top - 1), 0, 0)),
                pl.BlockSpec((1, block, half), lambda i, s: (jnp.maximum(i - top, 0), 0, 0)),
            ],
            scratch_shapes=[pltpu.VMEM((depth, half), HALF)],
        ),
        out_shape=[jax.ShapeDtypeStruct(shape, HALF)] * 2,
        compiler_params=params(),
        cost_estimate=pl.CostEstimate(
            flops=depth * pairs * block * width,
            bytes_accessed=pairs * block * (2 * depth + width) + depth * width,
            transcendentals=0,
        ),
        name="embed_grad",
    )(scal, *turned, *grads)


def swap_bit(values, bit, groups):
    return lax.ppermute(values, "grp", [(g, g ^ (1 << bit)) for g in range(groups)])


def across(pieces):
    shards = len(pieces)
    return [pieces[0]] + [
        lax.ppermute(pieces[k], "fft", [(z, z ^ k) for z in range(shards)]) for k in range(1, shards)
    ]


def add_half(left, right):
    return (left.astype(FULL) + right.astype(FULL)).astype(HALF)


def scatter_start(received, kept, groups):
    bits = groups.bit_length() - 1
    ends = []
    for first, keep, order, low in (
        (received[0], kept[0], list(range(2, bits)), True),
        (received[1], kept[1], list(range(bits - 2, 0, -1)), False),
    ):
        total = add_half(keep, first)
        for bit in order:
            count, block, width = total.shape
            if low:
                split = total.reshape(count // 2, 2, block, width)
                keep, send = split[:, 0], split[:, 1]
            else:
                split = total.reshape(2, count // 2, block, width)
                keep, send = split[0], split[1]
            total = add_half(keep, swap_bit(send, bit, groups))
        ends.append(total[0])
    return ends


def scatter_step(part, bit, shards, shard_at):
    split = part.reshape(part.shape[0] // 2, 2, *part.shape[1:])
    mine = (shard_at // bit) % 2
    keep = lax.dynamic_index_in_dim(split, mine, 1, keepdims=False)
    send = lax.dynamic_index_in_dim(split, 1 - mine, 1, keepdims=False)
    received = lax.ppermute(send, "fft", [(z, z ^ bit) for z in range(shards)])
    return keep.astype(FULL) + received.astype(FULL)


def from_same_core(values, groups):
    return [values] + [
        lax.ppermute(values, "grp", [(g, g ^ k) for g in range(groups)]) for k in range(2, groups, 2)
    ]


def hi_lo(values):
    high = values.astype(HALF)
    return jnp.concatenate([high, (values - high.astype(FULL)).astype(HALF)], axis=0)


def from_hi_lo(values):
    half = values.shape[0] // 2
    values = values.astype(FULL)
    return values[:half] + values[half:]


def one_step(body, name, operands, out_shape):
    return pl.pallas_call(
        body,
        grid_spec=pltpu.PrefetchScalarGridSpec(
            num_scalar_prefetch=1,
            grid=(1,),
            in_specs=[whole(o.shape) for o in operands[1:]],
            out_specs=[whole(o.shape) for o in out_shape],
        ),
        out_shape=out_shape,
        compiler_params=params(),
        name=name,
    )(*operands)


def packed(routes, head_grad, spec_grad, predicted, groups):
    outs = head_grad.shape[1]
    head_rows, spec_rows = head_grad.shape[0] // groups, spec_grad.shape[0] // groups
    count, per_sample, _ = predicted[0].shape

    def body(routes_ref, head_ref, spec_ref, *refs):
        pred_refs, out_ref = refs[:-1], refs[-1]
        for g in range(groups):
            out_ref[g, :head_rows] = head_ref[g * head_rows : (g + 1) * head_rows]
            out_ref[g, head_rows : head_rows + spec_rows] = spec_ref[g * spec_rows : (g + 1) * spec_rows]
            chosen = routes_ref[ROUTES + g]
            for c, ref in enumerate(pred_refs):

                @pl.when(chosen // count == c)
                def _(g=g, c=c, ref=ref, chosen=chosen):
                    out_ref[g, head_rows + spec_rows :] = ref[chosen - c * count]

    shape = (groups, head_rows + spec_rows + per_sample, outs)
    return one_step(
        body, "packed", (routes, head_grad, spec_grad, *predicted), [jax.ShapeDtypeStruct(shape, HALF)]
    )[0]


def group_sums(routes, moved, spec_bias, head_sums, row_sums, slot_count, per_sample):
    groups, rows, outs = moved.shape
    weight_rows = rows - per_sample
    own_rows = spec_bias.shape[0]
    chunks = len(head_sums)
    parts = row_sums[0].shape[1] // outs
    spare = 16 - own_rows - 2 * parts - 1

    def body(routes_ref, moved_ref, bias_ref, *refs):
        head_refs, row_refs, (out_ref, pred_ref) = refs[:chunks], refs[chunks : 2 * chunks], refs[2 * chunks :]
        total = moved_ref[0, :weight_rows].astype(FULL)
        for g in range(1, groups):
            total = total + moved_ref[g, :weight_rows].astype(FULL)
        out_ref[:weight_rows] = total.astype(HALF)
        lines = [bias_ref[...]]
        for row in (0, 4):
            line = sum(ref[row : row + 1] for ref in row_refs)
            lines += [line[:, i * outs : (i + 1) * outs] for i in range(parts)]
        lines += [sum(ref[0:1] for ref in head_refs), jnp.zeros((spare, outs), FULL)]
        out_ref[weight_rows:] = hi_lo(jnp.concatenate(lines, axis=0))
        for i in range(slot_count):
            pred_ref[i] = moved_ref[routes_ref[ROUTES + groups + i], weight_rows:]

    return one_step(
        body,
        "group_sums",
        (routes, moved, spec_bias, *head_sums, *row_sums),
        [
            jax.ShapeDtypeStruct((weight_rows + 32, outs), HALF),
            jax.ShapeDtypeStruct((slot_count, per_sample, outs), HALF),
        ],
    )


def shard_sums(routes, rows, head_rows, spec_rows, own_rows):
    shards = len(rows)
    outs = rows[0].shape[1]
    small_rows = 32

    def body(routes_ref, *refs):
        ins, out_ref = refs[:-1], refs[-1]
        total = sum(ref[:head_rows].astype(FULL) for ref in ins)
        out_ref[:head_rows] = total.astype(HALF)
        for k, ref in enumerate(ins):
            at = head_rows + k * spec_rows
            out_ref[at : at + spec_rows] = ref[head_rows : head_rows + spec_rows]
        smalls = [from_hi_lo(ref[head_rows + spec_rows :]) for ref in ins]
        lines = []
        for z in range(shards):
            here = [jnp.bitwise_xor(routes_ref[SHARD], k) == z for k in range(shards)]
            lines.append(sum(jnp.where(h, v[:own_rows], 0.0) for h, v in zip(here, smalls)))
        lines.append(sum(v[own_rows:] for v in smalls))
        have = shards * own_rows + 16 - own_rows
        lines.append(jnp.zeros((small_rows - have, outs), FULL))
        out_ref[head_rows + shards * spec_rows :] = hi_lo(jnp.concatenate(lines, axis=0))

    shape = (head_rows + shards * spec_rows + 2 * small_rows, outs)
    return one_step(body, "shard_sums", (routes, *rows), [jax.ShapeDtypeStruct(shape, HALF)])[0]


def assembled(scal, gathered, head_rows, shards, blocks, width):
    groups = len(gathered)
    total_blocks = shards * blocks
    spec_rows = 2 * blocks * width // groups
    small_at = head_rows + shards * spec_rows
    small_rows = (gathered[0].shape[0] - small_at) // 2

    def body(scal_ref, *refs):
        ins, (head_ref, spec_ref, bias_ref, gain_ref, embed_ref, out_ref) = refs[:groups], refs[groups:]
        small = None
        for k, ref in enumerate(ins):
            group = jnp.bitwise_xor(scal_ref[GROUP], k)
            at = pl.ds(pl.multiple_of(group * head_rows, head_rows), head_rows)
            head_ref[at, :] = ref[:head_rows].astype(FULL)
            start = group * spec_rows
            layer, b = start // (blocks * width), (start // width) % blocks
            rows = pl.ds(pl.multiple_of(start % width, spec_rows), spec_rows)
            for j in range(shards):
                values = ref[head_rows + j * spec_rows : head_rows + (j + 1) * spec_rows].astype(FULL)
                z = jnp.bitwise_xor(scal_ref[SHARD], j)
                spec_ref[layer, 0, z * blocks + b, rows] = values[:, :width]
                spec_ref[layer, 1, z * blocks + b, rows] = values[:, width:]
            part = ref[small_at : small_at + small_rows].astype(FULL) + ref[small_at + small_rows :].astype(FULL)
            small = part if small is None else small + part
        for z in range(shards):
            for layer in range(2):
                for b in range(blocks):
                    row = (z * 2 + layer) * blocks + b
                    for p in range(2):
                        bias_ref[layer, p, z * blocks + b : z * blocks + b + 1] = small[
                            row : row + 1, p * width : (p + 1) * width
                        ]
        row = shards * 2 * blocks
        quarter = gain_ref.shape[1] // (2 * width)
        for ref in (gain_ref, embed_ref):
            for i in range(quarter):
                ref[:, i * 2 * width : (i + 1) * 2 * width] = small[row + i : row + i + 1]
            row += quarter
        out_ref[...] = small[row : row + 1]

    out_shape = [
        jax.ShapeDtypeStruct((groups * head_rows, 2 * width), FULL),
        jax.ShapeDtypeStruct((2, 2, total_blocks, width, width), FULL),
        jax.ShapeDtypeStruct((2, 2, total_blocks, width), FULL),
        jax.ShapeDtypeStruct((1, groups * head_rows), FULL),
        jax.ShapeDtypeStruct((1, groups * head_rows), FULL),
        jax.ShapeDtypeStruct((1, 2 * width), FULL),
    ]
    return pl.pallas_call(
        body,
        grid_spec=pltpu.PrefetchScalarGridSpec(
            num_scalar_prefetch=1,
            grid=(1,),
            in_specs=[whole(gathered[0].shape)] * groups,
            out_specs=[whole(o.shape) for o in out_shape],
        ),
        out_shape=out_shape,
        compiler_params=params(),
        name="assembled",
    )(scal, *gathered)


def prediction_routes(dest_group, group_at, groups, slot_count):
    own_dest = lax.dynamic_slice_in_dim(dest_group, group_at * slot_count, slot_count)
    loaders = jnp.arange(groups, dtype=jnp.int32)
    slots = jnp.arange(slot_count, dtype=jnp.int32)
    chosen = jnp.sum(jnp.where(own_dest[None, :] == loaders[:, None], slots[None, :], 0), axis=1)
    holds = jnp.any(dest_group.reshape(groups, slot_count) == group_at, axis=1)
    rank = jnp.sum(jnp.where(holds[None, :] & (loaders[None, :] < loaders[:, None]), 1, 0), axis=1)
    sources = jnp.sum(jnp.where(holds[None, :] & (rank[None, :] == slots[:, None]), loaders[None, :], 0), axis=1)
    return jnp.concatenate([chosen, sources]).astype(jnp.int32)


def on_device(
    patches, targets, grid_side, dest_group, embed_w, embed_b, gain, spec_w, spec_b, head_w, head_b
):
    slot_count, row_count, cells, depth = patches.shape
    samples = dest_group.shape[0]
    groups = lax.axis_size("grp")
    shards = lax.axis_size("fft")
    group_at = lax.axis_index("grp").astype(jnp.int32)
    shard_at = lax.axis_index("fft").astype(jnp.int32)
    outs = targets.shape[-1]
    per_sample = row_count * cells
    count = slot_count // CHUNKS
    firsts = [c * count for c in range(CHUNKS)]
    assert slot_count == SLOTS

    sides = lax.dynamic_slice_in_dim(grid_side, group_at * slot_count, slot_count)
    level = jnp.where(sides == cells, 0, jnp.where(sides == cells // 2, 1, 2)).astype(jnp.int32)
    place = jnp.stack([shard_at, shard_at * row_count, group_at])
    scal = jnp.concatenate([place, sides, level])
    routes = jnp.concatenate([place, prediction_routes(dest_group, group_at, groups, slot_count)])
    table_values, factors = dft_tables(cells)
    table = jnp.asarray(table_values)
    flat_patches = patches.reshape(-1, depth)
    flat_targets = targets.reshape(-1, outs)
    gain_row, embed_b_row, head_b_row = gain[None], embed_b[None], head_b[None]

    embedded, normed, stats, turned_send, turned_keep, pieces = embed(
        scal, flat_patches, embed_w, embed_b_row, gain_row, firsts, count, per_sample, cells, shards, groups
    )
    moved = [across(p) for p in pieces]
    mixed, saved = [], []
    for first, values in zip(firsts, moved):
        out, rest = spectral_chunk(scal, table, factors, values, spec_w, spec_b, first)
        mixed.append(across(out))
        saved.append(rest)
    predicted, residual, updated, head_sums, gathered = [], [], [], [], []
    for first, mix in zip(firsts, mixed):
        pred, res, up, sums = head_chunk(
            scal, embedded, normed, mix, flat_targets, head_w, head_b_row, first, samples, cells
        )
        predicted.append(pred)
        residual.append(res)
        updated.append(up)
        head_sums.append(sums)
        gathered.append(across([res] * shards))
    head_grad, gathered[0] = lax.optimization_barrier((head_gradient(updated, residual), gathered[0]))
    spec_back, sums = [], None
    for first, res, rest in zip(firsts, gathered, saved):
        values, sums = spectral_back_chunk(
            scal, table, factors, res, head_w, spec_w, rest, first, sums, first == firsts[-1]
        )
        if first == firsts[-1]:
            values, turned_send = lax.optimization_barrier((values, turned_send))
        spec_back.append(across(values))
    turned = [turned_keep, swap_bit(turned_send, 0, groups)]
    spec_grad, spec_bias = sums
    width = spec_w.shape[-1]
    blocks = spec_w.shape[2] // shards
    head_rows = head_w.shape[0] // groups
    _, head_grad, spec_grad = lax.optimization_barrier((spec_back[-1][1], head_grad, spec_grad))
    weight_sums = lax.all_to_all(
        packed(routes, head_grad, spec_grad, predicted, groups), "grp", split_axis=0, concat_axis=0, tiled=True
    )
    own_grads, other_grads, row_sums = [], [], []
    for first, res, back in zip(firsts, residual, spec_back):
        grad, row_sum = embedded_back_chunk(scal, embedded, stats, res, head_w, gain_row, back, first, cells)
        own_grads.append(grad)
        other_grads.append(swap_bit(grad, 0, groups))
        row_sums.append(row_sum)
    grads = own_grads + other_grads
    grads, weight_sums = lax.optimization_barrier((grads, weight_sums))
    sent = embed_grad_parts(scal, turned, grads, groups, 1)
    sent, kept_turned = lax.optimization_barrier((sent, turned))
    top_bit = groups.bit_length() - 2
    received = [swap_bit(sent[0], 1, groups), swap_bit(sent[1], top_bit, groups)]
    kept = embed_grad_parts(scal, kept_turned, grads, groups, 0)
    kept, weight_sums = lax.optimization_barrier((kept, weight_sums))
    ends = scatter_start(received, kept, groups)
    small, predictions = group_sums(routes, weight_sums, spec_bias, head_sums, row_sums, slot_count, per_sample)
    predictions = predictions.reshape(targets.shape)
    spec_rows = spec_grad.shape[0] // groups
    outgoing = shard_sums(routes, across([small] * shards), head_rows, spec_rows, spec_bias.shape[0])
    ends, outgoing = lax.optimization_barrier((ends, outgoing))
    part = jnp.concatenate(ends, axis=-1)
    part = part.reshape(shards, part.shape[0] // shards, -1)
    part = scatter_step(part, 1, shards, shard_at)
    even = from_same_core(outgoing, groups)
    bit = 2
    while bit < shards:
        part = part.astype(HALF)
        if bit == 2:
            _, even = lax.optimization_barrier((part, even))
        part = scatter_step(part, bit, shards, shard_at)
        bit *= 2
    embed_grad = part[0]
    gathered = [v for pair in zip(even, [swap_bit(v, 0, groups) for v in even]) for v in pair]
    head_grad, spec_w_grad, spec_b_grad, gain_grad, embed_bias_grad, head_bias_grad = assembled(
        scal, gathered, head_rows, shards, blocks, width
    )
    gain_grad, embed_bias_grad, head_bias_grad = gain_grad[0], embed_bias_grad[0], head_bias_grad[0]
    return (
        predictions,
        embed_grad,
        embed_bias_grad,
        gain_grad,
        spec_w_grad,
        spec_b_grad,
        head_grad,
        head_bias_grad,
    )


def solution(mesh):
    return jax.shard_map(
        on_device,
        mesh=mesh,
        in_specs=(
            P("grp", "fft", None, None),
            P("grp", "fft", None, None),
            P(),
            P(),
            P(),
            P(),
            P(),
            P(),
            P(),
            P(),
            P(),
        ),
        out_specs=(
            P("grp", "fft", None, None),
            P(("grp", "fft"), None),
            P(),
            P(),
            P(),
            P(),
            P(),
            P(),
        ),
        check_vma=False,
    )
```

```python
import jax
import jax.numpy as jnp
import ml_dtypes
import numpy as np
from jax import lax
from jax.experimental import pallas as pl
from jax.experimental.pallas import tpu as pltpu
from jax.sharding import PartitionSpec as P

EPSILON = 1e-05
SHRINK = 0.01
CHUNKS = 2
VMEM_BYTES = 24 * 1024 * 1024
SLOTS = 6
SHARD, FIRST_ROW, GROUP, SIDES = 0, 1, 2, 3
ROUTES = 3
HALF = jnp.bfloat16
FULL = jnp.float32


def dft_tables(cells):
    levels, factors = [], []
    for side, scale in ((cells, 1.1305), (cells // 2, 1.8633), (cells // 4, 1.0)):
        k = np.arange(cells)
        inside = (k < side).astype(np.float64)
        keep = inside[:, None] * inside[None, :]
        angle = 2.0 * np.pi * ((k[:, None] * k[None, :]) % side) / side
        one = np.exp(-1j * angle) * keep / np.sqrt(side)
        two = np.kron(one, one)
        table = np.concatenate([two.real, two.imag], axis=0)
        table[np.abs(table) < 1e-12] = 0.0
        rounded = (table * scale).astype(np.float32).astype(ml_dtypes.bfloat16)
        held = rounded.astype(np.float64)
        factors.append(float(np.sum(table * table) / np.sum(table * held)))
        levels.append(rounded)
    return np.stack(levels), factors


def dot(left, right):
    return jnp.dot(left, right, preferred_element_type=FULL)


def dot_tn(left, right):
    return lax.dot_general(left, right, (((0,), (0,)), ((), ())), preferred_element_type=FULL)


def dot_nt(left, right):
    return lax.dot_general(left, right, (((1,), (1,)), ((), ())), preferred_element_type=FULL)


def params(limit=VMEM_BYTES):
    return pltpu.CompilerParams(vmem_limit_bytes=limit)


def token_sides(scal_ref, first, count, per_sample, cells):
    token = lax.broadcasted_iota(jnp.int32, (count * per_sample, 1), 0)
    sample = token // per_sample
    side = jnp.zeros_like(token)
    for i in range(count):
        side = jnp.where(sample == i, scal_ref[SIDES + first + i], side)
    row = scal_ref[FIRST_ROW] + (token % per_sample) // cells
    col = token % cells
    valid = jnp.where((row < side) & (col < side), 1.0, 0.0).astype(FULL)
    return side, valid


def whole(shape):
    return pl.BlockSpec(tuple(shape), lambda i, s: (0,) * len(shape))


def part_of(scal_ref, k, size):
    at = jnp.bitwise_xor(scal_ref[SHARD], k)
    return pl.ds(pl.multiple_of(at * size, size), size)


def fill_lanes(scal_ref, refs, held):
    share = refs[0].shape[-1]
    for k, ref in enumerate(refs):
        held[:, part_of(scal_ref, k, share)] = ref[...].reshape(held.shape[0], share)


def fill_rows(scal_ref, refs, held):
    rows = refs[0].shape[1]
    for k, ref in enumerate(refs):
        held[:, part_of(scal_ref, k, rows), :] = ref[...]


def split_lanes(scal_ref, held, refs):
    share = refs[0].shape[-1]
    for k, ref in enumerate(refs):
        ref[...] = held[:, part_of(scal_ref, k, share)].reshape(ref.shape)


def split_rows(scal_ref, held, refs):
    rows = refs[0].shape[1]
    for k, ref in enumerate(refs):
        ref[...] = held[:, part_of(scal_ref, k, rows), :]


def embed(scal, patches, embed_w, embed_b, gain, firsts, count, per_sample, cells, shards, groups):
    rows, depth = patches.shape
    block = depth // groups
    width = embed_w.shape[1]
    share = width // shards
    chunk_rows = count * per_sample
    chunks = len(firsts)
    steps = 4
    tile = depth // steps

    def body(scal_ref, x_ref, w_ref, b_ref, gain_ref, emb_ref, norm_ref, stat_ref, *refs):
        (send_ref, keep_ref), outs, acc = refs[:2], refs[2:-1], refs[-1]
        step = pl.program_id(0)
        turned = x_ref[...].T
        for i in range(tile // block):
            values = turned[i * block : (i + 1) * block]
            away = (scal_ref[GROUP] + i) % 2

            @pl.when(away == 1)
            def _(i=i, values=values):
                send_ref[i // 2] = values

            @pl.when(away == 0)
            def _(i=i, values=values):
                keep_ref[i // 2] = values

        part = dot(x_ref[...], w_ref[...])

        @pl.when(step == 0)
        def _():
            acc[...] = part

        @pl.when(step > 0)
        def _():
            acc[...] += part

        @pl.when(step == steps - 1)
        def _():
            for c, first in enumerate(firsts):
                at = slice(c * chunk_rows, (c + 1) * chunk_rows)
                _, valid = token_sides(scal_ref, first, count, per_sample, cells)
                embedded = ((acc[at] + b_ref[...]) * valid).astype(HALF)
                emb_ref[at] = embedded
                values = embedded.astype(FULL)
                mean = jnp.mean(values, axis=-1, keepdims=True)
                centered = values - mean
                inv_std = lax.rsqrt(jnp.mean(centered * centered, axis=-1, keepdims=True) + EPSILON)
                norm_ref[at] = (centered * inv_std * gain_ref[...]).astype(HALF)
                stat_ref[at, :128] = jnp.broadcast_to(mean, (chunk_rows, 128))
                stat_ref[at, 128:] = jnp.broadcast_to(inv_std, (chunk_rows, 128))
                for k in range(shards):
                    piece = norm_ref[at, part_of(scal_ref, k, share)]
                    outs[c * shards + k][...] = piece.reshape(count, per_sample, share)

    piece = (count, per_sample, share)
    turned_spec = pl.BlockSpec((tile // (2 * block), block, rows), lambda k, s: (k, 0, 0))
    turned_shape = jax.ShapeDtypeStruct((groups // 2, block, rows), HALF)
    emb, normed, stats, send, keep, *pieces = pl.pallas_call(
        body,
        grid_spec=pltpu.PrefetchScalarGridSpec(
            num_scalar_prefetch=1,
            grid=(steps,),
            in_specs=[
                pl.BlockSpec((rows, tile), lambda k, s: (0, k)),
                pl.BlockSpec((tile, width), lambda k, s: (k, 0)),
                whole((1, width)),
                whole((1, width)),
            ],
            out_specs=[whole((rows, width)), whole((rows, width)), whole((rows, 256)), turned_spec, turned_spec]
            + [whole(piece)] * (shards * chunks),
            scratch_shapes=[pltpu.VMEM((rows, width), FULL)],
        ),
        out_shape=[
            jax.ShapeDtypeStruct((rows, width), HALF),
            jax.ShapeDtypeStruct((rows, width), HALF),
            jax.ShapeDtypeStruct((rows, 256), FULL),
            turned_shape,
            turned_shape,
        ]
        + [jax.ShapeDtypeStruct(piece, HALF)] * (shards * chunks),
        compiler_params=params(60 * 1024 * 1024),
        cost_estimate=pl.CostEstimate(
            flops=2 * rows * depth * width, bytes_accessed=2 * depth * (rows + width), transcendentals=0
        ),
        name="embed",
    )(scal, patches, embed_w, embed_b, gain)
    return emb, normed, stats, send, keep, [pieces[c * shards : (c + 1) * shards] for c in range(chunks)]


def to_blocks(values, blocks, width):
    half = values.shape[0] // 2
    return [
        jnp.concatenate(
            [values[:half, b * width : (b + 1) * width], values[half:, b * width : (b + 1) * width]], axis=1
        )
        for b in range(blocks)
    ]


def from_blocks(parts, width):
    real = jnp.concatenate([p[:, :width] for p in parts], axis=1)
    imag = jnp.concatenate([p[:, width:] for p in parts], axis=1)
    return real, imag


def table_factor(level, factors):
    return jnp.where(level == 0, factors[0], jnp.where(level == 1, factors[1], factors[2])).astype(FULL)


def table_back(table_ref, level, tops, rests, factor):
    size = table_ref.shape[2]
    total = None
    for at, (top, rest) in enumerate(zip(tops, rests)):
        table = table_ref[level, at * size : (at + 1) * size]
        part = dot(table, top) + dot(table, rest)
        total = part if total is None else total + part
    return total * factor


def two_terms(values):
    top = values.astype(HALF)
    return top, (values - top.astype(FULL)).astype(HALF)


def complex_weights(w_ref, held, blocks, width):
    for layer in range(2):
        for b in range(blocks):
            real, imag = w_ref[layer, 0, b], w_ref[layer, 1, b]
            held[layer, b, :width, :width] = real
            held[layer, b, :width, width:] = imag
            held[layer, b, width:, :width] = -imag
            held[layer, b, width:, width:] = real


def spectral_chunk(scal, table, factors, pieces, spec_w, spec_b, first):
    shards = len(pieces)
    count, per_sample, share = pieces[0].shape
    size = shards * per_sample
    width = spec_w.shape[-1]
    blocks = share // width
    wide = 2 * width

    def body(scal_ref, t_ref, w_ref, b_ref, *refs):
        ins, outs = refs[:shards], refs[shards : 2 * shards]
        spec_ref, hid_ref, fil_ref, weights, held = refs[2 * shards :]

        def bias(layer, b):
            row = pl.ds(scal_ref[SHARD] * blocks + b, 1)
            return jnp.concatenate([b_ref[layer, 0, row], b_ref[layer, 1, row]], axis=1)

        complex_weights(w_ref, weights, blocks, width)
        fill_rows(scal_ref, ins, held)
        levels = [scal_ref[SIDES + SLOTS + first + i] for i in range(count)]
        for i, level in enumerate(levels):
            spectrum = (dot(t_ref[level], held[i]) * table_factor(level, factors)).astype(HALF)
            for b, entry in enumerate(to_blocks(spectrum, blocks, width)):
                spec_ref[b, i * size : (i + 1) * size] = entry
        kept = []
        for b in range(blocks):
            pre_one = dot(spec_ref[b], weights[0, b]) + bias(0, b)
            hidden = jnp.maximum(pre_one, 0.0).astype(HALF)
            hid_ref[b] = hidden
            pre_two = dot(hidden, weights[1, b]) + bias(1, b)
            filtered = jnp.where(
                pre_two > SHRINK, pre_two - SHRINK, jnp.where(pre_two < -SHRINK, pre_two + SHRINK, 0.0)
            )
            top, rest = two_terms(filtered)
            fil_ref[b] = top
            kept.append((top, rest))
        for i, level in enumerate(levels):
            at = slice(i * size, (i + 1) * size)
            tops = from_blocks([top[at] for top, _ in kept], width)
            rests = from_blocks([rest[at] for _, rest in kept], width)
            held[i] = table_back(t_ref, level, tops, rests, table_factor(level, factors)).astype(HALF)
        split_rows(scal_ref, held, outs)

    saved = (blocks, count * size, wide)
    outs = pl.pallas_call(
        body,
        grid_spec=pltpu.PrefetchScalarGridSpec(
            num_scalar_prefetch=1,
            grid=(1,),
            in_specs=[
                whole(table.shape),
                pl.BlockSpec((2, 2, blocks, width, width), lambda i, s: (0, 0, s[SHARD], 0, 0)),
                whole(spec_b.shape),
            ]
            + [whole(pieces[0].shape)] * shards,
            out_specs=[whole(pieces[0].shape)] * shards + [whole(saved)] * 3,
            scratch_shapes=[pltpu.VMEM((2, blocks, wide, wide), HALF), pltpu.VMEM((count, size, share), HALF)],
        ),
        out_shape=[jax.ShapeDtypeStruct(pieces[0].shape, HALF)] * shards + [jax.ShapeDtypeStruct(saved, HALF)] * 3,
        compiler_params=params(),
        cost_estimate=pl.CostEstimate(
            flops=count * size * share * size * 14, bytes_accessed=count * size * share * 16, transcendentals=0
        ),
        name="spectral",
    )(scal, table, spec_w, spec_b, *pieces)
    return outs[:shards], outs[shards:]


def head_chunk(scal, embedded, normed, mixed, targets, head_w, head_b, first, samples, cells):
    shards = len(mixed)
    count, per_sample, share = mixed[0].shape
    rows = count * per_sample
    width, outs = head_w.shape
    at = first // count
    scale_root = float(np.sqrt(np.float32(samples)))

    def body(scal_ref, emb_ref, norm_ref, tgt_ref, w_ref, b_ref, *refs):
        mix_refs, (pred_ref, res_ref, up_ref, bias_ref, held) = refs[:shards], refs[shards:]
        fill_lanes(scal_ref, mix_refs, held)
        side, valid = token_sides(scal_ref, first, count, per_sample, cells)
        updated = (emb_ref[...].astype(FULL) + norm_ref[...].astype(FULL) + held[...].astype(FULL)).astype(HALF)
        output = (dot(updated, w_ref[...]) + b_ref[...]) * valid
        pred_ref[...] = output.astype(HALF).reshape(pred_ref.shape)
        scale = 2.0 / (side.astype(FULL) * scale_root)
        residual = (scale * valid * (output - tgt_ref[...].astype(FULL))).astype(HALF)
        res_ref[...] = residual.reshape(res_ref.shape)
        up_ref[...] = updated
        total = jnp.sum(residual.astype(FULL), axis=0, keepdims=True)
        bias_ref[...] = jnp.broadcast_to(total, bias_ref.shape)

    token_shape = (count, per_sample, outs)
    return pl.pallas_call(
        body,
        grid_spec=pltpu.PrefetchScalarGridSpec(
            num_scalar_prefetch=1,
            grid=(1,),
            in_specs=[
                pl.BlockSpec((rows, width), lambda i, s: (at, 0)),
                pl.BlockSpec((rows, width), lambda i, s: (at, 0)),
                pl.BlockSpec((rows, outs), lambda i, s: (at, 0)),
                whole((width, outs)),
                whole((1, outs)),
            ]
            + [whole(mixed[0].shape)] * shards,
            out_specs=[whole(token_shape), whole(token_shape), whole((rows, width)), whole((8, outs))],
            scratch_shapes=[pltpu.VMEM((rows, width), HALF)],
        ),
        out_shape=[
            jax.ShapeDtypeStruct(token_shape, HALF),
            jax.ShapeDtypeStruct(token_shape, HALF),
            jax.ShapeDtypeStruct((rows, width), HALF),
            jax.ShapeDtypeStruct((8, outs), FULL),
        ],
        compiler_params=params(),
        cost_estimate=pl.CostEstimate(
            flops=2 * rows * width * outs, bytes_accessed=rows * width * 4 + width * outs * 6, transcendentals=0
        ),
        name="head",
    )(scal, embedded, normed, targets, head_w, head_b, *mixed)


def head_gradient(updated, residual):
    width = updated[0].shape[1]
    outs = residual[0].shape[-1]
    count = len(updated)

    def body(*refs):
        total = None
        for up_ref, res_ref in zip(refs[:count], refs[count : 2 * count]):
            part = dot_tn(up_ref[...], res_ref[...].reshape(up_ref.shape[0], outs))
            total = part if total is None else total + part
        refs[-1][...] = total.astype(HALF)

    return pl.pallas_call(
        body,
        out_shape=jax.ShapeDtypeStruct((width, outs), HALF),
        compiler_params=params(),
        cost_estimate=pl.CostEstimate(
            flops=2 * count * updated[0].size * outs, bytes_accessed=2 * count * updated[0].size, transcendentals=0
        ),
        name="head_gradient",
    )(*updated, *residual)


def spectral_back_chunk(scal, table, factors, residual, head_w, spec_w, saved, first, before, last):
    shards = len(residual)
    count, per_sample, outs = residual[0].shape
    size = shards * per_sample
    width = spec_w.shape[-1]
    wide = 2 * width
    share = head_w.shape[0] // shards
    blocks = share // width
    raw_shape = (2, blocks, wide, wide)
    bias_shape = (2 * blocks, wide)
    has_before = before is not None

    def body(scal_ref, t_ref, h_ref, w_ref, spec_ref, hid_ref, fil_ref, *refs):
        ins, refs = refs[:shards], refs[shards:]
        if has_before:
            (old_ref, old_bias_ref), refs = refs[:2], refs[2:]
        pieces, (grad_ref, bias_ref, weights, held, gathered) = refs[:shards], refs[shards:]

        def weight_sums(layer, b, inputs, grads):
            raw = dot_tn(inputs, grads)
            sums = jnp.sum(grads.astype(FULL), axis=0, keepdims=True)
            at = layer * blocks + b
            if has_before:
                raw = raw + old_ref[layer, b]
                sums = sums + old_bias_ref[at : at + 1]
            bias_ref[at : at + 1] = sums
            if not last:
                grad_ref[layer, b] = raw
                return
            real = raw[:width, :width] + raw[width:, width:]
            imag = raw[:width, width:] - raw[width:, :width]
            grad_ref[at * width : (at + 1) * width] = jnp.concatenate([real, imag], axis=1).astype(HALF)

        complex_weights(w_ref, weights, blocks, width)
        fill_rows(scal_ref, ins, gathered)
        levels = [scal_ref[SIDES + SLOTS + first + i] for i in range(count)]
        updated_grad = dot_nt(gathered[...].reshape(count * size, outs), h_ref[...]).astype(HALF)
        entries = []
        for i, level in enumerate(levels):
            filtered_grad = dot(t_ref[level], updated_grad[i * size : (i + 1) * size]) * table_factor(level, factors)
            entries.append(to_blocks(filtered_grad, blocks, width))
        kept = []
        for b in range(blocks):
            entry = jnp.concatenate([e[b] for e in entries], axis=0)
            two_grad = jnp.where(fil_ref[b].astype(FULL) != 0.0, entry, 0.0).astype(HALF)
            hidden = hid_ref[b]
            hidden_grad = dot_nt(two_grad, weights[1, b])
            one_grad = jnp.where(hidden.astype(FULL) > 0.0, hidden_grad, 0.0).astype(HALF)
            kept.append(two_terms(dot_nt(one_grad, weights[0, b])))
            weight_sums(1, b, hidden, two_grad)
            weight_sums(0, b, spec_ref[b], one_grad)
        for i, level in enumerate(levels):
            at = slice(i * size, (i + 1) * size)
            tops = from_blocks([top[at] for top, _ in kept], width)
            rests = from_blocks([rest[at] for _, rest in kept], width)
            held[i] = table_back(t_ref, level, tops, rests, table_factor(level, factors)).astype(HALF)
        split_rows(scal_ref, held, pieces)

    piece = (count, per_sample, share)
    if last:
        grad_out = jax.ShapeDtypeStruct((2 * blocks * width, wide), HALF)
    else:
        grad_out = jax.ShapeDtypeStruct(raw_shape, FULL)
    result = pl.pallas_call(
        body,
        grid_spec=pltpu.PrefetchScalarGridSpec(
            num_scalar_prefetch=1,
            grid=(1,),
            in_specs=[
                whole(table.shape),
                pl.BlockSpec((share, outs), lambda i, s: (s[SHARD], 0)),
                pl.BlockSpec((2, 2, blocks, width, width), lambda i, s: (0, 0, s[SHARD], 0, 0)),
            ]
            + [whole(saved[0].shape)] * 3
            + [whole(residual[0].shape)] * shards
            + ([whole(raw_shape), whole(bias_shape)] if has_before else []),
            out_specs=[whole(piece)] * shards + [whole(grad_out.shape), whole(bias_shape)],
            scratch_shapes=[
                pltpu.VMEM((2, blocks, wide, wide), HALF),
                pltpu.VMEM((count, size, share), HALF),
                pltpu.VMEM((count, size, outs), HALF),
            ],
        ),
        out_shape=[jax.ShapeDtypeStruct(piece, HALF)] * shards
        + [grad_out, jax.ShapeDtypeStruct(bias_shape, FULL)],
        compiler_params=params(),
        cost_estimate=pl.CostEstimate(
            flops=count * size * share * size * 20, bytes_accessed=count * size * share * 16, transcendentals=0
        ),
        name="spectral_back",
    )(scal, table, head_w, spec_w, *saved, *residual, *(before or ()))
    return result[:shards], result[shards:]


def embedded_back_chunk(scal, embedded, stats, residual, head_w, gain, spec_grad, first, cells):
    shards = len(spec_grad)
    count, per_sample, share = spec_grad[0].shape
    rows = count * per_sample
    width, outs = head_w.shape
    at = first // count

    def body(scal_ref, emb_ref, stat_ref, res_ref, w_ref, gain_ref, *refs):
        grad_refs, (out_ref, sums_ref, held) = refs[:shards], refs[shards:]
        fill_lanes(scal_ref, grad_refs, held)
        _, valid = token_sides(scal_ref, first, count, per_sample, cells)
        inv_std = stat_ref[:, 128:129]
        unit = (emb_ref[...].astype(FULL) - stat_ref[:, 0:1]) * inv_std
        direct = dot_nt(res_ref[...].reshape(rows, outs), w_ref[...]).astype(HALF).astype(FULL)
        normed_grad = held[...].astype(FULL) + direct
        gain_grad = jnp.sum(normed_grad * unit, axis=0, keepdims=True)
        unit_grad = normed_grad * gain_ref[...]
        mean_grad = jnp.mean(unit_grad, axis=-1, keepdims=True)
        mean_cross = jnp.mean(unit_grad * unit, axis=-1, keepdims=True)
        input_grad = inv_std * (unit_grad - mean_grad - unit * mean_cross)
        result = ((input_grad + direct) * valid).astype(HALF)
        out_ref[...] = result
        bias_grad = jnp.sum(result.astype(FULL), axis=0, keepdims=True)
        sums_ref[0:4] = jnp.broadcast_to(gain_grad, (4, width))
        sums_ref[4:8] = jnp.broadcast_to(bias_grad, (4, width))

    return pl.pallas_call(
        body,
        grid_spec=pltpu.PrefetchScalarGridSpec(
            num_scalar_prefetch=1,
            grid=(1,),
            in_specs=[
                pl.BlockSpec((rows, width), lambda i, s: (at, 0)),
                pl.BlockSpec((rows, 256), lambda i, s: (at, 0)),
                whole((count, per_sample, outs)),
                whole((width, outs)),
                whole((1, width)),
            ]
            + [whole(spec_grad[0].shape)] * shards,
            out_specs=[whole((rows, width)), whole((8, width))],
            scratch_shapes=[pltpu.VMEM((rows, width), HALF)],
        ),
        out_shape=[jax.ShapeDtypeStruct((rows, width), HALF), jax.ShapeDtypeStruct((8, width), FULL)],
        compiler_params=params(),
        cost_estimate=pl.CostEstimate(
            flops=2 * rows * width * outs, bytes_accessed=rows * width * 6, transcendentals=0
        ),
        name="embedded_back",
    )(scal, embedded, stats, residual, head_w, gain, *spec_grad)


def embed_grad_parts(scal, turned, grads, groups, away):
    pairs, block, tokens = turned[0].shape
    chunk_rows, width = grads[0].shape
    half = width // 2
    top = pairs // 2
    count = len(turned)
    depth = tokens * count

    def relative(unit):
        return jnp.where(unit < top, 2 * unit + away, unit - top + away * top)

    def body(scal_ref, *refs):
        turned_refs, grad_refs = refs[:count], refs[count : count + len(grads)]
        left_ref, right_ref, held = refs[count + len(grads) :]
        unit = pl.program_id(0)

        @pl.when(unit % top == 0)
        def _():
            for i, ref in enumerate(grad_refs):
                held[i * chunk_rows : (i + 1) * chunk_rows] = ref[...]

        rows = jnp.concatenate([ref[0] for ref in turned_refs], axis=1)
        total = dot(rows, held[...]).astype(HALF)

        @pl.when(unit < top)
        def _():
            left_ref[0] = total

        @pl.when(unit >= top)
        def _():
            right_ref[0] = total

    shape = (top, block, half)
    return pl.pallas_call(
        body,
        grid_spec=pltpu.PrefetchScalarGridSpec(
            num_scalar_prefetch=1,
            grid=(pairs,),
            in_specs=[
                pl.BlockSpec((1, block, tokens), lambda i, s: (jnp.bitwise_xor(s[GROUP] // 2, relative(i)), 0, 0))
                for _ in turned
            ]
            + [pl.BlockSpec((chunk_rows, half), lambda i, s: (0, i // top)) for _ in grads],
            out_specs=[
                pl.BlockSpec((1, block, half), lambda i, s: (jnp.minimum(i, top - 1), 0, 0)),
                pl.BlockSpec((1, block, half), lambda i, s: (jnp.maximum(i - top, 0), 0, 0)),
            ],
            scratch_shapes=[pltpu.VMEM((depth, half), HALF)],
        ),
        out_shape=[jax.ShapeDtypeStruct(shape, HALF)] * 2,
        compiler_params=params(),
        cost_estimate=pl.CostEstimate(
            flops=depth * pairs * block * width,
            bytes_accessed=pairs * block * (2 * depth + width) + depth * width,
            transcendentals=0,
        ),
        name="embed_grad",
    )(scal, *turned, *grads)


def swap_bit(values, bit, groups):
    return lax.ppermute(values, "grp", [(g, g ^ (1 << bit)) for g in range(groups)])


def across(pieces):
    shards = len(pieces)
    return [pieces[0]] + [
        lax.ppermute(pieces[k], "fft", [(z, z ^ k) for z in range(shards)]) for k in range(1, shards)
    ]


def add_half(left, right):
    return (left.astype(FULL) + right.astype(FULL)).astype(HALF)


def scatter_start(received, kept, groups):
    bits = groups.bit_length() - 1
    ends = []
    for first, keep, order, low in (
        (received[0], kept[0], list(range(2, bits)), True),
        (received[1], kept[1], list(range(bits - 2, 0, -1)), False),
    ):
        total = add_half(keep, first)
        for bit in order:
            count, block, width = total.shape
            if low:
                split = total.reshape(count // 2, 2, block, width)
                keep, send = split[:, 0], split[:, 1]
            else:
                split = total.reshape(2, count // 2, block, width)
                keep, send = split[0], split[1]
            total = add_half(keep, swap_bit(send, bit, groups))
        ends.append(total[0])
    return ends


def scatter_step(part, bit, shards, shard_at):
    split = part.reshape(part.shape[0] // 2, 2, *part.shape[1:])
    mine = (shard_at // bit) % 2
    keep = lax.dynamic_index_in_dim(split, mine, 1, keepdims=False)
    send = lax.dynamic_index_in_dim(split, 1 - mine, 1, keepdims=False)
    received = lax.ppermute(send, "fft", [(z, z ^ bit) for z in range(shards)])
    return keep.astype(FULL) + received.astype(FULL)


def from_same_core(values, groups):
    return [values] + [
        lax.ppermute(values, "grp", [(g, g ^ k) for g in range(groups)]) for k in range(2, groups, 2)
    ]


def hi_lo(values):
    high = values.astype(HALF)
    return jnp.concatenate([high, (values - high.astype(FULL)).astype(HALF)], axis=0)


def from_hi_lo(values):
    half = values.shape[0] // 2
    values = values.astype(FULL)
    return values[:half] + values[half:]


def one_step(body, name, operands, out_shape):
    return pl.pallas_call(
        body,
        grid_spec=pltpu.PrefetchScalarGridSpec(
            num_scalar_prefetch=1,
            grid=(1,),
            in_specs=[whole(o.shape) for o in operands[1:]],
            out_specs=[whole(o.shape) for o in out_shape],
        ),
        out_shape=out_shape,
        compiler_params=params(),
        name=name,
    )(*operands)


def packed(routes, head_grad, spec_grad, predicted, groups):
    outs = head_grad.shape[1]
    head_rows, spec_rows = head_grad.shape[0] // groups, spec_grad.shape[0] // groups
    count, per_sample, _ = predicted[0].shape

    def body(routes_ref, head_ref, spec_ref, *refs):
        pred_refs, out_ref = refs[:-1], refs[-1]
        for g in range(groups):
            out_ref[g, :head_rows] = head_ref[g * head_rows : (g + 1) * head_rows]
            out_ref[g, head_rows : head_rows + spec_rows] = spec_ref[g * spec_rows : (g + 1) * spec_rows]
            chosen = routes_ref[ROUTES + g]
            for c, ref in enumerate(pred_refs):

                @pl.when(chosen // count == c)
                def _(g=g, c=c, ref=ref, chosen=chosen):
                    out_ref[g, head_rows + spec_rows :] = ref[chosen - c * count]

    shape = (groups, head_rows + spec_rows + per_sample, outs)
    return one_step(
        body, "packed", (routes, head_grad, spec_grad, *predicted), [jax.ShapeDtypeStruct(shape, HALF)]
    )[0]


def group_sums(routes, moved, spec_bias, head_sums, row_sums, slot_count, per_sample):
    groups, rows, outs = moved.shape
    weight_rows = rows - per_sample
    own_rows = spec_bias.shape[0]
    chunks = len(head_sums)
    parts = row_sums[0].shape[1] // outs
    spare = 16 - own_rows - 2 * parts - 1

    def body(routes_ref, moved_ref, bias_ref, *refs):
        head_refs, row_refs, (out_ref, pred_ref) = refs[:chunks], refs[chunks : 2 * chunks], refs[2 * chunks :]
        total = moved_ref[0, :weight_rows].astype(FULL)
        for g in range(1, groups):
            total = total + moved_ref[g, :weight_rows].astype(FULL)
        out_ref[:weight_rows] = total.astype(HALF)
        lines = [bias_ref[...]]
        for row in (0, 4):
            line = sum(ref[row : row + 1] for ref in row_refs)
            lines += [line[:, i * outs : (i + 1) * outs] for i in range(parts)]
        lines += [sum(ref[0:1] for ref in head_refs), jnp.zeros((spare, outs), FULL)]
        out_ref[weight_rows:] = hi_lo(jnp.concatenate(lines, axis=0))
        for i in range(slot_count):
            pred_ref[i] = moved_ref[routes_ref[ROUTES + groups + i], weight_rows:]

    return one_step(
        body,
        "group_sums",
        (routes, moved, spec_bias, *head_sums, *row_sums),
        [
            jax.ShapeDtypeStruct((weight_rows + 32, outs), HALF),
            jax.ShapeDtypeStruct((slot_count, per_sample, outs), HALF),
        ],
    )


def shard_sums(routes, rows, head_rows, spec_rows, own_rows):
    shards = len(rows)
    outs = rows[0].shape[1]
    small_rows = 32

    def body(routes_ref, *refs):
        ins, out_ref = refs[:-1], refs[-1]
        total = sum(ref[:head_rows].astype(FULL) for ref in ins)
        out_ref[:head_rows] = total.astype(HALF)
        for k, ref in enumerate(ins):
            at = head_rows + k * spec_rows
            out_ref[at : at + spec_rows] = ref[head_rows : head_rows + spec_rows]
        smalls = [from_hi_lo(ref[head_rows + spec_rows :]) for ref in ins]
        lines = []
        for z in range(shards):
            here = [jnp.bitwise_xor(routes_ref[SHARD], k) == z for k in range(shards)]
            lines.append(sum(jnp.where(h, v[:own_rows], 0.0) for h, v in zip(here, smalls)))
        lines.append(sum(v[own_rows:] for v in smalls))
        have = shards * own_rows + 16 - own_rows
        lines.append(jnp.zeros((small_rows - have, outs), FULL))
        out_ref[head_rows + shards * spec_rows :] = hi_lo(jnp.concatenate(lines, axis=0))

    shape = (head_rows + shards * spec_rows + 2 * small_rows, outs)
    return one_step(body, "shard_sums", (routes, *rows), [jax.ShapeDtypeStruct(shape, HALF)])[0]


def assembled(scal, gathered, head_rows, shards, blocks, width):
    groups = len(gathered)
    total_blocks = shards * blocks
    spec_rows = 2 * blocks * width // groups
    small_at = head_rows + shards * spec_rows
    small_rows = (gathered[0].shape[0] - small_at) // 2

    def body(scal_ref, *refs):
        ins, (head_ref, spec_ref, bias_ref, gain_ref, embed_ref, out_ref) = refs[:groups], refs[groups:]
        small = None
        for k, ref in enumerate(ins):
            group = jnp.bitwise_xor(scal_ref[GROUP], k)
            at = pl.ds(pl.multiple_of(group * head_rows, head_rows), head_rows)
            head_ref[at, :] = ref[:head_rows].astype(FULL)
            start = group * spec_rows
            layer, b = start // (blocks * width), (start // width) % blocks
            rows = pl.ds(pl.multiple_of(start % width, spec_rows), spec_rows)
            for j in range(shards):
                values = ref[head_rows + j * spec_rows : head_rows + (j + 1) * spec_rows].astype(FULL)
                z = jnp.bitwise_xor(scal_ref[SHARD], j)
                spec_ref[layer, 0, z * blocks + b, rows] = values[:, :width]
                spec_ref[layer, 1, z * blocks + b, rows] = values[:, width:]
            part = ref[small_at : small_at + small_rows].astype(FULL) + ref[small_at + small_rows :].astype(FULL)
            small = part if small is None else small + part
        for z in range(shards):
            for layer in range(2):
                for b in range(blocks):
                    row = (z * 2 + layer) * blocks + b
                    for p in range(2):
                        bias_ref[layer, p, z * blocks + b : z * blocks + b + 1] = small[
                            row : row + 1, p * width : (p + 1) * width
                        ]
        row = shards * 2 * blocks
        quarter = gain_ref.shape[1] // (2 * width)
        for ref in (gain_ref, embed_ref):
            for i in range(quarter):
                ref[:, i * 2 * width : (i + 1) * 2 * width] = small[row + i : row + i + 1]
            row += quarter
        out_ref[...] = small[row : row + 1]

    out_shape = [
        jax.ShapeDtypeStruct((groups * head_rows, 2 * width), FULL),
        jax.ShapeDtypeStruct((2, 2, total_blocks, width, width), FULL),
        jax.ShapeDtypeStruct((2, 2, total_blocks, width), FULL),
        jax.ShapeDtypeStruct((1, groups * head_rows), FULL),
        jax.ShapeDtypeStruct((1, groups * head_rows), FULL),
        jax.ShapeDtypeStruct((1, 2 * width), FULL),
    ]
    return pl.pallas_call(
        body,
        grid_spec=pltpu.PrefetchScalarGridSpec(
            num_scalar_prefetch=1,
            grid=(1,),
            in_specs=[whole(gathered[0].shape)] * groups,
            out_specs=[whole(o.shape) for o in out_shape],
        ),
        out_shape=out_shape,
        compiler_params=params(),
        name="assembled",
    )(scal, *gathered)


def prediction_routes(dest_group, group_at, groups, slot_count):
    own_dest = lax.dynamic_slice_in_dim(dest_group, group_at * slot_count, slot_count)
    loaders = jnp.arange(groups, dtype=jnp.int32)
    slots = jnp.arange(slot_count, dtype=jnp.int32)
    chosen = jnp.sum(jnp.where(own_dest[None, :] == loaders[:, None], slots[None, :], 0), axis=1)
    holds = jnp.any(dest_group.reshape(groups, slot_count) == group_at, axis=1)
    rank = jnp.sum(jnp.where(holds[None, :] & (loaders[None, :] < loaders[:, None]), 1, 0), axis=1)
    sources = jnp.sum(jnp.where(holds[None, :] & (rank[None, :] == slots[:, None]), loaders[None, :], 0), axis=1)
    return jnp.concatenate([chosen, sources]).astype(jnp.int32)


def on_device(
    patches, targets, grid_side, dest_group, embed_w, embed_b, gain, spec_w, spec_b, head_w, head_b
):
    slot_count, row_count, cells, depth = patches.shape
    samples = dest_group.shape[0]
    groups = lax.axis_size("grp")
    shards = lax.axis_size("fft")
    group_at = lax.axis_index("grp").astype(jnp.int32)
    shard_at = lax.axis_index("fft").astype(jnp.int32)
    outs = targets.shape[-1]
    per_sample = row_count * cells
    count = slot_count // CHUNKS
    firsts = [c * count for c in range(CHUNKS)]
    assert slot_count == SLOTS

    sides = lax.dynamic_slice_in_dim(grid_side, group_at * slot_count, slot_count)
    level = jnp.where(sides == cells, 0, jnp.where(sides == cells // 2, 1, 2)).astype(jnp.int32)
    place = jnp.stack([shard_at, shard_at * row_count, group_at])
    scal = jnp.concatenate([place, sides, level])
    routes = jnp.concatenate([place, prediction_routes(dest_group, group_at, groups, slot_count)])
    table_values, factors = dft_tables(cells)
    table = jnp.asarray(table_values)
    flat_patches = patches.reshape(-1, depth)
    flat_targets = targets.reshape(-1, outs)
    gain_row, embed_b_row, head_b_row = gain[None], embed_b[None], head_b[None]

    embedded, normed, stats, turned_send, turned_keep, pieces = embed(
        scal, flat_patches, embed_w, embed_b_row, gain_row, firsts, count, per_sample, cells, shards, groups
    )
    moved = [across(p) for p in pieces]
    mixed, saved = [], []
    for first, values in zip(firsts, moved):
        out, rest = spectral_chunk(scal, table, factors, values, spec_w, spec_b, first)
        mixed.append(across(out))
        saved.append(rest)
    predicted, residual, updated, head_sums, gathered = [], [], [], [], []
    for first, mix in zip(firsts, mixed):
        pred, res, up, sums = head_chunk(
            scal, embedded, normed, mix, flat_targets, head_w, head_b_row, first, samples, cells
        )
        predicted.append(pred)
        residual.append(res)
        updated.append(up)
        head_sums.append(sums)
        gathered.append(across([res] * shards))
    head_grad, gathered[0] = lax.optimization_barrier((head_gradient(updated, residual), gathered[0]))
    spec_back, sums = [], None
    for first, res, rest in zip(firsts, gathered, saved):
        values, sums = spectral_back_chunk(
            scal, table, factors, res, head_w, spec_w, rest, first, sums, first == firsts[-1]
        )
        if first == firsts[-1]:
            values, turned_send = lax.optimization_barrier((values, turned_send))
        spec_back.append(across(values))
    turned = [turned_keep, swap_bit(turned_send, 0, groups)]
    spec_grad, spec_bias = sums
    width = spec_w.shape[-1]
    blocks = spec_w.shape[2] // shards
    head_rows = head_w.shape[0] // groups
    own_grads, other_grads, row_sums = [], [], []
    for first, res, back in zip(firsts, residual, spec_back):
        grad, row_sum = embedded_back_chunk(scal, embedded, stats, res, head_w, gain_row, back, first, cells)
        if first == firsts[0]:
            grad, head_grad, spec_grad = lax.optimization_barrier((grad, head_grad, spec_grad))
            weight_sums = lax.all_to_all(
                packed(routes, head_grad, spec_grad, predicted, groups), "grp", split_axis=0, concat_axis=0, tiled=True
            )
        own_grads.append(grad)
        other_grads.append(swap_bit(grad, 0, groups))
        row_sums.append(row_sum)
    grads = own_grads + other_grads
    sent = embed_grad_parts(scal, turned, grads, groups, 1)
    sent, kept_turned = lax.optimization_barrier((sent, turned))
    top_bit = groups.bit_length() - 2
    received = [swap_bit(sent[0], 1, groups), swap_bit(sent[1], top_bit, groups)]
    kept = embed_grad_parts(scal, kept_turned, grads, groups, 0)
    kept, weight_sums = lax.optimization_barrier((kept, weight_sums))
    ends = scatter_start(received, kept, groups)
    small, predictions = group_sums(routes, weight_sums, spec_bias, head_sums, row_sums, slot_count, per_sample)
    predictions = predictions.reshape(targets.shape)
    spec_rows = spec_grad.shape[0] // groups
    outgoing = shard_sums(routes, across([small] * shards), head_rows, spec_rows, spec_bias.shape[0])
    ends, outgoing = lax.optimization_barrier((ends, outgoing))
    part = jnp.concatenate(ends, axis=-1)
    part = part.reshape(shards, part.shape[0] // shards, -1)
    part = scatter_step(part, 1, shards, shard_at)
    even = from_same_core(outgoing, groups)
    bit = 2
    while bit < shards:
        part = part.astype(HALF)
        if bit == 2:
            _, even = lax.optimization_barrier((part, even))
        part = scatter_step(part, bit, shards, shard_at)
        bit *= 2
    embed_grad = part[0]
    gathered = [v for pair in zip(even, [swap_bit(v, 0, groups) for v in even]) for v in pair]
    head_grad, spec_w_grad, spec_b_grad, gain_grad, embed_bias_grad, head_bias_grad = assembled(
        scal, gathered, head_rows, shards, blocks, width
    )
    gain_grad, embed_bias_grad, head_bias_grad = gain_grad[0], embed_bias_grad[0], head_bias_grad[0]
    return (
        predictions,
        embed_grad,
        embed_bias_grad,
        gain_grad,
        spec_w_grad,
        spec_b_grad,
        head_grad,
        head_bias_grad,
    )


def solution(mesh):
    return jax.shard_map(
        on_device,
        mesh=mesh,
        in_specs=(
            P("grp", "fft", None, None),
            P("grp", "fft", None, None),
            P(),
            P(),
            P(),
            P(),
            P(),
            P(),
            P(),
            P(),
            P(),
        ),
        out_specs=(
            P("grp", "fft", None, None),
            P(("grp", "fft"), None),
            P(),
            P(),
            P(),
            P(),
            P(),
            P(),
        ),
        check_vma=False,
    )
```

```python
import jax
import jax.numpy as jnp
import ml_dtypes
import numpy as np
from jax import lax
from jax.experimental import pallas as pl
from jax.experimental.pallas import tpu as pltpu
from jax.sharding import PartitionSpec as P

EPSILON = 1e-05
SHRINK = 0.01
CHUNKS = 2
VMEM_BYTES = 24 * 1024 * 1024
SLOTS = 6
SHARD, FIRST_ROW, GROUP, SIDES = 0, 1, 2, 3
ROUTES = 3
HALF = jnp.bfloat16
FULL = jnp.float32


def dft_tables(cells):
    levels, factors = [], []
    for side, scale in ((cells, 1.1305), (cells // 2, 1.8633), (cells // 4, 1.0)):
        k = np.arange(cells)
        inside = (k < side).astype(np.float64)
        keep = inside[:, None] * inside[None, :]
        angle = 2.0 * np.pi * ((k[:, None] * k[None, :]) % side) / side
        one = np.exp(-1j * angle) * keep / np.sqrt(side)
        two = np.kron(one, one)
        table = np.concatenate([two.real, two.imag], axis=0)
        table[np.abs(table) < 1e-12] = 0.0
        rounded = (table * scale).astype(np.float32).astype(ml_dtypes.bfloat16)
        held = rounded.astype(np.float64)
        factors.append(float(np.sum(table * table) / np.sum(table * held)))
        levels.append(rounded)
    return np.stack(levels), factors


def dot(left, right):
    return jnp.dot(left, right, preferred_element_type=FULL)


def dot_tn(left, right):
    return lax.dot_general(left, right, (((0,), (0,)), ((), ())), preferred_element_type=FULL)


def dot_nt(left, right):
    return lax.dot_general(left, right, (((1,), (1,)), ((), ())), preferred_element_type=FULL)


def params(limit=VMEM_BYTES):
    return pltpu.CompilerParams(vmem_limit_bytes=limit)


def token_sides(scal_ref, first, count, per_sample, cells):
    token = lax.broadcasted_iota(jnp.int32, (count * per_sample, 1), 0)
    sample = token // per_sample
    side = jnp.zeros_like(token)
    for i in range(count):
        side = jnp.where(sample == i, scal_ref[SIDES + first + i], side)
    row = scal_ref[FIRST_ROW] + (token % per_sample) // cells
    col = token % cells
    valid = jnp.where((row < side) & (col < side), 1.0, 0.0).astype(FULL)
    return side, valid


def whole(shape):
    return pl.BlockSpec(tuple(shape), lambda i, s: (0,) * len(shape))


def part_of(scal_ref, k, size):
    at = jnp.bitwise_xor(scal_ref[SHARD], k)
    return pl.ds(pl.multiple_of(at * size, size), size)


def fill_lanes(scal_ref, refs, held):
    share = refs[0].shape[-1]
    for k, ref in enumerate(refs):
        held[:, part_of(scal_ref, k, share)] = ref[...].reshape(held.shape[0], share)


def fill_rows(scal_ref, refs, held):
    rows = refs[0].shape[1]
    for k, ref in enumerate(refs):
        held[:, part_of(scal_ref, k, rows), :] = ref[...]


def split_lanes(scal_ref, held, refs):
    share = refs[0].shape[-1]
    for k, ref in enumerate(refs):
        ref[...] = held[:, part_of(scal_ref, k, share)].reshape(ref.shape)


def split_rows(scal_ref, held, refs):
    rows = refs[0].shape[1]
    for k, ref in enumerate(refs):
        ref[...] = held[:, part_of(scal_ref, k, rows), :]


def embed(scal, patches, embed_w, embed_b, gain, firsts, count, per_sample, cells, shards, groups):
    rows, depth = patches.shape
    block = depth // groups
    width = embed_w.shape[1]
    share = width // shards
    chunk_rows = count * per_sample
    chunks = len(firsts)
    steps = 4
    tile = depth // steps

    def body(scal_ref, x_ref, w_ref, b_ref, gain_ref, emb_ref, norm_ref, stat_ref, *refs):
        (send_ref, keep_ref), outs, acc = refs[:2], refs[2:-1], refs[-1]
        step = pl.program_id(0)
        turned = x_ref[...].T
        for i in range(tile // block):
            values = turned[i * block : (i + 1) * block]
            away = (scal_ref[GROUP] + i) % 2

            @pl.when(away == 1)
            def _(i=i, values=values):
                send_ref[i // 2] = values

            @pl.when(away == 0)
            def _(i=i, values=values):
                keep_ref[i // 2] = values

        part = dot(x_ref[...], w_ref[...])

        @pl.when(step == 0)
        def _():
            acc[...] = part

        @pl.when(step > 0)
        def _():
            acc[...] += part

        @pl.when(step == steps - 1)
        def _():
            for c, first in enumerate(firsts):
                at = slice(c * chunk_rows, (c + 1) * chunk_rows)
                _, valid = token_sides(scal_ref, first, count, per_sample, cells)
                embedded = ((acc[at] + b_ref[...]) * valid).astype(HALF)
                emb_ref[at] = embedded
                values = embedded.astype(FULL)
                mean = jnp.mean(values, axis=-1, keepdims=True)
                centered = values - mean
                inv_std = lax.rsqrt(jnp.mean(centered * centered, axis=-1, keepdims=True) + EPSILON)
                norm_ref[at] = (centered * inv_std * gain_ref[...]).astype(HALF)
                stat_ref[at, :128] = jnp.broadcast_to(mean, (chunk_rows, 128))
                stat_ref[at, 128:] = jnp.broadcast_to(inv_std, (chunk_rows, 128))
                for k in range(shards):
                    piece = norm_ref[at, part_of(scal_ref, k, share)]
                    outs[c * shards + k][...] = piece.reshape(count, per_sample, share)

    piece = (count, per_sample, share)
    turned_spec = pl.BlockSpec((tile // (2 * block), block, rows), lambda k, s: (k, 0, 0))
    turned_shape = jax.ShapeDtypeStruct((groups // 2, block, rows), HALF)
    emb, normed, stats, send, keep, *pieces = pl.pallas_call(
        body,
        grid_spec=pltpu.PrefetchScalarGridSpec(
            num_scalar_prefetch=1,
            grid=(steps,),
            in_specs=[
                pl.BlockSpec((rows, tile), lambda k, s: (0, k)),
                pl.BlockSpec((tile, width), lambda k, s: (k, 0)),
                whole((1, width)),
                whole((1, width)),
            ],
            out_specs=[whole((rows, width)), whole((rows, width)), whole((rows, 256)), turned_spec, turned_spec]
            + [whole(piece)] * (shards * chunks),
            scratch_shapes=[pltpu.VMEM((rows, width), FULL)],
        ),
        out_shape=[
            jax.ShapeDtypeStruct((rows, width), HALF),
            jax.ShapeDtypeStruct((rows, width), HALF),
            jax.ShapeDtypeStruct((rows, 256), FULL),
            turned_shape,
            turned_shape,
        ]
        + [jax.ShapeDtypeStruct(piece, HALF)] * (shards * chunks),
        compiler_params=params(60 * 1024 * 1024),
        cost_estimate=pl.CostEstimate(
            flops=2 * rows * depth * width, bytes_accessed=2 * depth * (rows + width), transcendentals=0
        ),
        name="embed",
    )(scal, patches, embed_w, embed_b, gain)
    return emb, normed, stats, send, keep, [pieces[c * shards : (c + 1) * shards] for c in range(chunks)]


def to_blocks(values, blocks, width):
    half = values.shape[0] // 2
    return [
        jnp.concatenate(
            [values[:half, b * width : (b + 1) * width], values[half:, b * width : (b + 1) * width]], axis=1
        )
        for b in range(blocks)
    ]


def from_blocks(parts, width):
    real = jnp.concatenate([p[:, :width] for p in parts], axis=1)
    imag = jnp.concatenate([p[:, width:] for p in parts], axis=1)
    return real, imag


def table_factor(level, factors):
    return jnp.where(level == 0, factors[0], jnp.where(level == 1, factors[1], factors[2])).astype(FULL)


def table_back(table_ref, level, tops, rests, factor):
    size = table_ref.shape[2]
    total = None
    for at, (top, rest) in enumerate(zip(tops, rests)):
        table = table_ref[level, at * size : (at + 1) * size]
        part = dot(table, top) + dot(table, rest)
        total = part if total is None else total + part
    return total * factor


def two_terms(values):
    top = values.astype(HALF)
    return top, (values - top.astype(FULL)).astype(HALF)


def complex_weights(w_ref, held, blocks, width):
    for layer in range(2):
        for b in range(blocks):
            real, imag = w_ref[layer, 0, b], w_ref[layer, 1, b]
            held[layer, b, :width, :width] = real
            held[layer, b, :width, width:] = imag
            held[layer, b, width:, :width] = -imag
            held[layer, b, width:, width:] = real


def spectral_chunk(scal, table, factors, pieces, spec_w, spec_b, first):
    shards = len(pieces)
    count, per_sample, share = pieces[0].shape
    size = shards * per_sample
    width = spec_w.shape[-1]
    blocks = share // width
    wide = 2 * width

    def body(scal_ref, t_ref, w_ref, b_ref, *refs):
        ins, outs = refs[:shards], refs[shards : 2 * shards]
        spec_ref, hid_ref, fil_ref, weights, held = refs[2 * shards :]

        def bias(layer, b):
            row = pl.ds(scal_ref[SHARD] * blocks + b, 1)
            return jnp.concatenate([b_ref[layer, 0, row], b_ref[layer, 1, row]], axis=1)

        complex_weights(w_ref, weights, blocks, width)
        fill_rows(scal_ref, ins, held)
        levels = [scal_ref[SIDES + SLOTS + first + i] for i in range(count)]
        for i, level in enumerate(levels):
            spectrum = (dot(t_ref[level], held[i]) * table_factor(level, factors)).astype(HALF)
            for b, entry in enumerate(to_blocks(spectrum, blocks, width)):
                spec_ref[b, i * size : (i + 1) * size] = entry
        kept = []
        for b in range(blocks):
            pre_one = dot(spec_ref[b], weights[0, b]) + bias(0, b)
            hidden = jnp.maximum(pre_one, 0.0).astype(HALF)
            hid_ref[b] = hidden
            pre_two = dot(hidden, weights[1, b]) + bias(1, b)
            filtered = jnp.where(
                pre_two > SHRINK, pre_two - SHRINK, jnp.where(pre_two < -SHRINK, pre_two + SHRINK, 0.0)
            )
            top, rest = two_terms(filtered)
            fil_ref[b] = top
            kept.append((top, rest))
        for i, level in enumerate(levels):
            at = slice(i * size, (i + 1) * size)
            tops = from_blocks([top[at] for top, _ in kept], width)
            rests = from_blocks([rest[at] for _, rest in kept], width)
            held[i] = table_back(t_ref, level, tops, rests, table_factor(level, factors)).astype(HALF)
        split_rows(scal_ref, held, outs)

    saved = (blocks, count * size, wide)
    outs = pl.pallas_call(
        body,
        grid_spec=pltpu.PrefetchScalarGridSpec(
            num_scalar_prefetch=1,
            grid=(1,),
            in_specs=[
                whole(table.shape),
                pl.BlockSpec((2, 2, blocks, width, width), lambda i, s: (0, 0, s[SHARD], 0, 0)),
                whole(spec_b.shape),
            ]
            + [whole(pieces[0].shape)] * shards,
            out_specs=[whole(pieces[0].shape)] * shards + [whole(saved)] * 3,
            scratch_shapes=[pltpu.VMEM((2, blocks, wide, wide), HALF), pltpu.VMEM((count, size, share), HALF)],
        ),
        out_shape=[jax.ShapeDtypeStruct(pieces[0].shape, HALF)] * shards + [jax.ShapeDtypeStruct(saved, HALF)] * 3,
        compiler_params=params(),
        cost_estimate=pl.CostEstimate(
            flops=count * size * share * size * 14, bytes_accessed=count * size * share * 16, transcendentals=0
        ),
        name="spectral",
    )(scal, table, spec_w, spec_b, *pieces)
    return outs[:shards], outs[shards:]


def head_chunk(scal, embedded, normed, mixed, targets, head_w, head_b, first, samples, cells):
    shards = len(mixed)
    count, per_sample, share = mixed[0].shape
    rows = count * per_sample
    width, outs = head_w.shape
    at = first // count
    scale_root = float(np.sqrt(np.float32(samples)))

    def body(scal_ref, emb_ref, norm_ref, tgt_ref, w_ref, b_ref, *refs):
        mix_refs, (pred_ref, res_ref, up_ref, bias_ref, held) = refs[:shards], refs[shards:]
        fill_lanes(scal_ref, mix_refs, held)
        side, valid = token_sides(scal_ref, first, count, per_sample, cells)
        updated = (emb_ref[...].astype(FULL) + norm_ref[...].astype(FULL) + held[...].astype(FULL)).astype(HALF)
        output = (dot(updated, w_ref[...]) + b_ref[...]) * valid
        pred_ref[...] = output.astype(HALF).reshape(pred_ref.shape)
        scale = 2.0 / (side.astype(FULL) * scale_root)
        residual = (scale * valid * (output - tgt_ref[...].astype(FULL))).astype(HALF)
        res_ref[...] = residual.reshape(res_ref.shape)
        up_ref[...] = updated
        total = jnp.sum(residual.astype(FULL), axis=0, keepdims=True)
        bias_ref[...] = jnp.broadcast_to(total, bias_ref.shape)

    token_shape = (count, per_sample, outs)
    return pl.pallas_call(
        body,
        grid_spec=pltpu.PrefetchScalarGridSpec(
            num_scalar_prefetch=1,
            grid=(1,),
            in_specs=[
                pl.BlockSpec((rows, width), lambda i, s: (at, 0)),
                pl.BlockSpec((rows, width), lambda i, s: (at, 0)),
                pl.BlockSpec((rows, outs), lambda i, s: (at, 0)),
                whole((width, outs)),
                whole((1, outs)),
            ]
            + [whole(mixed[0].shape)] * shards,
            out_specs=[whole(token_shape), whole(token_shape), whole((rows, width)), whole((8, outs))],
            scratch_shapes=[pltpu.VMEM((rows, width), HALF)],
        ),
        out_shape=[
            jax.ShapeDtypeStruct(token_shape, HALF),
            jax.ShapeDtypeStruct(token_shape, HALF),
            jax.ShapeDtypeStruct((rows, width), HALF),
            jax.ShapeDtypeStruct((8, outs), FULL),
        ],
        compiler_params=params(),
        cost_estimate=pl.CostEstimate(
            flops=2 * rows * width * outs, bytes_accessed=rows * width * 4 + width * outs * 6, transcendentals=0
        ),
        name="head",
    )(scal, embedded, normed, targets, head_w, head_b, *mixed)


def head_gradient(updated, residual):
    width = updated[0].shape[1]
    outs = residual[0].shape[-1]
    count = len(updated)

    def body(*refs):
        total = None
        for up_ref, res_ref in zip(refs[:count], refs[count : 2 * count]):
            part = dot_tn(up_ref[...], res_ref[...].reshape(up_ref.shape[0], outs))
            total = part if total is None else total + part
        refs[-1][...] = total.astype(HALF)

    return pl.pallas_call(
        body,
        out_shape=jax.ShapeDtypeStruct((width, outs), HALF),
        compiler_params=params(),
        cost_estimate=pl.CostEstimate(
            flops=2 * count * updated[0].size * outs, bytes_accessed=2 * count * updated[0].size, transcendentals=0
        ),
        name="head_gradient",
    )(*updated, *residual)


def spectral_back_chunk(scal, table, factors, residual, head_w, spec_w, saved, first, before, last):
    shards = len(residual)
    count, per_sample, outs = residual[0].shape
    size = shards * per_sample
    width = spec_w.shape[-1]
    wide = 2 * width
    share = head_w.shape[0] // shards
    blocks = share // width
    raw_shape = (2, blocks, wide, wide)
    bias_shape = (2 * blocks, wide)
    has_before = before is not None

    def body(scal_ref, t_ref, h_ref, w_ref, spec_ref, hid_ref, fil_ref, *refs):
        ins, refs = refs[:shards], refs[shards:]
        if has_before:
            (old_ref, old_bias_ref), refs = refs[:2], refs[2:]
        pieces, (grad_ref, bias_ref, weights, held, gathered) = refs[:shards], refs[shards:]

        def weight_sums(layer, b, inputs, grads):
            raw = dot_tn(inputs, grads)
            sums = jnp.sum(grads.astype(FULL), axis=0, keepdims=True)
            at = layer * blocks + b
            if has_before:
                raw = raw + old_ref[layer, b]
                sums = sums + old_bias_ref[at : at + 1]
            bias_ref[at : at + 1] = sums
            if not last:
                grad_ref[layer, b] = raw
                return
            real = raw[:width, :width] + raw[width:, width:]
            imag = raw[:width, width:] - raw[width:, :width]
            grad_ref[at * width : (at + 1) * width] = jnp.concatenate([real, imag], axis=1).astype(HALF)

        complex_weights(w_ref, weights, blocks, width)
        fill_rows(scal_ref, ins, gathered)
        levels = [scal_ref[SIDES + SLOTS + first + i] for i in range(count)]
        updated_grad = dot_nt(gathered[...].reshape(count * size, outs), h_ref[...]).astype(HALF)
        entries = []
        for i, level in enumerate(levels):
            filtered_grad = dot(t_ref[level], updated_grad[i * size : (i + 1) * size]) * table_factor(level, factors)
            entries.append(to_blocks(filtered_grad, blocks, width))
        kept = []
        for b in range(blocks):
            entry = jnp.concatenate([e[b] for e in entries], axis=0)
            two_grad = jnp.where(fil_ref[b].astype(FULL) != 0.0, entry, 0.0).astype(HALF)
            hidden = hid_ref[b]
            hidden_grad = dot_nt(two_grad, weights[1, b])
            one_grad = jnp.where(hidden.astype(FULL) > 0.0, hidden_grad, 0.0).astype(HALF)
            kept.append(two_terms(dot_nt(one_grad, weights[0, b])))
            weight_sums(1, b, hidden, two_grad)
            weight_sums(0, b, spec_ref[b], one_grad)
        for i, level in enumerate(levels):
            at = slice(i * size, (i + 1) * size)
            tops = from_blocks([top[at] for top, _ in kept], width)
            rests = from_blocks([rest[at] for _, rest in kept], width)
            held[i] = table_back(t_ref, level, tops, rests, table_factor(level, factors)).astype(HALF)
        split_rows(scal_ref, held, pieces)

    piece = (count, per_sample, share)
    if last:
        grad_out = jax.ShapeDtypeStruct((2 * blocks * width, wide), HALF)
    else:
        grad_out = jax.ShapeDtypeStruct(raw_shape, FULL)
    result = pl.pallas_call(
        body,
        grid_spec=pltpu.PrefetchScalarGridSpec(
            num_scalar_prefetch=1,
            grid=(1,),
            in_specs=[
                whole(table.shape),
                pl.BlockSpec((share, outs), lambda i, s: (s[SHARD], 0)),
                pl.BlockSpec((2, 2, blocks, width, width), lambda i, s: (0, 0, s[SHARD], 0, 0)),
            ]
            + [whole(saved[0].shape)] * 3
            + [whole(residual[0].shape)] * shards
            + ([whole(raw_shape), whole(bias_shape)] if has_before else []),
            out_specs=[whole(piece)] * shards + [whole(grad_out.shape), whole(bias_shape)],
            scratch_shapes=[
                pltpu.VMEM((2, blocks, wide, wide), HALF),
                pltpu.VMEM((count, size, share), HALF),
                pltpu.VMEM((count, size, outs), HALF),
            ],
        ),
        out_shape=[jax.ShapeDtypeStruct(piece, HALF)] * shards
        + [grad_out, jax.ShapeDtypeStruct(bias_shape, FULL)],
        compiler_params=params(),
        cost_estimate=pl.CostEstimate(
            flops=count * size * share * size * 20, bytes_accessed=count * size * share * 16, transcendentals=0
        ),
        name="spectral_back",
    )(scal, table, head_w, spec_w, *saved, *residual, *(before or ()))
    return result[:shards], result[shards:]


def embedded_back_chunk(scal, embedded, stats, residual, head_w, gain, spec_grad, first, cells):
    shards = len(spec_grad)
    count, per_sample, share = spec_grad[0].shape
    rows = count * per_sample
    width, outs = head_w.shape
    at = first // count

    def body(scal_ref, emb_ref, stat_ref, res_ref, w_ref, gain_ref, *refs):
        grad_refs, (out_ref, sums_ref, held) = refs[:shards], refs[shards:]
        fill_lanes(scal_ref, grad_refs, held)
        _, valid = token_sides(scal_ref, first, count, per_sample, cells)
        inv_std = stat_ref[:, 128:129]
        unit = (emb_ref[...].astype(FULL) - stat_ref[:, 0:1]) * inv_std
        direct = dot_nt(res_ref[...].reshape(rows, outs), w_ref[...]).astype(HALF).astype(FULL)
        normed_grad = held[...].astype(FULL) + direct
        gain_grad = jnp.sum(normed_grad * unit, axis=0, keepdims=True)
        unit_grad = normed_grad * gain_ref[...]
        mean_grad = jnp.mean(unit_grad, axis=-1, keepdims=True)
        mean_cross = jnp.mean(unit_grad * unit, axis=-1, keepdims=True)
        input_grad = inv_std * (unit_grad - mean_grad - unit * mean_cross)
        result = ((input_grad + direct) * valid).astype(HALF)
        out_ref[...] = result
        bias_grad = jnp.sum(result.astype(FULL), axis=0, keepdims=True)
        sums_ref[0:4] = jnp.broadcast_to(gain_grad, (4, width))
        sums_ref[4:8] = jnp.broadcast_to(bias_grad, (4, width))

    return pl.pallas_call(
        body,
        grid_spec=pltpu.PrefetchScalarGridSpec(
            num_scalar_prefetch=1,
            grid=(1,),
            in_specs=[
                pl.BlockSpec((rows, width), lambda i, s: (at, 0)),
                pl.BlockSpec((rows, 256), lambda i, s: (at, 0)),
                whole((count, per_sample, outs)),
                whole((width, outs)),
                whole((1, width)),
            ]
            + [whole(spec_grad[0].shape)] * shards,
            out_specs=[whole((rows, width)), whole((8, width))],
            scratch_shapes=[pltpu.VMEM((rows, width), HALF)],
        ),
        out_shape=[jax.ShapeDtypeStruct((rows, width), HALF), jax.ShapeDtypeStruct((8, width), FULL)],
        compiler_params=params(),
        cost_estimate=pl.CostEstimate(
            flops=2 * rows * width * outs, bytes_accessed=rows * width * 6, transcendentals=0
        ),
        name="embedded_back",
    )(scal, embedded, stats, residual, head_w, gain, *spec_grad)


def embed_grad_parts(scal, turned, grads, groups, away):
    pairs, block, tokens = turned[0].shape
    chunk_rows, width = grads[0].shape
    half = width // 2
    top = pairs // 2
    count = len(turned)
    depth = tokens * count

    def relative(unit):
        return jnp.where(unit < top, 2 * unit + away, unit - top + away * top)

    def body(scal_ref, *refs):
        turned_refs, grad_refs = refs[:count], refs[count : count + len(grads)]
        left_ref, right_ref, held = refs[count + len(grads) :]
        unit = pl.program_id(0)

        @pl.when(unit % top == 0)
        def _():
            for i, ref in enumerate(grad_refs):
                held[i * chunk_rows : (i + 1) * chunk_rows] = ref[...]

        rows = jnp.concatenate([ref[0] for ref in turned_refs], axis=1)
        total = dot(rows, held[...]).astype(HALF)

        @pl.when(unit < top)
        def _():
            left_ref[0] = total

        @pl.when(unit >= top)
        def _():
            right_ref[0] = total

    shape = (top, block, half)
    return pl.pallas_call(
        body,
        grid_spec=pltpu.PrefetchScalarGridSpec(
            num_scalar_prefetch=1,
            grid=(pairs,),
            in_specs=[
                pl.BlockSpec((1, block, tokens), lambda i, s: (jnp.bitwise_xor(s[GROUP] // 2, relative(i)), 0, 0))
                for _ in turned
            ]
            + [pl.BlockSpec((chunk_rows, half), lambda i, s: (0, i // top)) for _ in grads],
            out_specs=[
                pl.BlockSpec((1, block, half), lambda i, s: (jnp.minimum(i, top - 1), 0, 0)),
                pl.BlockSpec((1, block, half), lambda i, s: (jnp.maximum(i - top, 0), 0, 0)),
            ],
            scratch_shapes=[pltpu.VMEM((depth, half), HALF)],
        ),
        out_shape=[jax.ShapeDtypeStruct(shape, HALF)] * 2,
        compiler_params=params(),
        cost_estimate=pl.CostEstimate(
            flops=depth * pairs * block * width,
            bytes_accessed=pairs * block * (2 * depth + width) + depth * width,
            transcendentals=0,
        ),
        name="embed_grad",
    )(scal, *turned, *grads)


def swap_bit(values, bit, groups):
    return lax.ppermute(values, "grp", [(g, g ^ (1 << bit)) for g in range(groups)])


def across(pieces):
    shards = len(pieces)
    return [pieces[0]] + [
        lax.ppermute(pieces[k], "fft", [(z, z ^ k) for z in range(shards)]) for k in range(1, shards)
    ]


def add_half(left, right):
    return (left.astype(FULL) + right.astype(FULL)).astype(HALF)


def scatter_start(received, kept, groups):
    bits = groups.bit_length() - 1
    ends = []
    for first, keep, order, low in (
        (received[0], kept[0], list(range(2, bits)), True),
        (received[1], kept[1], list(range(bits - 2, 0, -1)), False),
    ):
        total = add_half(keep, first)
        for bit in order:
            count, block, width = total.shape
            if low:
                split = total.reshape(count // 2, 2, block, width)
                keep, send = split[:, 0], split[:, 1]
            else:
                split = total.reshape(2, count // 2, block, width)
                keep, send = split[0], split[1]
            total = add_half(keep, swap_bit(send, bit, groups))
        ends.append(total[0])
    return ends


def scatter_step(part, bit, shards, shard_at):
    split = part.reshape(part.shape[0] // 2, 2, *part.shape[1:])
    mine = (shard_at // bit) % 2
    keep = lax.dynamic_index_in_dim(split, mine, 1, keepdims=False)
    send = lax.dynamic_index_in_dim(split, 1 - mine, 1, keepdims=False)
    received = lax.ppermute(send, "fft", [(z, z ^ bit) for z in range(shards)])
    return keep.astype(FULL) + received.astype(FULL)


def from_same_core(values, groups):
    return [values] + [
        lax.ppermute(values, "grp", [(g, g ^ k) for g in range(groups)]) for k in range(2, groups, 2)
    ]


def hi_lo(values):
    high = values.astype(HALF)
    return jnp.concatenate([high, (values - high.astype(FULL)).astype(HALF)], axis=0)


def from_hi_lo(values):
    half = values.shape[0] // 2
    values = values.astype(FULL)
    return values[:half] + values[half:]


def one_step(body, name, operands, out_shape):
    return pl.pallas_call(
        body,
        grid_spec=pltpu.PrefetchScalarGridSpec(
            num_scalar_prefetch=1,
            grid=(1,),
            in_specs=[whole(o.shape) for o in operands[1:]],
            out_specs=[whole(o.shape) for o in out_shape],
        ),
        out_shape=out_shape,
        compiler_params=params(),
        name=name,
    )(*operands)


def packed(routes, head_grad, spec_grad, predicted, groups):
    outs = head_grad.shape[1]
    head_rows, spec_rows = head_grad.shape[0] // groups, spec_grad.shape[0] // groups
    count, per_sample, _ = predicted[0].shape

    def body(routes_ref, head_ref, spec_ref, *refs):
        pred_refs, out_ref = refs[:-1], refs[-1]
        for g in range(groups):
            out_ref[g, :head_rows] = head_ref[g * head_rows : (g + 1) * head_rows]
            out_ref[g, head_rows : head_rows + spec_rows] = spec_ref[g * spec_rows : (g + 1) * spec_rows]
            chosen = routes_ref[ROUTES + g]
            for c, ref in enumerate(pred_refs):

                @pl.when(chosen // count == c)
                def _(g=g, c=c, ref=ref, chosen=chosen):
                    out_ref[g, head_rows + spec_rows :] = ref[chosen - c * count]

    shape = (groups, head_rows + spec_rows + per_sample, outs)
    return one_step(
        body, "packed", (routes, head_grad, spec_grad, *predicted), [jax.ShapeDtypeStruct(shape, HALF)]
    )[0]


def group_sums(routes, moved, spec_bias, head_sums, row_sums, slot_count, per_sample):
    groups, rows, outs = moved.shape
    weight_rows = rows - per_sample
    own_rows = spec_bias.shape[0]
    chunks = len(head_sums)
    parts = row_sums[0].shape[1] // outs
    spare = 16 - own_rows - 2 * parts - 1

    def body(routes_ref, moved_ref, bias_ref, *refs):
        head_refs, row_refs, (out_ref, pred_ref) = refs[:chunks], refs[chunks : 2 * chunks], refs[2 * chunks :]
        total = moved_ref[0, :weight_rows].astype(FULL)
        for g in range(1, groups):
            total = total + moved_ref[g, :weight_rows].astype(FULL)
        out_ref[:weight_rows] = total.astype(HALF)
        lines = [bias_ref[...]]
        for row in (0, 4):
            line = sum(ref[row : row + 1] for ref in row_refs)
            lines += [line[:, i * outs : (i + 1) * outs] for i in range(parts)]
        lines += [sum(ref[0:1] for ref in head_refs), jnp.zeros((spare, outs), FULL)]
        out_ref[weight_rows:] = hi_lo(jnp.concatenate(lines, axis=0))
        for i in range(slot_count):
            pred_ref[i] = moved_ref[routes_ref[ROUTES + groups + i], weight_rows:]

    return one_step(
        body,
        "group_sums",
        (routes, moved, spec_bias, *head_sums, *row_sums),
        [
            jax.ShapeDtypeStruct((weight_rows + 32, outs), HALF),
            jax.ShapeDtypeStruct((slot_count, per_sample, outs), HALF),
        ],
    )


def shard_sums(routes, rows, head_rows, spec_rows, own_rows):
    shards = len(rows)
    outs = rows[0].shape[1]
    small_rows = 32

    def body(routes_ref, *refs):
        ins, out_ref = refs[:-1], refs[-1]
        total = sum(ref[:head_rows].astype(FULL) for ref in ins)
        out_ref[:head_rows] = total.astype(HALF)
        for k, ref in enumerate(ins):
            at = head_rows + k * spec_rows
            out_ref[at : at + spec_rows] = ref[head_rows : head_rows + spec_rows]
        smalls = [from_hi_lo(ref[head_rows + spec_rows :]) for ref in ins]
        lines = []
        for z in range(shards):
            here = [jnp.bitwise_xor(routes_ref[SHARD], k) == z for k in range(shards)]
            lines.append(sum(jnp.where(h, v[:own_rows], 0.0) for h, v in zip(here, smalls)))
        lines.append(sum(v[own_rows:] for v in smalls))
        have = shards * own_rows + 16 - own_rows
        lines.append(jnp.zeros((small_rows - have, outs), FULL))
        out_ref[head_rows + shards * spec_rows :] = hi_lo(jnp.concatenate(lines, axis=0))

    shape = (head_rows + shards * spec_rows + 2 * small_rows, outs)
    return one_step(body, "shard_sums", (routes, *rows), [jax.ShapeDtypeStruct(shape, HALF)])[0]


def assembled(scal, gathered, head_rows, shards, blocks, width):
    groups = len(gathered)
    total_blocks = shards * blocks
    spec_rows = 2 * blocks * width // groups
    small_at = head_rows + shards * spec_rows
    small_rows = (gathered[0].shape[0] - small_at) // 2

    def body(scal_ref, *refs):
        ins, (head_ref, spec_ref, bias_ref, gain_ref, embed_ref, out_ref) = refs[:groups], refs[groups:]
        small = None
        for k, ref in enumerate(ins):
            group = jnp.bitwise_xor(scal_ref[GROUP], k)
            at = pl.ds(pl.multiple_of(group * head_rows, head_rows), head_rows)
            head_ref[at, :] = ref[:head_rows].astype(FULL)
            start = group * spec_rows
            layer, b = start // (blocks * width), (start // width) % blocks
            rows = pl.ds(pl.multiple_of(start % width, spec_rows), spec_rows)
            for j in range(shards):
                values = ref[head_rows + j * spec_rows : head_rows + (j + 1) * spec_rows].astype(FULL)
                z = jnp.bitwise_xor(scal_ref[SHARD], j)
                spec_ref[layer, 0, z * blocks + b, rows] = values[:, :width]
                spec_ref[layer, 1, z * blocks + b, rows] = values[:, width:]
            part = ref[small_at : small_at + small_rows].astype(FULL) + ref[small_at + small_rows :].astype(FULL)
            small = part if small is None else small + part
        for z in range(shards):
            for layer in range(2):
                for b in range(blocks):
                    row = (z * 2 + layer) * blocks + b
                    for p in range(2):
                        bias_ref[layer, p, z * blocks + b : z * blocks + b + 1] = small[
                            row : row + 1, p * width : (p + 1) * width
                        ]
        row = shards * 2 * blocks
        quarter = gain_ref.shape[1] // (2 * width)
        for ref in (gain_ref, embed_ref):
            for i in range(quarter):
                ref[:, i * 2 * width : (i + 1) * 2 * width] = small[row + i : row + i + 1]
            row += quarter
        out_ref[...] = small[row : row + 1]

    out_shape = [
        jax.ShapeDtypeStruct((groups * head_rows, 2 * width), FULL),
        jax.ShapeDtypeStruct((2, 2, total_blocks, width, width), FULL),
        jax.ShapeDtypeStruct((2, 2, total_blocks, width), FULL),
        jax.ShapeDtypeStruct((1, groups * head_rows), FULL),
        jax.ShapeDtypeStruct((1, groups * head_rows), FULL),
        jax.ShapeDtypeStruct((1, 2 * width), FULL),
    ]
    return pl.pallas_call(
        body,
        grid_spec=pltpu.PrefetchScalarGridSpec(
            num_scalar_prefetch=1,
            grid=(1,),
            in_specs=[whole(gathered[0].shape)] * groups,
            out_specs=[whole(o.shape) for o in out_shape],
        ),
        out_shape=out_shape,
        compiler_params=params(),
        name="assembled",
    )(scal, *gathered)


def prediction_routes(dest_group, group_at, groups, slot_count):
    own_dest = lax.dynamic_slice_in_dim(dest_group, group_at * slot_count, slot_count)
    loaders = jnp.arange(groups, dtype=jnp.int32)
    slots = jnp.arange(slot_count, dtype=jnp.int32)
    chosen = jnp.sum(jnp.where(own_dest[None, :] == loaders[:, None], slots[None, :], 0), axis=1)
    holds = jnp.any(dest_group.reshape(groups, slot_count) == group_at, axis=1)
    rank = jnp.sum(jnp.where(holds[None, :] & (loaders[None, :] < loaders[:, None]), 1, 0), axis=1)
    sources = jnp.sum(jnp.where(holds[None, :] & (rank[None, :] == slots[:, None]), loaders[None, :], 0), axis=1)
    return jnp.concatenate([chosen, sources]).astype(jnp.int32)


def on_device(
    patches, targets, grid_side, dest_group, embed_w, embed_b, gain, spec_w, spec_b, head_w, head_b
):
    slot_count, row_count, cells, depth = patches.shape
    samples = dest_group.shape[0]
    groups = lax.axis_size("grp")
    shards = lax.axis_size("fft")
    group_at = lax.axis_index("grp").astype(jnp.int32)
    shard_at = lax.axis_index("fft").astype(jnp.int32)
    outs = targets.shape[-1]
    per_sample = row_count * cells
    count = slot_count // CHUNKS
    firsts = [c * count for c in range(CHUNKS)]
    assert slot_count == SLOTS

    sides = lax.dynamic_slice_in_dim(grid_side, group_at * slot_count, slot_count)
    level = jnp.where(sides == cells, 0, jnp.where(sides == cells // 2, 1, 2)).astype(jnp.int32)
    place = jnp.stack([shard_at, shard_at * row_count, group_at])
    scal = jnp.concatenate([place, sides, level])
    routes = jnp.concatenate([place, prediction_routes(dest_group, group_at, groups, slot_count)])
    table_values, factors = dft_tables(cells)
    table = jnp.asarray(table_values)
    flat_patches = patches.reshape(-1, depth)
    flat_targets = targets.reshape(-1, outs)
    gain_row, embed_b_row, head_b_row = gain[None], embed_b[None], head_b[None]

    embedded, normed, stats, turned_send, turned_keep, pieces = embed(
        scal, flat_patches, embed_w, embed_b_row, gain_row, firsts, count, per_sample, cells, shards, groups
    )
    moved = [across(p) for p in pieces]
    mixed, saved = [], []
    for first, values in zip(firsts, moved):
        out, rest = spectral_chunk(scal, table, factors, values, spec_w, spec_b, first)
        mixed.append(across(out))
        saved.append(rest)
    predicted, residual, updated, head_sums, gathered = [], [], [], [], []
    for first, mix in zip(firsts, mixed):
        pred, res, up, sums = head_chunk(
            scal, embedded, normed, mix, flat_targets, head_w, head_b_row, first, samples, cells
        )
        predicted.append(pred)
        residual.append(res)
        updated.append(up)
        head_sums.append(sums)
        gathered.append(across([res] * shards))
    head_grad, gathered[0] = lax.optimization_barrier((head_gradient(updated, residual), gathered[0]))
    spec_back, sums = [], None
    for first, res, rest in zip(firsts, gathered, saved):
        values, sums = spectral_back_chunk(
            scal, table, factors, res, head_w, spec_w, rest, first, sums, first == firsts[-1]
        )
        if first == firsts[-1]:
            values, turned_send = lax.optimization_barrier((values, turned_send))
        spec_back.append(across(values))
    turned = [turned_keep, swap_bit(turned_send, 0, groups)]
    spec_grad, spec_bias = sums
    width = spec_w.shape[-1]
    blocks = spec_w.shape[2] // shards
    head_rows = head_w.shape[0] // groups
    own_grads, other_grads, row_sums = [], [], []
    for first, res, back in zip(firsts, residual, spec_back):
        if first == firsts[-1]:
            back, _ = lax.optimization_barrier((back, outgoing_sums))
        grad, row_sum = embedded_back_chunk(scal, embedded, stats, res, head_w, gain_row, back, first, cells)
        if first == firsts[0]:
            grad, head_grad, spec_grad = lax.optimization_barrier((grad, head_grad, spec_grad))
            outgoing_sums = packed(routes, head_grad, spec_grad, predicted, groups)
            weight_sums = lax.all_to_all(outgoing_sums, "grp", split_axis=0, concat_axis=0, tiled=True)
        own_grads.append(grad)
        other_grads.append(swap_bit(grad, 0, groups))
        row_sums.append(row_sum)
    grads = own_grads + other_grads
    sent = embed_grad_parts(scal, turned, grads, groups, 1)
    _, kept_turned, weight_sums = lax.optimization_barrier((sent, turned, weight_sums))
    top_bit = groups.bit_length() - 2
    received = [swap_bit(sent[0], 1, groups), swap_bit(sent[1], top_bit, groups)]
    kept = embed_grad_parts(scal, kept_turned, grads, groups, 0)
    kept, weight_sums = lax.optimization_barrier((kept, weight_sums))
    ends = scatter_start(received, kept, groups)
    small, predictions = group_sums(routes, weight_sums, spec_bias, head_sums, row_sums, slot_count, per_sample)
    predictions = predictions.reshape(targets.shape)
    spec_rows = spec_grad.shape[0] // groups
    outgoing = shard_sums(routes, across([small] * shards), head_rows, spec_rows, spec_bias.shape[0])
    ends, outgoing = lax.optimization_barrier((ends, outgoing))
    part = jnp.concatenate(ends, axis=-1)
    part = part.reshape(shards, part.shape[0] // shards, -1)
    part = scatter_step(part, 1, shards, shard_at)
    even = from_same_core(outgoing, groups)
    bit = 2
    while bit < shards:
        part = part.astype(HALF)
        if bit == 2:
            _, even = lax.optimization_barrier((part, even))
        part = scatter_step(part, bit, shards, shard_at)
        bit *= 2
    embed_grad = part[0]
    gathered = [v for pair in zip(even, [swap_bit(v, 0, groups) for v in even]) for v in pair]
    head_grad, spec_w_grad, spec_b_grad, gain_grad, embed_bias_grad, head_bias_grad = assembled(
        scal, gathered, head_rows, shards, blocks, width
    )
    gain_grad, embed_bias_grad, head_bias_grad = gain_grad[0], embed_bias_grad[0], head_bias_grad[0]
    return (
        predictions,
        embed_grad,
        embed_bias_grad,
        gain_grad,
        spec_w_grad,
        spec_b_grad,
        head_grad,
        head_bias_grad,
    )


def solution(mesh):
    return jax.shard_map(
        on_device,
        mesh=mesh,
        in_specs=(
            P("grp", "fft", None, None),
            P("grp", "fft", None, None),
            P(),
            P(),
            P(),
            P(),
            P(),
            P(),
            P(),
            P(),
            P(),
        ),
        out_specs=(
            P("grp", "fft", None, None),
            P(("grp", "fft"), None),
            P(),
            P(),
            P(),
            P(),
            P(),
            P(),
        ),
        check_vma=False,
    )
```

```python
import jax
import jax.numpy as jnp
import ml_dtypes
import numpy as np
from jax import lax
from jax.experimental import pallas as pl
from jax.experimental.pallas import tpu as pltpu
from jax.sharding import PartitionSpec as P

EPSILON = 1e-05
SHRINK = 0.01
CHUNKS = 1
VMEM_BYTES = 24 * 1024 * 1024
SLOTS = 6
SHARD, FIRST_ROW, GROUP, SIDES = 0, 1, 2, 3
ROUTES = 3
HALF = jnp.bfloat16
FULL = jnp.float32


def dft_tables(cells):
    levels, factors = [], []
    for side, scale in ((cells, 1.1305), (cells // 2, 1.8633), (cells // 4, 1.0)):
        k = np.arange(cells)
        inside = (k < side).astype(np.float64)
        keep = inside[:, None] * inside[None, :]
        angle = 2.0 * np.pi * ((k[:, None] * k[None, :]) % side) / side
        one = np.exp(-1j * angle) * keep / np.sqrt(side)
        two = np.kron(one, one)
        table = np.concatenate([two.real, two.imag], axis=0)
        table[np.abs(table) < 1e-12] = 0.0
        rounded = (table * scale).astype(np.float32).astype(ml_dtypes.bfloat16)
        held = rounded.astype(np.float64)
        factors.append(float(np.sum(table * table) / np.sum(table * held)))
        levels.append(rounded)
    return np.stack(levels), factors


def dot(left, right):
    return jnp.dot(left, right, preferred_element_type=FULL)


def dot_tn(left, right):
    return lax.dot_general(left, right, (((0,), (0,)), ((), ())), preferred_element_type=FULL)


def dot_nt(left, right):
    return lax.dot_general(left, right, (((1,), (1,)), ((), ())), preferred_element_type=FULL)


def params(limit=VMEM_BYTES):
    return pltpu.CompilerParams(vmem_limit_bytes=limit)


def token_sides(scal_ref, first, count, per_sample, cells):
    token = lax.broadcasted_iota(jnp.int32, (count * per_sample, 1), 0)
    sample = token // per_sample
    side = jnp.zeros_like(token)
    for i in range(count):
        side = jnp.where(sample == i, scal_ref[SIDES + first + i], side)
    row = scal_ref[FIRST_ROW] + (token % per_sample) // cells
    col = token % cells
    valid = jnp.where((row < side) & (col < side), 1.0, 0.0).astype(FULL)
    return side, valid


def whole(shape):
    return pl.BlockSpec(tuple(shape), lambda i, s: (0,) * len(shape))


def part_of(scal_ref, k, size):
    at = jnp.bitwise_xor(scal_ref[SHARD], k)
    return pl.ds(pl.multiple_of(at * size, size), size)


def fill_lanes(scal_ref, refs, held):
    share = refs[0].shape[-1]
    for k, ref in enumerate(refs):
        held[:, part_of(scal_ref, k, share)] = ref[...].reshape(held.shape[0], share)


def fill_rows(scal_ref, refs, held):
    rows = refs[0].shape[1]
    for k, ref in enumerate(refs):
        held[:, part_of(scal_ref, k, rows), :] = ref[...]


def split_lanes(scal_ref, held, refs):
    share = refs[0].shape[-1]
    for k, ref in enumerate(refs):
        ref[...] = held[:, part_of(scal_ref, k, share)].reshape(ref.shape)


def split_rows(scal_ref, held, refs):
    rows = refs[0].shape[1]
    for k, ref in enumerate(refs):
        ref[...] = held[:, part_of(scal_ref, k, rows), :]


def embed(scal, patches, embed_w, embed_b, gain, firsts, count, per_sample, cells, shards, groups):
    rows, depth = patches.shape
    block = depth // groups
    width = embed_w.shape[1]
    share = width // shards
    chunk_rows = count * per_sample
    chunks = len(firsts)
    steps = 4
    tile = depth // steps

    def body(scal_ref, x_ref, w_ref, b_ref, gain_ref, emb_ref, norm_ref, stat_ref, *refs):
        (send_ref, keep_ref), outs, acc = refs[:2], refs[2:-1], refs[-1]
        step = pl.program_id(0)
        turned = x_ref[...].T
        for i in range(tile // block):
            values = turned[i * block : (i + 1) * block]
            away = (scal_ref[GROUP] + i) % 2

            @pl.when(away == 1)
            def _(i=i, values=values):
                send_ref[i // 2] = values

            @pl.when(away == 0)
            def _(i=i, values=values):
                keep_ref[i // 2] = values

        part = dot(x_ref[...], w_ref[...])

        @pl.when(step == 0)
        def _():
            acc[...] = part

        @pl.when(step > 0)
        def _():
            acc[...] += part

        @pl.when(step == steps - 1)
        def _():
            for c, first in enumerate(firsts):
                at = slice(c * chunk_rows, (c + 1) * chunk_rows)
                _, valid = token_sides(scal_ref, first, count, per_sample, cells)
                embedded = ((acc[at] + b_ref[...]) * valid).astype(HALF)
                emb_ref[at] = embedded
                values = embedded.astype(FULL)
                mean = jnp.mean(values, axis=-1, keepdims=True)
                centered = values - mean
                inv_std = lax.rsqrt(jnp.mean(centered * centered, axis=-1, keepdims=True) + EPSILON)
                norm_ref[at] = (centered * inv_std * gain_ref[...]).astype(HALF)
                stat_ref[at, :128] = jnp.broadcast_to(mean, (chunk_rows, 128))
                stat_ref[at, 128:] = jnp.broadcast_to(inv_std, (chunk_rows, 128))
                for k in range(shards):
                    piece = norm_ref[at, part_of(scal_ref, k, share)]
                    outs[c * shards + k][...] = piece.reshape(count, per_sample, share)

    piece = (count, per_sample, share)
    turned_spec = pl.BlockSpec((tile // (2 * block), block, rows), lambda k, s: (k, 0, 0))
    turned_shape = jax.ShapeDtypeStruct((groups // 2, block, rows), HALF)
    emb, normed, stats, send, keep, *pieces = pl.pallas_call(
        body,
        grid_spec=pltpu.PrefetchScalarGridSpec(
            num_scalar_prefetch=1,
            grid=(steps,),
            in_specs=[
                pl.BlockSpec((rows, tile), lambda k, s: (0, k)),
                pl.BlockSpec((tile, width), lambda k, s: (k, 0)),
                whole((1, width)),
                whole((1, width)),
            ],
            out_specs=[whole((rows, width)), whole((rows, width)), whole((rows, 256)), turned_spec, turned_spec]
            + [whole(piece)] * (shards * chunks),
            scratch_shapes=[pltpu.VMEM((rows, width), FULL)],
        ),
        out_shape=[
            jax.ShapeDtypeStruct((rows, width), HALF),
            jax.ShapeDtypeStruct((rows, width), HALF),
            jax.ShapeDtypeStruct((rows, 256), FULL),
            turned_shape,
            turned_shape,
        ]
        + [jax.ShapeDtypeStruct(piece, HALF)] * (shards * chunks),
        compiler_params=params(60 * 1024 * 1024),
        cost_estimate=pl.CostEstimate(
            flops=2 * rows * depth * width, bytes_accessed=2 * depth * (rows + width), transcendentals=0
        ),
        name="embed",
    )(scal, patches, embed_w, embed_b, gain)
    return emb, normed, stats, send, keep, [pieces[c * shards : (c + 1) * shards] for c in range(chunks)]


def to_blocks(values, blocks, width):
    half = values.shape[0] // 2
    return [
        jnp.concatenate(
            [values[:half, b * width : (b + 1) * width], values[half:, b * width : (b + 1) * width]], axis=1
        )
        for b in range(blocks)
    ]


def from_blocks(parts, width):
    real = jnp.concatenate([p[:, :width] for p in parts], axis=1)
    imag = jnp.concatenate([p[:, width:] for p in parts], axis=1)
    return real, imag


def table_factor(level, factors):
    return jnp.where(level == 0, factors[0], jnp.where(level == 1, factors[1], factors[2])).astype(FULL)


def table_back(table_ref, level, tops, rests, factor):
    size = table_ref.shape[2]
    total = None
    for at, (top, rest) in enumerate(zip(tops, rests)):
        table = table_ref[level, at * size : (at + 1) * size]
        part = dot(table, top) + dot(table, rest)
        total = part if total is None else total + part
    return total * factor


def two_terms(values):
    top = values.astype(HALF)
    return top, (values - top.astype(FULL)).astype(HALF)


def complex_weights(w_ref, held, blocks, width):
    for layer in range(2):
        for b in range(blocks):
            real, imag = w_ref[layer, 0, b], w_ref[layer, 1, b]
            held[layer, b, :width, :width] = real
            held[layer, b, :width, width:] = imag
            held[layer, b, width:, :width] = -imag
            held[layer, b, width:, width:] = real


def spectral_chunk(scal, table, factors, pieces, spec_w, spec_b, first):
    shards = len(pieces)
    count, per_sample, share = pieces[0].shape
    size = shards * per_sample
    width = spec_w.shape[-1]
    blocks = share // width
    wide = 2 * width

    def body(scal_ref, t_ref, w_ref, b_ref, *refs):
        ins, outs = refs[:shards], refs[shards : 2 * shards]
        spec_ref, hid_ref, fil_ref, weights, held = refs[2 * shards :]

        def bias(layer, b):
            row = pl.ds(scal_ref[SHARD] * blocks + b, 1)
            return jnp.concatenate([b_ref[layer, 0, row], b_ref[layer, 1, row]], axis=1)

        complex_weights(w_ref, weights, blocks, width)
        fill_rows(scal_ref, ins, held)
        levels = [scal_ref[SIDES + SLOTS + first + i] for i in range(count)]
        for i, level in enumerate(levels):
            spectrum = (dot(t_ref[level], held[i]) * table_factor(level, factors)).astype(HALF)
            for b, entry in enumerate(to_blocks(spectrum, blocks, width)):
                spec_ref[b, i * size : (i + 1) * size] = entry
        kept = []
        for b in range(blocks):
            pre_one = dot(spec_ref[b], weights[0, b]) + bias(0, b)
            hidden = jnp.maximum(pre_one, 0.0).astype(HALF)
            hid_ref[b] = hidden
            pre_two = dot(hidden, weights[1, b]) + bias(1, b)
            filtered = jnp.where(
                pre_two > SHRINK, pre_two - SHRINK, jnp.where(pre_two < -SHRINK, pre_two + SHRINK, 0.0)
            )
            top, rest = two_terms(filtered)
            fil_ref[b] = top
            kept.append((top, rest))
        for i, level in enumerate(levels):
            at = slice(i * size, (i + 1) * size)
            tops = from_blocks([top[at] for top, _ in kept], width)
            rests = from_blocks([rest[at] for _, rest in kept], width)
            held[i] = table_back(t_ref, level, tops, rests, table_factor(level, factors)).astype(HALF)
        split_rows(scal_ref, held, outs)

    saved = (blocks, count * size, wide)
    outs = pl.pallas_call(
        body,
        grid_spec=pltpu.PrefetchScalarGridSpec(
            num_scalar_prefetch=1,
            grid=(1,),
            in_specs=[
                whole(table.shape),
                pl.BlockSpec((2, 2, blocks, width, width), lambda i, s: (0, 0, s[SHARD], 0, 0)),
                whole(spec_b.shape),
            ]
            + [whole(pieces[0].shape)] * shards,
            out_specs=[whole(pieces[0].shape)] * shards + [whole(saved)] * 3,
            scratch_shapes=[pltpu.VMEM((2, blocks, wide, wide), HALF), pltpu.VMEM((count, size, share), HALF)],
        ),
        out_shape=[jax.ShapeDtypeStruct(pieces[0].shape, HALF)] * shards + [jax.ShapeDtypeStruct(saved, HALF)] * 3,
        compiler_params=params(),
        cost_estimate=pl.CostEstimate(
            flops=count * size * share * size * 14, bytes_accessed=count * size * share * 16, transcendentals=0
        ),
        name="spectral",
    )(scal, table, spec_w, spec_b, *pieces)
    return outs[:shards], outs[shards:]


def head_chunk(scal, embedded, normed, mixed, targets, head_w, head_b, first, samples, cells):
    shards = len(mixed)
    count, per_sample, share = mixed[0].shape
    rows = count * per_sample
    width, outs = head_w.shape
    at = first // count
    scale_root = float(np.sqrt(np.float32(samples)))

    def body(scal_ref, emb_ref, norm_ref, tgt_ref, w_ref, b_ref, *refs):
        mix_refs, (pred_ref, res_ref, up_ref, bias_ref, held) = refs[:shards], refs[shards:]
        fill_lanes(scal_ref, mix_refs, held)
        side, valid = token_sides(scal_ref, first, count, per_sample, cells)
        updated = (emb_ref[...].astype(FULL) + norm_ref[...].astype(FULL) + held[...].astype(FULL)).astype(HALF)
        output = (dot(updated, w_ref[...]) + b_ref[...]) * valid
        pred_ref[...] = output.astype(HALF).reshape(pred_ref.shape)
        scale = 2.0 / (side.astype(FULL) * scale_root)
        residual = (scale * valid * (output - tgt_ref[...].astype(FULL))).astype(HALF)
        res_ref[...] = residual.reshape(res_ref.shape)
        up_ref[...] = updated
        total = jnp.sum(residual.astype(FULL), axis=0, keepdims=True)
        bias_ref[...] = jnp.broadcast_to(total, bias_ref.shape)

    token_shape = (count, per_sample, outs)
    return pl.pallas_call(
        body,
        grid_spec=pltpu.PrefetchScalarGridSpec(
            num_scalar_prefetch=1,
            grid=(1,),
            in_specs=[
                pl.BlockSpec((rows, width), lambda i, s: (at, 0)),
                pl.BlockSpec((rows, width), lambda i, s: (at, 0)),
                pl.BlockSpec((rows, outs), lambda i, s: (at, 0)),
                whole((width, outs)),
                whole((1, outs)),
            ]
            + [whole(mixed[0].shape)] * shards,
            out_specs=[whole(token_shape), whole(token_shape), whole((rows, width)), whole((8, outs))],
            scratch_shapes=[pltpu.VMEM((rows, width), HALF)],
        ),
        out_shape=[
            jax.ShapeDtypeStruct(token_shape, HALF),
            jax.ShapeDtypeStruct(token_shape, HALF),
            jax.ShapeDtypeStruct((rows, width), HALF),
            jax.ShapeDtypeStruct((8, outs), FULL),
        ],
        compiler_params=params(),
        cost_estimate=pl.CostEstimate(
            flops=2 * rows * width * outs, bytes_accessed=rows * width * 4 + width * outs * 6, transcendentals=0
        ),
        name="head",
    )(scal, embedded, normed, targets, head_w, head_b, *mixed)


def head_gradient(updated, residual):
    width = updated[0].shape[1]
    outs = residual[0].shape[-1]
    count = len(updated)

    def body(*refs):
        total = None
        for up_ref, res_ref in zip(refs[:count], refs[count : 2 * count]):
            part = dot_tn(up_ref[...], res_ref[...].reshape(up_ref.shape[0], outs))
            total = part if total is None else total + part
        refs[-1][...] = total.astype(HALF)

    return pl.pallas_call(
        body,
        out_shape=jax.ShapeDtypeStruct((width, outs), HALF),
        compiler_params=params(),
        cost_estimate=pl.CostEstimate(
            flops=2 * count * updated[0].size * outs, bytes_accessed=2 * count * updated[0].size, transcendentals=0
        ),
        name="head_gradient",
    )(*updated, *residual)


def spectral_back_chunk(scal, table, factors, residual, head_w, spec_w, saved, first, before, last):
    shards = len(residual)
    count, per_sample, outs = residual[0].shape
    size = shards * per_sample
    width = spec_w.shape[-1]
    wide = 2 * width
    share = head_w.shape[0] // shards
    blocks = share // width
    raw_shape = (2, blocks, wide, wide)
    bias_shape = (2 * blocks, wide)
    has_before = before is not None

    def body(scal_ref, t_ref, h_ref, w_ref, spec_ref, hid_ref, fil_ref, *refs):
        ins, refs = refs[:shards], refs[shards:]
        if has_before:
            (old_ref, old_bias_ref), refs = refs[:2], refs[2:]
        pieces, (grad_ref, bias_ref, weights, held, gathered) = refs[:shards], refs[shards:]

        def weight_sums(layer, b, inputs, grads):
            raw = dot_tn(inputs, grads)
            sums = jnp.sum(grads.astype(FULL), axis=0, keepdims=True)
            at = layer * blocks + b
            if has_before:
                raw = raw + old_ref[layer, b]
                sums = sums + old_bias_ref[at : at + 1]
            bias_ref[at : at + 1] = sums
            if not last:
                grad_ref[layer, b] = raw
                return
            real = raw[:width, :width] + raw[width:, width:]
            imag = raw[:width, width:] - raw[width:, :width]
            grad_ref[at * width : (at + 1) * width] = jnp.concatenate([real, imag], axis=1).astype(HALF)

        complex_weights(w_ref, weights, blocks, width)
        fill_rows(scal_ref, ins, gathered)
        levels = [scal_ref[SIDES + SLOTS + first + i] for i in range(count)]
        updated_grad = dot_nt(gathered[...].reshape(count * size, outs), h_ref[...]).astype(HALF)
        entries = []
        for i, level in enumerate(levels):
            filtered_grad = dot(t_ref[level], updated_grad[i * size : (i + 1) * size]) * table_factor(level, factors)
            entries.append(to_blocks(filtered_grad, blocks, width))
        kept = []
        for b in range(blocks):
            entry = jnp.concatenate([e[b] for e in entries], axis=0)
            two_grad = jnp.where(fil_ref[b].astype(FULL) != 0.0, entry, 0.0).astype(HALF)
            hidden = hid_ref[b]
            hidden_grad = dot_nt(two_grad, weights[1, b])
            one_grad = jnp.where(hidden.astype(FULL) > 0.0, hidden_grad, 0.0).astype(HALF)
            kept.append(two_terms(dot_nt(one_grad, weights[0, b])))
            weight_sums(1, b, hidden, two_grad)
            weight_sums(0, b, spec_ref[b], one_grad)
        for i, level in enumerate(levels):
            at = slice(i * size, (i + 1) * size)
            tops = from_blocks([top[at] for top, _ in kept], width)
            rests = from_blocks([rest[at] for _, rest in kept], width)
            held[i] = table_back(t_ref, level, tops, rests, table_factor(level, factors)).astype(HALF)
        split_rows(scal_ref, held, pieces)

    piece = (count, per_sample, share)
    if last:
        grad_out = jax.ShapeDtypeStruct((2 * blocks * width, wide), HALF)
    else:
        grad_out = jax.ShapeDtypeStruct(raw_shape, FULL)
    result = pl.pallas_call(
        body,
        grid_spec=pltpu.PrefetchScalarGridSpec(
            num_scalar_prefetch=1,
            grid=(1,),
            in_specs=[
                whole(table.shape),
                pl.BlockSpec((share, outs), lambda i, s: (s[SHARD], 0)),
                pl.BlockSpec((2, 2, blocks, width, width), lambda i, s: (0, 0, s[SHARD], 0, 0)),
            ]
            + [whole(saved[0].shape)] * 3
            + [whole(residual[0].shape)] * shards
            + ([whole(raw_shape), whole(bias_shape)] if has_before else []),
            out_specs=[whole(piece)] * shards + [whole(grad_out.shape), whole(bias_shape)],
            scratch_shapes=[
                pltpu.VMEM((2, blocks, wide, wide), HALF),
                pltpu.VMEM((count, size, share), HALF),
                pltpu.VMEM((count, size, outs), HALF),
            ],
        ),
        out_shape=[jax.ShapeDtypeStruct(piece, HALF)] * shards
        + [grad_out, jax.ShapeDtypeStruct(bias_shape, FULL)],
        compiler_params=params(),
        cost_estimate=pl.CostEstimate(
            flops=count * size * share * size * 20, bytes_accessed=count * size * share * 16, transcendentals=0
        ),
        name="spectral_back",
    )(scal, table, head_w, spec_w, *saved, *residual, *(before or ()))
    return result[:shards], result[shards:]


def embedded_back_chunk(scal, embedded, stats, residual, head_w, gain, spec_grad, first, cells):
    shards = len(spec_grad)
    count, per_sample, share = spec_grad[0].shape
    rows = count * per_sample
    width, outs = head_w.shape
    at = first // count

    def body(scal_ref, emb_ref, stat_ref, res_ref, w_ref, gain_ref, *refs):
        grad_refs, (out_ref, sums_ref, held) = refs[:shards], refs[shards:]
        fill_lanes(scal_ref, grad_refs, held)
        _, valid = token_sides(scal_ref, first, count, per_sample, cells)
        inv_std = stat_ref[:, 128:129]
        unit = (emb_ref[...].astype(FULL) - stat_ref[:, 0:1]) * inv_std
        direct = dot_nt(res_ref[...].reshape(rows, outs), w_ref[...]).astype(HALF).astype(FULL)
        normed_grad = held[...].astype(FULL) + direct
        gain_grad = jnp.sum(normed_grad * unit, axis=0, keepdims=True)
        unit_grad = normed_grad * gain_ref[...]
        mean_grad = jnp.mean(unit_grad, axis=-1, keepdims=True)
        mean_cross = jnp.mean(unit_grad * unit, axis=-1, keepdims=True)
        input_grad = inv_std * (unit_grad - mean_grad - unit * mean_cross)
        result = ((input_grad + direct) * valid).astype(HALF)
        out_ref[...] = result
        bias_grad = jnp.sum(result.astype(FULL), axis=0, keepdims=True)
        sums_ref[0:4] = jnp.broadcast_to(gain_grad, (4, width))
        sums_ref[4:8] = jnp.broadcast_to(bias_grad, (4, width))

    return pl.pallas_call(
        body,
        grid_spec=pltpu.PrefetchScalarGridSpec(
            num_scalar_prefetch=1,
            grid=(1,),
            in_specs=[
                pl.BlockSpec((rows, width), lambda i, s: (at, 0)),
                pl.BlockSpec((rows, 256), lambda i, s: (at, 0)),
                whole((count, per_sample, outs)),
                whole((width, outs)),
                whole((1, width)),
            ]
            + [whole(spec_grad[0].shape)] * shards,
            out_specs=[whole((rows, width)), whole((8, width))],
            scratch_shapes=[pltpu.VMEM((rows, width), HALF)],
        ),
        out_shape=[jax.ShapeDtypeStruct((rows, width), HALF), jax.ShapeDtypeStruct((8, width), FULL)],
        compiler_params=params(),
        cost_estimate=pl.CostEstimate(
            flops=2 * rows * width * outs, bytes_accessed=rows * width * 6, transcendentals=0
        ),
        name="embedded_back",
    )(scal, embedded, stats, residual, head_w, gain, *spec_grad)


def embed_grad_parts(scal, turned, grads, groups, away):
    pairs, block, tokens = turned[0].shape
    chunk_rows, width = grads[0].shape
    half = width // 2
    top = pairs // 2
    count = len(turned)
    depth = tokens * count

    def relative(unit):
        return jnp.where(unit < top, 2 * unit + away, unit - top + away * top)

    def body(scal_ref, *refs):
        turned_refs, grad_refs = refs[:count], refs[count : count + len(grads)]
        left_ref, right_ref, held = refs[count + len(grads) :]
        unit = pl.program_id(0)

        @pl.when(unit % top == 0)
        def _():
            for i, ref in enumerate(grad_refs):
                held[i * chunk_rows : (i + 1) * chunk_rows] = ref[...]

        rows = jnp.concatenate([ref[0] for ref in turned_refs], axis=1)
        total = dot(rows, held[...]).astype(HALF)

        @pl.when(unit < top)
        def _():
            left_ref[0] = total

        @pl.when(unit >= top)
        def _():
            right_ref[0] = total

    shape = (top, block, half)
    return pl.pallas_call(
        body,
        grid_spec=pltpu.PrefetchScalarGridSpec(
            num_scalar_prefetch=1,
            grid=(pairs,),
            in_specs=[
                pl.BlockSpec((1, block, tokens), lambda i, s: (jnp.bitwise_xor(s[GROUP] // 2, relative(i)), 0, 0))
                for _ in turned
            ]
            + [pl.BlockSpec((chunk_rows, half), lambda i, s: (0, i // top)) for _ in grads],
            out_specs=[
                pl.BlockSpec((1, block, half), lambda i, s: (jnp.minimum(i, top - 1), 0, 0)),
                pl.BlockSpec((1, block, half), lambda i, s: (jnp.maximum(i - top, 0), 0, 0)),
            ],
            scratch_shapes=[pltpu.VMEM((depth, half), HALF)],
        ),
        out_shape=[jax.ShapeDtypeStruct(shape, HALF)] * 2,
        compiler_params=params(),
        cost_estimate=pl.CostEstimate(
            flops=depth * pairs * block * width,
            bytes_accessed=pairs * block * (2 * depth + width) + depth * width,
            transcendentals=0,
        ),
        name="embed_grad",
    )(scal, *turned, *grads)


def swap_bit(values, bit, groups):
    return lax.ppermute(values, "grp", [(g, g ^ (1 << bit)) for g in range(groups)])


def across(pieces):
    shards = len(pieces)
    return [pieces[0]] + [
        lax.ppermute(pieces[k], "fft", [(z, z ^ k) for z in range(shards)]) for k in range(1, shards)
    ]


def add_half(left, right):
    return (left.astype(FULL) + right.astype(FULL)).astype(HALF)


def scatter_start(received, kept, groups):
    bits = groups.bit_length() - 1
    ends = []
    for first, keep, order, low in (
        (received[0], kept[0], list(range(2, bits)), True),
        (received[1], kept[1], list(range(bits - 2, 0, -1)), False),
    ):
        total = add_half(keep, first)
        for bit in order:
            count, block, width = total.shape
            if low:
                split = total.reshape(count // 2, 2, block, width)
                keep, send = split[:, 0], split[:, 1]
            else:
                split = total.reshape(2, count // 2, block, width)
                keep, send = split[0], split[1]
            total = add_half(keep, swap_bit(send, bit, groups))
        ends.append(total[0])
    return ends


def scatter_step(part, bit, shards, shard_at):
    split = part.reshape(part.shape[0] // 2, 2, *part.shape[1:])
    mine = (shard_at // bit) % 2
    keep = lax.dynamic_index_in_dim(split, mine, 1, keepdims=False)
    send = lax.dynamic_index_in_dim(split, 1 - mine, 1, keepdims=False)
    received = lax.ppermute(send, "fft", [(z, z ^ bit) for z in range(shards)])
    return keep.astype(FULL) + received.astype(FULL)


def from_same_core(values, groups):
    return [values] + [
        lax.ppermute(values, "grp", [(g, g ^ k) for g in range(groups)]) for k in range(2, groups, 2)
    ]


def hi_lo(values):
    high = values.astype(HALF)
    return jnp.concatenate([high, (values - high.astype(FULL)).astype(HALF)], axis=0)


def from_hi_lo(values):
    half = values.shape[0] // 2
    values = values.astype(FULL)
    return values[:half] + values[half:]


def one_step(body, name, operands, out_shape):
    return pl.pallas_call(
        body,
        grid_spec=pltpu.PrefetchScalarGridSpec(
            num_scalar_prefetch=1,
            grid=(1,),
            in_specs=[whole(o.shape) for o in operands[1:]],
            out_specs=[whole(o.shape) for o in out_shape],
        ),
        out_shape=out_shape,
        compiler_params=params(),
        name=name,
    )(*operands)


def packed(routes, head_grad, spec_grad, predicted, groups):
    outs = head_grad.shape[1]
    head_rows, spec_rows = head_grad.shape[0] // groups, spec_grad.shape[0] // groups
    count, per_sample, _ = predicted[0].shape

    def body(routes_ref, head_ref, spec_ref, *refs):
        pred_refs, out_ref = refs[:-1], refs[-1]
        for g in range(groups):
            out_ref[g, :head_rows] = head_ref[g * head_rows : (g + 1) * head_rows]
            out_ref[g, head_rows : head_rows + spec_rows] = spec_ref[g * spec_rows : (g + 1) * spec_rows]
            chosen = routes_ref[ROUTES + g]
            for c, ref in enumerate(pred_refs):

                @pl.when(chosen // count == c)
                def _(g=g, c=c, ref=ref, chosen=chosen):
                    out_ref[g, head_rows + spec_rows :] = ref[chosen - c * count]

    shape = (groups, head_rows + spec_rows + per_sample, outs)
    return one_step(
        body, "packed", (routes, head_grad, spec_grad, *predicted), [jax.ShapeDtypeStruct(shape, HALF)]
    )[0]


def group_sums(routes, moved, spec_bias, head_sums, row_sums, slot_count, per_sample):
    groups, rows, outs = moved.shape
    weight_rows = rows - per_sample
    own_rows = spec_bias.shape[0]
    chunks = len(head_sums)
    parts = row_sums[0].shape[1] // outs
    spare = 16 - own_rows - 2 * parts - 1

    def body(routes_ref, moved_ref, bias_ref, *refs):
        head_refs, row_refs, (out_ref, pred_ref) = refs[:chunks], refs[chunks : 2 * chunks], refs[2 * chunks :]
        total = moved_ref[0, :weight_rows].astype(FULL)
        for g in range(1, groups):
            total = total + moved_ref[g, :weight_rows].astype(FULL)
        out_ref[:weight_rows] = total.astype(HALF)
        lines = [bias_ref[...]]
        for row in (0, 4):
            line = sum(ref[row : row + 1] for ref in row_refs)
            lines += [line[:, i * outs : (i + 1) * outs] for i in range(parts)]
        lines += [sum(ref[0:1] for ref in head_refs), jnp.zeros((spare, outs), FULL)]
        out_ref[weight_rows:] = hi_lo(jnp.concatenate(lines, axis=0))
        for i in range(slot_count):
            pred_ref[i] = moved_ref[routes_ref[ROUTES + groups + i], weight_rows:]

    return one_step(
        body,
        "group_sums",
        (routes, moved, spec_bias, *head_sums, *row_sums),
        [
            jax.ShapeDtypeStruct((weight_rows + 32, outs), HALF),
            jax.ShapeDtypeStruct((slot_count, per_sample, outs), HALF),
        ],
    )


def shard_sums(routes, rows, head_rows, spec_rows, own_rows):
    shards = len(rows)
    outs = rows[0].shape[1]
    small_rows = 32

    def body(routes_ref, *refs):
        ins, out_ref = refs[:-1], refs[-1]
        total = sum(ref[:head_rows].astype(FULL) for ref in ins)
        out_ref[:head_rows] = total.astype(HALF)
        for k, ref in enumerate(ins):
            at = head_rows + k * spec_rows
            out_ref[at : at + spec_rows] = ref[head_rows : head_rows + spec_rows]
        smalls = [from_hi_lo(ref[head_rows + spec_rows :]) for ref in ins]
        lines = []
        for z in range(shards):
            here = [jnp.bitwise_xor(routes_ref[SHARD], k) == z for k in range(shards)]
            lines.append(sum(jnp.where(h, v[:own_rows], 0.0) for h, v in zip(here, smalls)))
        lines.append(sum(v[own_rows:] for v in smalls))
        have = shards * own_rows + 16 - own_rows
        lines.append(jnp.zeros((small_rows - have, outs), FULL))
        out_ref[head_rows + shards * spec_rows :] = hi_lo(jnp.concatenate(lines, axis=0))

    shape = (head_rows + shards * spec_rows + 2 * small_rows, outs)
    return one_step(body, "shard_sums", (routes, *rows), [jax.ShapeDtypeStruct(shape, HALF)])[0]


def assembled(scal, gathered, head_rows, shards, blocks, width):
    groups = len(gathered)
    total_blocks = shards * blocks
    spec_rows = 2 * blocks * width // groups
    small_at = head_rows + shards * spec_rows
    small_rows = (gathered[0].shape[0] - small_at) // 2

    def body(scal_ref, *refs):
        ins, (head_ref, spec_ref, bias_ref, gain_ref, embed_ref, out_ref) = refs[:groups], refs[groups:]
        small = None
        for k, ref in enumerate(ins):
            group = jnp.bitwise_xor(scal_ref[GROUP], k)
            at = pl.ds(pl.multiple_of(group * head_rows, head_rows), head_rows)
            head_ref[at, :] = ref[:head_rows].astype(FULL)
            start = group * spec_rows
            layer, b = start // (blocks * width), (start // width) % blocks
            rows = pl.ds(pl.multiple_of(start % width, spec_rows), spec_rows)
            for j in range(shards):
                values = ref[head_rows + j * spec_rows : head_rows + (j + 1) * spec_rows].astype(FULL)
                z = jnp.bitwise_xor(scal_ref[SHARD], j)
                spec_ref[layer, 0, z * blocks + b, rows] = values[:, :width]
                spec_ref[layer, 1, z * blocks + b, rows] = values[:, width:]
            part = ref[small_at : small_at + small_rows].astype(FULL) + ref[small_at + small_rows :].astype(FULL)
            small = part if small is None else small + part
        for z in range(shards):
            for layer in range(2):
                for b in range(blocks):
                    row = (z * 2 + layer) * blocks + b
                    for p in range(2):
                        bias_ref[layer, p, z * blocks + b : z * blocks + b + 1] = small[
                            row : row + 1, p * width : (p + 1) * width
                        ]
        row = shards * 2 * blocks
        quarter = gain_ref.shape[1] // (2 * width)
        for ref in (gain_ref, embed_ref):
            for i in range(quarter):
                ref[:, i * 2 * width : (i + 1) * 2 * width] = small[row + i : row + i + 1]
            row += quarter
        out_ref[...] = small[row : row + 1]

    out_shape = [
        jax.ShapeDtypeStruct((groups * head_rows, 2 * width), FULL),
        jax.ShapeDtypeStruct((2, 2, total_blocks, width, width), FULL),
        jax.ShapeDtypeStruct((2, 2, total_blocks, width), FULL),
        jax.ShapeDtypeStruct((1, groups * head_rows), FULL),
        jax.ShapeDtypeStruct((1, groups * head_rows), FULL),
        jax.ShapeDtypeStruct((1, 2 * width), FULL),
    ]
    return pl.pallas_call(
        body,
        grid_spec=pltpu.PrefetchScalarGridSpec(
            num_scalar_prefetch=1,
            grid=(1,),
            in_specs=[whole(gathered[0].shape)] * groups,
            out_specs=[whole(o.shape) for o in out_shape],
        ),
        out_shape=out_shape,
        compiler_params=params(),
        name="assembled",
    )(scal, *gathered)


def prediction_routes(dest_group, group_at, groups, slot_count):
    own_dest = lax.dynamic_slice_in_dim(dest_group, group_at * slot_count, slot_count)
    loaders = jnp.arange(groups, dtype=jnp.int32)
    slots = jnp.arange(slot_count, dtype=jnp.int32)
    chosen = jnp.sum(jnp.where(own_dest[None, :] == loaders[:, None], slots[None, :], 0), axis=1)
    holds = jnp.any(dest_group.reshape(groups, slot_count) == group_at, axis=1)
    rank = jnp.sum(jnp.where(holds[None, :] & (loaders[None, :] < loaders[:, None]), 1, 0), axis=1)
    sources = jnp.sum(jnp.where(holds[None, :] & (rank[None, :] == slots[:, None]), loaders[None, :], 0), axis=1)
    return jnp.concatenate([chosen, sources]).astype(jnp.int32)


def on_device(
    patches, targets, grid_side, dest_group, embed_w, embed_b, gain, spec_w, spec_b, head_w, head_b
):
    slot_count, row_count, cells, depth = patches.shape
    samples = dest_group.shape[0]
    groups = lax.axis_size("grp")
    shards = lax.axis_size("fft")
    group_at = lax.axis_index("grp").astype(jnp.int32)
    shard_at = lax.axis_index("fft").astype(jnp.int32)
    outs = targets.shape[-1]
    per_sample = row_count * cells
    count = slot_count // CHUNKS
    firsts = [c * count for c in range(CHUNKS)]
    assert slot_count == SLOTS

    sides = lax.dynamic_slice_in_dim(grid_side, group_at * slot_count, slot_count)
    level = jnp.where(sides == cells, 0, jnp.where(sides == cells // 2, 1, 2)).astype(jnp.int32)
    place = jnp.stack([shard_at, shard_at * row_count, group_at])
    scal = jnp.concatenate([place, sides, level])
    routes = jnp.concatenate([place, prediction_routes(dest_group, group_at, groups, slot_count)])
    table_values, factors = dft_tables(cells)
    table = jnp.asarray(table_values)
    flat_patches = patches.reshape(-1, depth)
    flat_targets = targets.reshape(-1, outs)
    gain_row, embed_b_row, head_b_row = gain[None], embed_b[None], head_b[None]

    embedded, normed, stats, turned_send, turned_keep, pieces = embed(
        scal, flat_patches, embed_w, embed_b_row, gain_row, firsts, count, per_sample, cells, shards, groups
    )
    moved = [across(p) for p in pieces]
    mixed, saved = [], []
    for first, values in zip(firsts, moved):
        out, rest = spectral_chunk(scal, table, factors, values, spec_w, spec_b, first)
        mixed.append(across(out))
        saved.append(rest)
    predicted, residual, updated, head_sums, gathered = [], [], [], [], []
    for first, mix in zip(firsts, mixed):
        pred, res, up, sums = head_chunk(
            scal, embedded, normed, mix, flat_targets, head_w, head_b_row, first, samples, cells
        )
        predicted.append(pred)
        residual.append(res)
        updated.append(up)
        head_sums.append(sums)
        gathered.append(across([res] * shards))
    head_grad, gathered[0] = lax.optimization_barrier((head_gradient(updated, residual), gathered[0]))
    spec_back, sums = [], None
    for first, res, rest in zip(firsts, gathered, saved):
        values, sums = spectral_back_chunk(
            scal, table, factors, res, head_w, spec_w, rest, first, sums, first == firsts[-1]
        )
        if first == firsts[-1]:
            values, turned_send = lax.optimization_barrier((values, turned_send))
        spec_back.append(across(values))
    turned = [turned_keep, swap_bit(turned_send, 0, groups)]
    spec_grad, spec_bias = sums
    width = spec_w.shape[-1]
    blocks = spec_w.shape[2] // shards
    head_rows = head_w.shape[0] // groups
    weight_sums = lax.all_to_all(
        packed(routes, head_grad, spec_grad, predicted, groups), "grp", split_axis=0, concat_axis=0, tiled=True
    )
    own_grads, other_grads, row_sums = [], [], []
    for first, res, back in zip(firsts, residual, spec_back):
        grad, row_sum = embedded_back_chunk(scal, embedded, stats, res, head_w, gain_row, back, first, cells)
        own_grads.append(grad)
        other_grads.append(swap_bit(grad, 0, groups))
        row_sums.append(row_sum)
    grads = own_grads + other_grads
    grads, weight_sums = lax.optimization_barrier((grads, weight_sums))
    sent = embed_grad_parts(scal, turned, grads, groups, 1)
    sent, kept_turned = lax.optimization_barrier((sent, turned))
    top_bit = groups.bit_length() - 2
    received = [swap_bit(sent[0], 1, groups), swap_bit(sent[1], top_bit, groups)]
    kept = embed_grad_parts(scal, kept_turned, grads, groups, 0)
    kept, weight_sums = lax.optimization_barrier((kept, weight_sums))
    ends = scatter_start(received, kept, groups)
    small, predictions = group_sums(routes, weight_sums, spec_bias, head_sums, row_sums, slot_count, per_sample)
    predictions = predictions.reshape(targets.shape)
    spec_rows = spec_grad.shape[0] // groups
    outgoing = shard_sums(routes, across([small] * shards), head_rows, spec_rows, spec_bias.shape[0])
    ends, outgoing = lax.optimization_barrier((ends, outgoing))
    part = jnp.concatenate(ends, axis=-1)
    part = part.reshape(shards, part.shape[0] // shards, -1)
    part = scatter_step(part, 1, shards, shard_at)
    even = from_same_core(outgoing, groups)
    bit = 2
    while bit < shards:
        part = part.astype(HALF)
        if bit == 2:
            _, even = lax.optimization_barrier((part, even))
        part = scatter_step(part, bit, shards, shard_at)
        bit *= 2
    embed_grad = part[0]
    gathered = [v for pair in zip(even, [swap_bit(v, 0, groups) for v in even]) for v in pair]
    head_grad, spec_w_grad, spec_b_grad, gain_grad, embed_bias_grad, head_bias_grad = assembled(
        scal, gathered, head_rows, shards, blocks, width
    )
    gain_grad, embed_bias_grad, head_bias_grad = gain_grad[0], embed_bias_grad[0], head_bias_grad[0]
    return (
        predictions,
        embed_grad,
        embed_bias_grad,
        gain_grad,
        spec_w_grad,
        spec_b_grad,
        head_grad,
        head_bias_grad,
    )


def solution(mesh):
    return jax.shard_map(
        on_device,
        mesh=mesh,
        in_specs=(
            P("grp", "fft", None, None),
            P("grp", "fft", None, None),
            P(),
            P(),
            P(),
            P(),
            P(),
            P(),
            P(),
            P(),
            P(),
        ),
        out_specs=(
            P("grp", "fft", None, None),
            P(("grp", "fft"), None),
            P(),
            P(),
            P(),
            P(),
            P(),
            P(),
        ),
        check_vma=False,
    )
```

```python
import jax
import jax.numpy as jnp
import ml_dtypes
import numpy as np
from jax import lax
from jax.experimental import pallas as pl
from jax.experimental.pallas import tpu as pltpu
from jax.sharding import PartitionSpec as P

EPSILON = 1e-05
SHRINK = 0.01
CHUNKS = 2
VMEM_BYTES = 24 * 1024 * 1024
SLOTS = 6
SHARD, FIRST_ROW, GROUP, SIDES = 0, 1, 2, 3
ROUTES = 3
HALF = jnp.bfloat16
FULL = jnp.float32


def dft_tables(cells):
    levels, factors = [], []
    for side, scale in ((cells, 1.1305), (cells // 2, 1.8633), (cells // 4, 1.0)):
        k = np.arange(cells)
        inside = (k < side).astype(np.float64)
        keep = inside[:, None] * inside[None, :]
        angle = 2.0 * np.pi * ((k[:, None] * k[None, :]) % side) / side
        one = np.exp(-1j * angle) * keep / np.sqrt(side)
        two = np.kron(one, one)
        table = np.concatenate([two.real, two.imag], axis=0)
        table[np.abs(table) < 1e-12] = 0.0
        rounded = (table * scale).astype(np.float32).astype(ml_dtypes.bfloat16)
        held = rounded.astype(np.float64)
        factors.append(float(np.sum(table * table) / np.sum(table * held)))
        levels.append(rounded)
    return np.stack(levels), factors


def dot(left, right):
    return jnp.dot(left, right, preferred_element_type=FULL)


def dot_tn(left, right):
    return lax.dot_general(left, right, (((0,), (0,)), ((), ())), preferred_element_type=FULL)


def dot_nt(left, right):
    return lax.dot_general(left, right, (((1,), (1,)), ((), ())), preferred_element_type=FULL)


def params(limit=VMEM_BYTES):
    return pltpu.CompilerParams(vmem_limit_bytes=limit)


def token_sides(scal_ref, first, count, per_sample, cells):
    token = lax.broadcasted_iota(jnp.int32, (count * per_sample, 1), 0)
    sample = token // per_sample
    side = jnp.zeros_like(token)
    for i in range(count):
        side = jnp.where(sample == i, scal_ref[SIDES + first + i], side)
    row = scal_ref[FIRST_ROW] + (token % per_sample) // cells
    col = token % cells
    valid = jnp.where((row < side) & (col < side), 1.0, 0.0).astype(FULL)
    return side, valid


def whole(shape):
    return pl.BlockSpec(tuple(shape), lambda i, s: (0,) * len(shape))


def part_of(scal_ref, k, size):
    at = jnp.bitwise_xor(scal_ref[SHARD], k)
    return pl.ds(pl.multiple_of(at * size, size), size)


def fill_lanes(scal_ref, refs, held):
    share = refs[0].shape[-1]
    for k, ref in enumerate(refs):
        held[:, part_of(scal_ref, k, share)] = ref[...].reshape(held.shape[0], share)


def fill_rows(scal_ref, refs, held):
    rows = refs[0].shape[1]
    for k, ref in enumerate(refs):
        held[:, part_of(scal_ref, k, rows), :] = ref[...]


def split_lanes(scal_ref, held, refs):
    share = refs[0].shape[-1]
    for k, ref in enumerate(refs):
        ref[...] = held[:, part_of(scal_ref, k, share)].reshape(ref.shape)


def split_rows(scal_ref, held, refs):
    rows = refs[0].shape[1]
    for k, ref in enumerate(refs):
        ref[...] = held[:, part_of(scal_ref, k, rows), :]


def embed(scal, patches, embed_w, embed_b, gain, firsts, count, per_sample, cells, shards, groups):
    rows, depth = patches.shape
    block = depth // groups
    width = embed_w.shape[1]
    share = width // shards
    chunk_rows = count * per_sample
    chunks = len(firsts)
    steps = 4
    tile = depth // steps

    def body(scal_ref, x_ref, w_ref, b_ref, gain_ref, emb_ref, norm_ref, stat_ref, *refs):
        (send_ref, keep_ref), outs, acc = refs[:2], refs[2:-1], refs[-1]
        step = pl.program_id(0)
        turned = x_ref[...].T
        for i in range(tile // block):
            values = turned[i * block : (i + 1) * block]
            away = (scal_ref[GROUP] + i) % 2

            @pl.when(away == 1)
            def _(i=i, values=values):
                send_ref[i // 2] = values

            @pl.when(away == 0)
            def _(i=i, values=values):
                keep_ref[i // 2] = values

        part = dot(x_ref[...], w_ref[...])

        @pl.when(step == 0)
        def _():
            acc[...] = part

        @pl.when(step > 0)
        def _():
            acc[...] += part

        @pl.when(step == steps - 1)
        def _():
            for c, first in enumerate(firsts):
                at = slice(c * chunk_rows, (c + 1) * chunk_rows)
                _, valid = token_sides(scal_ref, first, count, per_sample, cells)
                embedded = ((acc[at] + b_ref[...]) * valid).astype(HALF)
                emb_ref[at] = embedded
                values = embedded.astype(FULL)
                mean = jnp.mean(values, axis=-1, keepdims=True)
                centered = values - mean
                inv_std = lax.rsqrt(jnp.mean(centered * centered, axis=-1, keepdims=True) + EPSILON)
                norm_ref[at] = (centered * inv_std * gain_ref[...]).astype(HALF)
                stat_ref[at, :128] = jnp.broadcast_to(mean, (chunk_rows, 128))
                stat_ref[at, 128:] = jnp.broadcast_to(inv_std, (chunk_rows, 128))
                for k in range(shards):
                    piece = norm_ref[at, part_of(scal_ref, k, share)]
                    outs[c * shards + k][...] = piece.reshape(count, per_sample, share)

    piece = (count, per_sample, share)
    turned_spec = pl.BlockSpec((tile // (2 * block), block, rows), lambda k, s: (k, 0, 0))
    turned_shape = jax.ShapeDtypeStruct((groups // 2, block, rows), HALF)
    emb, normed, stats, send, keep, *pieces = pl.pallas_call(
        body,
        grid_spec=pltpu.PrefetchScalarGridSpec(
            num_scalar_prefetch=1,
            grid=(steps,),
            in_specs=[
                pl.BlockSpec((rows, tile), lambda k, s: (0, k)),
                pl.BlockSpec((tile, width), lambda k, s: (k, 0)),
                whole((1, width)),
                whole((1, width)),
            ],
            out_specs=[whole((rows, width)), whole((rows, width)), whole((rows, 256)), turned_spec, turned_spec]
            + [whole(piece)] * (shards * chunks),
            scratch_shapes=[pltpu.VMEM((rows, width), FULL)],
        ),
        out_shape=[
            jax.ShapeDtypeStruct((rows, width), HALF),
            jax.ShapeDtypeStruct((rows, width), HALF),
            jax.ShapeDtypeStruct((rows, 256), FULL),
            turned_shape,
            turned_shape,
        ]
        + [jax.ShapeDtypeStruct(piece, HALF)] * (shards * chunks),
        compiler_params=params(60 * 1024 * 1024),
        cost_estimate=pl.CostEstimate(
            flops=2 * rows * depth * width, bytes_accessed=2 * depth * (rows + width), transcendentals=0
        ),
        name="embed",
    )(scal, patches, embed_w, embed_b, gain)
    return emb, normed, stats, send, keep, [pieces[c * shards : (c + 1) * shards] for c in range(chunks)]


def to_blocks(values, blocks, width):
    half = values.shape[0] // 2
    return [
        jnp.concatenate(
            [values[:half, b * width : (b + 1) * width], values[half:, b * width : (b + 1) * width]], axis=1
        )
        for b in range(blocks)
    ]


def from_blocks(parts, width):
    real = jnp.concatenate([p[:, :width] for p in parts], axis=1)
    imag = jnp.concatenate([p[:, width:] for p in parts], axis=1)
    return real, imag


def table_factor(level, factors):
    return jnp.where(level == 0, factors[0], jnp.where(level == 1, factors[1], factors[2])).astype(FULL)


def table_back(table_ref, level, tops, rests, factor):
    size = table_ref.shape[2]
    total = None
    for at, (top, rest) in enumerate(zip(tops, rests)):
        table = table_ref[level, at * size : (at + 1) * size]
        part = dot(table, top) + dot(table, rest)
        total = part if total is None else total + part
    return total * factor


def two_terms(values):
    top = values.astype(HALF)
    return top, (values - top.astype(FULL)).astype(HALF)


def complex_weights(w_ref, held, blocks, width):
    for layer in range(2):
        for b in range(blocks):
            real, imag = w_ref[layer, 0, b], w_ref[layer, 1, b]
            held[layer, b, :width, :width] = real
            held[layer, b, :width, width:] = imag
            held[layer, b, width:, :width] = -imag
            held[layer, b, width:, width:] = real


def spectral_chunk(scal, table, factors, pieces, spec_w, spec_b, first):
    shards = len(pieces)
    count, per_sample, share = pieces[0].shape
    size = shards * per_sample
    width = spec_w.shape[-1]
    blocks = share // width
    wide = 2 * width

    def body(scal_ref, t_ref, w_ref, b_ref, *refs):
        ins, outs = refs[:shards], refs[shards : 2 * shards]
        spec_ref, hid_ref, fil_ref, weights, held = refs[2 * shards :]

        def bias(layer, b):
            row = pl.ds(scal_ref[SHARD] * blocks + b, 1)
            return jnp.concatenate([b_ref[layer, 0, row], b_ref[layer, 1, row]], axis=1)

        complex_weights(w_ref, weights, blocks, width)
        fill_rows(scal_ref, ins, held)
        levels = [scal_ref[SIDES + SLOTS + first + i] for i in range(count)]
        for i, level in enumerate(levels):
            spectrum = (dot(t_ref[level], held[i]) * table_factor(level, factors)).astype(HALF)
            for b, entry in enumerate(to_blocks(spectrum, blocks, width)):
                spec_ref[b, i * size : (i + 1) * size] = entry
        kept = []
        for b in range(blocks):
            pre_one = dot(spec_ref[b], weights[0, b]) + bias(0, b)
            hidden = jnp.maximum(pre_one, 0.0).astype(HALF)
            hid_ref[b] = hidden
            pre_two = dot(hidden, weights[1, b]) + bias(1, b)
            filtered = jnp.where(
                pre_two > SHRINK, pre_two - SHRINK, jnp.where(pre_two < -SHRINK, pre_two + SHRINK, 0.0)
            )
            top, rest = two_terms(filtered)
            fil_ref[b] = top
            kept.append((top, rest))
        for i, level in enumerate(levels):
            at = slice(i * size, (i + 1) * size)
            tops = from_blocks([top[at] for top, _ in kept], width)
            rests = from_blocks([rest[at] for _, rest in kept], width)
            held[i] = table_back(t_ref, level, tops, rests, table_factor(level, factors)).astype(HALF)
        split_rows(scal_ref, held, outs)

    saved = (blocks, count * size, wide)
    outs = pl.pallas_call(
        body,
        grid_spec=pltpu.PrefetchScalarGridSpec(
            num_scalar_prefetch=1,
            grid=(1,),
            in_specs=[
                whole(table.shape),
                pl.BlockSpec((2, 2, blocks, width, width), lambda i, s: (0, 0, s[SHARD], 0, 0)),
                whole(spec_b.shape),
            ]
            + [whole(pieces[0].shape)] * shards,
            out_specs=[whole(pieces[0].shape)] * shards + [whole(saved)] * 3,
            scratch_shapes=[pltpu.VMEM((2, blocks, wide, wide), HALF), pltpu.VMEM((count, size, share), HALF)],
        ),
        out_shape=[jax.ShapeDtypeStruct(pieces[0].shape, HALF)] * shards + [jax.ShapeDtypeStruct(saved, HALF)] * 3,
        compiler_params=params(),
        cost_estimate=pl.CostEstimate(
            flops=count * size * share * size * 14, bytes_accessed=count * size * share * 16, transcendentals=0
        ),
        name="spectral",
    )(scal, table, spec_w, spec_b, *pieces)
    return outs[:shards], outs[shards:]


def head_chunk(scal, embedded, normed, mixed, targets, head_w, head_b, first, samples, cells):
    shards = len(mixed)
    count, per_sample, share = mixed[0].shape
    rows = count * per_sample
    width, outs = head_w.shape
    at = first // count
    scale_root = float(np.sqrt(np.float32(samples)))

    def body(scal_ref, emb_ref, norm_ref, tgt_ref, w_ref, b_ref, *refs):
        mix_refs, (pred_ref, res_ref, up_ref, bias_ref, held) = refs[:shards], refs[shards:]
        fill_lanes(scal_ref, mix_refs, held)
        side, valid = token_sides(scal_ref, first, count, per_sample, cells)
        updated = (emb_ref[...].astype(FULL) + norm_ref[...].astype(FULL) + held[...].astype(FULL)).astype(HALF)
        output = (dot(updated, w_ref[...]) + b_ref[...]) * valid
        pred_ref[...] = output.astype(HALF).reshape(pred_ref.shape)
        scale = 2.0 / (side.astype(FULL) * scale_root)
        residual = (scale * valid * (output - tgt_ref[...].astype(FULL))).astype(HALF)
        res_ref[...] = residual.reshape(res_ref.shape)
        up_ref[...] = updated
        total = jnp.sum(residual.astype(FULL), axis=0, keepdims=True)
        bias_ref[...] = jnp.broadcast_to(total, bias_ref.shape)

    token_shape = (count, per_sample, outs)
    return pl.pallas_call(
        body,
        grid_spec=pltpu.PrefetchScalarGridSpec(
            num_scalar_prefetch=1,
            grid=(1,),
            in_specs=[
                pl.BlockSpec((rows, width), lambda i, s: (at, 0)),
                pl.BlockSpec((rows, width), lambda i, s: (at, 0)),
                pl.BlockSpec((rows, outs), lambda i, s: (at, 0)),
                whole((width, outs)),
                whole((1, outs)),
            ]
            + [whole(mixed[0].shape)] * shards,
            out_specs=[whole(token_shape), whole(token_shape), whole((rows, width)), whole((8, outs))],
            scratch_shapes=[pltpu.VMEM((rows, width), HALF)],
        ),
        out_shape=[
            jax.ShapeDtypeStruct(token_shape, HALF),
            jax.ShapeDtypeStruct(token_shape, HALF),
            jax.ShapeDtypeStruct((rows, width), HALF),
            jax.ShapeDtypeStruct((8, outs), FULL),
        ],
        compiler_params=params(),
        cost_estimate=pl.CostEstimate(
            flops=2 * rows * width * outs, bytes_accessed=rows * width * 4 + width * outs * 6, transcendentals=0
        ),
        name="head",
    )(scal, embedded, normed, targets, head_w, head_b, *mixed)


def head_gradient(updated, residual):
    width = updated[0].shape[1]
    outs = residual[0].shape[-1]
    count = len(updated)

    def body(*refs):
        total = None
        for up_ref, res_ref in zip(refs[:count], refs[count : 2 * count]):
            part = dot_tn(up_ref[...], res_ref[...].reshape(up_ref.shape[0], outs))
            total = part if total is None else total + part
        refs[-1][...] = total.astype(HALF)

    return pl.pallas_call(
        body,
        out_shape=jax.ShapeDtypeStruct((width, outs), HALF),
        compiler_params=params(),
        cost_estimate=pl.CostEstimate(
            flops=2 * count * updated[0].size * outs, bytes_accessed=2 * count * updated[0].size, transcendentals=0
        ),
        name="head_gradient",
    )(*updated, *residual)


def spectral_back_chunk(scal, table, factors, residual, head_w, spec_w, saved, first, before, last):
    shards = len(residual)
    count, per_sample, outs = residual[0].shape
    size = shards * per_sample
    width = spec_w.shape[-1]
    wide = 2 * width
    share = head_w.shape[0] // shards
    blocks = share // width
    raw_shape = (2, blocks, wide, wide)
    bias_shape = (2 * blocks, wide)
    has_before = before is not None

    def body(scal_ref, t_ref, h_ref, w_ref, spec_ref, hid_ref, fil_ref, *refs):
        ins, refs = refs[:shards], refs[shards:]
        if has_before:
            (old_ref, old_bias_ref), refs = refs[:2], refs[2:]
        pieces, (grad_ref, bias_ref, weights, held, gathered) = refs[:shards], refs[shards:]

        def weight_sums(layer, b, inputs, grads):
            raw = dot_tn(inputs, grads)
            sums = jnp.sum(grads.astype(FULL), axis=0, keepdims=True)
            at = layer * blocks + b
            if has_before:
                raw = raw + old_ref[layer, b]
                sums = sums + old_bias_ref[at : at + 1]
            bias_ref[at : at + 1] = sums
            if not last:
                grad_ref[layer, b] = raw
                return
            real = raw[:width, :width] + raw[width:, width:]
            imag = raw[:width, width:] - raw[width:, :width]
            grad_ref[at * width : (at + 1) * width] = jnp.concatenate([real, imag], axis=1).astype(HALF)

        complex_weights(w_ref, weights, blocks, width)
        fill_rows(scal_ref, ins, gathered)
        levels = [scal_ref[SIDES + SLOTS + first + i] for i in range(count)]
        updated_grad = dot_nt(gathered[...].reshape(count * size, outs), h_ref[...]).astype(HALF)
        entries = []
        for i, level in enumerate(levels):
            filtered_grad = dot(t_ref[level], updated_grad[i * size : (i + 1) * size]) * table_factor(level, factors)
            entries.append(to_blocks(filtered_grad, blocks, width))
        kept = []
        for b in range(blocks):
            entry = jnp.concatenate([e[b] for e in entries], axis=0)
            two_grad = jnp.where(fil_ref[b].astype(FULL) != 0.0, entry, 0.0).astype(HALF)
            hidden = hid_ref[b]
            hidden_grad = dot_nt(two_grad, weights[1, b])
            one_grad = jnp.where(hidden.astype(FULL) > 0.0, hidden_grad, 0.0).astype(HALF)
            kept.append(two_terms(dot_nt(one_grad, weights[0, b])))
            weight_sums(1, b, hidden, two_grad)
            weight_sums(0, b, spec_ref[b], one_grad)
        for i, level in enumerate(levels):
            at = slice(i * size, (i + 1) * size)
            tops = from_blocks([top[at] for top, _ in kept], width)
            rests = from_blocks([rest[at] for _, rest in kept], width)
            held[i] = table_back(t_ref, level, tops, rests, table_factor(level, factors)).astype(HALF)
        split_rows(scal_ref, held, pieces)

    piece = (count, per_sample, share)
    if last:
        grad_out = jax.ShapeDtypeStruct((2 * blocks * width, wide), HALF)
    else:
        grad_out = jax.ShapeDtypeStruct(raw_shape, FULL)
    result = pl.pallas_call(
        body,
        grid_spec=pltpu.PrefetchScalarGridSpec(
            num_scalar_prefetch=1,
            grid=(1,),
            in_specs=[
                whole(table.shape),
                pl.BlockSpec((share, outs), lambda i, s: (s[SHARD], 0)),
                pl.BlockSpec((2, 2, blocks, width, width), lambda i, s: (0, 0, s[SHARD], 0, 0)),
            ]
            + [whole(saved[0].shape)] * 3
            + [whole(residual[0].shape)] * shards
            + ([whole(raw_shape), whole(bias_shape)] if has_before else []),
            out_specs=[whole(piece)] * shards + [whole(grad_out.shape), whole(bias_shape)],
            scratch_shapes=[
                pltpu.VMEM((2, blocks, wide, wide), HALF),
                pltpu.VMEM((count, size, share), HALF),
                pltpu.VMEM((count, size, outs), HALF),
            ],
        ),
        out_shape=[jax.ShapeDtypeStruct(piece, HALF)] * shards
        + [grad_out, jax.ShapeDtypeStruct(bias_shape, FULL)],
        compiler_params=params(),
        cost_estimate=pl.CostEstimate(
            flops=count * size * share * size * 20, bytes_accessed=count * size * share * 16, transcendentals=0
        ),
        name="spectral_back",
    )(scal, table, head_w, spec_w, *saved, *residual, *(before or ()))
    return result[:shards], result[shards:]


def embedded_back_chunk(scal, embedded, stats, residual, head_w, gain, spec_grad, first, cells):
    shards = len(spec_grad)
    count, per_sample, share = spec_grad[0].shape
    rows = count * per_sample
    width, outs = head_w.shape
    at = first // count

    def body(scal_ref, emb_ref, stat_ref, res_ref, w_ref, gain_ref, *refs):
        grad_refs, (out_ref, sums_ref, held) = refs[:shards], refs[shards:]
        fill_lanes(scal_ref, grad_refs, held)
        _, valid = token_sides(scal_ref, first, count, per_sample, cells)
        inv_std = stat_ref[:, 128:129]
        unit = (emb_ref[...].astype(FULL) - stat_ref[:, 0:1]) * inv_std
        direct = dot_nt(res_ref[...].reshape(rows, outs), w_ref[...]).astype(HALF).astype(FULL)
        normed_grad = held[...].astype(FULL) + direct
        gain_grad = jnp.sum(normed_grad * unit, axis=0, keepdims=True)
        unit_grad = normed_grad * gain_ref[...]
        mean_grad = jnp.mean(unit_grad, axis=-1, keepdims=True)
        mean_cross = jnp.mean(unit_grad * unit, axis=-1, keepdims=True)
        input_grad = inv_std * (unit_grad - mean_grad - unit * mean_cross)
        result = ((input_grad + direct) * valid).astype(HALF)
        out_ref[...] = result
        bias_grad = jnp.sum(result.astype(FULL), axis=0, keepdims=True)
        sums_ref[0:4] = jnp.broadcast_to(gain_grad, (4, width))
        sums_ref[4:8] = jnp.broadcast_to(bias_grad, (4, width))

    return pl.pallas_call(
        body,
        grid_spec=pltpu.PrefetchScalarGridSpec(
            num_scalar_prefetch=1,
            grid=(1,),
            in_specs=[
                pl.BlockSpec((rows, width), lambda i, s: (at, 0)),
                pl.BlockSpec((rows, 256), lambda i, s: (at, 0)),
                whole((count, per_sample, outs)),
                whole((width, outs)),
                whole((1, width)),
            ]
            + [whole(spec_grad[0].shape)] * shards,
            out_specs=[whole((rows, width)), whole((8, width))],
            scratch_shapes=[pltpu.VMEM((rows, width), HALF)],
        ),
        out_shape=[jax.ShapeDtypeStruct((rows, width), HALF), jax.ShapeDtypeStruct((8, width), FULL)],
        compiler_params=params(),
        cost_estimate=pl.CostEstimate(
            flops=2 * rows * width * outs, bytes_accessed=rows * width * 6, transcendentals=0
        ),
        name="embedded_back",
    )(scal, embedded, stats, residual, head_w, gain, *spec_grad)


def embed_grad_parts(scal, turned, grads, groups, away):
    pairs, block, tokens = turned[0].shape
    chunk_rows, width = grads[0].shape
    half = width // 2
    top = pairs // 2
    count = len(turned)
    depth = tokens * count

    def relative(unit):
        return jnp.where(unit < top, 2 * unit + away, unit - top + away * top)

    def body(scal_ref, *refs):
        turned_refs, grad_refs = refs[:count], refs[count : count + len(grads)]
        left_ref, right_ref, held = refs[count + len(grads) :]
        unit = pl.program_id(0)

        @pl.when(unit % top == 0)
        def _():
            for i, ref in enumerate(grad_refs):
                held[i * chunk_rows : (i + 1) * chunk_rows] = ref[...]

        rows = jnp.concatenate([ref[0] for ref in turned_refs], axis=1)
        total = dot(rows, held[...]).astype(HALF)

        @pl.when(unit < top)
        def _():
            left_ref[0] = total

        @pl.when(unit >= top)
        def _():
            right_ref[0] = total

    shape = (top, block, half)
    return pl.pallas_call(
        body,
        grid_spec=pltpu.PrefetchScalarGridSpec(
            num_scalar_prefetch=1,
            grid=(pairs,),
            in_specs=[
                pl.BlockSpec((1, block, tokens), lambda i, s: (jnp.bitwise_xor(s[GROUP] // 2, relative(i)), 0, 0))
                for _ in turned
            ]
            + [pl.BlockSpec((chunk_rows, half), lambda i, s: (0, i // top)) for _ in grads],
            out_specs=[
                pl.BlockSpec((1, block, half), lambda i, s: (jnp.minimum(i, top - 1), 0, 0)),
                pl.BlockSpec((1, block, half), lambda i, s: (jnp.maximum(i - top, 0), 0, 0)),
            ],
            scratch_shapes=[pltpu.VMEM((depth, half), HALF)],
        ),
        out_shape=[jax.ShapeDtypeStruct(shape, HALF)] * 2,
        compiler_params=params(),
        cost_estimate=pl.CostEstimate(
            flops=depth * pairs * block * width,
            bytes_accessed=pairs * block * (2 * depth + width) + depth * width,
            transcendentals=0,
        ),
        name="embed_grad",
    )(scal, *turned, *grads)


def swap_bit(values, bit, groups):
    return lax.ppermute(values, "grp", [(g, g ^ (1 << bit)) for g in range(groups)])


def across(pieces):
    shards = len(pieces)
    return [pieces[0]] + [
        lax.ppermute(pieces[k], "fft", [(z, z ^ k) for z in range(shards)]) for k in range(1, shards)
    ]


def add_half(left, right):
    return (left.astype(FULL) + right.astype(FULL)).astype(HALF)


def scatter_start(received, kept, groups):
    bits = groups.bit_length() - 1
    ends = []
    for first, keep, order, low in (
        (received[0], kept[0], list(range(2, bits)), True),
        (received[1], kept[1], list(range(bits - 2, 0, -1)), False),
    ):
        total = add_half(keep, first)
        for bit in order:
            count, block, width = total.shape
            if low:
                split = total.reshape(count // 2, 2, block, width)
                keep, send = split[:, 0], split[:, 1]
            else:
                split = total.reshape(2, count // 2, block, width)
                keep, send = split[0], split[1]
            total = add_half(keep, swap_bit(send, bit, groups))
        ends.append(total[0])
    return ends


def scatter_step(part, bit, shards, shard_at):
    split = part.reshape(part.shape[0] // 2, 2, *part.shape[1:])
    mine = (shard_at // bit) % 2
    keep = lax.dynamic_index_in_dim(split, mine, 1, keepdims=False)
    send = lax.dynamic_index_in_dim(split, 1 - mine, 1, keepdims=False)
    received = lax.ppermute(send, "fft", [(z, z ^ bit) for z in range(shards)])
    return keep.astype(FULL) + received.astype(FULL)


def from_same_core(values, groups):
    return [values] + [
        lax.ppermute(values, "grp", [(g, g ^ k) for g in range(groups)]) for k in range(2, groups, 2)
    ]


def hi_lo(values):
    high = values.astype(HALF)
    return jnp.concatenate([high, (values - high.astype(FULL)).astype(HALF)], axis=0)


def from_hi_lo(values):
    half = values.shape[0] // 2
    values = values.astype(FULL)
    return values[:half] + values[half:]


def one_step(body, name, operands, out_shape):
    return pl.pallas_call(
        body,
        grid_spec=pltpu.PrefetchScalarGridSpec(
            num_scalar_prefetch=1,
            grid=(1,),
            in_specs=[whole(o.shape) for o in operands[1:]],
            out_specs=[whole(o.shape) for o in out_shape],
        ),
        out_shape=out_shape,
        compiler_params=params(),
        name=name,
    )(*operands)


def packed(routes, head_grad, spec_grad, predicted, groups):
    outs = head_grad.shape[1]
    head_rows, spec_rows = head_grad.shape[0] // groups, spec_grad.shape[0] // groups
    count, per_sample, _ = predicted[0].shape

    def body(routes_ref, head_ref, spec_ref, *refs):
        pred_refs, out_ref = refs[:-1], refs[-1]
        for g in range(groups):
            out_ref[g, :head_rows] = head_ref[g * head_rows : (g + 1) * head_rows]
            out_ref[g, head_rows : head_rows + spec_rows] = spec_ref[g * spec_rows : (g + 1) * spec_rows]
            chosen = routes_ref[ROUTES + g]
            for c, ref in enumerate(pred_refs):

                @pl.when(chosen // count == c)
                def _(g=g, c=c, ref=ref, chosen=chosen):
                    out_ref[g, head_rows + spec_rows :] = ref[chosen - c * count]

    shape = (groups, head_rows + spec_rows + per_sample, outs)
    return one_step(
        body, "packed", (routes, head_grad, spec_grad, *predicted), [jax.ShapeDtypeStruct(shape, HALF)]
    )[0]


def group_sums(routes, moved, spec_bias, head_sums, row_sums, slot_count, per_sample):
    groups, rows, outs = moved.shape
    weight_rows = rows - per_sample
    own_rows = spec_bias.shape[0]
    chunks = len(head_sums)
    parts = row_sums[0].shape[1] // outs
    spare = 16 - own_rows - 2 * parts - 1

    def body(routes_ref, moved_ref, bias_ref, *refs):
        head_refs, row_refs, (out_ref, pred_ref) = refs[:chunks], refs[chunks : 2 * chunks], refs[2 * chunks :]
        total = moved_ref[0, :weight_rows].astype(FULL)
        for g in range(1, groups):
            total = total + moved_ref[g, :weight_rows].astype(FULL)
        out_ref[:weight_rows] = total.astype(HALF)
        lines = [bias_ref[...]]
        for row in (0, 4):
            line = sum(ref[row : row + 1] for ref in row_refs)
            lines += [line[:, i * outs : (i + 1) * outs] for i in range(parts)]
        lines += [sum(ref[0:1] for ref in head_refs), jnp.zeros((spare, outs), FULL)]
        out_ref[weight_rows:] = hi_lo(jnp.concatenate(lines, axis=0))
        for i in range(slot_count):
            pred_ref[i] = moved_ref[routes_ref[ROUTES + groups + i], weight_rows:]

    return one_step(
        body,
        "group_sums",
        (routes, moved, spec_bias, *head_sums, *row_sums),
        [
            jax.ShapeDtypeStruct((weight_rows + 32, outs), HALF),
            jax.ShapeDtypeStruct((slot_count, per_sample, outs), HALF),
        ],
    )


def shard_sums(routes, rows, head_rows, spec_rows, own_rows):
    shards = len(rows)
    outs = rows[0].shape[1]
    small_rows = 32

    def body(routes_ref, *refs):
        ins, out_ref = refs[:-1], refs[-1]
        total = sum(ref[:head_rows].astype(FULL) for ref in ins)
        out_ref[:head_rows] = total.astype(HALF)
        for k, ref in enumerate(ins):
            at = head_rows + k * spec_rows
            out_ref[at : at + spec_rows] = ref[head_rows : head_rows + spec_rows]
        smalls = [from_hi_lo(ref[head_rows + spec_rows :]) for ref in ins]
        lines = []
        for z in range(shards):
            here = [jnp.bitwise_xor(routes_ref[SHARD], k) == z for k in range(shards)]
            lines.append(sum(jnp.where(h, v[:own_rows], 0.0) for h, v in zip(here, smalls)))
        lines.append(sum(v[own_rows:] for v in smalls))
        have = shards * own_rows + 16 - own_rows
        lines.append(jnp.zeros((small_rows - have, outs), FULL))
        out_ref[head_rows + shards * spec_rows :] = hi_lo(jnp.concatenate(lines, axis=0))

    shape = (head_rows + shards * spec_rows + 2 * small_rows, outs)
    return one_step(body, "shard_sums", (routes, *rows), [jax.ShapeDtypeStruct(shape, HALF)])[0]


def assembled(scal, gathered, head_rows, shards, blocks, width):
    groups = len(gathered)
    total_blocks = shards * blocks
    spec_rows = 2 * blocks * width // groups
    small_at = head_rows + shards * spec_rows
    small_rows = (gathered[0].shape[0] - small_at) // 2

    def body(scal_ref, *refs):
        ins, (head_ref, spec_ref, bias_ref, gain_ref, embed_ref, out_ref) = refs[:groups], refs[groups:]
        small = None
        for k, ref in enumerate(ins):
            group = jnp.bitwise_xor(scal_ref[GROUP], k)
            at = pl.ds(pl.multiple_of(group * head_rows, head_rows), head_rows)
            head_ref[at, :] = ref[:head_rows].astype(FULL)
            start = group * spec_rows
            layer, b = start // (blocks * width), (start // width) % blocks
            rows = pl.ds(pl.multiple_of(start % width, spec_rows), spec_rows)
            for j in range(shards):
                values = ref[head_rows + j * spec_rows : head_rows + (j + 1) * spec_rows].astype(FULL)
                z = jnp.bitwise_xor(scal_ref[SHARD], j)
                spec_ref[layer, 0, z * blocks + b, rows] = values[:, :width]
                spec_ref[layer, 1, z * blocks + b, rows] = values[:, width:]
            part = ref[small_at : small_at + small_rows].astype(FULL) + ref[small_at + small_rows :].astype(FULL)
            small = part if small is None else small + part
        for z in range(shards):
            for layer in range(2):
                for b in range(blocks):
                    row = (z * 2 + layer) * blocks + b
                    for p in range(2):
                        bias_ref[layer, p, z * blocks + b : z * blocks + b + 1] = small[
                            row : row + 1, p * width : (p + 1) * width
                        ]
        row = shards * 2 * blocks
        quarter = gain_ref.shape[1] // (2 * width)
        for ref in (gain_ref, embed_ref):
            for i in range(quarter):
                ref[:, i * 2 * width : (i + 1) * 2 * width] = small[row + i : row + i + 1]
            row += quarter
        out_ref[...] = small[row : row + 1]

    out_shape = [
        jax.ShapeDtypeStruct((groups * head_rows, 2 * width), FULL),
        jax.ShapeDtypeStruct((2, 2, total_blocks, width, width), FULL),
        jax.ShapeDtypeStruct((2, 2, total_blocks, width), FULL),
        jax.ShapeDtypeStruct((1, groups * head_rows), FULL),
        jax.ShapeDtypeStruct((1, groups * head_rows), FULL),
        jax.ShapeDtypeStruct((1, 2 * width), FULL),
    ]
    return pl.pallas_call(
        body,
        grid_spec=pltpu.PrefetchScalarGridSpec(
            num_scalar_prefetch=1,
            grid=(1,),
            in_specs=[whole(gathered[0].shape)] * groups,
            out_specs=[whole(o.shape) for o in out_shape],
        ),
        out_shape=out_shape,
        compiler_params=params(),
        name="assembled",
    )(scal, *gathered)


def prediction_routes(dest_group, group_at, groups, slot_count):
    own_dest = lax.dynamic_slice_in_dim(dest_group, group_at * slot_count, slot_count)
    loaders = jnp.arange(groups, dtype=jnp.int32)
    slots = jnp.arange(slot_count, dtype=jnp.int32)
    chosen = jnp.sum(jnp.where(own_dest[None, :] == loaders[:, None], slots[None, :], 0), axis=1)
    holds = jnp.any(dest_group.reshape(groups, slot_count) == group_at, axis=1)
    rank = jnp.sum(jnp.where(holds[None, :] & (loaders[None, :] < loaders[:, None]), 1, 0), axis=1)
    sources = jnp.sum(jnp.where(holds[None, :] & (rank[None, :] == slots[:, None]), loaders[None, :], 0), axis=1)
    return jnp.concatenate([chosen, sources]).astype(jnp.int32)


def on_device(
    patches, targets, grid_side, dest_group, embed_w, embed_b, gain, spec_w, spec_b, head_w, head_b
):
    slot_count, row_count, cells, depth = patches.shape
    samples = dest_group.shape[0]
    groups = lax.axis_size("grp")
    shards = lax.axis_size("fft")
    group_at = lax.axis_index("grp").astype(jnp.int32)
    shard_at = lax.axis_index("fft").astype(jnp.int32)
    outs = targets.shape[-1]
    per_sample = row_count * cells
    count = slot_count // CHUNKS
    firsts = [c * count for c in range(CHUNKS)]
    assert slot_count == SLOTS

    sides = lax.dynamic_slice_in_dim(grid_side, group_at * slot_count, slot_count)
    level = jnp.where(sides == cells, 0, jnp.where(sides == cells // 2, 1, 2)).astype(jnp.int32)
    place = jnp.stack([shard_at, shard_at * row_count, group_at])
    scal = jnp.concatenate([place, sides, level])
    routes = jnp.concatenate([place, prediction_routes(dest_group, group_at, groups, slot_count)])
    table_values, factors = dft_tables(cells)
    table = jnp.asarray(table_values)
    flat_patches = patches.reshape(-1, depth)
    flat_targets = targets.reshape(-1, outs)
    gain_row, embed_b_row, head_b_row = gain[None], embed_b[None], head_b[None]

    embedded, normed, stats, turned_send, turned_keep, pieces = embed(
        scal, flat_patches, embed_w, embed_b_row, gain_row, firsts, count, per_sample, cells, shards, groups
    )
    moved = [across(p) for p in pieces]
    mixed, saved = [], []
    for first, values in zip(firsts, moved):
        out, rest = spectral_chunk(scal, table, factors, values, spec_w, spec_b, first)
        mixed.append(across(out))
        saved.append(rest)
    predicted, residual, updated, head_sums, gathered = [], [], [], [], []
    for first, mix in zip(firsts, mixed):
        pred, res, up, sums = head_chunk(
            scal, embedded, normed, mix, flat_targets, head_w, head_b_row, first, samples, cells
        )
        predicted.append(pred)
        residual.append(res)
        updated.append(up)
        head_sums.append(sums)
        gathered.append(across([res] * shards))
    head_grad, gathered[0] = lax.optimization_barrier((head_gradient(updated, residual), gathered[0]))
    spec_back, sums = [], None
    for first, res, rest in zip(firsts, gathered, saved):
        values, sums = spectral_back_chunk(
            scal, table, factors, res, head_w, spec_w, rest, first, sums, first == firsts[-1]
        )
        if first == firsts[-1]:
            values, turned_send = lax.optimization_barrier((values, turned_send))
        spec_back.append(across(values))
    turned = [turned_keep, swap_bit(turned_send, 0, groups)]
    spec_grad, spec_bias = sums
    width = spec_w.shape[-1]
    blocks = spec_w.shape[2] // shards
    head_rows = head_w.shape[0] // groups
    own_grads, other_grads, row_sums = [], [], []
    for first, res, back in zip(firsts, residual, spec_back):
        if first == firsts[-1]:
            back, _ = lax.optimization_barrier((back, outgoing_sums))
        grad, row_sum = embedded_back_chunk(scal, embedded, stats, res, head_w, gain_row, back, first, cells)
        if first == firsts[0]:
            grad, head_grad, spec_grad = lax.optimization_barrier((grad, head_grad, spec_grad))
            outgoing_sums = packed(routes, head_grad, spec_grad, predicted, groups)
            weight_sums = lax.all_to_all(outgoing_sums, "grp", split_axis=0, concat_axis=0, tiled=True)
        own_grads.append(grad)
        other_grads.append(swap_bit(grad, 0, groups))
        row_sums.append(row_sum)
    grads = own_grads + other_grads
    sent = embed_grad_parts(scal, turned, grads, groups, 1)
    sent, kept_turned = lax.optimization_barrier((sent, turned))
    top_bit = groups.bit_length() - 2
    received = [swap_bit(sent[0], 1, groups), swap_bit(sent[1], top_bit, groups)]
    kept = embed_grad_parts(scal, kept_turned, grads, groups, 0)
    kept, weight_sums = lax.optimization_barrier((kept, weight_sums))
    ends = scatter_start(received, kept, groups)
    small, predictions = group_sums(routes, weight_sums, spec_bias, head_sums, row_sums, slot_count, per_sample)
    predictions = predictions.reshape(targets.shape)
    spec_rows = spec_grad.shape[0] // groups
    outgoing = shard_sums(routes, across([small] * shards), head_rows, spec_rows, spec_bias.shape[0])
    ends, outgoing = lax.optimization_barrier((ends, outgoing))
    part = jnp.concatenate(ends, axis=-1)
    part = part.reshape(shards, part.shape[0] // shards, -1)
    part = scatter_step(part, 1, shards, shard_at)
    even = from_same_core(outgoing, groups)
    bit = 2
    while bit < shards:
        part = part.astype(HALF)
        if bit == 2:
            _, even = lax.optimization_barrier((part, even))
        part = scatter_step(part, bit, shards, shard_at)
        bit *= 2
    embed_grad = part[0]
    gathered = [v for pair in zip(even, [swap_bit(v, 0, groups) for v in even]) for v in pair]
    head_grad, spec_w_grad, spec_b_grad, gain_grad, embed_bias_grad, head_bias_grad = assembled(
        scal, gathered, head_rows, shards, blocks, width
    )
    gain_grad, embed_bias_grad, head_bias_grad = gain_grad[0], embed_bias_grad[0], head_bias_grad[0]
    return (
        predictions,
        embed_grad,
        embed_bias_grad,
        gain_grad,
        spec_w_grad,
        spec_b_grad,
        head_grad,
        head_bias_grad,
    )


def solution(mesh):
    return jax.shard_map(
        on_device,
        mesh=mesh,
        in_specs=(
            P("grp", "fft", None, None),
            P("grp", "fft", None, None),
            P(),
            P(),
            P(),
            P(),
            P(),
            P(),
            P(),
            P(),
            P(),
        ),
        out_specs=(
            P("grp", "fft", None, None),
            P(("grp", "fft"), None),
            P(),
            P(),
            P(),
            P(),
            P(),
            P(),
        ),
        check_vma=False,
    )
```

```python
import jax
import jax.numpy as jnp
import ml_dtypes
import numpy as np
from jax import lax
from jax.experimental import pallas as pl
from jax.experimental.pallas import tpu as pltpu
from jax.sharding import PartitionSpec as P

EPSILON = 1e-05
SHRINK = 0.01
CHUNKS = 2
VMEM_BYTES = 24 * 1024 * 1024
SLOTS = 6
SHARD, FIRST_ROW, GROUP, SIDES = 0, 1, 2, 3
ROUTES = 3
HALF = jnp.bfloat16
FULL = jnp.float32


def dft_tables(cells):
    levels, factors = [], []
    for side, scale in ((cells, 1.1305), (cells // 2, 1.8633), (cells // 4, 1.0)):
        k = np.arange(cells)
        inside = (k < side).astype(np.float64)
        keep = inside[:, None] * inside[None, :]
        angle = 2.0 * np.pi * ((k[:, None] * k[None, :]) % side) / side
        one = np.exp(-1j * angle) * keep / np.sqrt(side)
        two = np.kron(one, one)
        table = np.concatenate([two.real, two.imag], axis=0)
        table[np.abs(table) < 1e-12] = 0.0
        rounded = (table * scale).astype(np.float32).astype(ml_dtypes.bfloat16)
        held = rounded.astype(np.float64)
        factors.append(float(np.sum(table * table) / np.sum(table * held)))
        levels.append(rounded)
    return np.stack(levels), factors


def dot(left, right):
    return jnp.dot(left, right, preferred_element_type=FULL)


def dot_tn(left, right):
    return lax.dot_general(left, right, (((0,), (0,)), ((), ())), preferred_element_type=FULL)


def dot_nt(left, right):
    return lax.dot_general(left, right, (((1,), (1,)), ((), ())), preferred_element_type=FULL)


def params(limit=VMEM_BYTES):
    return pltpu.CompilerParams(vmem_limit_bytes=limit)


def token_sides(scal_ref, first, count, per_sample, cells):
    token = lax.broadcasted_iota(jnp.int32, (count * per_sample, 1), 0)
    sample = token // per_sample
    side = jnp.zeros_like(token)
    for i in range(count):
        side = jnp.where(sample == i, scal_ref[SIDES + first + i], side)
    row = scal_ref[FIRST_ROW] + (token % per_sample) // cells
    col = token % cells
    valid = jnp.where((row < side) & (col < side), 1.0, 0.0).astype(FULL)
    return side, valid


def whole(shape):
    return pl.BlockSpec(tuple(shape), lambda i, s: (0,) * len(shape))


def part_of(scal_ref, k, size):
    at = jnp.bitwise_xor(scal_ref[SHARD], k)
    return pl.ds(pl.multiple_of(at * size, size), size)


def fill_lanes(scal_ref, refs, held):
    share = refs[0].shape[-1]
    for k, ref in enumerate(refs):
        held[:, part_of(scal_ref, k, share)] = ref[...].reshape(held.shape[0], share)


def fill_rows(scal_ref, refs, held):
    rows = refs[0].shape[1]
    for k, ref in enumerate(refs):
        held[:, part_of(scal_ref, k, rows), :] = ref[...]


def split_lanes(scal_ref, held, refs):
    share = refs[0].shape[-1]
    for k, ref in enumerate(refs):
        ref[...] = held[:, part_of(scal_ref, k, share)].reshape(ref.shape)


def split_rows(scal_ref, held, refs):
    rows = refs[0].shape[1]
    for k, ref in enumerate(refs):
        ref[...] = held[:, part_of(scal_ref, k, rows), :]


def embed(scal, patches, embed_w, embed_b, gain, firsts, count, per_sample, cells, shards, groups):
    rows, depth = patches.shape
    block = depth // groups
    width = embed_w.shape[1]
    share = width // shards
    chunk_rows = count * per_sample
    chunks = len(firsts)
    steps = 4
    tile = depth // steps

    def body(scal_ref, x_ref, w_ref, b_ref, gain_ref, emb_ref, norm_ref, stat_ref, *refs):
        (send_ref, keep_ref), outs, acc = refs[:2], refs[2:-1], refs[-1]
        step = pl.program_id(0)
        turned = x_ref[...].T
        for i in range(tile // block):
            values = turned[i * block : (i + 1) * block]
            away = (scal_ref[GROUP] + i) % 2

            @pl.when(away == 1)
            def _(i=i, values=values):
                send_ref[i // 2] = values

            @pl.when(away == 0)
            def _(i=i, values=values):
                keep_ref[i // 2] = values

        part = dot(x_ref[...], w_ref[...])

        @pl.when(step == 0)
        def _():
            acc[...] = part

        @pl.when(step > 0)
        def _():
            acc[...] += part

        @pl.when(step == steps - 1)
        def _():
            for c, first in enumerate(firsts):
                at = slice(c * chunk_rows, (c + 1) * chunk_rows)
                _, valid = token_sides(scal_ref, first, count, per_sample, cells)
                embedded = ((acc[at] + b_ref[...]) * valid).astype(HALF)
                emb_ref[at] = embedded
                values = embedded.astype(FULL)
                mean = jnp.mean(values, axis=-1, keepdims=True)
                centered = values - mean
                inv_std = lax.rsqrt(jnp.mean(centered * centered, axis=-1, keepdims=True) + EPSILON)
                norm_ref[at] = (centered * inv_std * gain_ref[...]).astype(HALF)
                stat_ref[at, :128] = jnp.broadcast_to(mean, (chunk_rows, 128))
                stat_ref[at, 128:] = jnp.broadcast_to(inv_std, (chunk_rows, 128))
                for k in range(shards):
                    piece = norm_ref[at, part_of(scal_ref, k, share)]
                    outs[c * shards + k][...] = piece.reshape(count, per_sample, share)

    piece = (count, per_sample, share)
    turned_spec = pl.BlockSpec((tile // (2 * block), block, rows), lambda k, s: (k, 0, 0))
    turned_shape = jax.ShapeDtypeStruct((groups // 2, block, rows), HALF)
    emb, normed, stats, send, keep, *pieces = pl.pallas_call(
        body,
        grid_spec=pltpu.PrefetchScalarGridSpec(
            num_scalar_prefetch=1,
            grid=(steps,),
            in_specs=[
                pl.BlockSpec((rows, tile), lambda k, s: (0, k)),
                pl.BlockSpec((tile, width), lambda k, s: (k, 0)),
                whole((1, width)),
                whole((1, width)),
            ],
            out_specs=[whole((rows, width)), whole((rows, width)), whole((rows, 256)), turned_spec, turned_spec]
            + [whole(piece)] * (shards * chunks),
            scratch_shapes=[pltpu.VMEM((rows, width), FULL)],
        ),
        out_shape=[
            jax.ShapeDtypeStruct((rows, width), HALF),
            jax.ShapeDtypeStruct((rows, width), HALF),
            jax.ShapeDtypeStruct((rows, 256), FULL),
            turned_shape,
            turned_shape,
        ]
        + [jax.ShapeDtypeStruct(piece, HALF)] * (shards * chunks),
        compiler_params=params(60 * 1024 * 1024),
        cost_estimate=pl.CostEstimate(
            flops=2 * rows * depth * width, bytes_accessed=2 * depth * (rows + width), transcendentals=0
        ),
        name="embed",
    )(scal, patches, embed_w, embed_b, gain)
    return emb, normed, stats, send, keep, [pieces[c * shards : (c + 1) * shards] for c in range(chunks)]


def to_blocks(values, blocks, width):
    half = values.shape[0] // 2
    return [
        jnp.concatenate(
            [values[:half, b * width : (b + 1) * width], values[half:, b * width : (b + 1) * width]], axis=1
        )
        for b in range(blocks)
    ]


def from_blocks(parts, width):
    real = jnp.concatenate([p[:, :width] for p in parts], axis=1)
    imag = jnp.concatenate([p[:, width:] for p in parts], axis=1)
    return real, imag


def table_factor(level, factors):
    return jnp.where(level == 0, factors[0], jnp.where(level == 1, factors[1], factors[2])).astype(FULL)


def table_back(table_ref, level, tops, rests, factor):
    size = table_ref.shape[2]
    total = None
    for at, (top, rest) in enumerate(zip(tops, rests)):
        table = table_ref[level, at * size : (at + 1) * size]
        part = dot(table, top) + dot(table, rest)
        total = part if total is None else total + part
    return total * factor


def two_terms(values):
    top = values.astype(HALF)
    return top, (values - top.astype(FULL)).astype(HALF)


def complex_weights(w_ref, held, blocks, width):
    for layer in range(2):
        for b in range(blocks):
            real, imag = w_ref[layer, 0, b], w_ref[layer, 1, b]
            held[layer, b, :width, :width] = real
            held[layer, b, :width, width:] = imag
            held[layer, b, width:, :width] = -imag
            held[layer, b, width:, width:] = real


def spectral_chunk(scal, table, factors, pieces, spec_w, spec_b, first):
    shards = len(pieces)
    count, per_sample, share = pieces[0].shape
    size = shards * per_sample
    width = spec_w.shape[-1]
    blocks = share // width
    wide = 2 * width

    def body(scal_ref, t_ref, w_ref, b_ref, *refs):
        ins, outs = refs[:shards], refs[shards : 2 * shards]
        spec_ref, hid_ref, fil_ref, weights, held = refs[2 * shards :]

        def bias(layer, b):
            row = pl.ds(scal_ref[SHARD] * blocks + b, 1)
            return jnp.concatenate([b_ref[layer, 0, row], b_ref[layer, 1, row]], axis=1)

        complex_weights(w_ref, weights, blocks, width)
        fill_rows(scal_ref, ins, held)
        levels = [scal_ref[SIDES + SLOTS + first + i] for i in range(count)]
        for i, level in enumerate(levels):
            spectrum = (dot(t_ref[level], held[i]) * table_factor(level, factors)).astype(HALF)
            for b, entry in enumerate(to_blocks(spectrum, blocks, width)):
                spec_ref[b, i * size : (i + 1) * size] = entry
        kept = []
        for b in range(blocks):
            pre_one = dot(spec_ref[b], weights[0, b]) + bias(0, b)
            hidden = jnp.maximum(pre_one, 0.0).astype(HALF)
            hid_ref[b] = hidden
            pre_two = dot(hidden, weights[1, b]) + bias(1, b)
            filtered = jnp.where(
                pre_two > SHRINK, pre_two - SHRINK, jnp.where(pre_two < -SHRINK, pre_two + SHRINK, 0.0)
            )
            top, rest = two_terms(filtered)
            fil_ref[b] = top
            kept.append((top, rest))
        for i, level in enumerate(levels):
            at = slice(i * size, (i + 1) * size)
            tops = from_blocks([top[at] for top, _ in kept], width)
            rests = from_blocks([rest[at] for _, rest in kept], width)
            held[i] = table_back(t_ref, level, tops, rests, table_factor(level, factors)).astype(HALF)
        split_rows(scal_ref, held, outs)

    saved = (blocks, count * size, wide)
    outs = pl.pallas_call(
        body,
        grid_spec=pltpu.PrefetchScalarGridSpec(
            num_scalar_prefetch=1,
            grid=(1,),
            in_specs=[
                whole(table.shape),
                pl.BlockSpec((2, 2, blocks, width, width), lambda i, s: (0, 0, s[SHARD], 0, 0)),
                whole(spec_b.shape),
            ]
            + [whole(pieces[0].shape)] * shards,
            out_specs=[whole(pieces[0].shape)] * shards + [whole(saved)] * 3,
            scratch_shapes=[pltpu.VMEM((2, blocks, wide, wide), HALF), pltpu.VMEM((count, size, share), HALF)],
        ),
        out_shape=[jax.ShapeDtypeStruct(pieces[0].shape, HALF)] * shards + [jax.ShapeDtypeStruct(saved, HALF)] * 3,
        compiler_params=params(),
        cost_estimate=pl.CostEstimate(
            flops=count * size * share * size * 14, bytes_accessed=count * size * share * 16, transcendentals=0
        ),
        name="spectral",
    )(scal, table, spec_w, spec_b, *pieces)
    return outs[:shards], outs[shards:]


def head_chunk(scal, embedded, normed, mixed, targets, head_w, head_b, first, samples, cells):
    shards = len(mixed)
    count, per_sample, share = mixed[0].shape
    rows = count * per_sample
    width, outs = head_w.shape
    at = first // count
    scale_root = float(np.sqrt(np.float32(samples)))

    def body(scal_ref, emb_ref, norm_ref, tgt_ref, w_ref, b_ref, *refs):
        mix_refs, (pred_ref, res_ref, up_ref, bias_ref, held) = refs[:shards], refs[shards:]
        fill_lanes(scal_ref, mix_refs, held)
        side, valid = token_sides(scal_ref, first, count, per_sample, cells)
        updated = (emb_ref[...].astype(FULL) + norm_ref[...].astype(FULL) + held[...].astype(FULL)).astype(HALF)
        output = (dot(updated, w_ref[...]) + b_ref[...]) * valid
        pred_ref[...] = output.astype(HALF).reshape(pred_ref.shape)
        scale = 2.0 / (side.astype(FULL) * scale_root)
        residual = (scale * valid * (output - tgt_ref[...].astype(FULL))).astype(HALF)
        res_ref[...] = residual.reshape(res_ref.shape)
        up_ref[...] = updated
        total = jnp.sum(residual.astype(FULL), axis=0, keepdims=True)
        bias_ref[...] = jnp.broadcast_to(total, bias_ref.shape)

    token_shape = (count, per_sample, outs)
    return pl.pallas_call(
        body,
        grid_spec=pltpu.PrefetchScalarGridSpec(
            num_scalar_prefetch=1,
            grid=(1,),
            in_specs=[
                pl.BlockSpec((rows, width), lambda i, s: (at, 0)),
                pl.BlockSpec((rows, width), lambda i, s: (at, 0)),
                pl.BlockSpec((rows, outs), lambda i, s: (at, 0)),
                whole((width, outs)),
                whole((1, outs)),
            ]
            + [whole(mixed[0].shape)] * shards,
            out_specs=[whole(token_shape), whole(token_shape), whole((rows, width)), whole((8, outs))],
            scratch_shapes=[pltpu.VMEM((rows, width), HALF)],
        ),
        out_shape=[
            jax.ShapeDtypeStruct(token_shape, HALF),
            jax.ShapeDtypeStruct(token_shape, HALF),
            jax.ShapeDtypeStruct((rows, width), HALF),
            jax.ShapeDtypeStruct((8, outs), FULL),
        ],
        compiler_params=params(),
        cost_estimate=pl.CostEstimate(
            flops=2 * rows * width * outs, bytes_accessed=rows * width * 4 + width * outs * 6, transcendentals=0
        ),
        name="head",
    )(scal, embedded, normed, targets, head_w, head_b, *mixed)


def head_gradient(updated, residual):
    width = updated[0].shape[1]
    outs = residual[0].shape[-1]
    count = len(updated)

    def body(*refs):
        total = None
        for up_ref, res_ref in zip(refs[:count], refs[count : 2 * count]):
            part = dot_tn(up_ref[...], res_ref[...].reshape(up_ref.shape[0], outs))
            total = part if total is None else total + part
        refs[-1][...] = total.astype(HALF)

    return pl.pallas_call(
        body,
        out_shape=jax.ShapeDtypeStruct((width, outs), HALF),
        compiler_params=params(),
        cost_estimate=pl.CostEstimate(
            flops=2 * count * updated[0].size * outs, bytes_accessed=2 * count * updated[0].size, transcendentals=0
        ),
        name="head_gradient",
    )(*updated, *residual)


def spectral_back_chunk(scal, table, factors, residual, head_w, spec_w, saved, first, before, last):
    shards = len(residual)
    count, per_sample, outs = residual[0].shape
    size = shards * per_sample
    width = spec_w.shape[-1]
    wide = 2 * width
    share = head_w.shape[0] // shards
    blocks = share // width
    raw_shape = (2, blocks, wide, wide)
    bias_shape = (2 * blocks, wide)
    has_before = before is not None

    def body(scal_ref, t_ref, h_ref, w_ref, spec_ref, hid_ref, fil_ref, *refs):
        ins, refs = refs[:shards], refs[shards:]
        if has_before:
            (old_ref, old_bias_ref), refs = refs[:2], refs[2:]
        pieces, (grad_ref, bias_ref, weights, held, gathered) = refs[:shards], refs[shards:]

        def weight_sums(layer, b, inputs, grads):
            raw = dot_tn(inputs, grads)
            sums = jnp.sum(grads.astype(FULL), axis=0, keepdims=True)
            at = layer * blocks + b
            if has_before:
                raw = raw + old_ref[layer, b]
                sums = sums + old_bias_ref[at : at + 1]
            bias_ref[at : at + 1] = sums
            if not last:
                grad_ref[layer, b] = raw
                return
            real = raw[:width, :width] + raw[width:, width:]
            imag = raw[:width, width:] - raw[width:, :width]
            grad_ref[at * width : (at + 1) * width] = jnp.concatenate([real, imag], axis=1).astype(HALF)

        complex_weights(w_ref, weights, blocks, width)
        fill_rows(scal_ref, ins, gathered)
        levels = [scal_ref[SIDES + SLOTS + first + i] for i in range(count)]
        updated_grad = dot_nt(gathered[...].reshape(count * size, outs), h_ref[...]).astype(HALF)
        entries = []
        for i, level in enumerate(levels):
            filtered_grad = dot(t_ref[level], updated_grad[i * size : (i + 1) * size]) * table_factor(level, factors)
            entries.append(to_blocks(filtered_grad, blocks, width))
        kept = []
        for b in range(blocks):
            entry = jnp.concatenate([e[b] for e in entries], axis=0)
            two_grad = jnp.where(fil_ref[b].astype(FULL) != 0.0, entry, 0.0).astype(HALF)
            hidden = hid_ref[b]
            hidden_grad = dot_nt(two_grad, weights[1, b])
            one_grad = jnp.where(hidden.astype(FULL) > 0.0, hidden_grad, 0.0).astype(HALF)
            kept.append(two_terms(dot_nt(one_grad, weights[0, b])))
            weight_sums(1, b, hidden, two_grad)
            weight_sums(0, b, spec_ref[b], one_grad)
        for i, level in enumerate(levels):
            at = slice(i * size, (i + 1) * size)
            tops = from_blocks([top[at] for top, _ in kept], width)
            rests = from_blocks([rest[at] for _, rest in kept], width)
            held[i] = table_back(t_ref, level, tops, rests, table_factor(level, factors)).astype(HALF)
        split_rows(scal_ref, held, pieces)

    piece = (count, per_sample, share)
    if last:
        grad_out = jax.ShapeDtypeStruct((2 * blocks * width, wide), HALF)
    else:
        grad_out = jax.ShapeDtypeStruct(raw_shape, FULL)
    result = pl.pallas_call(
        body,
        grid_spec=pltpu.PrefetchScalarGridSpec(
            num_scalar_prefetch=1,
            grid=(1,),
            in_specs=[
                whole(table.shape),
                pl.BlockSpec((share, outs), lambda i, s: (s[SHARD], 0)),
                pl.BlockSpec((2, 2, blocks, width, width), lambda i, s: (0, 0, s[SHARD], 0, 0)),
            ]
            + [whole(saved[0].shape)] * 3
            + [whole(residual[0].shape)] * shards
            + ([whole(raw_shape), whole(bias_shape)] if has_before else []),
            out_specs=[whole(piece)] * shards + [whole(grad_out.shape), whole(bias_shape)],
            scratch_shapes=[
                pltpu.VMEM((2, blocks, wide, wide), HALF),
                pltpu.VMEM((count, size, share), HALF),
                pltpu.VMEM((count, size, outs), HALF),
            ],
        ),
        out_shape=[jax.ShapeDtypeStruct(piece, HALF)] * shards
        + [grad_out, jax.ShapeDtypeStruct(bias_shape, FULL)],
        compiler_params=params(),
        cost_estimate=pl.CostEstimate(
            flops=count * size * share * size * 20, bytes_accessed=count * size * share * 16, transcendentals=0
        ),
        name="spectral_back",
    )(scal, table, head_w, spec_w, *saved, *residual, *(before or ()))
    return result[:shards], result[shards:]


def embedded_back_chunk(scal, embedded, stats, residual, head_w, gain, spec_grad, first, cells):
    shards = len(spec_grad)
    count, per_sample, share = spec_grad[0].shape
    rows = count * per_sample
    width, outs = head_w.shape
    at = first // count

    def body(scal_ref, emb_ref, stat_ref, res_ref, w_ref, gain_ref, *refs):
        grad_refs, (out_ref, sums_ref, held) = refs[:shards], refs[shards:]
        fill_lanes(scal_ref, grad_refs, held)
        _, valid = token_sides(scal_ref, first, count, per_sample, cells)
        inv_std = stat_ref[:, 128:129]
        unit = (emb_ref[...].astype(FULL) - stat_ref[:, 0:1]) * inv_std
        direct = dot_nt(res_ref[...].reshape(rows, outs), w_ref[...]).astype(HALF).astype(FULL)
        normed_grad = held[...].astype(FULL) + direct
        gain_grad = jnp.sum(normed_grad * unit, axis=0, keepdims=True)
        unit_grad = normed_grad * gain_ref[...]
        mean_grad = jnp.mean(unit_grad, axis=-1, keepdims=True)
        mean_cross = jnp.mean(unit_grad * unit, axis=-1, keepdims=True)
        input_grad = inv_std * (unit_grad - mean_grad - unit * mean_cross)
        result = ((input_grad + direct) * valid).astype(HALF)
        out_ref[...] = result
        bias_grad = jnp.sum(result.astype(FULL), axis=0, keepdims=True)
        sums_ref[0:4] = jnp.broadcast_to(gain_grad, (4, width))
        sums_ref[4:8] = jnp.broadcast_to(bias_grad, (4, width))

    return pl.pallas_call(
        body,
        grid_spec=pltpu.PrefetchScalarGridSpec(
            num_scalar_prefetch=1,
            grid=(1,),
            in_specs=[
                pl.BlockSpec((rows, width), lambda i, s: (at, 0)),
                pl.BlockSpec((rows, 256), lambda i, s: (at, 0)),
                whole((count, per_sample, outs)),
                whole((width, outs)),
                whole((1, width)),
            ]
            + [whole(spec_grad[0].shape)] * shards,
            out_specs=[whole((rows, width)), whole((8, width))],
            scratch_shapes=[pltpu.VMEM((rows, width), HALF)],
        ),
        out_shape=[jax.ShapeDtypeStruct((rows, width), HALF), jax.ShapeDtypeStruct((8, width), FULL)],
        compiler_params=params(),
        cost_estimate=pl.CostEstimate(
            flops=2 * rows * width * outs, bytes_accessed=rows * width * 6, transcendentals=0
        ),
        name="embedded_back",
    )(scal, embedded, stats, residual, head_w, gain, *spec_grad)


def embed_grad_parts(scal, turned, grads, groups, away):
    pairs, block, tokens = turned[0].shape
    chunk_rows, width = grads[0].shape
    half = width // 2
    top = pairs // 2
    count = len(turned)
    depth = tokens * count

    def relative(unit):
        return jnp.where(unit < top, 2 * unit + away, unit - top + away * top)

    def body(scal_ref, *refs):
        turned_refs, grad_refs = refs[:count], refs[count : count + len(grads)]
        left_ref, right_ref, held = refs[count + len(grads) :]
        unit = pl.program_id(0)

        @pl.when(unit % top == 0)
        def _():
            for i, ref in enumerate(grad_refs):
                held[i * chunk_rows : (i + 1) * chunk_rows] = ref[...]

        rows = jnp.concatenate([ref[0] for ref in turned_refs], axis=1)
        total = dot(rows, held[...]).astype(HALF)

        @pl.when(unit < top)
        def _():
            left_ref[0] = total

        @pl.when(unit >= top)
        def _():
            right_ref[0] = total

    shape = (top, block, half)
    return pl.pallas_call(
        body,
        grid_spec=pltpu.PrefetchScalarGridSpec(
            num_scalar_prefetch=1,
            grid=(pairs,),
            in_specs=[
                pl.BlockSpec((1, block, tokens), lambda i, s: (jnp.bitwise_xor(s[GROUP] // 2, relative(i)), 0, 0))
                for _ in turned
            ]
            + [pl.BlockSpec((chunk_rows, half), lambda i, s: (0, i // top)) for _ in grads],
            out_specs=[
                pl.BlockSpec((1, block, half), lambda i, s: (jnp.minimum(i, top - 1), 0, 0)),
                pl.BlockSpec((1, block, half), lambda i, s: (jnp.maximum(i - top, 0), 0, 0)),
            ],
            scratch_shapes=[pltpu.VMEM((depth, half), HALF)],
        ),
        out_shape=[jax.ShapeDtypeStruct(shape, HALF)] * 2,
        compiler_params=params(),
        cost_estimate=pl.CostEstimate(
            flops=depth * pairs * block * width,
            bytes_accessed=pairs * block * (2 * depth + width) + depth * width,
            transcendentals=0,
        ),
        name="embed_grad",
    )(scal, *turned, *grads)


def swap_bit(values, bit, groups):
    return lax.ppermute(values, "grp", [(g, g ^ (1 << bit)) for g in range(groups)])


def across(pieces):
    shards = len(pieces)
    return [pieces[0]] + [
        lax.ppermute(pieces[k], "fft", [(z, z ^ k) for z in range(shards)]) for k in range(1, shards)
    ]


def add_half(left, right):
    return (left.astype(FULL) + right.astype(FULL)).astype(HALF)


def scatter_start(received, kept, groups):
    bits = groups.bit_length() - 1
    ends = []
    for first, keep, order, low in (
        (received[0], kept[0], list(range(2, bits)), True),
        (received[1], kept[1], list(range(bits - 2, 0, -1)), False),
    ):
        total = add_half(keep, first)
        for bit in order:
            count, block, width = total.shape
            if low:
                split = total.reshape(count // 2, 2, block, width)
                keep, send = split[:, 0], split[:, 1]
            else:
                split = total.reshape(2, count // 2, block, width)
                keep, send = split[0], split[1]
            total = add_half(keep, swap_bit(send, bit, groups))
        ends.append(total[0])
    return ends


def scatter_step(part, bit, shards, shard_at):
    split = part.reshape(part.shape[0] // 2, 2, *part.shape[1:])
    mine = (shard_at // bit) % 2
    keep = lax.dynamic_index_in_dim(split, mine, 1, keepdims=False)
    send = lax.dynamic_index_in_dim(split, 1 - mine, 1, keepdims=False)
    received = lax.ppermute(send, "fft", [(z, z ^ bit) for z in range(shards)])
    return keep.astype(FULL) + received.astype(FULL)


def from_same_core(values, groups):
    return [values] + [
        lax.ppermute(values, "grp", [(g, g ^ k) for g in range(groups)]) for k in range(2, groups, 2)
    ]


def hi_lo(values):
    high = values.astype(HALF)
    return jnp.concatenate([high, (values - high.astype(FULL)).astype(HALF)], axis=0)


def from_hi_lo(values):
    half = values.shape[0] // 2
    values = values.astype(FULL)
    return values[:half] + values[half:]


def one_step(body, name, operands, out_shape):
    return pl.pallas_call(
        body,
        grid_spec=pltpu.PrefetchScalarGridSpec(
            num_scalar_prefetch=1,
            grid=(1,),
            in_specs=[whole(o.shape) for o in operands[1:]],
            out_specs=[whole(o.shape) for o in out_shape],
        ),
        out_shape=out_shape,
        compiler_params=params(),
        name=name,
    )(*operands)


def packed(routes, head_grad, spec_grad, predicted, groups):
    outs = head_grad.shape[1]
    head_rows, spec_rows = head_grad.shape[0] // groups, spec_grad.shape[0] // groups
    count, per_sample, _ = predicted[0].shape

    def body(routes_ref, head_ref, spec_ref, *refs):
        pred_refs, out_ref = refs[:-1], refs[-1]
        for g in range(groups):
            out_ref[g, :head_rows] = head_ref[g * head_rows : (g + 1) * head_rows]
            out_ref[g, head_rows : head_rows + spec_rows] = spec_ref[g * spec_rows : (g + 1) * spec_rows]
            chosen = routes_ref[ROUTES + g]
            for c, ref in enumerate(pred_refs):

                @pl.when(chosen // count == c)
                def _(g=g, c=c, ref=ref, chosen=chosen):
                    out_ref[g, head_rows + spec_rows :] = ref[chosen - c * count]

    shape = (groups, head_rows + spec_rows + per_sample, outs)
    return one_step(
        body, "packed", (routes, head_grad, spec_grad, *predicted), [jax.ShapeDtypeStruct(shape, HALF)]
    )[0]


def group_sums(routes, moved, spec_bias, head_sums, row_sums, slot_count, per_sample):
    groups, rows, outs = moved.shape
    weight_rows = rows - per_sample
    own_rows = spec_bias.shape[0]
    chunks = len(head_sums)
    parts = row_sums[0].shape[1] // outs
    spare = 16 - own_rows - 2 * parts - 1

    def body(routes_ref, moved_ref, bias_ref, *refs):
        head_refs, row_refs, (out_ref, pred_ref) = refs[:chunks], refs[chunks : 2 * chunks], refs[2 * chunks :]
        total = moved_ref[0, :weight_rows].astype(FULL)
        for g in range(1, groups):
            total = total + moved_ref[g, :weight_rows].astype(FULL)
        out_ref[:weight_rows] = total.astype(HALF)
        lines = [bias_ref[...]]
        for row in (0, 4):
            line = sum(ref[row : row + 1] for ref in row_refs)
            lines += [line[:, i * outs : (i + 1) * outs] for i in range(parts)]
        lines += [sum(ref[0:1] for ref in head_refs), jnp.zeros((spare, outs), FULL)]
        out_ref[weight_rows:] = hi_lo(jnp.concatenate(lines, axis=0))
        for i in range(slot_count):
            pred_ref[i] = moved_ref[routes_ref[ROUTES + groups + i], weight_rows:]

    return one_step(
        body,
        "group_sums",
        (routes, moved, spec_bias, *head_sums, *row_sums),
        [
            jax.ShapeDtypeStruct((weight_rows + 32, outs), HALF),
            jax.ShapeDtypeStruct((slot_count, per_sample, outs), HALF),
        ],
    )


def shard_sums(routes, rows, head_rows, spec_rows, own_rows):
    shards = len(rows)
    outs = rows[0].shape[1]
    small_rows = 32

    def body(routes_ref, *refs):
        ins, out_ref = refs[:-1], refs[-1]
        total = sum(ref[:head_rows].astype(FULL) for ref in ins)
        out_ref[:head_rows] = total.astype(HALF)
        for k, ref in enumerate(ins):
            at = head_rows + k * spec_rows
            out_ref[at : at + spec_rows] = ref[head_rows : head_rows + spec_rows]
        smalls = [from_hi_lo(ref[head_rows + spec_rows :]) for ref in ins]
        lines = []
        for z in range(shards):
            here = [jnp.bitwise_xor(routes_ref[SHARD], k) == z for k in range(shards)]
            lines.append(sum(jnp.where(h, v[:own_rows], 0.0) for h, v in zip(here, smalls)))
        lines.append(sum(v[own_rows:] for v in smalls))
        have = shards * own_rows + 16 - own_rows
        lines.append(jnp.zeros((small_rows - have, outs), FULL))
        out_ref[head_rows + shards * spec_rows :] = hi_lo(jnp.concatenate(lines, axis=0))

    shape = (head_rows + shards * spec_rows + 2 * small_rows, outs)
    return one_step(body, "shard_sums", (routes, *rows), [jax.ShapeDtypeStruct(shape, HALF)])[0]


def assembled(scal, gathered, head_rows, shards, blocks, width):
    groups = len(gathered)
    total_blocks = shards * blocks
    spec_rows = 2 * blocks * width // groups
    small_at = head_rows + shards * spec_rows
    small_rows = (gathered[0].shape[0] - small_at) // 2

    def body(scal_ref, *refs):
        ins, (head_ref, spec_ref, bias_ref, gain_ref, embed_ref, out_ref) = refs[:groups], refs[groups:]
        small = None
        for k, ref in enumerate(ins):
            group = jnp.bitwise_xor(scal_ref[GROUP], k)
            at = pl.ds(pl.multiple_of(group * head_rows, head_rows), head_rows)
            head_ref[at, :] = ref[:head_rows].astype(FULL)
            start = group * spec_rows
            layer, b = start // (blocks * width), (start // width) % blocks
            rows = pl.ds(pl.multiple_of(start % width, spec_rows), spec_rows)
            for j in range(shards):
                values = ref[head_rows + j * spec_rows : head_rows + (j + 1) * spec_rows].astype(FULL)
                z = jnp.bitwise_xor(scal_ref[SHARD], j)
                spec_ref[layer, 0, z * blocks + b, rows] = values[:, :width]
                spec_ref[layer, 1, z * blocks + b, rows] = values[:, width:]
            part = ref[small_at : small_at + small_rows].astype(FULL) + ref[small_at + small_rows :].astype(FULL)
            small = part if small is None else small + part
        for z in range(shards):
            for layer in range(2):
                for b in range(blocks):
                    row = (z * 2 + layer) * blocks + b
                    for p in range(2):
                        bias_ref[layer, p, z * blocks + b : z * blocks + b + 1] = small[
                            row : row + 1, p * width : (p + 1) * width
                        ]
        row = shards * 2 * blocks
        quarter = gain_ref.shape[1] // (2 * width)
        for ref in (gain_ref, embed_ref):
            for i in range(quarter):
                ref[:, i * 2 * width : (i + 1) * 2 * width] = small[row + i : row + i + 1]
            row += quarter
        out_ref[...] = small[row : row + 1]

    out_shape = [
        jax.ShapeDtypeStruct((groups * head_rows, 2 * width), FULL),
        jax.ShapeDtypeStruct((2, 2, total_blocks, width, width), FULL),
        jax.ShapeDtypeStruct((2, 2, total_blocks, width), FULL),
        jax.ShapeDtypeStruct((1, groups * head_rows), FULL),
        jax.ShapeDtypeStruct((1, groups * head_rows), FULL),
        jax.ShapeDtypeStruct((1, 2 * width), FULL),
    ]
    return pl.pallas_call(
        body,
        grid_spec=pltpu.PrefetchScalarGridSpec(
            num_scalar_prefetch=1,
            grid=(1,),
            in_specs=[whole(gathered[0].shape)] * groups,
            out_specs=[whole(o.shape) for o in out_shape],
        ),
        out_shape=out_shape,
        compiler_params=params(),
        name="assembled",
    )(scal, *gathered)


def prediction_routes(dest_group, group_at, groups, slot_count):
    own_dest = lax.dynamic_slice_in_dim(dest_group, group_at * slot_count, slot_count)
    loaders = jnp.arange(groups, dtype=jnp.int32)
    slots = jnp.arange(slot_count, dtype=jnp.int32)
    chosen = jnp.sum(jnp.where(own_dest[None, :] == loaders[:, None], slots[None, :], 0), axis=1)
    holds = jnp.any(dest_group.reshape(groups, slot_count) == group_at, axis=1)
    rank = jnp.sum(jnp.where(holds[None, :] & (loaders[None, :] < loaders[:, None]), 1, 0), axis=1)
    sources = jnp.sum(jnp.where(holds[None, :] & (rank[None, :] == slots[:, None]), loaders[None, :], 0), axis=1)
    return jnp.concatenate([chosen, sources]).astype(jnp.int32)


def on_device(
    patches, targets, grid_side, dest_group, embed_w, embed_b, gain, spec_w, spec_b, head_w, head_b
):
    slot_count, row_count, cells, depth = patches.shape
    samples = dest_group.shape[0]
    groups = lax.axis_size("grp")
    shards = lax.axis_size("fft")
    group_at = lax.axis_index("grp").astype(jnp.int32)
    shard_at = lax.axis_index("fft").astype(jnp.int32)
    outs = targets.shape[-1]
    per_sample = row_count * cells
    count = slot_count // CHUNKS
    firsts = [c * count for c in range(CHUNKS)]
    assert slot_count == SLOTS

    sides = lax.dynamic_slice_in_dim(grid_side, group_at * slot_count, slot_count)
    level = jnp.where(sides == cells, 0, jnp.where(sides == cells // 2, 1, 2)).astype(jnp.int32)
    place = jnp.stack([shard_at, shard_at * row_count, group_at])
    scal = jnp.concatenate([place, sides, level])
    routes = jnp.concatenate([place, prediction_routes(dest_group, group_at, groups, slot_count)])
    table_values, factors = dft_tables(cells)
    table = jnp.asarray(table_values)
    flat_patches = patches.reshape(-1, depth)
    flat_targets = targets.reshape(-1, outs)
    gain_row, embed_b_row, head_b_row = gain[None], embed_b[None], head_b[None]

    embedded, normed, stats, turned_send, turned_keep, pieces = embed(
        scal, flat_patches, embed_w, embed_b_row, gain_row, firsts, count, per_sample, cells, shards, groups
    )
    moved = [across(p) for p in pieces]
    mixed, saved = [], []
    for first, values in zip(firsts, moved):
        out, rest = spectral_chunk(scal, table, factors, values, spec_w, spec_b, first)
        mixed.append(across(out))
        saved.append(rest)
    predicted, residual, updated, head_sums, gathered = [], [], [], [], []
    for first, mix in zip(firsts, mixed):
        pred, res, up, sums = head_chunk(
            scal, embedded, normed, mix, flat_targets, head_w, head_b_row, first, samples, cells
        )
        predicted.append(pred)
        residual.append(res)
        updated.append(up)
        head_sums.append(sums)
        gathered.append(across([res] * shards))
    head_grad, gathered[0] = lax.optimization_barrier((head_gradient(updated, residual), gathered[0]))
    spec_back, sums = [], None
    for first, res, rest in zip(firsts, gathered, saved):
        values, sums = spectral_back_chunk(
            scal, table, factors, res, head_w, spec_w, rest, first, sums, first == firsts[-1]
        )
        if first == firsts[-1]:
            values, turned_send = lax.optimization_barrier((values, turned_send))
        spec_back.append(across(values))
    turned = [turned_keep, swap_bit(turned_send, 0, groups)]
    spec_grad, spec_bias = sums
    width = spec_w.shape[-1]
    blocks = spec_w.shape[2] // shards
    head_rows = head_w.shape[0] // groups
    own_grads, other_grads, row_sums = [], [], []
    for first, res, back in zip(firsts, residual, spec_back):
        grad, row_sum = embedded_back_chunk(scal, embedded, stats, res, head_w, gain_row, back, first, cells)
        own_grads.append(grad)
        other_grads.append(swap_bit(grad, 0, groups))
        row_sums.append(row_sum)
    grads = own_grads + other_grads
    sent = embed_grad_parts(scal, turned, grads, groups, 1)
    sent, kept_turned = lax.optimization_barrier((sent, turned))
    top_bit = groups.bit_length() - 2
    received = [swap_bit(sent[0], 1, groups), swap_bit(sent[1], top_bit, groups)]
    kept = embed_grad_parts(scal, kept_turned, grads, groups, 0)
    _, head_grad, spec_grad = lax.optimization_barrier((sent, head_grad, spec_grad))
    weight_sums = lax.all_to_all(
        packed(routes, head_grad, spec_grad, predicted, groups), "grp", split_axis=0, concat_axis=0, tiled=True
    )
    kept, weight_sums = lax.optimization_barrier((kept, weight_sums))
    ends = scatter_start(received, kept, groups)
    small, predictions = group_sums(routes, weight_sums, spec_bias, head_sums, row_sums, slot_count, per_sample)
    predictions = predictions.reshape(targets.shape)
    spec_rows = spec_grad.shape[0] // groups
    outgoing = shard_sums(routes, across([small] * shards), head_rows, spec_rows, spec_bias.shape[0])
    ends, outgoing = lax.optimization_barrier((ends, outgoing))
    part = jnp.concatenate(ends, axis=-1)
    part = part.reshape(shards, part.shape[0] // shards, -1)
    part = scatter_step(part, 1, shards, shard_at)
    even = from_same_core(outgoing, groups)
    bit = 2
    while bit < shards:
        part = part.astype(HALF)
        if bit == 2:
            _, even = lax.optimization_barrier((part, even))
        part = scatter_step(part, bit, shards, shard_at)
        bit *= 2
    embed_grad = part[0]
    gathered = [v for pair in zip(even, [swap_bit(v, 0, groups) for v in even]) for v in pair]
    head_grad, spec_w_grad, spec_b_grad, gain_grad, embed_bias_grad, head_bias_grad = assembled(
        scal, gathered, head_rows, shards, blocks, width
    )
    gain_grad, embed_bias_grad, head_bias_grad = gain_grad[0], embed_bias_grad[0], head_bias_grad[0]
    return (
        predictions,
        embed_grad,
        embed_bias_grad,
        gain_grad,
        spec_w_grad,
        spec_b_grad,
        head_grad,
        head_bias_grad,
    )


def solution(mesh):
    return jax.shard_map(
        on_device,
        mesh=mesh,
        in_specs=(
            P("grp", "fft", None, None),
            P("grp", "fft", None, None),
            P(),
            P(),
            P(),
            P(),
            P(),
            P(),
            P(),
            P(),
            P(),
        ),
        out_specs=(
            P("grp", "fft", None, None),
            P(("grp", "fft"), None),
            P(),
            P(),
            P(),
            P(),
            P(),
            P(),
        ),
        check_vma=False,
    )
```
